128 devices in a mesh: ctx: 16 (over z, x_lo, core), fsdp: 8 (over y, x_hi).
Axes of the slice: x: 4 (x_hi: 2, x_lo: 2; x = x_hi * 2 + x_lo), y: 4, z: 4, core: 2. Of those that a mesh axis runs over, the one named last changes fastest.
Arguments:
- hidden: bfloat16 [8, 2048, 2048], P('fsdp', 'ctx'), may hold values from -6 to 6
- positions: int32 [8, 2048], P('fsdp', 'ctx'), may hold values from 0 to 2047, as said below
- gain_attn: bfloat16 [2048], replicated, may hold values from 0.5 to 1.5
- w_qkv: bfloat16 [2560, 2048], P('fsdp'), may hold values from -0.125 to 0.125
- w_out: bfloat16 [2048, 2048], P('fsdp'), may hold values from -3 to 3
- gain_mlp: bfloat16 [2048], replicated, may hold values from 0.5 to 1.5
- w_gate_up: bfloat16 [2, 5632, 2048], P(None, 'fsdp'), may hold values from -0.125 to 0.125
- w_down: bfloat16 [2048, 5632], P(None, 'fsdp'), may hold values from -0.078125 to 0.078125
- cotangent: bfloat16 [8, 2048, 2048], P('fsdp', 'ctx'), may hold values from -6 to 6
Outputs:
- output: bfloat16 [8, 2048, 2048], P('fsdp', 'ctx')
- grad_hidden: float32 [8, 2048, 2048], P('fsdp', 'ctx')
- grad_gain_attn: float32 [2048], P('fsdp')
- grad_w_qkv: float32 [2560, 2048], P('fsdp')
- grad_w_out: float32 [2048, 2048], P('fsdp')
- grad_gain_mlp: float32 [2048], P('fsdp')
- grad_w_gate_up: float32 [2, 5632, 2048], P(None, 'fsdp')
- grad_w_down: float32 [2048, 5632], P(None, 'fsdp')
The draws below stay inside these ranges and needn't reach their ends.
Inputs may be any that keep to these rules, and one draw needn't show every extreme that they name: Each row lists the positions of one sequence's stored tokens: a permutation of 0 to 2047 made of runs of 64 consecutive rising values, each run starting at a multiple of 64.
All inputs are finite; a program needn't handle non-finite values.
Results may differ from the reference program's by a relative error of at most 0.03.
Values may be sent and summed in bfloat16 or wider, within the bound.
A program may use at most 384 MiB of HBM per device.

```python
import jax
import jax.numpy as jnp
from jax import lax

D = 2048
H = 32
KV = 4
HD = 64
FF = 5632
TOK_DEV = 128
LEN = 2048
SEQS = 8
QKV = 2560


def draw_positions(key, part):
    key = jax.random.fold_in(key, 7)
    half_run = TOK_DEV // 2
    block_count = LEN // half_run
    seq_keys = jax.random.split(key, SEQS)

    def one_order(seq_key):
        return jax.random.permutation(seq_key, block_count)
    orders = jax.vmap(one_order)(seq_keys).astype(jnp.int32)
    run_values = orders[:, :, None] * half_run + jnp.arange(half_run, dtype=jnp.int32)[None, None, :]
    return run_values.reshape(SEQS, LEN).astype(jnp.int32)


def level_of(stream_key, dims, cuts, low, top_value):
    factor_of, own = 1.0, jax.random.fold_in(stream_key, 6)
    for dim, blocks in cuts:
        draws = jnp.exp(jax.random.uniform(jax.random.fold_in(own, dim), (blocks,), jnp.float32, low / len(cuts), top_value / len(cuts)))
        factor_of = factor_of * jnp.repeat(draws, dims[dim] // blocks).reshape([-1 if axis == dim else 1 for axis in range(len(dims))])
    return factor_of


def gaussian(own_key, dims, deviation, limit, cuts=(), held_as=jnp.bfloat16):
    level = level_of(own_key, dims, cuts, -0.22, 0.18) if cuts else 1.0
    drawn = jax.random.normal(own_key, dims, jnp.float32) * deviation * level
    return jnp.minimum(jnp.maximum(drawn, -limit), limit).astype(held_as)


def setup_inputs(seed: int = 0) -> dict:
    streams_of = jax.random.split(jax.random.key(seed), 10)
    hidden = gaussian(streams_of[0], (SEQS, LEN, D), 1.0, 6.0, ((0, 8), (1, 16)))
    positions = draw_positions(jax.random.fold_in(streams_of[9], 71), 0)
    gain_attn = jnp.clip(1.0 + 0.1 * jax.random.normal(streams_of[2], (D,), jnp.float32), 0.5, 1.5).astype(jnp.bfloat16)
    w_qkv = gaussian(streams_of[3], (QKV, D), D ** -0.5, 0.125, ((0, 8),))
    w_out = gaussian(streams_of[4], (D, H * HD), (max(1, 4 * H * HD // LEN)) ** -0.5, 3.0, ((0, 8),))
    gain_mlp = jnp.clip(1.0 + 0.1 * jax.random.normal(streams_of[5], (D,), jnp.float32), 0.5, 1.5).astype(jnp.bfloat16)
    w_gate_up = gaussian(streams_of[6], (2, FF, D), D ** -0.5, 0.125, ((1, 8),))
    w_down = gaussian(streams_of[7], (D, FF), FF ** -0.5, 0.078125, ((1, 8),))
    cotangent = gaussian(streams_of[8], (SEQS, LEN, D), 1.0, 6.0, ((0, 8), (1, 16)))
    return dict(hidden=hidden, positions=positions, gain_attn=gain_attn, w_qkv=w_qkv, w_out=w_out, gain_mlp=gain_mlp, w_gate_up=w_gate_up, w_down=w_down, cotangent=cotangent)


EPSILON = 1e-05
FILLER = -1e+30
HIGHEST = lax.Precision.HIGHEST

@jax.custom_vjp
def low(v):
    return lax.optimization_barrier(v.astype(jnp.bfloat16)).astype(jnp.float32)

@jax.custom_vjp
def low_back(v):
    return v

def low_keep(v):
    return (low(v), None)

def low_pass(kept, grad):
    return (grad,)

def back_keep(v):
    return (v, None)

def back_low(kept, grad):
    return (low(grad),)
low.defvjp(low_keep, low_pass)
low_back.defvjp(back_keep, back_low)

def rotary(values_in, cosine, sine_part):
    half_width = values_in.shape[-1] // 2
    turned = jnp.concatenate([-values_in[..., half_width:], values_in[..., :half_width]], axis=-1)
    return values_in * cosine + turned * sine_part

def angles(places):
    steps_half = jnp.arange(HD // 2, dtype=jnp.float32)
    inverse = jnp.power(10000.0, steps_half * (-2.0 / HD))
    turning = places.astype(jnp.float32)[:, None] * inverse[None, :]
    turning = jnp.concatenate([turning, turning], axis=-1)
    return (jnp.cos(turning), jnp.sin(turning))

def normalize(values_in):
    inverse = lax.rsqrt(lax.optimization_barrier(jnp.mean(values_in * values_in, axis=-1, keepdims=True)) + EPSILON)
    return values_in * inverse

def attention(query_heads, key_heads, value_heads, places):
    group_size = H // KV
    keys_wide = jnp.repeat(key_heads, group_size, axis=1)
    values_wide = jnp.repeat(value_heads, group_size, axis=1)
    length = places.shape[0]
    block_rows = min(512, length)
    queries = query_heads.reshape(length // block_rows, block_rows, H, HD)
    query_places = places.reshape(length // block_rows, block_rows)
    factor = HD ** (-0.5)

    @jax.checkpoint
    def one_block(pieces):
        query_block, place_block = pieces
        scores = low_back(jnp.einsum('qhd,khd->hqk', query_block, keys_wide, precision=HIGHEST) * factor)
        allowed = places[None, None, :] <= place_block[None, :, None]
        scores = jnp.where(allowed, scores, FILLER)
        shifted = jnp.exp(scores - lax.optimization_barrier(jnp.max(scores, axis=-1, keepdims=True)))
        weights = low(shifted / lax.optimization_barrier(jnp.sum(shifted, axis=-1, keepdims=True)))
        return jnp.einsum('hqk,khd->qhd', weights, values_wide, precision=HIGHEST)
    return lax.map(one_block, (queries, query_places)).reshape(length, H * HD)

def layer(tokens, places, gain_attn, w_qkv, w_out, gain_mlp, w_gate_up, w_down):
    length = tokens.shape[0]
    width_q = H * HD
    width_kv = KV * HD
    input_one = low(normalize(tokens) * gain_attn)
    projected = low_back(jnp.dot(input_one, w_qkv.T, precision=HIGHEST))
    cosine, sine_part = angles(places)
    cosine = cosine[:, None, :]
    sine_part = sine_part[:, None, :]
    query_heads = low(rotary(projected[:, :width_q].reshape(length, H, HD), cosine, sine_part))
    key_heads = low(rotary(projected[:, width_q:width_q + width_kv].reshape(length, KV, HD), cosine, sine_part))
    value_heads = low(projected[:, width_q + width_kv:].reshape(length, KV, HD))
    attended = low(low_back(attention(query_heads, key_heads, value_heads, places)))
    middle = tokens + low_back(jnp.dot(attended, w_out.T, precision=HIGHEST))
    input_two = low(normalize(middle) * gain_mlp)
    gate_values = low_back(jnp.dot(input_two, w_gate_up[0].T, precision=HIGHEST))
    upward = low_back(jnp.dot(input_two, w_gate_up[1].T, precision=HIGHEST))
    active = low(gate_values * jax.nn.sigmoid(gate_values) * upward)
    return middle + low_back(jnp.dot(active, w_down.T, precision=HIGHEST))

def reference(hidden, positions, gain_attn, w_qkv, w_out, gain_mlp, w_gate_up, w_down, cotangent):
    params = (gain_attn.astype(jnp.float32), w_qkv.astype(jnp.float32), w_out.astype(jnp.float32), gain_mlp.astype(jnp.float32), w_gate_up.astype(jnp.float32), w_down.astype(jnp.float32))

    def one_sequence(totals, inputs):
        tokens, places, pulled = inputs

        def forward(tokens_in, gain_one, qkv_one, out_one, gain_two, gate_up_one, down_one):
            return layer(tokens_in, places, gain_one, qkv_one, out_one, gain_two, gate_up_one, down_one)
        result, pullback = jax.vjp(forward, tokens.astype(jnp.float32), *params)
        gradients = pullback(pulled.astype(jnp.float32))
        totals = tuple((earlier + latest for earlier, latest in zip(totals, gradients[1:])))
        return (totals, (result.astype(jnp.bfloat16), gradients[0]))
    zero_sums = tuple((jnp.zeros_like(matrix) for matrix in params))
    totals, (outputs, grad_tokens) = lax.scan(one_sequence, zero_sums, (hidden, positions, cotangent))
    return (outputs, grad_tokens, totals[0], totals[1], totals[2], totals[3], totals[4], totals[5])
```

```python
import jax
import jax.numpy as jnp
from jax import lax
from jax.experimental import pallas as pl
from jax.experimental.pallas import tpu as pltpu
from jax.sharding import Mesh
from jax.sharding import PartitionSpec as P

D = 2048
H = 32
KV = 4
HD = 64
FF = 5632
TOK = 128
HALF = 64
FF_DEV = 704
Q_DEV = 256
EPSILON = 1e-05
FILLER = -1e30
AXES = ("z", "xl", "c", "y", "xh")
ANY = pl.BlockSpec(memory_space=pl.ANY)
VMEM = pl.BlockSpec(memory_space=pltpu.VMEM)
BF16 = jnp.bfloat16
F32 = jnp.float32


class Place:
    def __init__(self):
        self.z, self.xl, self.c, self.y, self.xh = (lax.axis_index(a) for a in AXES)

    def at(self, dz=0, dy=0, core=None, xl=None, xh=None, y=None):
        z = lax.rem(self.z + dz + 4, 4) if dz else self.z
        y = (lax.rem(self.y + dy + 4, 4) if dy else self.y) if y is None else y
        return (
            z,
            self.xl if xl is None else xl,
            self.c if core is None else core,
            y,
            self.xh if xh is None else xh,
        )


class Edges:
    def __init__(self, send, recv):
        self.send, self.recv, self.count, self.started = send, recv, 0, []

    def copy(self, src, dst, device, start=True):
        i = self.count
        self.count += 1
        d = pltpu.make_async_remote_copy(
            src_ref=src,
            dst_ref=dst,
            send_sem=self.send.at[i],
            recv_sem=self.recv.at[i],
            device_id=device,
            device_id_type=pl.DeviceIdType.MESH,
        )
        self.started.append(d)
        if start:
            d.start()
        return d

    def finish(self):
        for d in self.started:
            d.wait_send()


def greet(devices):
    barrier = pltpu.get_barrier_semaphore()
    for device in devices:
        pl.semaphore_signal(
            barrier, inc=1, device_id=device, device_id_type=pl.DeviceIdType.MESH
        )
    pl.semaphore_wait(barrier, len(devices))


def group_members(me):
    found = [me.at(core=1 - me.c)]
    for dy in (1, 2, 3):
        found += [me.at(dy=dy), me.at(dy=dy, core=1 - me.c)]
    return found


class RingGather:
    def __init__(self, me, edges, own, out):
        self.me, self.edges, self.out = me, edges, out
        self.core = me.at(core=1 - me.c)
        self.up, self.down = me.at(dy=1), me.at(dy=-1)
        a, b = pl.ds(0, HALF), pl.ds(HALF, HALF)
        self.a, self.b = a, b
        mine = self.slot(0)
        self.up_a = edges.copy(own.at[a], out.at[mine, a], self.up)
        self.down_b = edges.copy(own.at[b], out.at[mine, b], self.down)
        self.up_b = edges.copy(own.at[b], out.at[mine, b], self.up)
        self.down_a = edges.copy(own.at[a], out.at[mine, a], self.down)
        self.to_core = [edges.copy(own, out.at[mine], self.core)]

    def slot(self, dy):
        return 2 * lax.rem(self.me.y + dy + 4, 4) + self.me.c

    def pass_core(self, dy, part):
        ref = self.out.at[self.slot(dy), part]
        self.to_core.append(self.edges.copy(ref, ref, self.core))

    def relay(self):
        out = self.out
        self.up_a.wait_recv()
        ref = out.at[self.slot(-1), self.a]
        self.on_a = self.edges.copy(ref, ref, self.up)
        self.down_b.wait_recv()
        ref = out.at[self.slot(1), self.b]
        self.on_b = self.edges.copy(ref, ref, self.down)
        self.pass_core(-1, self.a)
        self.pass_core(1, self.b)

    def rest(self):
        self.up_b.wait_recv()
        self.pass_core(-1, self.b)
        self.down_a.wait_recv()
        self.pass_core(1, self.a)
        self.on_a.wait_recv()
        self.pass_core(2, self.a)
        self.on_b.wait_recv()
        self.pass_core(2, self.b)
        for d in self.to_core:
            d.wait_recv()


GATHER_EDGES = 13


class RingScatter:
    def __init__(self, me, edges, parts, got, both, relayed, last):
        self.me, self.edges, self.parts = me, edges, parts
        self.got, self.both, self.relayed, self.last = got, both, relayed, last
        self.up, self.down = me.at(dy=1), me.at(dy=-1)
        self.from_core = {}
        for k in (2, 1, 3, 0):
            row = 2 * lax.rem(me.y + k, 4) + 1 - me.c
            self.from_core[k] = edges.copy(
                parts.at[row], got.at[k], me.at(core=1 - me.c)
            )

    def add_core(self, k):
        self.from_core[k].wait_recv()
        row = 2 * lax.rem(self.me.y + k, 4) + self.me.c
        self.both[k] = (
            self.parts[row].astype(F32) + self.got[k].astype(F32)
        ).astype(BF16)

    def first(self):
        a, b = pl.ds(0, HALF), pl.ds(HALF, HALF)
        e, both = self.edges, self.both
        self.add_core(2)
        self.r_a = e.copy(both.at[2, a], self.relayed.at[0], self.up)
        self.r_b = e.copy(both.at[2, b], self.relayed.at[1], self.down)
        self.add_core(1)
        self.u_b = e.copy(both.at[1, b], self.last.at[0, b], self.up)
        self.add_core(3)
        self.d_a = e.copy(both.at[3, a], self.last.at[1, a], self.down)
        self.add_core(0)

    def second(self):
        a, b = pl.ds(0, HALF), pl.ds(HALF, HALF)
        e, both = self.edges, self.both
        self.r_a.wait_recv()
        both[1, a] = (both[1, a].astype(F32) + self.relayed[0].astype(F32)).astype(BF16)
        self.u_a = e.copy(both.at[1, a], self.last.at[0, a], self.up)
        self.r_b.wait_recv()
        both[3, b] = (both[3, b].astype(F32) + self.relayed[1].astype(F32)).astype(BF16)
        self.d_b = e.copy(both.at[3, b], self.last.at[1, b], self.down)

    def total(self, out):
        for d in (self.u_b, self.d_a, self.u_a, self.d_b):
            d.wait_recv()
        out[...] = (
            self.both[0].astype(F32)
            + self.last[0].astype(F32)
            + self.last[1].astype(F32)
        )


SCATTER_EDGES = 10


def scatter_scratch():
    return [
        pltpu.VMEM((4, TOK, D), BF16),
        pltpu.VMEM((4, TOK, D), BF16),
        pltpu.VMEM((2, HALF, D), BF16),
        pltpu.VMEM((2, TOK, D), BF16),
    ]


def sems(n):
    return [pltpu.SemaphoreType.DMA((n,)), pltpu.SemaphoreType.DMA((n,))]


def shape(dims, dtype=BF16):
    return jax.ShapeDtypeStruct(dims, dtype)


def remote_params(number):
    return pltpu.CompilerParams(
        collective_id=number, has_side_effects=True, vmem_limit_bytes=48 * 2**20
    )


def block_place(block):
    is_kv = block >= 32
    other = block - 32
    rank = block // 4
    y = jnp.where(is_kv, lax.rem(other + 32, 4), rank // 2)
    core = jnp.where(is_kv, other // 4, lax.rem(rank, 2))
    return y, core, jnp.where(is_kv, 4, lax.rem(block, 4))


def own_block(me, j):
    if j == 4:
        return 32 + 4 * me.c + me.y
    return 4 * (2 * me.y + me.c) + j


def send_block(me, src, dst, send_sem, recv_sem, target, stays):
    @pl.when(stays)
    def _():
        pltpu.make_async_copy(src, dst, recv_sem).start()

    @pl.when(jnp.logical_not(stays))
    def _():
        pltpu.make_async_remote_copy(
            src_ref=src,
            dst_ref=dst,
            send_sem=send_sem,
            recv_sem=recv_sem,
            device_id=target,
            device_id_type=pl.DeviceIdType.MESH,
        ).start()


def wait_sent(src, send_sem, stays):
    @pl.when(jnp.logical_not(stays))
    def _():
        pltpu.make_async_copy(src, src, send_sem).wait()


def wait_got(dst, recv_sem):
    pltpu.make_async_copy(dst, dst, recv_sem).wait()


def opening_kernel(
    x, pos, wqkv, wout, wgu, wdn,
    xs, poss, wq, wo, gu, dn,
    send, recv, qs, qr, os_, orr, ws, wr, local,
):
    me = Place()
    partner = {"xl": 1 - me.xl, "xh": 1 - me.xh}
    members = group_members(me)
    others = [
        me.at(y=lax.rem(me.y + dy, 4), core=core, **partner)
        for dy in range(4)
        for core in (0, 1)
    ]
    depth = [me.at(dz=dz) for dz in (1, 2, 3)]
    greet(members + others + depth)
    edges = Edges(send, recv)
    keep = pltpu.make_async_copy(x, xs.at[2 * me.y + me.c], local.at[0])
    keep.start()
    keep_pos = pltpu.make_async_copy(pos, poss.at[2 * me.y + me.c], local.at[1])
    keep_pos.start()
    pos_copies = [edges.copy(pos, poss.at[2 * me.y + me.c], m) for m in members]
    ring = RingGather(me, edges, x, xs)

    own = 2 * me.y + me.xh
    own_column = me.c == 0
    to_xl = jnp.where(own_column, me.xl, 1 - me.xl)
    to_xh = jnp.where(own_column, me.xh, 1 - me.xh)
    blocks = []
    for i in range(5):
        y, core, slot = block_place(5 * own + i)
        stays = own_column & (y == me.y) & (core == me.c)
        src = wqkv.at[pl.ds(64 * i, 64)]
        send_block(
            me, src, wq.at[slot], qs.at[i], qr.at[slot], (me.z, to_xl, core, y, to_xh), stays
        )
        blocks.append((src, qs.at[i], stays))
    swap = me.c != me.xh
    rows_gu, rows_dn = 2 * FF_DEV // 4, D // 4
    gu_mine = pl.ds(rows_gu * me.z, rows_gu)
    dn_mine = pl.ds(rows_dn * me.z, rows_dn)
    across = me.at(core=1 - me.c, **partner)

    def over(src, dst, i, device):
        return pltpu.make_async_remote_copy(
            src_ref=src,
            dst_ref=dst,
            send_sem=ws.at[i],
            recv_sem=wr.at[i],
            device_id=device,
            device_id_type=pl.DeviceIdType.MESH,
        )

    @pl.when(swap)
    def _():
        over(wgu.at[gu_mine], gu.at[gu_mine], 0, across).start()
        over(wdn.at[dn_mine], dn.at[dn_mine], 1, across).start()

    @pl.when(jnp.logical_not(swap))
    def _():
        pltpu.make_async_copy(wgu, gu, local.at[2]).start()
        pltpu.make_async_copy(wdn, dn, local.at[3]).start()

    ring.relay()
    for i in range(8):
        dy, other = i // 2, i % 2
        y = lax.rem(me.y + dy, 4)
        core = me.c if other == 0 else 1 - me.c
        stays = own_column if i == 0 else me.c < 0
        src = wout.at[:, pl.ds(pl.multiple_of(Q_DEV * (2 * y + core), Q_DEV), Q_DEV)]
        dst = wo.at[own]
        send_block(
            me, src, dst, os_.at[i], orr.at[own], (me.z, to_xl, core, y, to_xh), stays
        )
        blocks.append((src, os_.at[i], stays))
    ring.rest()

    @pl.when(swap)
    def _():
        over(wgu.at[gu_mine], gu.at[gu_mine], 0, across).wait_recv()
        for k in (1, 2, 3):
            over(gu.at[gu_mine], gu.at[gu_mine], 2 * k, me.at(dz=k)).start()
        over(wdn.at[dn_mine], dn.at[dn_mine], 1, across).wait_recv()
        for k in (1, 2, 3):
            over(dn.at[dn_mine], dn.at[dn_mine], 2 * k + 1, me.at(dz=k)).start()
        over(wgu.at[gu_mine], gu.at[gu_mine], 0, across).wait_send()
        over(wdn.at[dn_mine], dn.at[dn_mine], 1, across).wait_send()
        for k in (1, 2, 3):
            over(gu.at[gu_mine], gu.at[gu_mine], 2 * k, me.at(dz=k)).wait()
            over(dn.at[dn_mine], dn.at[dn_mine], 2 * k + 1, me.at(dz=k)).wait()

    @pl.when(jnp.logical_not(swap))
    def _():
        pltpu.make_async_copy(wgu, gu, local.at[2]).wait()
        pltpu.make_async_copy(wdn, dn, local.at[3]).wait()

    for d in pos_copies:
        d.wait_recv()
    for i in range(5):
        wait_got(wq.at[i], qr.at[i])
    for i in range(8):
        wait_got(wo.at[i], orr.at[i])
    for src, sem, stays in blocks:
        wait_sent(src, sem, stays)
    edges.finish()
    keep.wait()
    keep_pos.wait()


def opening(x, pos, wqkv, wout, wgu, wdn):
    return pl.pallas_call(
        opening_kernel,
        out_shape=(
            shape((8, TOK, D)),
            shape((8, 8, TOK), jnp.int32),
            shape((5, 64, D)),
            shape((8, 256, Q_DEV)),
            shape((2 * FF_DEV, D)),
            shape((D, FF_DEV)),
        ),
        in_specs=[ANY] * 6,
        out_specs=(ANY,) * 6,
        scratch_shapes=sems(7 + GATHER_EDGES) + sems(5) + sems(8) + sems(8)
        + [pltpu.SemaphoreType.DMA((4,))],
        compiler_params=remote_params(0),
        name="opening",
    )(x, pos, wqkv, wout, wgu, wdn)


def chips_in_sequence(me):
    return [(dz, dl) for dz in range(4) for dl in (0, 1)][1:]


def keys_kernel(kv, pos, cot, kvs, poss, cots, send, recv, local):
    me = Place()
    core = me.at(core=1 - me.c)
    far = [
        me.at(dz=dz, xl=(1 - me.xl) if dl else me.xl) for dz, dl in chips_in_sequence(me)
    ]
    greet(far + [core, me.at(dy=1), me.at(dy=-1)])
    edges = Edges(send, recv)
    chip = 2 * me.z + me.xl
    keeps = [
        pltpu.make_async_copy(kv, kvs.at[me.c, chip], local.at[0]),
        pltpu.make_async_copy(pos, poss.at[chip], local.at[1]),
        pltpu.make_async_copy(cot, cots.at[2 * me.y + me.c], local.at[2]),
    ]
    for d in keeps:
        d.start()
    pos_copies = [edges.copy(pos, poss.at[chip], d) for d in far]
    kv_copies = [edges.copy(kv, kvs.at[me.c, chip], d) for d in far]
    over = [edges.copy(kv, kvs.at[me.c, chip], core)]
    ring = RingGather(me, edges, cot, cots)
    ring.relay()
    for (dz, dl), d in zip(chips_in_sequence(me), kv_copies):
        d.wait_recv()
        source = 2 * lax.rem(me.z - dz + 4, 4) + ((1 - me.xl) if dl else me.xl)
        ref = kvs.at[me.c, source]
        over.append(edges.copy(ref, ref, core))
    ring.rest()
    for d in over + pos_copies:
        d.wait_recv()
    edges.finish()
    for d in keeps:
        d.wait()


def exchange_keys(kv, pos, cot):
    return pl.pallas_call(
        keys_kernel,
        out_shape=(
            shape((2, 8, 512, 128)),
            shape((8, 8, 8, TOK), jnp.int32),
            shape((8, TOK, D)),
        ),
        in_specs=[ANY] * 3,
        out_specs=(ANY,) * 3,
        scratch_shapes=sems(7 + 7 + 8 + GATHER_EDGES) + [pltpu.SemaphoreType.DMA((3,))],
        compiler_params=remote_params(1),
        name="exchange_keys",
    )(kv, pos, cot)


def split_heads(rows):
    return jnp.concatenate([rows[:, HD * h : HD * (h + 1)] for h in range(4)], axis=0)


def join_heads(rows):
    return jnp.concatenate([rows[64 * h : 64 * (h + 1), :] for h in range(4)], axis=1)


def dot_last(a, b):
    return lax.dot_general(a, b, (((1,), (1,)), ((), ())), preferred_element_type=F32)


def dot_first(a, b):
    return lax.dot_general(a, b, (((0,), (0,)), ((), ())), preferred_element_type=F32)


def dot(a, b):
    return lax.dot_general(a, b, (((1,), (0,)), ((), ())), preferred_element_type=F32)


TILE = 256


def sort_keys(runs, seq, kv_ref, keys, values):
    for j in range(32):
        chip, core, u = j // 4, (j // 2) % 2, j % 2
        to = pl.ds(pl.multiple_of(runs[seq * 32 + j] * 64, 64), 64)
        rows, lanes = slice(64 * u, 64 * u + 64), slice(HD * core, HD * core + HD)
        keys[to, :] = kv_ref[0, chip, rows, lanes]
        values[to, :] = kv_ref[1, chip, rows, lanes]


def allowed_tile(tile, run):
    key = lax.broadcasted_iota(jnp.int32, (TILE, 256), 0) + tile * TILE
    query = lax.rem(lax.broadcasted_iota(jnp.int32, (TILE, 256), 1), 64) + run * 64
    return key <= query


def attend_kernel(key_runs, query_runs, q_ref, kv_ref, att_ref, ot_ref, lse_ref, keys, values):
    seq = pl.program_id(0)
    sort_keys(key_runs, seq, kv_ref, keys, values)

    def one_run(r, _):
        run = query_runs[seq * 4 + r]
        rows = pl.ds(pl.multiple_of(r * 64, 64), 64)
        query = split_heads(q_ref[rows, :])
        last = run // 4

        def tile_step(tile, carried, masked):
            high, total, acc = carried
            at = pl.ds(pl.multiple_of(tile * TILE, TILE), TILE)
            scores = dot_last(keys[at, :], query)
            if masked:
                allowed = allowed_tile(tile, run)
                scores = jnp.where(allowed, scores, FILLER)
            new_high = jnp.maximum(high, jnp.max(scores, axis=0, keepdims=True))
            weights = jnp.exp(scores - new_high)
            scale = jnp.exp(high - new_high)
            total = total * scale + jnp.sum(weights, axis=0, keepdims=True)
            acc = acc * scale + dot_first(values[at, :], weights.astype(BF16))
            return new_high, total, acc

        start = (
            jnp.full((1, 256), FILLER, F32),
            jnp.zeros((1, 256), F32),
            jnp.zeros((HD, 256), F32),
        )
        carried = lax.fori_loop(0, last, lambda t, s: tile_step(t, s, False), start)
        high, total, acc = tile_step(last, carried, True)
        out = acc / total
        ot_ref[r] = out
        lse_ref[r] = high + jnp.log(total)
        att_ref[rows, :] = join_heads(out.T).astype(BF16)
        return 0

    lax.fori_loop(0, 4, one_run, 0)


def attend(key_runs, query_runs, q, kv):
    return pl.pallas_call(
        attend_kernel,
        out_shape=(shape((1024, 256)), shape((16, HD, 256), F32), shape((16, 1, 256), F32)),
        grid_spec=pltpu.PrefetchScalarGridSpec(
            num_scalar_prefetch=2,
            grid=(4,),
            in_specs=[
                pl.BlockSpec((256, 256), lambda i, *_: (i, 0)),
                pl.BlockSpec((2, 8, 128, 128), lambda i, *_: (0, 0, i, 0)),
            ],
            out_specs=[
                pl.BlockSpec((256, 256), lambda i, *_: (i, 0)),
                pl.BlockSpec((4, HD, 256), lambda i, *_: (i, 0, 0)),
                pl.BlockSpec((4, 1, 256), lambda i, *_: (i, 0, 0)),
            ],
            scratch_shapes=[pltpu.VMEM((2048, HD), BF16), pltpu.VMEM((2048, HD), BF16)],
        ),
        compiler_params=pltpu.CompilerParams(vmem_limit_bytes=40 * 2**20),
        name="attend",
    )(key_runs, query_runs, q, kv)


def attend_back_kernel(
    key_runs, query_runs, q_ref, kv_ref, da_ref, ot_ref, lse_ref,
    dq_ref, dkv_ref, keys, values, dkeys, dvalues,
):
    seq = pl.program_id(0)
    sort_keys(key_runs, seq, kv_ref, keys, values)
    dkeys[...] = jnp.zeros_like(dkeys)
    dvalues[...] = jnp.zeros_like(dvalues)

    def one_run(r, _):
        run = query_runs[seq * 4 + r]
        rows = pl.ds(pl.multiple_of(r * 64, 64), 64)
        query = split_heads(q_ref[rows, :])
        grad = split_heads(da_ref[rows, :])
        lse = lse_ref[r]
        delta = jnp.sum(grad.astype(F32).T * ot_ref[r], axis=0, keepdims=True)
        last = run // 4

        def tile_step(tile, dq, masked):
            at = pl.ds(pl.multiple_of(tile * TILE, TILE), TILE)
            key = keys[at, :]
            probs = jnp.exp(dot_last(key, query) - lse)
            if masked:
                probs = jnp.where(allowed_tile(tile, run), probs, 0.0)
            grad_probs = dot_last(values[at, :], grad)
            grad_scores = (probs * (grad_probs - delta)).astype(BF16)
            dvalues[at, :] += dot(probs.astype(BF16), grad)
            dkeys[at, :] += dot(grad_scores, query)
            return dq + dot_first(key, grad_scores)

        dq = lax.fori_loop(
            0, last, lambda t, s: tile_step(t, s, False), jnp.zeros((HD, 256), F32)
        )
        dq = tile_step(last, dq, True)
        dq_ref[rows, :] = join_heads((dq * 0.125).T)
        return 0

    lax.fori_loop(0, 4, one_run, 0)
    for j in range(32):
        chip, core, u = j // 4, (j // 2) % 2, j % 2
        at = pl.ds(pl.multiple_of(key_runs[seq * 32 + j] * 64, 64), 64)
        rows, lanes = slice(64 * u, 64 * u + 64), slice(HD * core, HD * core + HD)
        dkv_ref[0, chip, rows, lanes] = dkeys[at, :].astype(BF16)
        dkv_ref[1, chip, rows, lanes] = dvalues[at, :].astype(BF16)


def attend_back(key_runs, query_runs, q, kv, grad, ot, lse):
    return pl.pallas_call(
        attend_back_kernel,
        out_shape=(shape((1024, 256), F32), shape((2, 8, 512, 128))),
        grid_spec=pltpu.PrefetchScalarGridSpec(
            num_scalar_prefetch=2,
            grid=(4,),
            in_specs=[
                pl.BlockSpec((256, 256), lambda i, *_: (i, 0)),
                pl.BlockSpec((2, 8, 128, 128), lambda i, *_: (0, 0, i, 0)),
                pl.BlockSpec((256, 256), lambda i, *_: (i, 0)),
                pl.BlockSpec((4, HD, 256), lambda i, *_: (i, 0, 0)),
                pl.BlockSpec((4, 1, 256), lambda i, *_: (i, 0, 0)),
            ],
            out_specs=[
                pl.BlockSpec((256, 256), lambda i, *_: (i, 0)),
                pl.BlockSpec((2, 8, 128, 128), lambda i, *_: (0, 0, i, 0)),
            ],
            scratch_shapes=[
                pltpu.VMEM((2048, HD), BF16),
                pltpu.VMEM((2048, HD), BF16),
                pltpu.VMEM((2048, HD), F32),
                pltpu.VMEM((2048, HD), F32),
            ],
        ),
        compiler_params=pltpu.CompilerParams(vmem_limit_bytes=40 * 2**20),
        name="attend_back",
    )(key_runs, query_runs, q, kv, grad, ot, lse)


def gather_kernel(x, xs, send, recv, local):
    me = Place()
    greet([me.at(core=1 - me.c), me.at(dy=1), me.at(dy=-1)])
    edges = Edges(send, recv)
    keep = pltpu.make_async_copy(x, xs.at[2 * me.y + me.c], local)
    keep.start()
    ring = RingGather(me, edges, x, xs)
    ring.relay()
    ring.rest()
    edges.finish()
    keep.wait()


def gather_group(x, number, name):
    return pl.pallas_call(
        gather_kernel,
        out_shape=shape((8, TOK, D)),
        in_specs=[ANY],
        out_specs=ANY,
        scratch_shapes=sems(GATHER_EDGES) + [pltpu.SemaphoreType.DMA],
        compiler_params=remote_params(number),
        name=name,
    )(x)


def scatter_kernel(parts, out, got, both, relayed, last, send, recv):
    me = Place()
    greet([me.at(core=1 - me.c), me.at(dy=1), me.at(dy=-1)])
    edges = Edges(send, recv)
    ring = RingScatter(me, edges, parts, got, both, relayed, last)
    ring.first()
    ring.second()
    ring.total(out)
    edges.finish()


def scatter_group(parts, number, name):
    return pl.pallas_call(
        scatter_kernel,
        out_shape=shape((TOK, D), F32),
        in_specs=[VMEM],
        out_specs=VMEM,
        scratch_shapes=scatter_scratch() + sems(SCATTER_EDGES),
        compiler_params=remote_params(number),
        name=name,
    )(parts)


def scatter_two_kernel(
    parts_a, parts_b, out_a, out_b, g1, b1, r1, l1, g2, b2, r2, l2, send, recv
):
    me = Place()
    greet([me.at(core=1 - me.c), me.at(dy=1), me.at(dy=-1)])
    edges = Edges(send, recv)
    ring_a = RingScatter(me, edges, parts_a, g1, b1, r1, l1)
    ring_b = RingScatter(me, edges, parts_b, g2, b2, r2, l2)
    ring_a.first()
    ring_b.first()
    ring_a.second()
    ring_b.second()
    ring_a.total(out_a)
    ring_b.total(out_b)
    edges.finish()


def scatter_two(parts_a, parts_b, number, name):
    return pl.pallas_call(
        scatter_two_kernel,
        out_shape=(shape((TOK, D), F32),) * 2,
        in_specs=[VMEM] * 2,
        out_specs=(VMEM,) * 2,
        scratch_shapes=scatter_scratch() * 2 + sems(2 * SCATTER_EDGES),
        compiler_params=remote_params(number),
        name=name,
    )(parts_a, parts_b)


def key_grads_kernel(dkv, gwo, out, rows, got, both, last, send, recv, os_, orr, load):
    me = Place()
    core = me.at(core=1 - me.c)
    far = [
        me.at(dz=dz, xl=(1 - me.xl) if dl else me.xl) for dz, dl in chips_in_sequence(me)
    ]
    greet(far + group_members(me))
    edges = Edges(send, recv)
    order = []
    for dz, dl in chips_in_sequence(me) + [(0, 0)]:
        chip = 2 * lax.rem(me.z + dz, 4) + ((1 - me.xl) if dl else me.xl)
        order.append((chip, edges.copy(dkv.at[1 - me.c, chip], got.at[chip], core)))
    own = 2 * me.y + me.c
    sent = []
    for i in range(8):
        dy, other = i // 2, i % 2
        y = lax.rem(me.y + dy, 4)
        to_core = me.c if other == 0 else 1 - me.c
        src = gwo.at[2 * y + to_core]
        dst = rows.at[:, pl.ds(pl.multiple_of(Q_DEV * own, Q_DEV), Q_DEV)]
        if i == 0:
            pltpu.make_async_copy(src, dst, orr.at[own]).start()
        else:
            d = pltpu.make_async_remote_copy(
                src_ref=src,
                dst_ref=dst,
                send_sem=os_.at[i],
                recv_sem=orr.at[own],
                device_id=me.at(dy=dy, core=to_core),
                device_id_type=pl.DeviceIdType.MESH,
            )
            d.start()
            sent.append(d)
    far_copies = []
    for i, (chip, d) in enumerate(order):
        d.wait_recv()
        both[chip] = (dkv[me.c, chip].astype(F32) + got[chip].astype(F32)).astype(BF16)
        if i < 7:
            far_copies.append(edges.copy(both.at[chip], last.at[i], far[i]))
    total = both[2 * me.z + me.xl].astype(F32)
    for i, d in enumerate(far_copies):
        d.wait_recv()
        total = total + last[i].astype(F32)
    out[...] = total
    for i in range(8):
        wait_got(rows.at[:, pl.ds(Q_DEV * i, Q_DEV)], orr.at[i])
    for d in sent:
        d.wait_send()
    edges.finish()


def sum_key_grads(dkv, gwo):
    return pl.pallas_call(
        key_grads_kernel,
        out_shape=(shape((512, 128), F32), shape((256, D))),
        in_specs=[VMEM, ANY],
        out_specs=(VMEM, ANY),
        scratch_shapes=[
            pltpu.VMEM((8, 512, 128), BF16),
            pltpu.VMEM((8, 512, 128), BF16),
            pltpu.VMEM((7, 512, 128), BF16),
        ]
        + sems(15)
        + sems(8)
        + [pltpu.SemaphoreType.DMA],
        compiler_params=remote_params(2),
        name="sum_key_grads",
    )(dkv, gwo)


def closing_kernel(parts, gwq, out, rows, got, both, relayed, last, send, recv, qs, qr):
    me = Place()
    greet(group_members(me))
    edges = Edges(send, recv)
    ring = RingScatter(me, edges, parts, got, both, relayed, last)
    sent = []
    for j in range(5):
        block = own_block(me, j)
        owner, slot = block // 5, lax.rem(block, 5)
        y, core = owner // 2, lax.rem(owner, 2)
        stays = (y == me.y) & (core == me.c)
        src = gwq.at[j]
        send_block(
            me, src, rows.at[slot], qs.at[j], qr.at[slot], me.at(y=y, core=core), stays
        )
        sent.append((src, qs.at[j], stays))
    ring.first()
    ring.second()
    ring.total(out)
    for i in range(5):
        wait_got(rows.at[i], qr.at[i])
    for src, sem, stays in sent:
        wait_sent(src, sem, stays)
    edges.finish()


def closing(parts, gwq):
    return pl.pallas_call(
        closing_kernel,
        out_shape=(shape((TOK, D), F32), shape((5, 64, D))),
        in_specs=[VMEM, ANY],
        out_specs=(VMEM, ANY),
        scratch_shapes=scatter_scratch() + sems(SCATTER_EDGES) + sems(5),
        compiler_params=remote_params(3),
        name="closing",
    )(parts, gwq)


def rotate(rows, cosine, sine):
    turned = jnp.concatenate([-rows[..., HD // 2 :], rows[..., : HD // 2]], axis=-1)
    return rows * cosine + turned * sine


def norm_back(grad_norm, normal, inverse):
    return inverse * (grad_norm - normal * jnp.mean(grad_norm * normal, axis=-1, keepdims=True))


def reduce_grads(parts):
    rows, width = parts.shape
    shares = parts.reshape(16, rows // 16, width)
    share = lax.psum_scatter(shares, ("z", "xl", "xh"), scatter_dimension=0, tiled=True)
    route = []
    for z in range(4):
        for xl in range(2):
            for c in range(2):
                for y in range(4):
                    for xh in range(2):
                        here = (((z * 2 + xl) * 2 + c) * 4 + y) * 2 + xh
                        there = (((z * 2 + xl) * 2 + xh) * 4 + y) * 2 + c
                        route.append((here, there))
    share = lax.ppermute(share, AXES, route)
    full = lax.all_gather(share, ("z", "xl", "c"), axis=0, tiled=True)
    return full.reshape(rows, width).astype(F32)


def body(hidden, positions, gain_attn, w_qkv, w_out, gain_mlp, w_gate_up, w_down, cotangent):
    tokens = hidden[0].astype(F32)
    core = lax.axis_index("c")
    gain_one = gain_attn.astype(F32)
    gain_two = gain_mlp.astype(F32)
    inverse_one = lax.rsqrt(jnp.mean(tokens * tokens, axis=-1, keepdims=True) + EPSILON)
    normal_one = tokens * inverse_one
    input_one = (normal_one * gain_one).astype(BF16)
    xs, poss, wq, wo, gu, dn = opening(
        input_one,
        jnp.broadcast_to(positions, (8, TOK)),
        w_qkv,
        w_out,
        w_gate_up.reshape(2 * FF_DEV, D),
        w_down,
    )
    xs = xs.reshape(1024, D)
    wq = wq.reshape(320, D)
    wo = wo.reshape(D, Q_DEV)
    places = poss[:, 0, :].reshape(1024)

    steps_half = jnp.arange(HD // 2, dtype=F32)
    inverse = jnp.power(10000.0, steps_half * (-2.0 / HD))
    turning = places.astype(F32)[:, None] * inverse[None, :]
    cosine, sine = jnp.cos(turning), jnp.sin(turning)
    cosine = jnp.concatenate([cosine, cosine], axis=-1)
    sine = jnp.concatenate([sine, sine], axis=-1)
    kv_cosine = jnp.where(core == 0, cosine, 1.0)
    kv_sine = jnp.where(core == 0, sine, 0.0)

    projected = dot_last(xs, wq)
    query = rotate(
        projected[:, :Q_DEV].reshape(1024, 4, HD), cosine[:, None, :], sine[:, None, :]
    )
    query = (query.astype(BF16) * 0.125).astype(BF16).reshape(1024, Q_DEV)
    kv = rotate(projected[:, Q_DEV:], kv_cosine, kv_sine).astype(BF16)
    kv = kv.reshape(4, 2, TOK, HD).transpose(0, 2, 1, 3).reshape(512, 128)
    kvs, places_all, cots = exchange_keys(kv, poss, cotangent[0])
    cots = cots.reshape(1024, D)
    key_runs = (
        places_all[:, :, 0, ::64].reshape(8, 4, 2, 2).transpose(1, 0, 2, 3).reshape(128) // 64
    )
    query_runs = places.reshape(16, 64)[:, 0] // 64
    att, ot, lse = attend(key_runs, query_runs, query, kvs)
    parts = dot_last(att, wo).astype(BF16)
    middle = tokens + scatter_group(parts.reshape(8, TOK, D), 4, "sum_attended")
    inverse_two = lax.rsqrt(jnp.mean(middle * middle, axis=-1, keepdims=True) + EPSILON)
    normal_two = middle * inverse_two
    input_two = (normal_two * gain_two).astype(BF16)
    x2 = gather_group(input_two, 5, "gather_two").reshape(1024, D)

    gate = dot_last(x2, gu[:FF_DEV])
    upward = dot_last(x2, gu[FF_DEV:])
    grad_active = dot(cots, dn)
    sigmoid = jax.nn.sigmoid(gate)
    swish = gate * sigmoid
    active = (swish * upward).astype(BF16)
    grad_upward = (grad_active * swish).astype(BF16)
    grad_gate = (grad_active * upward * sigmoid * (1.0 + gate * (1.0 - sigmoid))).astype(BF16)
    branch_parts = dot_last(active, dn).astype(BF16).reshape(8, TOK, D)
    grad_two_parts = (dot(grad_gate, gu[:FF_DEV]) + dot(grad_upward, gu[FF_DEV:])).astype(BF16)
    grad_gu = jnp.concatenate([dot_first(grad_gate, x2), dot_first(grad_upward, x2)]).astype(BF16)
    grad_dn = dot_first(cots, active).astype(BF16)
    branch, grad_two = scatter_two(
        branch_parts, grad_two_parts.reshape(8, TOK, D), 6, "sum_mlp"
    )
    output = (middle + branch).astype(BF16)
    grad_gain_two = jnp.sum(normal_two * grad_two, axis=0)
    grad_output = cotangent[0].astype(F32)
    grad_middle = grad_output + norm_back(grad_two * gain_two, normal_two, inverse_two)
    gb = gather_group(grad_middle.astype(BF16), 7, "gather_branch").reshape(1024, D)
    grad_att = dot(gb, wo).astype(BF16)
    grad_wo = dot_first(gb, att).astype(BF16)
    dq, dkv = attend_back(key_runs, query_runs, query, kvs, grad_att, ot, lse)
    dkv, wo_rows = sum_key_grads(dkv, grad_wo.reshape(8, 256, Q_DEV))
    dq = rotate(dq.reshape(1024, 4, HD), cosine[:, None, :], -sine[:, None, :])
    dkv = dkv.reshape(4, TOK, 2, HD).transpose(0, 2, 1, 3).reshape(1024, HD)
    dkv = rotate(dkv, kv_cosine, -kv_sine)
    grad_projected = jnp.concatenate([dq.reshape(1024, Q_DEV), dkv], axis=1).astype(BF16)
    grad_one_parts = dot(grad_projected, wq).astype(BF16).reshape(8, TOK, D)
    grad_wq = dot_first(grad_projected, xs).astype(BF16).reshape(5, 64, D)
    grad_one, wq_rows = closing(grad_one_parts, grad_wq)
    grad_gain_one = jnp.sum(normal_one * grad_one, axis=0)
    grad_tokens = grad_middle + norm_back(grad_one * gain_one, normal_one, inverse_one)

    gains = jnp.stack([grad_gain_one, grad_gain_two])
    gains = lax.psum(gains, AXES)
    owner = 2 * lax.axis_index("y") + lax.axis_index("xh")
    gains = lax.dynamic_slice_in_dim(gains, owner * 256, 256, axis=1)
    return (
        output[None],
        grad_tokens[None],
        gains[0],
        reduce_grads(wq_rows.reshape(320, D)),
        reduce_grads(wo_rows),
        gains[1],
        reduce_grads(grad_gu).reshape(2, FF_DEV, D),
        reduce_grads(grad_dn),
    )


def solution(mesh):
    fine = Mesh(mesh.devices.reshape(4, 2, 2, 4, 2), AXES)
    ctx, fsdp = ("z", "xl", "c"), ("y", "xh")
    weight = P(fsdp, None)
    return jax.shard_map(
        body,
        mesh=fine,
        in_specs=(
            P(fsdp, ctx, None),
            P(fsdp, ctx),
            P(),
            weight,
            weight,
            P(),
            P(None, fsdp, None),
            P(None, fsdp),
            P(fsdp, ctx, None),
        ),
        out_specs=(
            P(fsdp, ctx, None),
            P(fsdp, ctx, None),
            P(fsdp),
            weight,
            weight,
            P(fsdp),
            P(None, fsdp, None),
            P(None, fsdp),
        ),
        check_vma=False,
    )
```

```python
import jax
import jax.numpy as jnp
import numpy as np
from jax import lax
from jax.experimental import pallas as pl
from jax.experimental.pallas import tpu as pltpu
from jax.sharding import Mesh
from jax.sharding import PartitionSpec as P

D = 2048
H = 32
KV = 4
HD = 64
FF = 5632
TOK = 128
HALF = 64
FF_DEV = 704
Q_DEV = 256
EPSILON = 1e-05
FILLER = -1e30
AXES = ("z", "xl", "c", "y", "xh")
ANY = pl.BlockSpec(memory_space=pl.ANY)
VMEM = pl.BlockSpec(memory_space=pltpu.VMEM)
BF16 = jnp.bfloat16
F32 = jnp.float32


class Place:
    def __init__(self):
        self.z, self.xl, self.c, self.y, self.xh = (lax.axis_index(a) for a in AXES)

    def at(self, dz=0, dy=0, core=None, xl=None, xh=None, y=None):
        z = lax.rem(self.z + dz + 4, 4) if dz else self.z
        y = (lax.rem(self.y + dy + 4, 4) if dy else self.y) if y is None else y
        return (
            z,
            self.xl if xl is None else xl,
            self.c if core is None else core,
            y,
            self.xh if xh is None else xh,
        )


class Edges:
    def __init__(self, send, recv):
        self.send, self.recv, self.count, self.started = send, recv, 0, []

    def copy(self, src, dst, device, start=True):
        i = self.count
        self.count += 1
        d = pltpu.make_async_remote_copy(
            src_ref=src,
            dst_ref=dst,
            send_sem=self.send.at[i],
            recv_sem=self.recv.at[i],
            device_id=device,
            device_id_type=pl.DeviceIdType.MESH,
        )
        self.started.append(d)
        if start:
            d.start()
        return d

    def finish(self):
        for d in self.started:
            d.wait_send()


def greet(devices):
    barrier = pltpu.get_barrier_semaphore()
    for device in devices:
        pl.semaphore_signal(
            barrier, inc=1, device_id=device, device_id_type=pl.DeviceIdType.MESH
        )
    pl.semaphore_wait(barrier, len(devices))


def group_members(me):
    found = [me.at(core=1 - me.c)]
    for dy in (1, 2, 3):
        found += [me.at(dy=dy), me.at(dy=dy, core=1 - me.c)]
    return found


class RingGather:
    def __init__(self, me, edges, own, out):
        self.me, self.edges, self.out = me, edges, out
        self.core = me.at(core=1 - me.c)
        self.up, self.down = me.at(dy=1), me.at(dy=-1)
        a, b = pl.ds(0, HALF), pl.ds(HALF, HALF)
        self.a, self.b = a, b
        mine = self.slot(0)
        self.up_a = edges.copy(own.at[a], out.at[mine, a], self.up)
        self.down_b = edges.copy(own.at[b], out.at[mine, b], self.down)
        self.up_b = edges.copy(own.at[b], out.at[mine, b], self.up)
        self.down_a = edges.copy(own.at[a], out.at[mine, a], self.down)
        self.to_core = [edges.copy(own, out.at[mine], self.core)]

    def slot(self, dy):
        return 2 * lax.rem(self.me.y + dy + 4, 4) + self.me.c

    def pass_core(self, dy, part):
        ref = self.out.at[self.slot(dy), part]
        self.to_core.append(self.edges.copy(ref, ref, self.core))

    def relay(self):
        out = self.out
        self.up_a.wait_recv()
        ref = out.at[self.slot(-1), self.a]
        self.on_a = self.edges.copy(ref, ref, self.up)
        self.down_b.wait_recv()
        ref = out.at[self.slot(1), self.b]
        self.on_b = self.edges.copy(ref, ref, self.down)
        self.pass_core(-1, self.a)
        self.pass_core(1, self.b)

    def rest(self):
        self.up_b.wait_recv()
        self.pass_core(-1, self.b)
        self.down_a.wait_recv()
        self.pass_core(1, self.a)
        self.on_a.wait_recv()
        self.pass_core(2, self.a)
        self.on_b.wait_recv()
        self.pass_core(2, self.b)
        for d in self.to_core:
            d.wait_recv()


GATHER_EDGES = 13


class RingScatter:
    def __init__(self, me, edges, parts, got, both, relayed, last):
        self.me, self.edges, self.parts = me, edges, parts
        self.got, self.both, self.relayed, self.last = got, both, relayed, last
        self.up, self.down = me.at(dy=1), me.at(dy=-1)
        self.from_core = {}
        for k in (2, 1, 3, 0):
            row = 2 * lax.rem(me.y + k, 4) + 1 - me.c
            self.from_core[k] = edges.copy(
                parts.at[row], got.at[k], me.at(core=1 - me.c)
            )

    def add_core(self, k):
        self.from_core[k].wait_recv()
        row = 2 * lax.rem(self.me.y + k, 4) + self.me.c
        self.both[k] = (
            self.parts[row].astype(F32) + self.got[k].astype(F32)
        ).astype(BF16)

    def first(self):
        a, b = pl.ds(0, HALF), pl.ds(HALF, HALF)
        e, both = self.edges, self.both
        self.add_core(2)
        self.r_a = e.copy(both.at[2, a], self.relayed.at[0], self.up)
        self.r_b = e.copy(both.at[2, b], self.relayed.at[1], self.down)
        self.add_core(1)
        self.u_b = e.copy(both.at[1, b], self.last.at[0, b], self.up)
        self.add_core(3)
        self.d_a = e.copy(both.at[3, a], self.last.at[1, a], self.down)
        self.add_core(0)

    def second(self):
        a, b = pl.ds(0, HALF), pl.ds(HALF, HALF)
        e, both = self.edges, self.both
        self.r_a.wait_recv()
        both[1, a] = (both[1, a].astype(F32) + self.relayed[0].astype(F32)).astype(BF16)
        self.u_a = e.copy(both.at[1, a], self.last.at[0, a], self.up)
        self.r_b.wait_recv()
        both[3, b] = (both[3, b].astype(F32) + self.relayed[1].astype(F32)).astype(BF16)
        self.d_b = e.copy(both.at[3, b], self.last.at[1, b], self.down)

    def total(self, out):
        for d in (self.u_b, self.d_a, self.u_a, self.d_b):
            d.wait_recv()
        out[...] = (
            self.both[0].astype(F32)
            + self.last[0].astype(F32)
            + self.last[1].astype(F32)
        )


SCATTER_EDGES = 10


def scatter_scratch():
    return [
        pltpu.VMEM((4, TOK, D), BF16),
        pltpu.VMEM((4, TOK, D), BF16),
        pltpu.VMEM((2, HALF, D), BF16),
        pltpu.VMEM((2, TOK, D), BF16),
    ]


def sems(n):
    return [pltpu.SemaphoreType.DMA((n,)), pltpu.SemaphoreType.DMA((n,))]


def shape(dims, dtype=BF16):
    return jax.ShapeDtypeStruct(dims, dtype)


def remote_params(number):
    return pltpu.CompilerParams(
        collective_id=number, has_side_effects=True, vmem_limit_bytes=48 * 2**20
    )


def block_place(block):
    is_kv = block >= 32
    other = block - 32
    rank = block // 4
    y = jnp.where(is_kv, lax.rem(other + 32, 4), rank // 2)
    core = jnp.where(is_kv, other // 4, lax.rem(rank, 2))
    return y, core, jnp.where(is_kv, 4, lax.rem(block, 4))


def own_block(me, j):
    if j == 4:
        return 32 + 4 * me.c + me.y
    return 4 * (2 * me.y + me.c) + j


def send_block(me, src, dst, send_sem, recv_sem, target, stays):
    @pl.when(stays)
    def _():
        pltpu.make_async_copy(src, dst, recv_sem).start()

    @pl.when(jnp.logical_not(stays))
    def _():
        pltpu.make_async_remote_copy(
            src_ref=src,
            dst_ref=dst,
            send_sem=send_sem,
            recv_sem=recv_sem,
            device_id=target,
            device_id_type=pl.DeviceIdType.MESH,
        ).start()


def wait_sent(src, send_sem, stays):
    @pl.when(jnp.logical_not(stays))
    def _():
        pltpu.make_async_copy(src, src, send_sem).wait()


def wait_got(dst, recv_sem):
    pltpu.make_async_copy(dst, dst, recv_sem).wait()


def x_of(me):
    return 2 * me.xh + me.xl


def around(me, dz, dx):
    x = lax.rem(x_of(me) + dx, 4)
    return me.at(dz=dz, xl=lax.rem(x, 2), xh=x // 2)


STEPS = [(dz, dx) for dz in range(4) for dx in range(4)][1:]


class SumOfSixteen:
    def __init__(self, me, src, piece, own, got, send, recv, local):
        self.me, self.src, self.piece, self.own, self.got = me, src, piece, own, got
        self.send, self.recv = send, recv
        self.keep = pltpu.make_async_copy(
            src.at[piece(4 * me.z + x_of(me))], own, local
        )
        self.keep.start()
        for k, (dz, dx) in enumerate(STEPS):
            to = 4 * lax.rem(me.z + dz, 4) + lax.rem(x_of(me) + dx, 4)
            self.copy(src.at[piece(to)], k, around(me, dz, dx)).start()

    def copy(self, src, k, device):
        return pltpu.make_async_remote_copy(
            src_ref=src,
            dst_ref=self.got.at[k],
            send_sem=self.send.at[k],
            recv_sem=self.recv,
            device_id=device,
            device_id_type=pl.DeviceIdType.MESH,
        )

    def total(self):
        self.keep.wait()
        pltpu.make_async_copy(self.got, self.got, self.recv).wait()
        total = self.own[...].astype(F32)
        for k in range(15):
            total = total + self.got[k].astype(F32)
        return total

    def finish(self):
        for k in range(15):
            src = self.src.at[self.piece(0)]
            pltpu.make_async_copy(src, src, self.send.at[k]).wait()


def same(me, z, xl, core, y, xh):
    return (z == me.z) & (xl == me.xl) & (core == me.c) & (y == me.y) & (xh == me.xh)


class Deliver:
    def __init__(self, me, send, recv):
        self.me, self.send, self.recv, self.sent = me, send, recv, []

    def to_owner(self, src, dst, core, y, xh):
        me = self.me
        for dz in range(4):
            for dl in (0, 1):
                z = lax.rem(me.z + dz, 4)
                xl = 1 - me.xl if dl else me.xl
                stays = same(me, z, xl, core, y, xh)
                sem = self.send.at[len(self.sent)]
                send_block(me, src, dst, sem, self.recv, (z, xl, core, y, xh), stays)
                self.sent.append((src, sem, stays))

    def finish(self):
        for src, sem, stays in self.sent:
            wait_sent(src, sem, stays)


def opening_kernel(x, pos, wqkv, xs, poss, wq, send, recv, qs, qr, local):
    me = Place()
    partner = {"xl": 1 - me.xl, "xh": 1 - me.xh}
    members = group_members(me)
    others = [
        me.at(y=lax.rem(me.y + dy, 4), core=core, **partner)
        for dy in range(4)
        for core in (0, 1)
    ]
    greet(members + others)
    edges = Edges(send, recv)
    own_rank = 2 * me.y + me.c
    keep = pltpu.make_async_copy(x, xs.at[own_rank], local.at[0])
    keep.start()
    keep_pos = pltpu.make_async_copy(pos, poss.at[own_rank], local.at[1])
    keep_pos.start()
    pos_copies = [edges.copy(pos, poss.at[own_rank], m) for m in members]
    ring = RingGather(me, edges, x, xs)

    own = 2 * me.y + me.xh
    own_column = me.c == 0
    to_xl = jnp.where(own_column, me.xl, 1 - me.xl)
    to_xh = jnp.where(own_column, me.xh, 1 - me.xh)
    blocks = []
    for i in range(5):
        y, core, slot = block_place(5 * own + i)
        stays = own_column & (y == me.y) & (core == me.c)
        src = wqkv.at[pl.ds(64 * i, 64)]
        send_block(
            me, src, wq.at[slot], qs.at[i], qr.at[slot], (me.z, to_xl, core, y, to_xh), stays
        )
        blocks.append((src, qs.at[i], stays))
    ring.relay()
    ring.rest()
    for d in pos_copies:
        d.wait_recv()
    for i in range(5):
        wait_got(wq.at[i], qr.at[i])
    for src, sem, stays in blocks:
        wait_sent(src, sem, stays)
    edges.finish()
    keep.wait()
    keep_pos.wait()


def opening(x, pos, wqkv):
    return pl.pallas_call(
        opening_kernel,
        out_shape=(
            shape((8, TOK, D)),
            shape((8, 8, TOK), jnp.int32),
            shape((5, 64, D)),
        ),
        in_specs=[ANY] * 3,
        out_specs=(ANY,) * 3,
        scratch_shapes=sems(7 + GATHER_EDGES) + sems(5) + [pltpu.SemaphoreType.DMA((2,))],
        compiler_params=remote_params(0),
        name="opening",
    )(x, pos, wqkv)


def rotary_table():
    steps = np.arange(HD // 2, dtype=np.float32)
    inverse = np.power(np.float32(10000.0), steps * np.float32(-2.0 / HD)).astype(np.float32)
    turning = np.arange(2048, dtype=np.float32)[:, None] * inverse[None, :]
    cosine, sine = np.cos(turning), np.sin(turning)
    return np.concatenate([cosine, cosine, -sine, sine], axis=1).astype(np.float32)


def halves_swapped(rows):
    return jnp.concatenate([rows[:, HD // 2 :], rows[:, : HD // 2]], axis=1)


def rotate(rows, table, back=False):
    turned = halves_swapped(rows) * table[:, HD:]
    return rows * table[:, :HD] + (-turned if back else turned)


def table_rows(table_ref, run):
    return table_ref[pl.ds(pl.multiple_of(run * 64, 64), 64), :]


def project_kernel(runs, core, xs_ref, wq_ref, table_ref, q_ref, kv_ref):
    seq = pl.program_id(0)
    projected = dot_last(xs_ref[...], wq_ref[...])
    is_key = core[0] == 0
    for r in range(4):
        table = table_rows(table_ref, runs[seq * 4 + r])
        rows = projected[64 * r : 64 * r + 64]
        heads = [rotate(rows[:, HD * h : HD * h + HD], table) for h in range(4)]
        query = jnp.concatenate(heads, axis=1).astype(BF16)
        q_ref[64 * r : 64 * r + 64, :] = (query.astype(F32) * 0.125).astype(BF16)
        plain = rows[:, Q_DEV:]
        kv = jnp.where(is_key, rotate(plain, table), plain)
        half, u = r // 2, r % 2
        kv_ref[64 * u : 64 * u + 64, HD * half : HD * half + HD] = kv.astype(BF16)


def whole(dims):
    return pl.BlockSpec(dims, lambda i, *_: (0,) * len(dims))


def project(runs, core, xs, wq, table):
    return pl.pallas_call(
        project_kernel,
        out_shape=(shape((1024, Q_DEV)), shape((512, 128))),
        grid_spec=pltpu.PrefetchScalarGridSpec(
            num_scalar_prefetch=2,
            grid=(4,),
            in_specs=[
                pl.BlockSpec((256, D), lambda i, *_: (i, 0)),
                whole((320, D)),
                whole((2048, 128)),
            ],
            out_specs=[
                pl.BlockSpec((256, Q_DEV), lambda i, *_: (i, 0)),
                pl.BlockSpec((128, 128), lambda i, *_: (i, 0)),
            ],
        ),
        compiler_params=pltpu.CompilerParams(vmem_limit_bytes=40 * 2**20),
        name="project",
    )(runs, core, xs, wq, table)


def project_back_kernel(runs, core, dq_ref, dkv_ref, xs_ref, wq_ref, table_ref, parts_ref, gwq_ref, acc):
    seq = pl.program_id(0)
    is_key = core[0] == 0
    kv = []
    for r in range(4):
        table = table_rows(table_ref, runs[seq * 4 + r])
        half, u = r // 2, r % 2
        plain = dkv_ref[64 * u : 64 * u + 64, HD * half : HD * half + HD]
        kv.append(jnp.where(is_key, rotate(plain, table, back=True), plain))
    grads = jnp.concatenate([dq_ref[...], jnp.concatenate(kv, axis=0).astype(BF16)], axis=1)
    parts_ref[...] = dot(grads, wq_ref[...]).astype(BF16)
    term = dot_first(grads, xs_ref[...])

    @pl.when(seq == 0)
    def _():
        acc[...] = term

    @pl.when(seq > 0)
    def _():
        acc[...] += term

    @pl.when(seq == 3)
    def _():
        gwq_ref[...] = acc[...].astype(BF16)


def project_back(runs, core, dq, dkv, xs, wq, table):
    return pl.pallas_call(
        project_back_kernel,
        out_shape=(shape((1024, D)), shape((320, D))),
        grid_spec=pltpu.PrefetchScalarGridSpec(
            num_scalar_prefetch=2,
            grid=(4,),
            in_specs=[
                pl.BlockSpec((256, Q_DEV), lambda i, *_: (i, 0)),
                pl.BlockSpec((128, 128), lambda i, *_: (i, 0)),
                pl.BlockSpec((256, D), lambda i, *_: (i, 0)),
                whole((320, D)),
                whole((2048, 128)),
            ],
            out_specs=[
                pl.BlockSpec((256, D), lambda i, *_: (i, 0)),
                whole((320, D)),
            ],
            scratch_shapes=[pltpu.VMEM((320, D), F32)],
        ),
        compiler_params=pltpu.CompilerParams(vmem_limit_bytes=40 * 2**20),
        name="project_back",
    )(runs, core, dq, dkv, xs, wq, table)


def chips_in_sequence(me):
    return [(dz, dl) for dz in range(4) for dl in (0, 1)][1:]


def keys_kernel(
    kv, pos, cot, wout, kvs, poss, cots, wo, send, recv, os_, orr, local
):
    me = Place()
    partner = {"xl": 1 - me.xl, "xh": 1 - me.xh}
    core = me.at(core=1 - me.c)
    far = [
        me.at(dz=dz, xl=(1 - me.xl) if dl else me.xl) for dz, dl in chips_in_sequence(me)
    ]
    others = [
        me.at(y=lax.rem(me.y + dy, 4), core=c, **partner) for dy in range(4) for c in (0, 1)
    ]
    greet(far + group_members(me) + others)
    edges = Edges(send, recv)
    chip = 2 * me.z + me.xl
    keeps = [
        pltpu.make_async_copy(kv, kvs.at[me.c, chip], local.at[0]),
        pltpu.make_async_copy(pos, poss.at[chip], local.at[1]),
        pltpu.make_async_copy(cot, cots.at[2 * me.y + me.c], local.at[2]),
    ]
    for d in keeps:
        d.start()
    pos_copies = [edges.copy(pos, poss.at[chip], d) for d in far]
    kv_copies = [edges.copy(kv, kvs.at[me.c, chip], d) for d in far]
    over = [edges.copy(kv, kvs.at[me.c, chip], core)]
    ring = RingGather(me, edges, cot, cots)

    own = 2 * me.y + me.xh
    own_column = me.c == 0
    to_xl = jnp.where(own_column, me.xl, 1 - me.xl)
    to_xh = jnp.where(own_column, me.xh, 1 - me.xh)
    blocks = []
    for i in range(8):
        dy, other = i // 2, i % 2
        y = lax.rem(me.y + dy, 4)
        to_core = me.c if other == 0 else 1 - me.c
        stays = own_column if i == 0 else me.c < 0
        src = wout.at[:, pl.ds(pl.multiple_of(Q_DEV * (2 * y + to_core), Q_DEV), Q_DEV)]
        target = (me.z, to_xl, to_core, y, to_xh)
        send_block(me, src, wo.at[own], os_.at[i], orr.at[own], target, stays)
        blocks.append((src, os_.at[i], stays))
    ring.relay()
    for (dz, dl), d in zip(chips_in_sequence(me), kv_copies):
        d.wait_recv()
        source = 2 * lax.rem(me.z - dz + 4, 4) + ((1 - me.xl) if dl else me.xl)
        ref = kvs.at[me.c, source]
        over.append(edges.copy(ref, ref, core))
    ring.rest()
    for d in over + pos_copies:
        d.wait_recv()
    for i in range(8):
        wait_got(wo.at[i], orr.at[i])
    for src, sem, stays in blocks:
        wait_sent(src, sem, stays)
    edges.finish()
    for d in keeps:
        d.wait()


def exchange_keys(kv, pos, cot, wout):
    return pl.pallas_call(
        keys_kernel,
        out_shape=(
            shape((2, 8, 512, 128)),
            shape((8, 8, 8, TOK), jnp.int32),
            shape((8, TOK, D)),
            shape((8, 256, Q_DEV)),
        ),
        in_specs=[ANY] * 4,
        out_specs=(ANY,) * 4,
        scratch_shapes=sems(7 + 7 + 8 + GATHER_EDGES)
        + sems(8)
        + [pltpu.SemaphoreType.DMA((3,))],
        compiler_params=remote_params(1),
        name="exchange_keys",
    )(kv, pos, cot, wout)


def split_heads(rows):
    return jnp.concatenate([rows[:, HD * h : HD * (h + 1)] for h in range(4)], axis=0)


def join_heads(rows):
    return jnp.concatenate([rows[64 * h : 64 * (h + 1), :] for h in range(4)], axis=1)


def dot_last(a, b):
    return lax.dot_general(a, b, (((1,), (1,)), ((), ())), preferred_element_type=F32)


def dot_first(a, b):
    return lax.dot_general(a, b, (((0,), (0,)), ((), ())), preferred_element_type=F32)


def dot(a, b):
    return lax.dot_general(a, b, (((1,), (0,)), ((), ())), preferred_element_type=F32)


TILE = 256
WIDE = 4


def sort_keys(runs, seq, kv_ref, keys, values):
    for j in range(32):
        chip, core, u = j // 4, (j // 2) % 2, j % 2
        to = pl.ds(pl.multiple_of(runs[seq * 32 + j] * 64, 64), 64)
        rows, lanes = slice(64 * u, 64 * u + 64), slice(HD * core, HD * core + HD)
        keys[to, :] = kv_ref[0, chip, rows, lanes]
        values[to, :] = kv_ref[1, chip, rows, lanes]


def allowed_tile(tile, run):
    key = lax.broadcasted_iota(jnp.int32, (TILE, 256), 0) + tile * TILE
    query = lax.rem(lax.broadcasted_iota(jnp.int32, (TILE, 256), 1), 64) + run * 64
    return key <= query


def tile_rows(tile):
    return pl.ds(pl.multiple_of(tile * TILE, TILE), TILE)


def attend_kernel(
    key_runs, query_runs, q_ref, kv_ref, att_ref, ot_ref, lse_ref, keys, values, high_ref, total_ref, acc_ref
):
    seq = pl.program_id(0)
    sort_keys(key_runs, seq, kv_ref, keys, values)

    def one_run(r, _):
        run = query_runs[seq * 4 + r]
        rows = pl.ds(pl.multiple_of(r * 64, 64), 64)
        query = split_heads(q_ref[rows, :])
        last = run // 4
        high_ref[...] = jnp.full((1, 256), FILLER, F32)
        total_ref[...] = jnp.zeros((1, 256), F32)
        acc_ref[...] = jnp.zeros((HD, 256), F32)

        def tiles(first, count, masked):
            scores = []
            for k in range(count):
                score = dot_last(keys[tile_rows(first + k), :], query)
                if masked and k == count - 1:
                    score = jnp.where(allowed_tile(first + k, run), score, FILLER)
                scores.append(score)
            high = high_ref[...]
            new_high = high
            for score in scores:
                new_high = jnp.maximum(new_high, jnp.max(score, axis=0, keepdims=True))
            scale = jnp.exp(high - new_high)
            total = total_ref[...] * scale
            acc = acc_ref[...] * scale
            for k, score in enumerate(scores):
                weights = jnp.exp(score - new_high)
                total = total + jnp.sum(weights, axis=0, keepdims=True)
                acc = acc + dot_first(values[tile_rows(first + k), :], weights.astype(BF16))
            high_ref[...] = new_high
            total_ref[...] = total
            acc_ref[...] = acc

        @pl.when(last >= WIDE)
        def _():
            tiles(0, WIDE, False)

        start = (last // WIDE) * WIDE
        for n in range(WIDE):

            @pl.when(last - start == n)
            def _():
                tiles(start, n + 1, True)

        total = total_ref[...]
        out = acc_ref[...] / total
        ot_ref[r] = out
        lse_ref[r] = high_ref[...] + jnp.log(total)
        att_ref[rows, :] = join_heads(out.T).astype(BF16)
        return 0

    lax.fori_loop(0, 4, one_run, 0)


def attend(key_runs, query_runs, q, kv):
    return pl.pallas_call(
        attend_kernel,
        out_shape=(shape((1024, 256)), shape((16, HD, 256), F32), shape((16, 1, 256), F32)),
        grid_spec=pltpu.PrefetchScalarGridSpec(
            num_scalar_prefetch=2,
            grid=(4,),
            in_specs=[
                pl.BlockSpec((256, 256), lambda i, *_: (i, 0)),
                pl.BlockSpec((2, 8, 128, 128), lambda i, *_: (0, 0, i, 0)),
            ],
            out_specs=[
                pl.BlockSpec((256, 256), lambda i, *_: (i, 0)),
                pl.BlockSpec((4, HD, 256), lambda i, *_: (i, 0, 0)),
                pl.BlockSpec((4, 1, 256), lambda i, *_: (i, 0, 0)),
            ],
            scratch_shapes=[
                pltpu.VMEM((2048, HD), BF16),
                pltpu.VMEM((2048, HD), BF16),
                pltpu.VMEM((1, 256), F32),
                pltpu.VMEM((1, 256), F32),
                pltpu.VMEM((HD, 256), F32),
            ],
        ),
        compiler_params=pltpu.CompilerParams(vmem_limit_bytes=40 * 2**20),
        name="attend",
    )(key_runs, query_runs, q, kv)


def attend_back_kernel(
    key_runs, query_runs, q_ref, kv_ref, da_ref, ot_ref, lse_ref, table_ref,
    dq_ref, dkv_ref, keys, values, dkeys, dvalues, dq_acc,
):
    seq = pl.program_id(0)
    sort_keys(key_runs, seq, kv_ref, keys, values)
    dkeys[...] = jnp.zeros_like(dkeys)
    dvalues[...] = jnp.zeros_like(dvalues)

    def one_run(r, _):
        run = query_runs[seq * 4 + r]
        rows = pl.ds(pl.multiple_of(r * 64, 64), 64)
        query = split_heads(q_ref[rows, :])
        grad = split_heads(da_ref[rows, :])
        lse = lse_ref[r]
        delta = jnp.sum(grad.astype(F32).T * ot_ref[r], axis=0, keepdims=True)
        last = run // 4
        dq_acc[...] = jnp.zeros((HD, 256), F32)

        def tiles(first, count, masked):
            dq = dq_acc[...]
            for k in range(count):
                at = tile_rows(first + k)
                key = keys[at, :]
                probs = jnp.exp(dot_last(key, query) - lse)
                if masked and k == count - 1:
                    probs = jnp.where(allowed_tile(first + k, run), probs, 0.0)
                grad_probs = dot_last(values[at, :], grad)
                grad_scores = (probs * (grad_probs - delta)).astype(BF16)
                dvalues[at, :] += dot(probs.astype(BF16), grad)
                dkeys[at, :] += dot(grad_scores, query)
                dq = dq + dot_first(key, grad_scores)
            dq_acc[...] = dq

        @pl.when(last >= WIDE)
        def _():
            tiles(0, WIDE, False)

        start = (last // WIDE) * WIDE
        for n in range(WIDE):

            @pl.when(last - start == n)
            def _():
                tiles(start, n + 1, True)

        table = table_rows(table_ref, run)
        dq = (dq_acc[...] * 0.125).T
        heads = [rotate(dq[64 * h : 64 * h + 64], table, back=True) for h in range(4)]
        dq_ref[rows, :] = jnp.concatenate(heads, axis=1).astype(BF16)
        return 0

    lax.fori_loop(0, 4, one_run, 0)
    for j in range(32):
        chip, core, u = j // 4, (j // 2) % 2, j % 2
        at = pl.ds(pl.multiple_of(key_runs[seq * 32 + j] * 64, 64), 64)
        rows, lanes = slice(64 * u, 64 * u + 64), slice(HD * core, HD * core + HD)
        dkv_ref[0, chip, rows, lanes] = dkeys[at, :].astype(BF16)
        dkv_ref[1, chip, rows, lanes] = dvalues[at, :].astype(BF16)


def attend_back(key_runs, query_runs, q, kv, grad, ot, lse, table):
    return pl.pallas_call(
        attend_back_kernel,
        out_shape=(shape((1024, 256)), shape((2, 8, 512, 128))),
        grid_spec=pltpu.PrefetchScalarGridSpec(
            num_scalar_prefetch=2,
            grid=(4,),
            in_specs=[
                pl.BlockSpec((256, 256), lambda i, *_: (i, 0)),
                pl.BlockSpec((2, 8, 128, 128), lambda i, *_: (0, 0, i, 0)),
                pl.BlockSpec((256, 256), lambda i, *_: (i, 0)),
                pl.BlockSpec((4, HD, 256), lambda i, *_: (i, 0, 0)),
                pl.BlockSpec((4, 1, 256), lambda i, *_: (i, 0, 0)),
                whole((2048, 128)),
            ],
            out_specs=[
                pl.BlockSpec((256, 256), lambda i, *_: (i, 0)),
                pl.BlockSpec((2, 8, 128, 128), lambda i, *_: (0, 0, i, 0)),
            ],
            scratch_shapes=[
                pltpu.VMEM((2048, HD), BF16),
                pltpu.VMEM((2048, HD), BF16),
                pltpu.VMEM((2048, HD), F32),
                pltpu.VMEM((2048, HD), F32),
                pltpu.VMEM((HD, 256), F32),
            ],
        ),
        compiler_params=pltpu.CompilerParams(vmem_limit_bytes=40 * 2**20),
        name="attend_back",
    )(key_runs, query_runs, q, kv, grad, ot, lse, table)


ROWS = 16


def in_chunks(step):
    def one(i, _):
        step(pl.ds(pl.multiple_of(i * ROWS, ROWS), ROWS))
        return 0

    lax.fori_loop(0, TOK // ROWS, one, 0)


def mean_last(rows):
    return jnp.mean(rows, axis=-1, keepdims=True)


def middle_kernel(
    parts, tokens, gain, middle, xs, got, both, relayed, last, total, low, send, recv, local
):
    me = Place()
    greet([me.at(core=1 - me.c), me.at(dy=1), me.at(dy=-1)])
    edges = Edges(send, recv)
    ring = RingScatter(me, edges, parts, got, both, relayed, last)
    ring.first()
    ring.second()
    ring.total(total)

    def norm(at):
        rows = tokens[at, :].astype(F32) + total[at, :]
        middle[at, :] = rows
        normal = rows * lax.rsqrt(mean_last(rows * rows) + EPSILON)
        low[at, :] = (normal * gain[...]).astype(BF16)

    in_chunks(norm)
    keep = pltpu.make_async_copy(low, xs.at[2 * me.y + me.c], local)
    keep.start()
    gather = RingGather(me, edges, low, xs)
    gather.relay()
    gather.rest()
    edges.finish()
    keep.wait()


def to_middle(parts, tokens, gain):
    return pl.pallas_call(
        middle_kernel,
        out_shape=(shape((TOK, D), F32), shape((8, TOK, D))),
        in_specs=[VMEM] * 3,
        out_specs=(VMEM, ANY),
        scratch_shapes=scatter_scratch()
        + [pltpu.VMEM((TOK, D), F32), pltpu.VMEM((TOK, D), BF16)]
        + sems(SCATTER_EDGES + GATHER_EDGES)
        + [pltpu.SemaphoreType.DMA],
        compiler_params=remote_params(2),
        name="to_middle",
    )(parts, tokens, gain)


class SumOfFour:
    def __init__(self, me, along_z, src, piece, own, got, send, recv, local):
        self.src, self.piece, self.own, self.got = src, piece, own, got
        self.send, self.recv = send, recv
        here = me.z if along_z else x_of(me)
        self.keep = pltpu.make_async_copy(src.at[piece(here)], own, local)
        self.keep.start()
        for k in (1, 2, 3):
            device = around(me, k, 0) if along_z else around(me, 0, k)
            pltpu.make_async_remote_copy(
                src_ref=src.at[piece(lax.rem(here + k, 4))],
                dst_ref=got.at[k - 1],
                send_sem=send.at[k - 1],
                recv_sem=recv,
                device_id=device,
                device_id_type=pl.DeviceIdType.MESH,
            ).start()

    def total(self, out, rows):
        self.keep.wait()
        pltpu.make_async_copy(self.got, self.got, self.recv).wait()
        own, got = self.own, self.got

        def one(i, _):
            at = pl.ds(pl.multiple_of(i * rows, rows), rows)
            total = own[at, :].astype(F32)
            for k in range(3):
                total = total + got[k, at, :].astype(F32)
            out[at, :] = total.astype(BF16)
            return 0

        lax.fori_loop(0, out.shape[0] // rows, one, 0)

    def finish(self):
        for k in range(3):
            src = self.src.at[self.piece(0)]
            pltpu.make_async_copy(src, src, self.send.at[k]).wait()


def columns(width):
    return lambda i: (slice(None), pl.ds(pl.multiple_of(i * width, width), width))


def row_block(height, start=0):
    return lambda i: (pl.ds(pl.multiple_of(start + i * height, height), height), slice(None))


def mlp_back_kernel(
    branch_parts, grad_parts, middle, cot, gain, ggate, gup, gdn,
    output, grad_middle, gain_grad, gbs, gate_out, up_out, top_out, low_out,
    g1, b1, r1, l1, g2, b2, r2, l2, total, low,
    gate_own, gate_got, up_own, up_got, top_own, top_got, low_own, low_got,
    gate_q, up_q, top_q, low_q,
    gate_own2, gate_got2, up_own2, up_got2, top_own2, top_got2, low_own2, low_got2,
    send, recv, qs, qr, ql, local,
):
    me = Place()
    greet(
        [me.at(core=1 - me.c), me.at(dy=1), me.at(dy=-1)]
        + [around(me, k, 0) for k in (1, 2, 3)]
        + [around(me, 0, k) for k in (1, 2, 3)]
    )
    edges = Edges(send, recv)
    ring = RingScatter(me, edges, grad_parts, g2, b2, r2, l2)

    def quarter(i, along_z, src, piece, own, got):
        return SumOfFour(
            me, along_z, src, piece, own, got, qs.at[i], qr.at[i], ql.at[i]
        )

    gate_sum = quarter(0, True, ggate, columns(512), gate_own, gate_got)
    up_sum = quarter(1, False, gup, columns(512), up_own, up_got)
    top_sum = quarter(2, True, gdn, row_block(256), top_own, top_got)
    low_sum = quarter(3, False, gdn, row_block(256, 1024), low_own, low_got)
    ring.first()
    ring.second()
    ring.total(total)
    gain_grad[...] = jnp.zeros_like(gain_grad)

    def back(at):
        rows = middle[at, :]
        inverse = lax.rsqrt(mean_last(rows * rows) + EPSILON)
        normal = rows * inverse
        grad = total[at, :]
        gain_grad[...] += jnp.sum(normal * grad, axis=0, keepdims=True)
        scaled = grad * gain[...]
        result = cot[at, :].astype(F32) + inverse * (
            scaled - normal * mean_last(scaled * normal)
        )
        grad_middle[at, :] = result
        low[at, :] = result.astype(BF16)

    in_chunks(back)
    keep = pltpu.make_async_copy(low, gbs.at[2 * me.y + me.c], local)
    keep.start()
    gather = RingGather(me, edges, low, gbs)
    branch = RingScatter(me, edges, branch_parts, g1, b1, r1, l1)
    gather.relay()
    branch.first()
    gate_sum.total(gate_q, 64)
    up_sum.total(up_q, 64)
    top_sum.total(top_q, 64)
    low_sum.total(low_q, 64)
    branch.second()
    gate_two = quarter(4, False, gate_q, columns(128), gate_own2, gate_got2)
    up_two = quarter(5, True, up_q, columns(128), up_own2, up_got2)
    top_two = quarter(6, False, top_q, row_block(64), top_own2, top_got2)
    low_two = quarter(7, True, low_q, row_block(64), low_own2, low_got2)
    gather.rest()
    branch.total(total)

    def out(at):
        output[at, :] = (middle[at, :] + total[at, :]).astype(BF16)

    in_chunks(out)
    gate_two.total(gate_out, 64)
    up_two.total(up_out, 64)
    top_two.total(top_out, 64)
    low_two.total(low_out, 64)
    for d in (gate_sum, up_sum, top_sum, low_sum, gate_two, up_two, top_two, low_two):
        d.finish()
    edges.finish()
    keep.wait()


def mlp_back(branch_parts, grad_parts, middle, cot, gain, ggate, gup, gdn):
    def own_and_got(rows, width):
        return [pltpu.VMEM((rows, width), BF16), pltpu.VMEM((3, rows, width), BF16)]

    return pl.pallas_call(
        mlp_back_kernel,
        out_shape=(
            shape((TOK, D)),
            shape((TOK, D), F32),
            shape((1, D), F32),
            shape((8, TOK, D)),
            shape((FF_DEV, 128)),
            shape((FF_DEV, 128)),
            shape((64, FF_DEV)),
            shape((64, FF_DEV)),
        ),
        in_specs=[VMEM] * 5 + [ANY] * 3,
        out_specs=(VMEM, VMEM, VMEM, ANY, VMEM, VMEM, VMEM, VMEM),
        scratch_shapes=scatter_scratch() * 2
        + [pltpu.VMEM((TOK, D), F32), pltpu.VMEM((TOK, D), BF16)]
        + own_and_got(FF_DEV, 512) * 2
        + own_and_got(256, FF_DEV) * 2
        + [pltpu.VMEM((FF_DEV, 512), BF16)] * 2
        + [pltpu.VMEM((256, FF_DEV), BF16)] * 2
        + own_and_got(FF_DEV, 128) * 2
        + own_and_got(64, FF_DEV) * 2
        + sems(2 * SCATTER_EDGES + GATHER_EDGES)
        + [
            pltpu.SemaphoreType.DMA((8, 3)),
            pltpu.SemaphoreType.DMA((8,)),
            pltpu.SemaphoreType.DMA((8,)),
            pltpu.SemaphoreType.DMA,
        ],
        compiler_params=remote_params(3),
        name="mlp_back",
    )(branch_parts, grad_parts, middle, cot, gain, ggate, gup, gdn)


def key_grads_kernel(
    dkv, gwo, out, wo_out, got, both, last, wo_own, wo_got, wo_piece, wo_all,
    send, recv, ws, wr, local, ds, dr,
):
    me = Place()
    core = me.at(core=1 - me.c)
    far = [
        me.at(dz=dz, xl=(1 - me.xl) if dl else me.xl) for dz, dl in chips_in_sequence(me)
    ]
    wide = [around(me, dz, dx) for dz, dx in STEPS]
    greet(far + wide + group_members(me))
    edges = Edges(send, recv)
    order = []
    for dz, dl in chips_in_sequence(me) + [(0, 0)]:
        chip = 2 * lax.rem(me.z + dz, 4) + ((1 - me.xl) if dl else me.xl)
        order.append((chip, edges.copy(dkv.at[1 - me.c, chip], got.at[chip], core)))
    far_copies = []
    for i, (chip, d) in enumerate(order):
        d.wait_recv()
        both[chip] = (dkv[me.c, chip].astype(F32) + got[chip].astype(F32)).astype(BF16)
        if i < 7:
            far_copies.append(edges.copy(both.at[chip], last.at[i], far[i]))
    wo_sum = SumOfSixteen(me, gwo, row_block(128), wo_own, wo_got, ws, wr, local)
    total = both[2 * me.z + me.xl].astype(F32)
    for i, d in enumerate(far_copies):
        d.wait_recv()
        total = total + last[i].astype(F32)
    out[...] = total
    wo_piece[...] = wo_sum.total().astype(BF16)
    deliver = Deliver(me, ds, dr)
    rank = 2 * me.y + me.c
    dst = wo_all.at[
        pl.ds(pl.multiple_of(128 * me.xl, 128), 128),
        pl.ds(pl.multiple_of(Q_DEV * rank, Q_DEV), Q_DEV),
    ]
    deliver.to_owner(wo_piece, dst, me.y // 2, me.z, me.xh)
    half = wo_all.at[:, pl.ds(pl.multiple_of(1024 * me.c, 1024), 1024)]
    wait_got(half, dr)
    edges.copy(half, half, core).wait_recv()
    wo_out[...] = wo_all[...].astype(F32)
    wo_sum.finish()
    deliver.finish()
    edges.finish()


def sum_key_grads(dkv, gwo):
    return pl.pallas_call(
        key_grads_kernel,
        out_shape=(shape((512, 128), F32), shape((256, D), F32)),
        in_specs=[VMEM, ANY],
        out_specs=(VMEM, VMEM),
        scratch_shapes=[
            pltpu.VMEM((8, 512, 128), BF16),
            pltpu.VMEM((8, 512, 128), BF16),
            pltpu.VMEM((7, 512, 128), BF16),
            pltpu.VMEM((128, Q_DEV), BF16),
            pltpu.VMEM((15, 128, Q_DEV), BF16),
            pltpu.VMEM((128, Q_DEV), BF16),
            pltpu.VMEM((256, D), BF16),
        ]
        + sems(16)
        + [
            pltpu.SemaphoreType.DMA((15,)),
            pltpu.SemaphoreType.DMA,
            pltpu.SemaphoreType.DMA,
            pltpu.SemaphoreType.DMA((8,)),
            pltpu.SemaphoreType.DMA,
        ],
        compiler_params=remote_params(4),
        name="sum_key_grads",
    )(dkv, gwo)


def closing_kernel(
    parts, gwq, tokens, gain, grad_middle, gain_two,
    grad_tokens, gains, wq_out,
    got, both, relayed, last, total, wq_own, wq_got, wq_piece, wq_all,
    mine, near, near_sum, owners,
    send, recv, ws, wr, local, ds, dr, gs, gr, hs, hr,
):
    me = Place()
    members = group_members(me)
    greet(members + [around(me, dz, dx) for dz, dx in STEPS])
    edges = Edges(send, recv)
    ring = RingScatter(me, edges, parts, got, both, relayed, last)
    wq_sum = SumOfSixteen(me, gwq, columns(128), wq_own, wq_got, ws, wr, local)
    ring.first()
    ring.second()
    wq_piece[...] = wq_sum.total().astype(BF16)
    deliver = Deliver(me, ds, dr)
    piece = 4 * me.z + x_of(me)
    for j in range(5):
        block = own_block(me, j)
        owner, slot = block // 5, lax.rem(block, 5)
        dst = wq_all.at[
            pl.ds(pl.multiple_of(64 * slot, 64), 64),
            pl.ds(pl.multiple_of(128 * piece, 128), 128),
        ]
        deliver.to_owner(
            wq_piece.at[pl.ds(64 * j, 64)], dst, me.z // 2, owner // 2, lax.rem(owner, 2)
        )
    ring.total(total)
    mine[...] = jnp.zeros_like(mine)
    mine[1:2, :] = gain_two[...]

    def back(at):
        rows = tokens[at, :].astype(F32)
        inverse = lax.rsqrt(mean_last(rows * rows) + EPSILON)
        normal = rows * inverse
        grad = total[at, :]
        mine[0:1, :] += jnp.sum(normal * grad, axis=0, keepdims=True)
        scaled = grad * gain[...]
        grad_tokens[at, :] = grad_middle[at, :] + inverse * (
            scaled - normal * mean_last(scaled * normal)
        )

    in_chunks(back)

    def slice_of(rank):
        return mine.at[:, pl.ds(pl.multiple_of(256 * rank, 256), 256)]

    near_copies = []
    for k in range(1, 8):
        dy, other = k // 2, k % 2
        y = lax.rem(me.y + dy, 4)
        to_core = 1 - me.c if other else me.c
        d = pltpu.make_async_remote_copy(
            src_ref=slice_of(2 * y + to_core),
            dst_ref=near.at[k - 1],
            send_sem=gs.at[k - 1],
            recv_sem=gr,
            device_id=me.at(y=y, core=to_core),
            device_id_type=pl.DeviceIdType.MESH,
        )
        d.start()
        near_copies.append(d)
    own = mine[:, pl.ds(pl.multiple_of(256 * (2 * me.y + me.c), 256), 256)]
    wait_got(near, gr)
    for k in range(7):
        own = own + near[k]
    near_sum[...] = own
    far = Deliver(me, hs, hr)
    for to_core in (0, 1):
        far.to_owner(near_sum, owners.at[piece], to_core, me.y, me.c)

    half = wq_all.at[:, pl.ds(pl.multiple_of(1024 * me.c, 1024), 1024)]
    wait_got(half, dr)
    over = edges.copy(half, half, me.at(core=1 - me.c))
    wait_got(owners, hr)
    sum_all = owners[0]
    for k in range(1, 16):
        sum_all = sum_all + owners[k]
    gains[...] = sum_all
    over.wait_recv()
    wq_out[...] = wq_all[...].astype(F32)
    wq_sum.finish()
    deliver.finish()
    for d in near_copies:
        d.wait_send()
    far.finish()
    edges.finish()


def closing(parts, gwq, tokens, gain, grad_middle, gain_two):
    return pl.pallas_call(
        closing_kernel,
        out_shape=(
            shape((TOK, D), F32),
            shape((8, 256), F32),
            shape((320, D), F32),
        ),
        in_specs=[VMEM, ANY] + [VMEM] * 4,
        out_specs=(VMEM,) * 3,
        scratch_shapes=scatter_scratch()
        + [
            pltpu.VMEM((TOK, D), F32),
            pltpu.VMEM((320, 128), BF16),
            pltpu.VMEM((15, 320, 128), BF16),
            pltpu.VMEM((320, 128), BF16),
            pltpu.VMEM((320, D), BF16),
            pltpu.VMEM((8, D), F32),
            pltpu.VMEM((7, 8, 256), F32),
            pltpu.VMEM((8, 256), F32),
            pltpu.VMEM((16, 8, 256), F32),
        ]
        + sems(SCATTER_EDGES + 1)
        + [
            pltpu.SemaphoreType.DMA((15,)),
            pltpu.SemaphoreType.DMA,
            pltpu.SemaphoreType.DMA,
            pltpu.SemaphoreType.DMA((40,)),
            pltpu.SemaphoreType.DMA,
            pltpu.SemaphoreType.DMA((7,)),
            pltpu.SemaphoreType.DMA,
            pltpu.SemaphoreType.DMA((16,)),
            pltpu.SemaphoreType.DMA,
        ],
        compiler_params=remote_params(5),
        name="closing",
    )(parts, gwq, tokens, gain, grad_middle, gain_two)


def route(step):
    pairs = []
    for z in range(4):
        for xl in range(2):
            for c in range(2):
                for y in range(4):
                    for xh in range(2):
                        here = (((z * 2 + xl) * 2 + c) * 4 + y) * 2 + xh
                        z_to, xl_to, c_to, y_to, xh_to = step(z, xl, c, y, xh)
                        there = (((z_to * 2 + xl_to) * 2 + c_to) * 4 + y_to) * 2 + xh_to
                        pairs.append((here, there))
    return pairs


def to_worker(z, xl, c, y, xh):
    return (z, xl, c, y, xh) if c == xh else (z, 1 - xl, 1 - c, y, 1 - xh)


def to_owner(z, xl, c, y, xh):
    return (z, xl, xh, y, c)


def worker_shard(shard):
    rows = shard.shape[0] // 4
    mine = lax.dynamic_slice_in_dim(shard, lax.axis_index("z") * rows, rows)
    mine = lax.ppermute(mine, AXES, route(to_worker))
    return lax.all_gather(mine, "z", axis=0, tiled=True)


def gather_owned(piece):
    piece = lax.ppermute(piece, AXES, route(to_owner))
    return lax.all_gather(piece, ("z", "xl", "c"), axis=0).reshape((4, 2, 2) + piece.shape)


def body(hidden, positions, gain_attn, w_qkv, w_out, gain_mlp, w_gate_up, w_down, cotangent):
    core = lax.axis_index("c").reshape(1)
    gain_one = gain_attn.astype(F32).reshape(1, D)
    gain_two = gain_mlp.astype(F32).reshape(1, D)
    tokens = hidden[0].astype(F32)
    inverse_one = lax.rsqrt(jnp.mean(tokens * tokens, axis=-1, keepdims=True) + EPSILON)
    input_one = (tokens * inverse_one * gain_one).astype(BF16)
    table = jnp.asarray(rotary_table())
    xs, poss, wq = opening(input_one, jnp.broadcast_to(positions, (8, TOK)), w_qkv)
    gu = worker_shard(w_gate_up.reshape(2 * FF_DEV, D))
    dn = worker_shard(w_down)
    xs = xs.reshape(1024, D)
    wq = wq.reshape(320, D)
    query_runs = poss[:, 0, ::64].reshape(16) // 64
    query, kv = project(query_runs, core, xs, wq, table)
    kvs, places, cots, wo = exchange_keys(kv, poss, cotangent[0], w_out)
    cots = cots.reshape(1024, D)
    wo = wo.reshape(D, Q_DEV)
    key_runs = (
        places[:, :, 0, ::64].reshape(8, 4, 2, 2).transpose(1, 0, 2, 3).reshape(128) // 64
    )
    att, ot, lse = attend(key_runs, query_runs, query, kvs)
    parts = dot_last(att, wo).astype(BF16)
    middle, x2 = to_middle(parts.reshape(8, TOK, D), hidden[0], gain_two)
    x2 = x2.reshape(1024, D)

    gate = dot_last(x2, gu[:FF_DEV])
    upward = dot_last(x2, gu[FF_DEV:])
    grad_active = dot(cots, dn)
    sigmoid = jax.nn.sigmoid(gate)
    swish = gate * sigmoid
    active = (swish * upward).astype(BF16)
    grad_upward = (grad_active * swish).astype(BF16)
    grad_gate = (grad_active * upward * sigmoid * (1.0 + gate * (1.0 - sigmoid))).astype(BF16)
    branch_parts = dot_last(active, dn).astype(BF16).reshape(8, TOK, D)
    grad_parts = (dot(grad_gate, gu[:FF_DEV]) + dot(grad_upward, gu[FF_DEV:])).astype(BF16)
    ggate = dot_first(grad_gate, x2).astype(BF16)
    gup = dot_first(grad_upward, x2).astype(BF16)
    gdn = dot_first(cots, active).astype(BF16)
    output, grad_middle, gain_grad, gbs, gate_piece, up_piece, top_piece, low_piece = mlp_back(
        branch_parts, grad_parts.reshape(8, TOK, D), middle, cotangent[0], gain_two,
        ggate, gup, gdn,
    )
    gb = gbs.reshape(1024, D)
    grad_att = dot(gb, wo).astype(BF16)
    grad_wo = dot_first(gb, att).astype(BF16)
    grad_gu = gather_owned(jnp.stack([gate_piece, up_piece]))
    grad_dn = gather_owned(jnp.stack([top_piece, low_piece]))
    dq, dkv = attend_back(key_runs, query_runs, query, kvs, grad_att, ot, lse, table)
    dkv, grad_w_out = sum_key_grads(dkv, grad_wo)
    one_parts, gwq = project_back(query_runs, core, dq, dkv, xs, wq, table)
    grad_tokens, gains, grad_w_qkv = closing(
        one_parts.reshape(8, TOK, D), gwq, hidden[0], gain_one, grad_middle, gain_grad
    )

    gate_full = grad_gu[:, :, :, 0].transpose(3, 0, 2, 1, 4).reshape(FF_DEV, D)
    up_full = grad_gu[:, :, :, 1].transpose(3, 2, 1, 0, 4).reshape(FF_DEV, D)
    top_full = grad_dn[:, :, :, 0].transpose(0, 2, 1, 3, 4).reshape(1024, FF_DEV)
    low_full = grad_dn[:, :, :, 1].transpose(2, 1, 0, 3, 4).reshape(1024, FF_DEV)
    return (
        output[None],
        grad_tokens[None],
        gains[0],
        grad_w_qkv,
        grad_w_out,
        gains[1],
        jnp.stack([gate_full, up_full]).astype(F32),
        jnp.concatenate([top_full, low_full]).astype(F32),
    )


def solution(mesh):
    fine = Mesh(mesh.devices.reshape(4, 2, 2, 4, 2), AXES)
    ctx, fsdp = ("z", "xl", "c"), ("y", "xh")
    weight = P(fsdp, None)
    return jax.shard_map(
        body,
        mesh=fine,
        in_specs=(
            P(fsdp, ctx, None),
            P(fsdp, ctx),
            P(),
            weight,
            weight,
            P(),
            P(None, fsdp, None),
            P(None, fsdp),
            P(fsdp, ctx, None),
        ),
        out_specs=(
            P(fsdp, ctx, None),
            P(fsdp, ctx, None),
            P(fsdp),
            weight,
            weight,
            P(fsdp),
            P(None, fsdp, None),
            P(None, fsdp),
        ),
        check_vma=False,
    )
```

```python
import jax
import jax.numpy as jnp
import numpy as np
from jax import lax
from jax.experimental import pallas as pl
from jax.experimental.pallas import tpu as pltpu
from jax.sharding import Mesh
from jax.sharding import PartitionSpec as P

D = 2048
H = 32
KV = 4
HD = 64
FF = 5632
TOK = 128
HALF = 64
FF_DEV = 704
Q_DEV = 256
EPSILON = 1e-05
FILLER = -1e30
AXES = ("z", "xl", "c", "y", "xh")
ANY = pl.BlockSpec(memory_space=pl.ANY)
VMEM = pl.BlockSpec(memory_space=pltpu.VMEM)
BF16 = jnp.bfloat16
F32 = jnp.float32


class Place:
    def __init__(self):
        self.z, self.xl, self.c, self.y, self.xh = (lax.axis_index(a) for a in AXES)

    def at(self, dz=0, dy=0, core=None, xl=None, xh=None, y=None):
        z = lax.rem(self.z + dz + 4, 4) if dz else self.z
        y = (lax.rem(self.y + dy + 4, 4) if dy else self.y) if y is None else y
        return (
            z,
            self.xl if xl is None else xl,
            self.c if core is None else core,
            y,
            self.xh if xh is None else xh,
        )


class Edges:
    def __init__(self, send, recv):
        self.send, self.recv, self.count, self.started = send, recv, 0, []

    def copy(self, src, dst, device, start=True):
        i = self.count
        self.count += 1
        d = pltpu.make_async_remote_copy(
            src_ref=src,
            dst_ref=dst,
            send_sem=self.send.at[i],
            recv_sem=self.recv.at[i],
            device_id=device,
            device_id_type=pl.DeviceIdType.MESH,
        )
        self.started.append(d)
        if start:
            d.start()
        return d

    def sent(self, copies):
        for d in copies:
            d.wait_send()
        self.started = [d for d in self.started if all(d is not e for e in copies)]

    def finish(self):
        for d in self.started:
            d.wait_send()


def greet(devices):
    barrier = pltpu.get_barrier_semaphore()
    for device in devices:
        pl.semaphore_signal(
            barrier, inc=1, device_id=device, device_id_type=pl.DeviceIdType.MESH
        )
    pl.semaphore_wait(barrier, len(devices))


def group_members(me):
    found = [me.at(core=1 - me.c)]
    for dy in (1, 2, 3):
        found += [me.at(dy=dy), me.at(dy=dy, core=1 - me.c)]
    return found


class RingGather:
    def __init__(self, me, edges, own, out):
        self.me, self.edges, self.out = me, edges, out
        self.core = me.at(core=1 - me.c)
        self.up, self.down = me.at(dy=1), me.at(dy=-1)
        a, b = pl.ds(0, HALF), pl.ds(HALF, HALF)
        self.a, self.b = a, b
        mine = self.slot(0)
        self.up_a = edges.copy(own.at[a], out.at[mine, a], self.up)
        self.down_b = edges.copy(own.at[b], out.at[mine, b], self.down)
        self.up_b = edges.copy(own.at[b], out.at[mine, b], self.up)
        self.down_a = edges.copy(own.at[a], out.at[mine, a], self.down)
        self.to_core = [edges.copy(own, out.at[mine], self.core)]

    def slot(self, dy):
        return 2 * lax.rem(self.me.y + dy + 4, 4) + self.me.c

    def pass_core(self, dy, part):
        ref = self.out.at[self.slot(dy), part]
        self.to_core.append(self.edges.copy(ref, ref, self.core))

    def relay(self):
        out = self.out
        self.up_a.wait_recv()
        ref = out.at[self.slot(-1), self.a]
        self.on_a = self.edges.copy(ref, ref, self.up)
        self.down_b.wait_recv()
        ref = out.at[self.slot(1), self.b]
        self.on_b = self.edges.copy(ref, ref, self.down)
        self.pass_core(-1, self.a)
        self.pass_core(1, self.b)

    def near(self):
        self.up_b.wait_recv()
        self.pass_core(-1, self.b)
        self.down_a.wait_recv()
        self.pass_core(1, self.a)

    def far(self):
        self.on_a.wait_recv()
        self.pass_core(2, self.a)
        self.on_b.wait_recv()
        self.pass_core(2, self.b)

    def from_core(self, first, last):
        for d in self.to_core[first:last]:
            d.wait_recv()

    def rest(self):
        self.near()
        self.far()
        self.from_core(0, 7)


GATHER_EDGES = 13


class RingScatter:
    def __init__(self, me, edges, parts, scratch):
        self.me, self.edges, self.parts = me, edges, parts
        self.got, self.both, self.relayed, self.last = scratch
        self.up, self.down = me.at(dy=1), me.at(dy=-1)
        self.cores = {}
        self.a, self.b = pl.ds(0, HALF), pl.ds(HALF, HALF)

    def send_core(self, k):
        row = 2 * lax.rem(self.me.y + k, 4) + 1 - self.me.c
        core = self.me.at(core=1 - self.me.c)
        self.cores[k] = self.edges.copy(self.parts.at[row], self.got.at[k], core)

    def add_core(self, k):
        self.cores[k].wait_recv()
        row = 2 * lax.rem(self.me.y + k, 4) + self.me.c

        def add(at):
            self.both[k, at] = (
                self.parts[row, at].astype(F32) + self.got[k, at].astype(F32)
            ).astype(BF16)

        in_chunks(add)

    def far(self):
        self.add_core(2)
        e, both = self.edges, self.both
        self.r_a = e.copy(both.at[2, self.a], self.relayed.at[0], self.up)
        self.r_b = e.copy(both.at[2, self.b], self.relayed.at[1], self.down)

    def near(self):
        e, both = self.edges, self.both
        self.add_core(1)
        self.u_b = e.copy(both.at[1, self.b], self.last.at[0, self.b], self.up)
        self.add_core(3)
        self.d_a = e.copy(both.at[3, self.a], self.last.at[1, self.a], self.down)

    def first(self):
        for k in (2, 1, 3, 0):
            self.send_core(k)
        self.far()
        self.near()
        self.add_core(0)

    def second(self):
        a, b, e, both = self.a, self.b, self.edges, self.both
        self.r_a.wait_recv()
        both[1, a] = (both[1, a].astype(F32) + self.relayed[0].astype(F32)).astype(BF16)
        self.u_a = e.copy(both.at[1, a], self.last.at[0, a], self.up)
        self.r_b.wait_recv()
        both[3, b] = (both[3, b].astype(F32) + self.relayed[1].astype(F32)).astype(BF16)
        self.d_b = e.copy(both.at[3, b], self.last.at[1, b], self.down)

    def arrived(self):
        for d in (self.u_b, self.d_a, self.u_a, self.d_b):
            d.wait_recv()

    def rows(self, at):
        return (
            self.both[0, at].astype(F32)
            + self.last[0, at].astype(F32)
            + self.last[1, at].astype(F32)
        )

    def release(self):
        ring = [self.r_a, self.r_b, self.u_b, self.d_a, self.u_a, self.d_b]
        self.edges.sent(ring + list(self.cores.values()))


SCATTER_EDGES = 10


def scatter_scratch():
    return [
        pltpu.VMEM((4, TOK, D), BF16),
        pltpu.VMEM((4, TOK, D), BF16),
        pltpu.VMEM((2, HALF, D), BF16),
        pltpu.VMEM((2, TOK, D), BF16),
    ]


def sems(n):
    return [pltpu.SemaphoreType.DMA((n,)), pltpu.SemaphoreType.DMA((n,))]


def shape(dims, dtype=BF16):
    return jax.ShapeDtypeStruct(dims, dtype)


def remote_params(number):
    return pltpu.CompilerParams(
        collective_id=number, has_side_effects=True, vmem_limit_bytes=48 * 2**20
    )


def block_place(block):
    is_kv = block >= 32
    other = block - 32
    rank = block // 4
    y = jnp.where(is_kv, lax.rem(other + 32, 4), rank // 2)
    core = jnp.where(is_kv, other // 4, lax.rem(rank, 2))
    return y, core, jnp.where(is_kv, 4, lax.rem(block, 4))


def own_block(me, j):
    if j == 4:
        return 32 + 4 * me.c + me.y
    return 4 * (2 * me.y + me.c) + j


def send_block(me, src, dst, send_sem, recv_sem, target, stays):
    @pl.when(stays)
    def _():
        pltpu.make_async_copy(src, dst, recv_sem).start()

    @pl.when(jnp.logical_not(stays))
    def _():
        pltpu.make_async_remote_copy(
            src_ref=src,
            dst_ref=dst,
            send_sem=send_sem,
            recv_sem=recv_sem,
            device_id=target,
            device_id_type=pl.DeviceIdType.MESH,
        ).start()


def wait_sent(src, send_sem, stays):
    @pl.when(jnp.logical_not(stays))
    def _():
        pltpu.make_async_copy(src, src, send_sem).wait()


def wait_got(dst, recv_sem):
    pltpu.make_async_copy(dst, dst, recv_sem).wait()


def x_of(me):
    return 2 * me.xh + me.xl


def around(me, dz, dx):
    x = lax.rem(x_of(me) + dx, 4)
    return me.at(dz=dz, xl=lax.rem(x, 2), xh=x // 2)


STEPS = [(dz, dx) for dz in range(4) for dx in range(4)][1:]


class SumOfSixteen:
    def __init__(self, me, src, piece, own, got, send, recv, local):
        self.me, self.src, self.piece, self.own, self.got = me, src, piece, own, got
        self.send, self.recv = send, recv
        self.keep = pltpu.make_async_copy(
            src.at[piece(4 * me.z + x_of(me))], own, local
        )
        self.keep.start()
        for k, (dz, dx) in enumerate(STEPS):
            to = 4 * lax.rem(me.z + dz, 4) + lax.rem(x_of(me) + dx, 4)
            self.copy(src.at[piece(to)], k, around(me, dz, dx)).start()

    def copy(self, src, k, device):
        return pltpu.make_async_remote_copy(
            src_ref=src,
            dst_ref=self.got.at[k],
            send_sem=self.send.at[k],
            recv_sem=self.recv,
            device_id=device,
            device_id_type=pl.DeviceIdType.MESH,
        )

    def total(self):
        self.keep.wait()
        pltpu.make_async_copy(self.got, self.got, self.recv).wait()
        total = self.own[...].astype(F32)
        for k in range(15):
            total = total + self.got[k].astype(F32)
        return total

    def finish(self):
        for k in range(15):
            src = self.src.at[self.piece(0)]
            pltpu.make_async_copy(src, src, self.send.at[k]).wait()


def same(me, z, xl, core, y, xh):
    return (z == me.z) & (xl == me.xl) & (core == me.c) & (y == me.y) & (xh == me.xh)


class Deliver:
    def __init__(self, me, send, recv):
        self.me, self.send, self.recv, self.sent = me, send, recv, []

    def to_owner(self, src, dst, core, y, xh):
        me = self.me
        for dz in range(4):
            for dl in (0, 1):
                z = lax.rem(me.z + dz, 4)
                xl = 1 - me.xl if dl else me.xl
                stays = same(me, z, xl, core, y, xh)
                sem = self.send.at[len(self.sent)]
                send_block(me, src, dst, sem, self.recv, (z, xl, core, y, xh), stays)
                self.sent.append((src, sem, stays))

    def finish(self):
        for src, sem, stays in self.sent:
            wait_sent(src, sem, stays)


def opening_kernel(
    x, pos, wqkv, wgu, wdn, xs, poss, wq, wswap, send, recv, qs, qr, ws, wr, local
):
    me = Place()
    partner = {"xl": 1 - me.xl, "xh": 1 - me.xh}
    members = group_members(me)
    others = [
        me.at(y=lax.rem(me.y + dy, 4), core=core, **partner)
        for dy in range(4)
        for core in (0, 1)
    ]
    greet(members + others)
    edges = Edges(send, recv)
    own_rank = 2 * me.y + me.c
    keep = pltpu.make_async_copy(x, xs.at[own_rank], local.at[0])
    keep.start()
    keep_pos = pltpu.make_async_copy(pos, poss.at[own_rank], local.at[1])
    keep_pos.start()
    pos_copies = [edges.copy(pos, poss.at[own_rank], m) for m in members]
    ring = RingGather(me, edges, x, xs)

    own = 2 * me.y + me.xh
    own_column = me.c == 0
    to_xl = jnp.where(own_column, me.xl, 1 - me.xl)
    to_xh = jnp.where(own_column, me.xh, 1 - me.xh)
    blocks = []
    for i in range(5):
        y, core, slot = block_place(5 * own + i)
        stays = own_column & (y == me.y) & (core == me.c)
        src = wqkv.at[pl.ds(64 * i, 64)]
        send_block(
            me, src, wq.at[slot], qs.at[i], qr.at[slot], (me.z, to_xl, core, y, to_xh), stays
        )
        blocks.append((src, qs.at[i], stays))
    swaps = swap_copies(me, wgu, wdn, wswap, ws, wr)

    @pl.when(me.c != me.xh)
    def _():
        for d in swaps:
            d.start()

    ring.relay()
    ring.rest()

    @pl.when(me.c != me.xh)
    def _():
        for d in swaps:
            d.wait()

    for d in pos_copies:
        d.wait_recv()
    for i in range(5):
        wait_got(wq.at[i], qr.at[i])
    for src, sem, stays in blocks:
        wait_sent(src, sem, stays)
    edges.finish()
    keep.wait()
    keep_pos.wait()


GU_QUARTER = 2 * FF_DEV // 4
DN_QUARTER = FF_DEV // 4
QUARTER = GU_QUARTER + DN_QUARTER


def swap_copies(me, wgu, wdn, wswap, send, recv):
    found = []
    across = me.at(core=1 - me.c, xl=1 - me.xl, xh=1 - me.xh)
    for i, (src, rows, start) in enumerate(
        ((wgu, GU_QUARTER, 0), (wdn, DN_QUARTER, GU_QUARTER))
    ):
        found.append(
            pltpu.make_async_remote_copy(
                src_ref=src.at[pl.ds(pl.multiple_of(rows * me.z, 16), rows)],
                dst_ref=wswap.at[pl.ds(start, rows)],
                send_sem=send.at[i],
                recv_sem=recv.at[i],
                device_id=across,
                device_id_type=pl.DeviceIdType.MESH,
            )
        )
    return found


def opening(x, pos, wqkv, wgu, wdn):
    return pl.pallas_call(
        opening_kernel,
        out_shape=(
            shape((8, TOK, D)),
            shape((8, 8, TOK), jnp.int32),
            shape((5, 64, D)),
            shape((QUARTER, D)),
        ),
        in_specs=[ANY] * 5,
        out_specs=(ANY,) * 4,
        scratch_shapes=sems(7 + GATHER_EDGES)
        + sems(5)
        + sems(2)
        + [pltpu.SemaphoreType.DMA((2,))],
        compiler_params=remote_params(0),
        name="opening",
    )(x, pos, wqkv, wgu, wdn)


def rotary_table():
    steps = np.arange(HD // 2, dtype=np.float32)
    inverse = np.power(np.float32(10000.0), steps * np.float32(-2.0 / HD)).astype(np.float32)
    turning = np.arange(2048, dtype=np.float32)[:, None] * inverse[None, :]
    cosine, sine = np.cos(turning), np.sin(turning)
    return np.concatenate([cosine, cosine, -sine, sine], axis=1).astype(np.float32)


def halves_swapped(rows):
    return jnp.concatenate([rows[:, HD // 2 :], rows[:, : HD // 2]], axis=1)


def rotate(rows, table, back=False):
    turned = halves_swapped(rows) * table[:, HD:]
    return rows * table[:, :HD] + (-turned if back else turned)


def table_rows(table_ref, run):
    return table_ref[pl.ds(pl.multiple_of(run * 64, 64), 64), :]


def project_kernel(runs, core, xs_ref, wq_ref, table_ref, q_ref, kv_ref):
    seq = pl.program_id(0)
    projected = dot_last(xs_ref[...], wq_ref[...])
    is_key = core[0] == 0
    for r in range(4):
        table = table_rows(table_ref, runs[seq * 4 + r])
        rows = projected[64 * r : 64 * r + 64]
        heads = [rotate(rows[:, HD * h : HD * h + HD], table) for h in range(4)]
        query = jnp.concatenate(heads, axis=1).astype(BF16)
        q_ref[64 * r : 64 * r + 64, :] = (query.astype(F32) * 0.125).astype(BF16)
        plain = rows[:, Q_DEV:]
        kv = jnp.where(is_key, rotate(plain, table), plain)
        half, u = r // 2, r % 2
        kv_ref[64 * u : 64 * u + 64, HD * half : HD * half + HD] = kv.astype(BF16)


def whole(dims):
    return pl.BlockSpec(dims, lambda i, *_: (0,) * len(dims))


def project(runs, core, xs, wq, table):
    return pl.pallas_call(
        project_kernel,
        out_shape=(shape((1024, Q_DEV)), shape((512, 128))),
        grid_spec=pltpu.PrefetchScalarGridSpec(
            num_scalar_prefetch=2,
            grid=(4,),
            in_specs=[
                pl.BlockSpec((256, D), lambda i, *_: (i, 0)),
                whole((320, D)),
                whole((2048, 128)),
            ],
            out_specs=[
                pl.BlockSpec((256, Q_DEV), lambda i, *_: (i, 0)),
                pl.BlockSpec((128, 128), lambda i, *_: (i, 0)),
            ],
        ),
        compiler_params=pltpu.CompilerParams(vmem_limit_bytes=40 * 2**20),
        name="project",
    )(runs, core, xs, wq, table)


def project_back_kernel(runs, core, dq_ref, dkv_ref, xs_ref, wq_ref, table_ref, parts_ref, gwq_ref, acc):
    seq = pl.program_id(0)
    is_key = core[0] == 0
    kv = []
    for r in range(4):
        table = table_rows(table_ref, runs[seq * 4 + r])
        half, u = r // 2, r % 2
        plain = dkv_ref[64 * u : 64 * u + 64, HD * half : HD * half + HD]
        kv.append(jnp.where(is_key, rotate(plain, table, back=True), plain))
    grads = jnp.concatenate([dq_ref[...], jnp.concatenate(kv, axis=0).astype(BF16)], axis=1)
    parts_ref[...] = dot(grads, wq_ref[...]).astype(BF16)
    term = dot_first(grads, xs_ref[...])

    @pl.when(seq == 0)
    def _():
        acc[...] = term

    @pl.when(seq > 0)
    def _():
        acc[...] += term

    @pl.when(seq == 3)
    def _():
        gwq_ref[...] = acc[...].astype(BF16)


def project_back(runs, core, dq, dkv, xs, wq, table):
    return pl.pallas_call(
        project_back_kernel,
        out_shape=(shape((1024, D)), shape((320, D))),
        grid_spec=pltpu.PrefetchScalarGridSpec(
            num_scalar_prefetch=2,
            grid=(4,),
            in_specs=[
                pl.BlockSpec((256, Q_DEV), lambda i, *_: (i, 0)),
                pl.BlockSpec((128, 128), lambda i, *_: (i, 0)),
                pl.BlockSpec((256, D), lambda i, *_: (i, 0)),
                whole((320, D)),
                whole((2048, 128)),
            ],
            out_specs=[
                pl.BlockSpec((256, D), lambda i, *_: (i, 0)),
                whole((320, D)),
            ],
            scratch_shapes=[pltpu.VMEM((320, D), F32)],
        ),
        compiler_params=pltpu.CompilerParams(vmem_limit_bytes=40 * 2**20),
        name="project_back",
    )(runs, core, dq, dkv, xs, wq, table)


def chips_in_sequence(me):
    return [(dz, dl) for dz in range(4) for dl in (0, 1)][1:]


def keys_kernel(
    kv, pos, cot, wout, wswap, kvs, poss, cots, wo, wnear, send, recv, os_, orr, ws, wr, local
):
    me = Place()
    partner = {"xl": 1 - me.xl, "xh": 1 - me.xh}
    core = me.at(core=1 - me.c)
    far = [
        me.at(dz=dz, xl=(1 - me.xl) if dl else me.xl) for dz, dl in chips_in_sequence(me)
    ]
    others = [
        me.at(y=lax.rem(me.y + dy, 4), core=c, **partner) for dy in range(4) for c in (0, 1)
    ]
    depth = [me.at(dz=1), me.at(dz=-1)]
    greet(far + group_members(me) + others)
    edges = Edges(send, recv)
    chip = 2 * me.z + me.xl
    steps = [
        pltpu.make_async_remote_copy(
            src_ref=wswap,
            dst_ref=wnear.at[i],
            send_sem=ws.at[i],
            recv_sem=wr.at[i],
            device_id=depth[i],
            device_id_type=pl.DeviceIdType.MESH,
        )
        for i in range(2)
    ]
    keeps = [
        pltpu.make_async_copy(kv, kvs.at[me.c, chip], local.at[0]),
        pltpu.make_async_copy(pos, poss.at[chip], local.at[1]),
        pltpu.make_async_copy(cot, cots.at[2 * me.y + me.c], local.at[2]),
    ]
    for d in keeps:
        d.start()
    pos_copies = [edges.copy(pos, poss.at[chip], d) for d in far]
    kv_copies = [edges.copy(kv, kvs.at[me.c, chip], d) for d in far]
    over = [edges.copy(kv, kvs.at[me.c, chip], core)]
    ring = RingGather(me, edges, cot, cots)

    own = 2 * me.y + me.xh
    own_column = me.c == 0
    to_xl = jnp.where(own_column, me.xl, 1 - me.xl)
    to_xh = jnp.where(own_column, me.xh, 1 - me.xh)
    blocks = []
    for i in range(8):
        dy, other = i // 2, i % 2
        y = lax.rem(me.y + dy, 4)
        to_core = me.c if other == 0 else 1 - me.c
        stays = own_column if i == 0 else me.c < 0
        src = wout.at[:, pl.ds(pl.multiple_of(Q_DEV * (2 * y + to_core), Q_DEV), Q_DEV)]
        target = (me.z, to_xl, to_core, y, to_xh)
        send_block(me, src, wo.at[own], os_.at[i], orr.at[own], target, stays)
        blocks.append((src, os_.at[i], stays))

    @pl.when(me.c != me.xh)
    def _():
        for d in steps:
            d.start()

    ring.relay()
    for (dz, dl), d in zip(chips_in_sequence(me), kv_copies):
        d.wait_recv()
        source = 2 * lax.rem(me.z - dz + 4, 4) + ((1 - me.xl) if dl else me.xl)
        ref = kvs.at[me.c, source]
        over.append(edges.copy(ref, ref, core))
    ring.rest()
    for d in over + pos_copies:
        d.wait_recv()
    for i in range(8):
        wait_got(wo.at[i], orr.at[i])
    for src, sem, stays in blocks:
        wait_sent(src, sem, stays)

    @pl.when(me.c != me.xh)
    def _():
        for d in steps:
            d.wait()

    edges.finish()
    for d in keeps:
        d.wait()


def exchange_keys(kv, pos, cot, wout, wswap):
    return pl.pallas_call(
        keys_kernel,
        out_shape=(
            shape((2, 8, 512, 128)),
            shape((8, 8, 8, TOK), jnp.int32),
            shape((8, TOK, D)),
            shape((8, 256, Q_DEV)),
            shape((2, QUARTER, D)),
        ),
        in_specs=[ANY] * 5,
        out_specs=(ANY,) * 5,
        scratch_shapes=sems(7 + 7 + 8 + GATHER_EDGES)
        + sems(8)
        + sems(2)
        + [pltpu.SemaphoreType.DMA((3,))],
        compiler_params=remote_params(1),
        name="exchange_keys",
    )(kv, pos, cot, wout, wswap)


def split_heads(rows):
    return jnp.concatenate([rows[:, HD * h : HD * (h + 1)] for h in range(4)], axis=0)


def join_heads(rows):
    return jnp.concatenate([rows[64 * h : 64 * (h + 1), :] for h in range(4)], axis=1)


def dot_last(a, b):
    return lax.dot_general(a, b, (((1,), (1,)), ((), ())), preferred_element_type=F32)


def dot_first(a, b):
    return lax.dot_general(a, b, (((0,), (0,)), ((), ())), preferred_element_type=F32)


def dot(a, b):
    return lax.dot_general(a, b, (((1,), (0,)), ((), ())), preferred_element_type=F32)


TILE = 256
WIDE = 4


def sort_keys(runs, seq, kv_ref, keys, values):
    for j in range(32):
        chip, core, u = j // 4, (j // 2) % 2, j % 2
        to = pl.ds(pl.multiple_of(runs[seq * 32 + j] * 64, 64), 64)
        rows, lanes = slice(64 * u, 64 * u + 64), slice(HD * core, HD * core + HD)
        keys[to, :] = kv_ref[0, chip, rows, lanes]
        values[to, :] = kv_ref[1, chip, rows, lanes]


def allowed_tile(tile, run):
    key = lax.broadcasted_iota(jnp.int32, (TILE, 256), 0) + tile * TILE
    query = lax.rem(lax.broadcasted_iota(jnp.int32, (TILE, 256), 1), 64) + run * 64
    return key <= query


def tile_rows(tile):
    return pl.ds(pl.multiple_of(tile * TILE, TILE), TILE)


def attend_kernel(
    key_runs, query_runs, q_ref, kv_ref, att_ref, ot_ref, lse_ref, keys, values, high_ref, total_ref, acc_ref
):
    seq = pl.program_id(0)
    sort_keys(key_runs, seq, kv_ref, keys, values)

    def one_run(r, _):
        run = query_runs[seq * 4 + r]
        rows = pl.ds(pl.multiple_of(r * 64, 64), 64)
        query = split_heads(q_ref[rows, :])
        last = run // 4
        high_ref[...] = jnp.full((1, 256), FILLER, F32)
        total_ref[...] = jnp.zeros((1, 256), F32)
        acc_ref[...] = jnp.zeros((HD, 256), F32)

        def tiles(first, count, masked):
            scores = []
            for k in range(count):
                score = dot_last(keys[tile_rows(first + k), :], query)
                if masked and k == count - 1:
                    score = jnp.where(allowed_tile(first + k, run), score, FILLER)
                scores.append(score)
            high = high_ref[...]
            new_high = high
            for score in scores:
                new_high = jnp.maximum(new_high, jnp.max(score, axis=0, keepdims=True))
            scale = jnp.exp(high - new_high)
            total = total_ref[...] * scale
            acc = acc_ref[...] * scale
            for k, score in enumerate(scores):
                weights = jnp.exp(score - new_high)
                total = total + jnp.sum(weights, axis=0, keepdims=True)
                acc = acc + dot_first(values[tile_rows(first + k), :], weights.astype(BF16))
            high_ref[...] = new_high
            total_ref[...] = total
            acc_ref[...] = acc

        @pl.when(last >= WIDE)
        def _():
            tiles(0, WIDE, False)

        start = (last // WIDE) * WIDE
        for n in range(WIDE):

            @pl.when(last - start == n)
            def _():
                tiles(start, n + 1, True)

        total = total_ref[...]
        out = acc_ref[...] / total
        ot_ref[r] = out
        lse_ref[r] = high_ref[...] + jnp.log(total)
        att_ref[rows, :] = join_heads(out.T).astype(BF16)
        return 0

    lax.fori_loop(0, 4, one_run, 0)


def attend(key_runs, query_runs, q, kv):
    return pl.pallas_call(
        attend_kernel,
        out_shape=(shape((1024, 256)), shape((16, HD, 256), F32), shape((16, 1, 256), F32)),
        grid_spec=pltpu.PrefetchScalarGridSpec(
            num_scalar_prefetch=2,
            grid=(4,),
            in_specs=[
                pl.BlockSpec((256, 256), lambda i, *_: (i, 0)),
                pl.BlockSpec((2, 8, 128, 128), lambda i, *_: (0, 0, i, 0)),
            ],
            out_specs=[
                pl.BlockSpec((256, 256), lambda i, *_: (i, 0)),
                pl.BlockSpec((4, HD, 256), lambda i, *_: (i, 0, 0)),
                pl.BlockSpec((4, 1, 256), lambda i, *_: (i, 0, 0)),
            ],
            scratch_shapes=[
                pltpu.VMEM((2048, HD), BF16),
                pltpu.VMEM((2048, HD), BF16),
                pltpu.VMEM((1, 256), F32),
                pltpu.VMEM((1, 256), F32),
                pltpu.VMEM((HD, 256), F32),
            ],
        ),
        compiler_params=pltpu.CompilerParams(vmem_limit_bytes=40 * 2**20),
        name="attend",
    )(key_runs, query_runs, q, kv)


def attend_back_kernel(
    key_runs, query_runs, q_ref, kv_ref, da_ref, ot_ref, lse_ref, table_ref,
    dq_ref, dkv_ref, keys, values, dkeys, dvalues, dq_acc,
):
    seq = pl.program_id(0)
    sort_keys(key_runs, seq, kv_ref, keys, values)
    dkeys[...] = jnp.zeros_like(dkeys)
    dvalues[...] = jnp.zeros_like(dvalues)

    def one_run(r, _):
        run = query_runs[seq * 4 + r]
        rows = pl.ds(pl.multiple_of(r * 64, 64), 64)
        query = split_heads(q_ref[rows, :])
        grad = split_heads(da_ref[rows, :])
        lse = lse_ref[r]
        delta = jnp.sum(grad.astype(F32).T * ot_ref[r], axis=0, keepdims=True)
        last = run // 4
        dq_acc[...] = jnp.zeros((HD, 256), F32)

        def tiles(first, count, masked):
            dq = dq_acc[...]
            for k in range(count):
                at = tile_rows(first + k)
                key = keys[at, :]
                probs = jnp.exp(dot_last(key, query) - lse)
                if masked and k == count - 1:
                    probs = jnp.where(allowed_tile(first + k, run), probs, 0.0)
                grad_probs = dot_last(values[at, :], grad)
                grad_scores = (probs * (grad_probs - delta)).astype(BF16)
                dvalues[at, :] += dot(probs.astype(BF16), grad)
                dkeys[at, :] += dot(grad_scores, query)
                dq = dq + dot_first(key, grad_scores)
            dq_acc[...] = dq

        @pl.when(last >= WIDE)
        def _():
            tiles(0, WIDE, False)

        start = (last // WIDE) * WIDE
        for n in range(WIDE):

            @pl.when(last - start == n)
            def _():
                tiles(start, n + 1, True)

        table = table_rows(table_ref, run)
        dq = (dq_acc[...] * 0.125).T
        heads = [rotate(dq[64 * h : 64 * h + 64], table, back=True) for h in range(4)]
        dq_ref[rows, :] = jnp.concatenate(heads, axis=1).astype(BF16)
        return 0

    lax.fori_loop(0, 4, one_run, 0)
    for j in range(32):
        chip, core, u = j // 4, (j // 2) % 2, j % 2
        at = pl.ds(pl.multiple_of(key_runs[seq * 32 + j] * 64, 64), 64)
        rows, lanes = slice(64 * u, 64 * u + 64), slice(HD * core, HD * core + HD)
        dkv_ref[0, chip, rows, lanes] = dkeys[at, :].astype(BF16)
        dkv_ref[1, chip, rows, lanes] = dvalues[at, :].astype(BF16)


def attend_back(key_runs, query_runs, q, kv, grad, ot, lse, table):
    return pl.pallas_call(
        attend_back_kernel,
        out_shape=(shape((1024, 256)), shape((2, 8, 512, 128))),
        grid_spec=pltpu.PrefetchScalarGridSpec(
            num_scalar_prefetch=2,
            grid=(4,),
            in_specs=[
                pl.BlockSpec((256, 256), lambda i, *_: (i, 0)),
                pl.BlockSpec((2, 8, 128, 128), lambda i, *_: (0, 0, i, 0)),
                pl.BlockSpec((256, 256), lambda i, *_: (i, 0)),
                pl.BlockSpec((4, HD, 256), lambda i, *_: (i, 0, 0)),
                pl.BlockSpec((4, 1, 256), lambda i, *_: (i, 0, 0)),
                whole((2048, 128)),
            ],
            out_specs=[
                pl.BlockSpec((256, 256), lambda i, *_: (i, 0)),
                pl.BlockSpec((2, 8, 128, 128), lambda i, *_: (0, 0, i, 0)),
            ],
            scratch_shapes=[
                pltpu.VMEM((2048, HD), BF16),
                pltpu.VMEM((2048, HD), BF16),
                pltpu.VMEM((2048, HD), F32),
                pltpu.VMEM((2048, HD), F32),
                pltpu.VMEM((HD, 256), F32),
            ],
        ),
        compiler_params=pltpu.CompilerParams(vmem_limit_bytes=40 * 2**20),
        name="attend_back",
    )(key_runs, query_runs, q, kv, grad, ot, lse, table)


ROWS = 16


def in_chunks(step):
    def one(i, _):
        step(pl.ds(pl.multiple_of(i * ROWS, ROWS), ROWS))
        return 0

    lax.fori_loop(0, TOK // ROWS, one, 0)


def mean_last(rows):
    return jnp.mean(rows, axis=-1, keepdims=True)


PART = 3 * FF_DEV // 2
PART_HALF = PART // 2


class RingSum:
    def __init__(self, me, edges, along_z, src, start, width, step, relayed, last):
        self.edges, self.src, self.start, self.width, self.step = edges, src, start, width, step
        self.relayed, self.last = relayed, last
        self.here = me.z if along_z else x_of(me)
        self.up = around(me, 1, 0) if along_z else around(me, 0, 1)
        self.down = around(me, -1, 0) if along_z else around(me, 0, 3)
        self.a, self.b = pl.ds(0, PART_HALF), pl.ds(PART_HALF, PART_HALF)

    def columns(self, k):
        at = self.width * lax.rem(self.here + k, 4)
        return pl.ds(pl.multiple_of(at, self.width), self.width)

    def piece(self, k, half):
        rows = pl.ds(self.start + PART_HALF * half, PART_HALF)
        return self.src.at[rows, self.columns(k)]

    def far(self):
        self.r_a = self.edges.copy(self.piece(2, 0), self.relayed.at[0], self.up)
        self.r_b = self.edges.copy(self.piece(2, 1), self.relayed.at[1], self.down)

    def near_up(self):
        self.u_b = self.edges.copy(self.piece(1, 1), self.last.at[0, self.b], self.up)

    def near_down(self):
        self.d_a = self.edges.copy(self.piece(3, 0), self.last.at[1, self.a], self.down)

    def add(self, k, half):
        step, start, cols = self.step, self.start + PART_HALF * half, self.columns(k)

        def one(i, _):
            at = pl.ds(pl.multiple_of(start + i * step, 16), step)
            from_ = pl.ds(pl.multiple_of(i * step, 16), step)
            self.src[at, cols] = (
                self.src[at, cols].astype(F32) + self.relayed[half, from_, :].astype(F32)
            ).astype(BF16)
            return 0

        lax.fori_loop(0, PART_HALF // step, one, 0)

    def second(self):
        self.r_a.wait_recv()
        self.add(1, 0)
        self.u_a = self.edges.copy(self.piece(1, 0), self.last.at[0, self.a], self.up)
        self.r_b.wait_recv()
        self.add(3, 1)
        self.d_b = self.edges.copy(self.piece(3, 1), self.last.at[1, self.b], self.down)

    def total(self, out):
        for d in (self.u_b, self.d_a, self.u_a, self.d_b):
            d.wait_recv()
        step, cols = self.step, self.columns(0)

        def one(i, _):
            at = pl.ds(pl.multiple_of(self.start + i * step, 16), step)
            from_ = pl.ds(pl.multiple_of(i * step, 16), step)
            out[from_, :] = (
                self.src[at, cols].astype(F32)
                + self.last[0, from_, :].astype(F32)
                + self.last[1, from_, :].astype(F32)
            ).astype(BF16)
            return 0

        lax.fori_loop(0, PART // step, one, 0)


SUM_EDGES = 6


def feed_forward_kernel(
    parts, tokens, gain, cots, wgu, wdn, wswap, wnear,
    output, grad_middle, gain_grad, gbs, z_out, x_out,
    xs, p, c, gp, w, act_t, gate_t, up_t, act, dgate, dup, middle, low,
    g1, b1, r1, l1, g2, b2, r2, l2,
    z_relayed, z_last, x_relayed, x_last, z_q, x_q,
    z_relayed2, z_last2, x_relayed2, x_last2,
    send, recv, fs, fr, local,
):
    me = Place()
    core = me.at(core=1 - me.c)
    greet(
        [core, me.at(dy=1), me.at(dy=-1)]
        + [around(me, k, 0) for k in (1, 2, 3)]
        + [around(me, 0, 1), around(me, 0, 3)]
    )
    edges = Edges(send, recv)
    mine = 2 * me.y + me.c
    moved = me.c != me.xh
    load_p = pltpu.make_async_copy(parts, p, local.at[0])
    load_c = pltpu.make_async_copy(cots, c, local.at[1])
    load_p.start()
    load_c.start()

    def w_rows(dz):
        z = lax.rem(me.z + dz + 4, 4)
        return (
            pl.ds(pl.multiple_of(GU_QUARTER * z, 16), GU_QUARTER),
            pl.ds(pl.multiple_of(2 * FF_DEV + DN_QUARTER * z, 16), DN_QUARTER),
        )

    gu_part, dn_part = pl.ds(0, GU_QUARTER), pl.ds(GU_QUARTER, DN_QUARTER)
    kept = [
        pltpu.make_async_copy(wgu, w.at[pl.ds(0, 2 * FF_DEV)], local.at[2]),
        pltpu.make_async_copy(wdn, w.at[pl.ds(2 * FF_DEV, FF_DEV)], local.at[3]),
    ]
    near_w = []
    for i, (src, dz) in enumerate(((wswap, 0), (wnear.at[0], -1), (wnear.at[1], 1))):
        gu_rows, dn_rows = w_rows(dz)
        near_w.append(pltpu.make_async_copy(src.at[gu_part], w.at[gu_rows], local.at[4 + 2 * i]))
        near_w.append(pltpu.make_async_copy(src.at[dn_part], w.at[dn_rows], local.at[5 + 2 * i]))
    far_w = [
        pltpu.make_async_remote_copy(
            src_ref=wswap.at[part],
            dst_ref=w.at[rows],
            send_sem=fs.at[i],
            recv_sem=fr.at[i],
            device_id=me.at(dz=2),
            device_id_type=pl.DeviceIdType.MESH,
        )
        for i, (part, rows) in enumerate(zip((gu_part, dn_part), w_rows(0)))
    ]

    @pl.when(moved)
    def _():
        for d in far_w + near_w:
            d.start()

    @pl.when(jnp.logical_not(moved))
    def _():
        for d in kept:
            d.start()

    load_p.wait()
    ring = RingScatter(me, edges, p, (g1, b1, r1, l1))
    ring.first()
    ring.second()
    ring.arrived()

    def norm(at):
        rows = tokens[at, :].astype(F32) + ring.rows(at)
        middle[at, :] = rows
        normal = rows * lax.rsqrt(mean_last(rows * rows) + EPSILON)
        low[at, :] = (normal * gain[...]).astype(BF16)

    in_chunks(norm)
    keep = pltpu.make_async_copy(low, xs.at[mine], local.at[10])
    keep.start()
    gather = RingGather(me, edges, low, xs)
    ring.release()

    @pl.when(moved)
    def _():
        for d in near_w:
            d.wait()
        for d in far_w:
            d.wait()

    @pl.when(jnp.logical_not(moved))
    def _():
        for d in kept:
            d.wait()

    load_c.wait()
    keep.wait()

    def compute(pair):
        at = pl.ds(2 * pair, 2)
        x = xs[at].reshape(2 * TOK, D)
        g = c[at].reshape(2 * TOK, D)
        here = pl.ds(pl.multiple_of(2 * TOK * pair, 2 * TOK), 2 * TOK)
        for n0, n1 in ((0, 256), (256, 512), (512, FF_DEV)):
            gate = dot_last(x, w[n0:n1, :])
            upward = dot_last(x, w[FF_DEV + n0 : FF_DEV + n1, :])
            grad = dot_last(g, w[2 * FF_DEV + n0 : 2 * FF_DEV + n1, :])
            sigmoid = 1.0 / (1.0 + jnp.exp(-gate))
            swish = gate * sigmoid
            active = swish * upward
            grad_up = grad * swish
            grad_gate = grad * upward * sigmoid * (1.0 + gate * (1.0 - sigmoid))
            act[:, n0:n1] = active.astype(BF16)
            dup[:, n0:n1] = grad_up.astype(BF16)
            dgate[:, n0:n1] = grad_gate.astype(BF16)
            act_t[n0:n1, here] = active.T.astype(BF16)
            up_t[n0:n1, here] = grad_up.T.astype(BF16)
            gate_t[n0:n1, here] = grad_gate.T.astype(BF16)

        def block(i, _):
            cols = pl.ds(pl.multiple_of(512 * i, 512), 512)
            branch = dot(act[...], w[2 * FF_DEV :, cols])
            p[at, :, cols] = branch.astype(BF16).reshape(2, TOK, 512)
            grads = dot(dgate[...], w[:FF_DEV, cols]) + dot(dup[...], w[FF_DEV : 2 * FF_DEV, cols])
            gp[at, :, cols] = grads.astype(BF16).reshape(2, TOK, 512)
            return 0

        lax.fori_loop(0, 4, block, 0)

    def pair(k):
        return lax.rem(me.y + k, 4)

    two = RingScatter(me, edges, gp, (g1, b1, r1, l1))
    gather.from_core(0, 1)
    compute(pair(0))
    two.send_core(0)
    gather.relay()
    gather.near()
    gather.from_core(1, 5)

    def sides(i, _):
        compute(pair(1 + 2 * i))
        return 0

    lax.fori_loop(0, 2, sides, 0)
    two.send_core(1)
    two.send_core(3)
    gather.far()
    two.near()
    gather.from_core(5, 7)
    compute(pair(2))
    two.send_core(2)
    two.add_core(0)

    z_sum = RingSum(me, edges, True, w, 0, 512, 48, z_relayed, z_last)
    x_sum = RingSum(me, edges, False, w, PART, 512, 48, x_relayed, x_last)
    split = PART - FF_DEV

    def z_task(k):
        cols = z_sum.columns(k)
        x = xs[:, :, cols].reshape(8 * TOK, 512)
        w[:FF_DEV, cols] = dot(gate_t[...], x).astype(BF16)
        w[FF_DEV:PART, cols] = dot(up_t[:split, :], x).astype(BF16)

    def x_task(k):
        cols = x_sum.columns(k)
        x = xs[:, :, cols].reshape(8 * TOK, 512)
        g = c[:, :, cols].reshape(8 * TOK, 512)
        w[PART : 2 * FF_DEV, cols] = dot(up_t[split:, :], x).astype(BF16)
        w[2 * FF_DEV :, cols] = dot(act_t[...], g).astype(BF16)

    two.far()
    z_task(2)
    z_sum.far()
    x_task(2)
    x_sum.far()
    z_task(1)
    z_sum.near_up()
    x_task(1)
    x_sum.near_up()
    two.second()
    z_task(3)
    z_sum.near_down()
    x_task(3)
    x_sum.near_down()
    z_task(0)
    x_task(0)
    two.arrived()
    gain_grad[...] = jnp.zeros_like(gain_grad)

    def back(at):
        rows = middle[at, :]
        inverse = lax.rsqrt(mean_last(rows * rows) + EPSILON)
        normal = rows * inverse
        grad = two.rows(at)
        gain_grad[...] += jnp.sum(normal * grad, axis=0, keepdims=True)
        scaled = grad * gain[...]
        result = c[mine, at].astype(F32) + inverse * (
            scaled - normal * mean_last(scaled * normal)
        )
        grad_middle[at, :] = result
        low[at, :] = result.astype(BF16)

    edges.sent([gather.up_a, gather.up_b, gather.down_a, gather.down_b, gather.to_core[0]])
    in_chunks(back)
    keep = pltpu.make_async_copy(low, gbs.at[mine], local.at[10])
    keep.start()
    gather = RingGather(me, edges, low, gbs)
    branch = RingScatter(me, edges, p, (g2, b2, r2, l2))
    for k in (2, 1, 3, 0):
        branch.send_core(k)
    z_sum.second()
    x_sum.second()
    gather.relay()
    branch.far()
    branch.near()
    branch.add_core(0)
    z_sum.total(z_q)
    z_two = RingSum(me, edges, False, z_q, 0, 128, 176, z_relayed2, z_last2)
    z_two.far()
    z_two.near_up()
    z_two.near_down()
    x_sum.total(x_q)
    x_two = RingSum(me, edges, True, x_q, 0, 128, 176, x_relayed2, x_last2)
    x_two.far()
    x_two.near_up()
    x_two.near_down()
    gather.near()
    gather.far()
    branch.second()
    z_two.second()
    x_two.second()
    gather.from_core(0, 7)
    branch.arrived()

    def out(at):
        output[at, :] = (middle[at, :] + branch.rows(at)).astype(BF16)

    in_chunks(out)
    z_two.total(z_out)
    x_two.total(x_out)
    edges.finish()
    keep.wait()


def feed_forward(parts, tokens, gain, cots, wgu, wdn, wswap, wnear):
    block = pltpu.VMEM((8, TOK, D), BF16)
    turned = pltpu.VMEM((FF_DEV, 8 * TOK), BF16)
    pair = pltpu.VMEM((2 * TOK, FF_DEV), BF16)

    def ring(width):
        return [
            pltpu.VMEM((2, PART_HALF, width), BF16),
            pltpu.VMEM((2, PART, width), BF16),
        ] * 2

    return pl.pallas_call(
        feed_forward_kernel,
        out_shape=(
            shape((TOK, D)),
            shape((TOK, D), F32),
            shape((1, D), F32),
            shape((8, TOK, D)),
            shape((PART, 128)),
            shape((PART, 128)),
        ),
        in_specs=[ANY, VMEM, VMEM] + [ANY] * 5,
        out_specs=(VMEM, VMEM, VMEM, ANY, VMEM, VMEM),
        scratch_shapes=[block] * 4
        + [pltpu.VMEM((3 * FF_DEV, D), BF16)]
        + [turned] * 3
        + [pair] * 3
        + [pltpu.VMEM((TOK, D), F32), pltpu.VMEM((TOK, D), BF16)]
        + scatter_scratch() * 2
        + ring(512)
        + [pltpu.VMEM((PART, 512), BF16)] * 2
        + ring(128)
        + sems(3 * SCATTER_EDGES + 2 * GATHER_EDGES + 4 * SUM_EDGES)
        + sems(2)
        + [pltpu.SemaphoreType.DMA((11,))],
        compiler_params=pltpu.CompilerParams(
            collective_id=2, has_side_effects=True, vmem_limit_bytes=62 * 2**20
        ),
        name="feed_forward",
    )(parts, tokens, gain, cots, wgu, wdn, wswap, wnear)


def columns(width):
    return lambda i: (slice(None), pl.ds(pl.multiple_of(i * width, width), width))


def row_block(height, start=0):
    return lambda i: (pl.ds(pl.multiple_of(start + i * height, height), height), slice(None))


def plane_devices(me):
    found = [me.at(core=1 - me.c)]
    for dz, dx in STEPS:
        z, xl, core, y, xh = around(me, dz, dx)
        found += [(z, xl, core, y, xh), (z, xl, 1 - core, y, xh)]
    return found


def key_grads_kernel(
    dkv, gwo, z_piece, out, wo_out, z_all, got, both, last, wo_own, wo_got, wo_piece, wo_all,
    send, recv, ws, wr, local, ds, dr, zs, zr,
):
    me = Place()
    core = me.at(core=1 - me.c)
    far = [
        me.at(dz=dz, xl=(1 - me.xl) if dl else me.xl) for dz, dl in chips_in_sequence(me)
    ]
    greet(plane_devices(me) + group_members(me)[1:])
    edges = Edges(send, recv)
    order = []
    for dz, dl in chips_in_sequence(me) + [(0, 0)]:
        chip = 2 * lax.rem(me.z + dz, 4) + ((1 - me.xl) if dl else me.xl)
        order.append((chip, edges.copy(dkv.at[1 - me.c, chip], got.at[chip], core)))
    wo_sum = SumOfSixteen(me, gwo, row_block(128), wo_own, wo_got, ws, wr, local)
    far_copies = []
    for i, (chip, d) in enumerate(order):
        d.wait_recv()
        both[chip] = (dkv[me.c, chip].astype(F32) + got[chip].astype(F32)).astype(BF16)
        if i < 7:
            far_copies.append(edges.copy(both.at[chip], last.at[i], far[i]))
    place = 4 * me.z + x_of(me)
    z_deliver = Deliver(me, zs, zr)
    z_deliver.to_owner(
        z_piece, z_all.at[columns(128)(place)], me.z // 2, me.y, me.c
    )
    total = both[2 * me.z + me.xl].astype(F32)
    for i, d in enumerate(far_copies):
        d.wait_recv()
        total = total + last[i].astype(F32)
    out[...] = total
    wo_piece[...] = wo_sum.total().astype(BF16)
    deliver = Deliver(me, ds, dr)
    rank = 2 * me.y + me.c
    dst = wo_all.at[
        pl.ds(pl.multiple_of(128 * me.xl, 128), 128),
        pl.ds(pl.multiple_of(Q_DEV * rank, Q_DEV), Q_DEV),
    ]
    deliver.to_owner(wo_piece, dst, me.y // 2, me.z, me.xh)
    half = wo_all.at[:, pl.ds(pl.multiple_of(1024 * me.c, 1024), 1024)]
    wait_got(half, dr)
    over = edges.copy(half, half, core)
    half = z_all.at[:, pl.ds(pl.multiple_of(1024 * me.c, 1024), 1024)]
    wait_got(half, zr)
    z_over = edges.copy(half, half, core)
    over.wait_recv()
    wo_out[...] = wo_all[...]
    z_over.wait_recv()
    wo_sum.finish()
    deliver.finish()
    z_deliver.finish()
    edges.finish()


def sum_key_grads(dkv, gwo, z_piece):
    return pl.pallas_call(
        key_grads_kernel,
        out_shape=(shape((512, 128), F32), shape((256, D)), shape((PART, D))),
        in_specs=[VMEM, ANY, VMEM],
        out_specs=(VMEM, VMEM, ANY),
        scratch_shapes=[
            pltpu.VMEM((8, 512, 128), BF16),
            pltpu.VMEM((8, 512, 128), BF16),
            pltpu.VMEM((7, 512, 128), BF16),
            pltpu.VMEM((128, Q_DEV), BF16),
            pltpu.VMEM((15, 128, Q_DEV), BF16),
            pltpu.VMEM((128, Q_DEV), BF16),
            pltpu.VMEM((256, D), BF16),
        ]
        + sems(17)
        + [
            pltpu.SemaphoreType.DMA((15,)),
            pltpu.SemaphoreType.DMA,
            pltpu.SemaphoreType.DMA,
            pltpu.SemaphoreType.DMA((8,)),
            pltpu.SemaphoreType.DMA,
            pltpu.SemaphoreType.DMA((8,)),
            pltpu.SemaphoreType.DMA,
        ],
        compiler_params=remote_params(4),
        name="sum_key_grads",
    )(dkv, gwo, z_piece)


def closing_kernel(
    parts, gwq, tokens, gain, grad_middle, gain_two, x_piece,
    grad_tokens, gains, wq_out, x_all,
    got, both, relayed, last, wq_own, wq_got, wq_piece, wq_all,
    mine, near, near_sum, owners,
    send, recv, ws, wr, local, ds, dr, gs, gr, hs, hr, xs_, xr,
):
    me = Place()
    greet(plane_devices(me) + group_members(me)[1:])
    edges = Edges(send, recv)
    ring = RingScatter(me, edges, parts, (got, both, relayed, last))
    for k in (2, 1, 3, 0):
        ring.send_core(k)
    wq_sum = SumOfSixteen(me, gwq, columns(128), wq_own, wq_got, ws, wr, local)
    ring.far()
    ring.near()
    ring.add_core(0)
    x_deliver = Deliver(me, xs_, xr)
    x_deliver.to_owner(
        x_piece, x_all.at[columns(128)(4 * x_of(me) + me.z)], me.xh, me.y, me.c
    )
    ring.second()
    wq_piece[...] = wq_sum.total().astype(BF16)
    deliver = Deliver(me, ds, dr)
    piece = 4 * me.z + x_of(me)
    for j in range(5):
        block = own_block(me, j)
        owner, slot = block // 5, lax.rem(block, 5)
        dst = wq_all.at[
            pl.ds(pl.multiple_of(64 * slot, 64), 64),
            pl.ds(pl.multiple_of(128 * piece, 128), 128),
        ]
        deliver.to_owner(
            wq_piece.at[pl.ds(64 * j, 64)], dst, me.z // 2, owner // 2, lax.rem(owner, 2)
        )
    ring.arrived()
    mine[...] = jnp.zeros_like(mine)
    mine[1:2, :] = gain_two[...]

    def back(at):
        rows = tokens[at, :].astype(F32)
        inverse = lax.rsqrt(mean_last(rows * rows) + EPSILON)
        normal = rows * inverse
        grad = ring.rows(at)
        mine[0:1, :] += jnp.sum(normal * grad, axis=0, keepdims=True)
        scaled = grad * gain[...]
        grad_tokens[at, :] = grad_middle[at, :] + inverse * (
            scaled - normal * mean_last(scaled * normal)
        )

    in_chunks(back)

    def slice_of(rank):
        return mine.at[:, pl.ds(pl.multiple_of(256 * rank, 256), 256)]

    near_copies = []
    for k in range(1, 8):
        dy, other = k // 2, k % 2
        y = lax.rem(me.y + dy, 4)
        to_core = 1 - me.c if other else me.c
        d = pltpu.make_async_remote_copy(
            src_ref=slice_of(2 * y + to_core),
            dst_ref=near.at[k - 1],
            send_sem=gs.at[k - 1],
            recv_sem=gr,
            device_id=me.at(y=y, core=to_core),
            device_id_type=pl.DeviceIdType.MESH,
        )
        d.start()
        near_copies.append(d)
    own = mine[:, pl.ds(pl.multiple_of(256 * (2 * me.y + me.c), 256), 256)]
    wait_got(near, gr)
    for k in range(7):
        own = own + near[k]
    near_sum[...] = own
    far = Deliver(me, hs, hr)
    for to_core in (0, 1):
        far.to_owner(near_sum, owners.at[piece], to_core, me.y, me.c)

    half = wq_all.at[:, pl.ds(pl.multiple_of(1024 * me.c, 1024), 1024)]
    wait_got(half, dr)
    over = edges.copy(half, half, me.at(core=1 - me.c))
    wait_got(owners, hr)
    sum_all = owners[0]
    for k in range(1, 16):
        sum_all = sum_all + owners[k]
    gains[...] = sum_all
    half = x_all.at[:, pl.ds(pl.multiple_of(1024 * me.c, 1024), 1024)]
    wait_got(half, xr)
    x_over = edges.copy(half, half, me.at(core=1 - me.c))
    over.wait_recv()
    wq_out[...] = wq_all[...]
    x_over.wait_recv()
    wq_sum.finish()
    deliver.finish()
    x_deliver.finish()
    for d in near_copies:
        d.wait_send()
    far.finish()
    edges.finish()


def closing(parts, gwq, tokens, gain, grad_middle, gain_two, x_piece):
    return pl.pallas_call(
        closing_kernel,
        out_shape=(
            shape((TOK, D), F32),
            shape((8, 256), F32),
            shape((320, D)),
            shape((PART, D)),
        ),
        in_specs=[VMEM, ANY] + [VMEM] * 5,
        out_specs=(VMEM,) * 3 + (ANY,),
        scratch_shapes=scatter_scratch()
        + [
            pltpu.VMEM((320, 128), BF16),
            pltpu.VMEM((15, 320, 128), BF16),
            pltpu.VMEM((320, 128), BF16),
            pltpu.VMEM((320, D), BF16),
            pltpu.VMEM((8, D), F32),
            pltpu.VMEM((7, 8, 256), F32),
            pltpu.VMEM((8, 256), F32),
            pltpu.VMEM((16, 8, 256), F32),
        ]
        + sems(SCATTER_EDGES + 2)
        + [
            pltpu.SemaphoreType.DMA((15,)),
            pltpu.SemaphoreType.DMA,
            pltpu.SemaphoreType.DMA,
            pltpu.SemaphoreType.DMA((40,)),
            pltpu.SemaphoreType.DMA,
            pltpu.SemaphoreType.DMA((7,)),
            pltpu.SemaphoreType.DMA,
            pltpu.SemaphoreType.DMA((16,)),
            pltpu.SemaphoreType.DMA,
            pltpu.SemaphoreType.DMA((8,)),
            pltpu.SemaphoreType.DMA,
        ],
        compiler_params=remote_params(5),
        name="closing",
    )(parts, gwq, tokens, gain, grad_middle, gain_two, x_piece)


def widen_kernel(z_ref, x_ref, gu_ref, dn_ref):
    i = pl.program_id(0)

    @pl.when(i < 3)
    def _():
        gu_ref[...] = z_ref[...].astype(F32)

    @pl.when(i == 3)
    def _():
        gu_ref[...] = x_ref[...].astype(F32)

    @pl.when(i > 3)
    def _():
        dn_ref[...] = x_ref[...].astype(F32)


def widen(z_all, x_all):
    rows = PART // 3
    return pl.pallas_call(
        widen_kernel,
        out_shape=(shape((2 * FF_DEV, D), F32), shape((FF_DEV, D), F32)),
        grid=(6,),
        in_specs=[
            pl.BlockSpec((rows, D), lambda i: (jnp.minimum(i, 2), 0)),
            pl.BlockSpec((rows, D), lambda i: (jnp.maximum(i - 3, 0), 0)),
        ],
        out_specs=(
            pl.BlockSpec((rows, D), lambda i: (jnp.minimum(i, 3), 0)),
            pl.BlockSpec((rows, D), lambda i: (jnp.maximum(i - 4, 0), 0)),
        ),
        compiler_params=pltpu.CompilerParams(vmem_limit_bytes=40 * 2**20),
        name="widen",
    )(z_all, x_all)


def body(hidden, positions, gain_attn, w_qkv, w_out, gain_mlp, w_gate_up, w_down, cotangent):
    core = lax.axis_index("c").reshape(1)
    gain_one = gain_attn.astype(F32).reshape(1, D)
    gain_two = gain_mlp.astype(F32).reshape(1, D)
    tokens = hidden[0].astype(F32)
    inverse_one = lax.rsqrt(jnp.mean(tokens * tokens, axis=-1, keepdims=True) + EPSILON)
    input_one = (tokens * inverse_one * gain_one).astype(BF16)
    table = jnp.asarray(rotary_table())
    wgu = w_gate_up.reshape(2 * FF_DEV, D)
    wdn = w_down.T
    xs, poss, wq, wswap = opening(
        input_one, jnp.broadcast_to(positions, (8, TOK)), w_qkv, wgu, wdn
    )
    xs = xs.reshape(1024, D)
    wq = wq.reshape(320, D)
    query_runs = poss[:, 0, ::64].reshape(16) // 64
    query, kv = project(query_runs, core, xs, wq, table)
    kvs, places, cots, wo, wnear = exchange_keys(kv, poss, cotangent[0], w_out, wswap)
    wo = wo.reshape(D, Q_DEV)
    key_runs = (
        places[:, :, 0, ::64].reshape(8, 4, 2, 2).transpose(1, 0, 2, 3).reshape(128) // 64
    )
    att, ot, lse = attend(key_runs, query_runs, query, kvs)
    parts = dot_last(att, wo).astype(BF16).reshape(8, TOK, D)
    output, grad_middle, gain_grad, gbs, z_piece, x_piece = feed_forward(
        parts, hidden[0], gain_two, cots, wgu, wdn, wswap, wnear
    )
    gb = gbs.reshape(1024, D)
    grad_att = dot(gb, wo).astype(BF16)
    grad_wo = dot_first(gb, att).astype(BF16)
    dq, dkv = attend_back(key_runs, query_runs, query, kvs, grad_att, ot, lse, table)
    dkv, grad_w_out, z_all = sum_key_grads(dkv, grad_wo, z_piece)
    one_parts, gwq = project_back(query_runs, core, dq, dkv, xs, wq, table)
    grad_tokens, gains, grad_w_qkv, x_all = closing(
        one_parts.reshape(8, TOK, D),
        gwq,
        hidden[0],
        gain_one,
        grad_middle,
        gain_grad,
        x_piece,
    )
    grad_gu, grad_dn = widen(z_all, x_all)
    return (
        output[None],
        grad_tokens[None],
        gains[0],
        grad_w_qkv.astype(F32),
        grad_w_out.astype(F32),
        gains[1],
        grad_gu.reshape(2, FF_DEV, D),
        grad_dn.T,
    )


def solution(mesh):
    fine = Mesh(mesh.devices.reshape(4, 2, 2, 4, 2), AXES)
    ctx, fsdp = ("z", "xl", "c"), ("y", "xh")
    weight = P(fsdp, None)
    return jax.shard_map(
        body,
        mesh=fine,
        in_specs=(
            P(fsdp, ctx, None),
            P(fsdp, ctx),
            P(),
            weight,
            weight,
            P(),
            P(None, fsdp, None),
            P(None, fsdp),
            P(fsdp, ctx, None),
        ),
        out_specs=(
            P(fsdp, ctx, None),
            P(fsdp, ctx, None),
            P(fsdp),
            weight,
            weight,
            P(fsdp),
            P(None, fsdp, None),
            P(None, fsdp),
        ),
        check_vma=False,
    )
```

```python
import jax
import jax.numpy as jnp
from jax import lax
from jax.experimental import pallas as pl
from jax.experimental.pallas import tpu as pltpu
from jax.sharding import Mesh
from jax.sharding import PartitionSpec as P

D = 2048
H = 32
KV = 4
HD = 64
FF = 5632
TOK = 128
HALF = 64
FF_DEV = 704
Q_DEV = 256
EPSILON = 1e-05
FILLER = -1e30
AXES = ("z", "xl", "c", "y", "xh")
ANY = pl.BlockSpec(memory_space=pl.ANY)
VMEM = pl.BlockSpec(memory_space=pltpu.VMEM)
BF16 = jnp.bfloat16
F32 = jnp.float32


class Place:
    def __init__(self):
        self.z, self.xl, self.c, self.y, self.xh = (lax.axis_index(a) for a in AXES)

    def at(self, dz=0, dy=0, core=None, xl=None, xh=None, y=None):
        z = lax.rem(self.z + dz + 4, 4) if dz else self.z
        y = (lax.rem(self.y + dy + 4, 4) if dy else self.y) if y is None else y
        return (
            z,
            self.xl if xl is None else xl,
            self.c if core is None else core,
            y,
            self.xh if xh is None else xh,
        )


class Edges:
    def __init__(self, send, recv):
        self.send, self.recv, self.count, self.started = send, recv, 0, []

    def copy(self, src, dst, device, start=True):
        i = self.count
        self.count += 1
        d = pltpu.make_async_remote_copy(
            src_ref=src,
            dst_ref=dst,
            send_sem=self.send.at[i],
            recv_sem=self.recv.at[i],
            device_id=device,
            device_id_type=pl.DeviceIdType.MESH,
        )
        self.started.append(d)
        if start:
            d.start()
        return d

    def sent(self, copies):
        for d in copies:
            d.wait_send()
        self.started = [d for d in self.started if all(d is not e for e in copies)]

    def finish(self):
        for d in self.started:
            d.wait_send()


def greet(devices):
    barrier = pltpu.get_barrier_semaphore()
    for device in devices:
        pl.semaphore_signal(
            barrier, inc=1, device_id=device, device_id_type=pl.DeviceIdType.MESH
        )
    pl.semaphore_wait(barrier, len(devices))


def group_members(me):
    found = [me.at(core=1 - me.c)]
    for dy in (1, 2, 3):
        found += [me.at(dy=dy), me.at(dy=dy, core=1 - me.c)]
    return found


class RingGather:
    def __init__(self, me, edges, own, out):
        self.me, self.edges, self.out = me, edges, out
        self.core = me.at(core=1 - me.c)
        self.up, self.down = me.at(dy=1), me.at(dy=-1)
        a, b = pl.ds(0, HALF), pl.ds(HALF, HALF)
        self.a, self.b = a, b
        mine = self.slot(0)
        self.up_a = edges.copy(own.at[a], out.at[mine, a], self.up)
        self.down_b = edges.copy(own.at[b], out.at[mine, b], self.down)
        self.up_b = edges.copy(own.at[b], out.at[mine, b], self.up)
        self.down_a = edges.copy(own.at[a], out.at[mine, a], self.down)
        self.to_core = [edges.copy(own, out.at[mine], self.core)]

    def slot(self, dy):
        return 2 * lax.rem(self.me.y + dy + 4, 4) + self.me.c

    def pass_core(self, dy, part):
        ref = self.out.at[self.slot(dy), part]
        self.to_core.append(self.edges.copy(ref, ref, self.core))

    def relay(self):
        out = self.out
        self.up_a.wait_recv()
        ref = out.at[self.slot(-1), self.a]
        self.on_a = self.edges.copy(ref, ref, self.up)
        self.down_b.wait_recv()
        ref = out.at[self.slot(1), self.b]
        self.on_b = self.edges.copy(ref, ref, self.down)
        self.pass_core(-1, self.a)
        self.pass_core(1, self.b)

    def near(self):
        self.up_b.wait_recv()
        self.pass_core(-1, self.b)
        self.down_a.wait_recv()
        self.pass_core(1, self.a)

    def far(self):
        self.on_a.wait_recv()
        self.pass_core(2, self.a)
        self.on_b.wait_recv()
        self.pass_core(2, self.b)

    def from_core(self, first, last):
        for d in self.to_core[first:last]:
            d.wait_recv()

    def rest(self):
        self.near()
        self.far()
        self.from_core(0, 7)


GATHER_EDGES = 13


class RingScatter:
    def __init__(self, me, edges, parts, scratch):
        self.me, self.edges, self.parts = me, edges, parts
        self.got, self.both, self.relayed, self.last = scratch
        self.up, self.down = me.at(dy=1), me.at(dy=-1)
        self.cores = {}
        self.a, self.b = pl.ds(0, HALF), pl.ds(HALF, HALF)

    def send_core(self, k):
        row = 2 * lax.rem(self.me.y + k, 4) + 1 - self.me.c
        core = self.me.at(core=1 - self.me.c)
        self.cores[k] = self.edges.copy(self.parts.at[row], self.got.at[k], core)

    def add_core(self, k):
        self.cores[k].wait_recv()
        row = 2 * lax.rem(self.me.y + k, 4) + self.me.c

        def add(at):
            self.both[k, at] = (
                self.parts[row, at].astype(F32) + self.got[k, at].astype(F32)
            ).astype(BF16)

        in_chunks(add)

    def far(self):
        self.add_core(2)
        e, both = self.edges, self.both
        self.r_a = e.copy(both.at[2, self.a], self.relayed.at[0], self.up)
        self.r_b = e.copy(both.at[2, self.b], self.relayed.at[1], self.down)

    def near(self):
        e, both = self.edges, self.both
        self.add_core(1)
        self.u_b = e.copy(both.at[1, self.b], self.last.at[0, self.b], self.up)
        self.add_core(3)
        self.d_a = e.copy(both.at[3, self.a], self.last.at[1, self.a], self.down)

    def first(self):
        for k in (2, 1, 3, 0):
            self.send_core(k)
        self.far()
        self.near()
        self.add_core(0)

    def second(self):
        a, b, e, both = self.a, self.b, self.edges, self.both
        self.r_a.wait_recv()
        both[1, a] = (both[1, a].astype(F32) + self.relayed[0].astype(F32)).astype(BF16)
        self.u_a = e.copy(both.at[1, a], self.last.at[0, a], self.up)
        self.r_b.wait_recv()
        both[3, b] = (both[3, b].astype(F32) + self.relayed[1].astype(F32)).astype(BF16)
        self.d_b = e.copy(both.at[3, b], self.last.at[1, b], self.down)

    def arrived(self):
        for d in (self.u_b, self.d_a, self.u_a, self.d_b):
            d.wait_recv()

    def rows(self, at):
        return (
            self.both[0, at].astype(F32)
            + self.last[0, at].astype(F32)
            + self.last[1, at].astype(F32)
        )

    def release(self):
        ring = [self.r_a, self.r_b, self.u_b, self.d_a, self.u_a, self.d_b]
        self.edges.sent(ring + list(self.cores.values()))


SCATTER_EDGES = 10


def scatter_scratch():
    return [
        pltpu.VMEM((4, TOK, D), BF16),
        pltpu.VMEM((4, TOK, D), BF16),
        pltpu.VMEM((2, HALF, D), BF16),
        pltpu.VMEM((2, TOK, D), BF16),
    ]


def sems(n):
    return [pltpu.SemaphoreType.DMA((n,)), pltpu.SemaphoreType.DMA((n,))]


def shape(dims, dtype=BF16):
    return jax.ShapeDtypeStruct(dims, dtype)


def remote_params(number):
    return pltpu.CompilerParams(
        collective_id=number, has_side_effects=True, vmem_limit_bytes=48 * 2**20
    )


def block_place(block):
    is_kv = block >= 32
    other = block - 32
    rank = block // 4
    y = jnp.where(is_kv, lax.rem(other + 32, 4), rank // 2)
    core = jnp.where(is_kv, other // 4, lax.rem(rank, 2))
    return y, core, jnp.where(is_kv, 4, lax.rem(block, 4))


def own_block(me, j):
    if j == 4:
        return 32 + 4 * me.c + me.y
    return 4 * (2 * me.y + me.c) + j


def send_block(me, src, dst, send_sem, recv_sem, target, stays):
    @pl.when(stays)
    def _():
        pltpu.make_async_copy(src, dst, recv_sem).start()

    @pl.when(jnp.logical_not(stays))
    def _():
        pltpu.make_async_remote_copy(
            src_ref=src,
            dst_ref=dst,
            send_sem=send_sem,
            recv_sem=recv_sem,
            device_id=target,
            device_id_type=pl.DeviceIdType.MESH,
        ).start()


def wait_sent(src, send_sem, stays):
    @pl.when(jnp.logical_not(stays))
    def _():
        pltpu.make_async_copy(src, src, send_sem).wait()


def wait_got(dst, recv_sem):
    pltpu.make_async_copy(dst, dst, recv_sem).wait()


def x_of(me):
    return 2 * me.xh + me.xl


def around(me, dz, dx):
    x = lax.rem(x_of(me) + dx, 4)
    return me.at(dz=dz, xl=lax.rem(x, 2), xh=x // 2)


STEPS = [(dz, dx) for dz in range(4) for dx in range(4)][1:]


class SumOfSixteen:
    def __init__(self, me, src, piece, own, got, send, recv, local):
        self.me, self.src, self.piece, self.own, self.got = me, src, piece, own, got
        self.send, self.recv = send, recv
        self.keep = pltpu.make_async_copy(
            src.at[piece(4 * me.z + x_of(me))], own, local
        )
        self.keep.start()
        for k, (dz, dx) in enumerate(STEPS):
            to = 4 * lax.rem(me.z + dz, 4) + lax.rem(x_of(me) + dx, 4)
            self.copy(src.at[piece(to)], k, around(me, dz, dx)).start()

    def copy(self, src, k, device):
        return pltpu.make_async_remote_copy(
            src_ref=src,
            dst_ref=self.got.at[k],
            send_sem=self.send.at[k],
            recv_sem=self.recv,
            device_id=device,
            device_id_type=pl.DeviceIdType.MESH,
        )

    def total(self):
        self.keep.wait()
        pltpu.make_async_copy(self.got, self.got, self.recv).wait()
        total = self.own[...].astype(F32)
        for k in range(15):
            total = total + self.got[k].astype(F32)
        return total

    def finish(self):
        for k in range(15):
            src = self.src.at[self.piece(0)]
            pltpu.make_async_copy(src, src, self.send.at[k]).wait()


def same(me, z, xl, core, y, xh):
    return (z == me.z) & (xl == me.xl) & (core == me.c) & (y == me.y) & (xh == me.xh)


class Deliver:
    def __init__(self, me, send, recv):
        self.me, self.send, self.recv, self.sent = me, send, recv, []

    def to_owner(self, src, dst, core, y, xh):
        me = self.me
        for dz in range(4):
            for dl in (0, 1):
                z = lax.rem(me.z + dz, 4)
                xl = 1 - me.xl if dl else me.xl
                stays = same(me, z, xl, core, y, xh)
                sem = self.send.at[len(self.sent)]
                send_block(me, src, dst, sem, self.recv, (z, xl, core, y, xh), stays)
                self.sent.append((src, sem, stays))

    def finish(self):
        for src, sem, stays in self.sent:
            wait_sent(src, sem, stays)


def rotary_rows(places):
    steps = jnp.arange(HD // 2, dtype=F32)
    inverse = jnp.power(10000.0, steps * (-2.0 / HD))
    turning = places.astype(F32)[:, None] * inverse[None, :]
    rows = jnp.concatenate([jnp.cos(turning), jnp.sin(turning)], axis=1)
    return rows.reshape(2, 64, HD).transpose(1, 0, 2).reshape(64, 2 * HD)


def halves_swapped(rows):
    return jnp.concatenate([rows[:, HD // 2 :], rows[:, : HD // 2]], axis=1)


def rotate(rows, table, back=False):
    turned = halves_swapped(rows) * table[:, HD:]
    return rows * table[:, :HD] + (-turned if back else turned)


def rotary_of(rows, u):
    cosine = rows[:, HD * u : HD * u + HD // 2]
    sine = rows[:, HD * u + HD // 2 : HD * u + HD]
    return jnp.concatenate([cosine, cosine, -sine, sine], axis=1)


ROWS = 16


def in_chunks(step, rows=TOK):
    def one(i, _):
        step(pl.ds(pl.multiple_of(i * ROWS, ROWS), ROWS))
        return 0

    lax.fori_loop(0, rows // ROWS, one, 0)


def mean_last(rows):
    return jnp.mean(rows, axis=-1, keepdims=True)


GU_QUARTER = 2 * FF_DEV // 4
DN_QUARTER = FF_DEV // 4
QUARTER = GU_QUARTER + DN_QUARTER


def swap_copies(me, wgu, wdn, wswap, send, recv):
    found = []
    across = me.at(core=1 - me.c, xl=1 - me.xl, xh=1 - me.xh)
    for i, (src, rows, start) in enumerate(
        ((wgu, GU_QUARTER, 0), (wdn, DN_QUARTER, GU_QUARTER))
    ):
        found.append(
            pltpu.make_async_remote_copy(
                src_ref=src.at[pl.ds(pl.multiple_of(rows * me.z, 16), rows)],
                dst_ref=wswap.at[pl.ds(start, rows)],
                send_sem=send.at[i],
                recv_sem=recv.at[i],
                device_id=across,
                device_id_type=pl.DeviceIdType.MESH,
            )
        )
    return found


def chips_in_sequence(me):
    return [(dz, dl) for dz in range(4) for dl in (0, 1)][1:]


def begin_kernel(
    tokens, gain, pos, trig, wqkv, wgu, wdn, cot, wout,
    q, kv_table, trigs, xs_out, wq_out, poss, kvs, places, cots, wo, wswap, wnear,
    low, xs, wq, kv,
    send, recv, qs, qr, os_, orr, ws, wr, ns, nr, local,
):
    me = Place()
    partner = {"xl": 1 - me.xl, "xh": 1 - me.xh}
    core = me.at(core=1 - me.c)
    members = group_members(me)
    others = [
        me.at(y=lax.rem(me.y + dy, 4), core=c, **partner) for dy in range(4) for c in (0, 1)
    ]
    far = [
        me.at(dz=dz, xl=(1 - me.xl) if dl else me.xl) for dz, dl in chips_in_sequence(me)
    ]
    greet(members + others + far)
    edges = Edges(send, recv)
    mine = 2 * me.y + me.c
    chip = 2 * me.z + me.xl

    spread = pl.ds(pl.multiple_of(512 * me.z, 512), 512)
    spread_rows = pl.ds(pl.multiple_of(64 * me.z, 64), 64)
    own = 2 * me.y + me.xh
    own_column = me.c == 0
    to_xl = jnp.where(own_column, me.xl, 1 - me.xl)
    to_xh = jnp.where(own_column, me.xh, 1 - me.xh)
    blocks = []
    for i in range(5):
        y, to_core, slot = block_place(5 * own + i)
        stays = own_column & (y == me.y) & (to_core == me.c)
        src = wqkv.at[pl.ds(64 * i, 64), spread]
        dst = wq.at[pl.ds(pl.multiple_of(64 * slot, 64), 64), spread]
        target = (me.z, to_xl, to_core, y, to_xh)
        send_block(me, src, dst, qs.at[i], qr.at[slot], target, stays)
        blocks.append((src, qs.at[i], stays))

    def norm(at):
        rows = tokens[at, :].astype(F32)
        inverse = lax.rsqrt(mean_last(rows * rows) + EPSILON)
        low[at, :] = (rows * inverse * gain[...]).astype(BF16)

    in_chunks(norm)
    keep = pltpu.make_async_copy(low, xs.at[mine], local.at[0])
    keep.start()
    keep_pos = pltpu.make_async_copy(pos, poss.at[mine], local.at[1])
    keep_pos.start()
    pos_copies = [edges.copy(pos, poss.at[mine], m) for m in members]
    trigs[mine] = trig[...]
    trig_copies = [edges.copy(trig, trigs.at[mine], me.at(dy=k)) for k in (1, 2, 3)]
    trig_over = [edges.copy(trig, trigs.at[mine], core)]
    ring = RingGather(me, edges, low, xs)
    moved = me.c != me.xh
    swaps = swap_copies(me, wgu, wdn, wswap, ws, wr)

    @pl.when(moved)
    def _():
        for d in swaps:
            d.start()

    for i in range(5):
        wait_got(wq.at[pl.ds(64 * i, 64), spread], qr.at[i])
    wq_copies = [
        edges.copy(wq.at[:, spread], wq.at[:, spread], me.at(dz=k)) for k in (1, 3, 2)
    ]
    for k, d in zip((1, 2, 3), trig_copies):
        d.wait_recv()
        ref = trigs.at[2 * lax.rem(me.y - k + 4, 4) + me.c]
        trig_over.append(edges.copy(ref, ref, core))
    ring.relay()
    keep_pos.wait()
    for d in pos_copies + trig_over:
        d.wait_recv()
    keep.wait()
    for d in wq_copies:
        d.wait_recv()
    wq_save = pltpu.make_async_copy(wq, wq_out, local.at[2])
    wq_save.start()
    is_key = me.c == 0

    def compute(pair):
        at = pl.ds(2 * pair, 2)
        projected = dot_last(xs[at].reshape(2 * TOK, D), wq[...])
        for r in range(4):
            half, u = r // 2, r % 2
            rows = rotary_of(trigs[2 * pair + half], u)
            values = projected[64 * r : 64 * r + 64]
            heads = [rotate(values[:, HD * h : HD * h + HD], rows) for h in range(4)]
            query = jnp.concatenate(heads, axis=1).astype(BF16)
            to = pl.ds(pl.multiple_of(2 * TOK * pair + 64 * r, 64), 64)
            q[to, :] = (query.astype(F32) * 0.125).astype(BF16)
            rows = jnp.concatenate(
                [
                    jnp.where(is_key, rows[:, :HD], 1.0),
                    jnp.where(is_key, rows[:, HD:], 0.0),
                ],
                axis=1,
            )
            to = pl.ds(pl.multiple_of(TOK * pair + 64 * u, 64), 64)
            lanes = slice(HD * half, HD * half + HD)
            kv[to, lanes] = rotate(values[:, Q_DEV:], rows).astype(BF16)
            kv_table[0, to, lanes] = rows[:, :HD]
            kv_table[1, to, lanes] = rows[:, HD:]

    def pair(k):
        return lax.rem(me.y + k, 4)

    ring.from_core(0, 1)
    compute(pair(0))
    ring.near()
    ring.from_core(1, 5)

    def sides(i, _):
        compute(pair(1 + 2 * i))
        return 0

    lax.fori_loop(0, 2, sides, 0)
    ring.far()
    ring.from_core(5, 7)
    compute(pair(2))

    keeps = [
        pltpu.make_async_copy(kv, kvs.at[me.c, chip], local.at[0]),
        pltpu.make_async_copy(poss, places.at[chip], local.at[1]),
        pltpu.make_async_copy(xs, xs_out, local.at[4]),
        pltpu.make_async_copy(cot, cots.at[mine], local.at[5]),
    ]
    for d in keeps:
        d.start()
    pos_copies = [edges.copy(poss, places.at[chip], d) for d in far]
    kv_copies = [edges.copy(kv, kvs.at[me.c, chip], d) for d in far]
    over = [edges.copy(kv, kvs.at[me.c, chip], core)]
    ring = RingGather(me, edges, cot, cots)
    for i in range(8):
        dy, other = i // 2, i % 2
        y = lax.rem(me.y + dy, 4)
        to_core = me.c if other == 0 else 1 - me.c
        stays = own_column if i == 0 else me.c < 0
        cols = pl.ds(pl.multiple_of(Q_DEV * (2 * y + to_core), Q_DEV), Q_DEV)
        src = wout.at[spread_rows, cols]
        dst = wo.at[own, spread_rows]
        target = (me.z, to_xl, to_core, y, to_xh)
        send_block(me, src, dst, os_.at[i], orr.at[own], target, stays)
        blocks.append((src, os_.at[i], stays))
    steps = [
        pltpu.make_async_remote_copy(
            src_ref=wswap,
            dst_ref=wnear.at[i],
            send_sem=ns.at[i],
            recv_sem=nr.at[i],
            device_id=me.at(dz=1 - 2 * i),
            device_id_type=pl.DeviceIdType.MESH,
        )
        for i in range(2)
    ]

    @pl.when(moved)
    def _():
        for d in swaps:
            d.wait()
        for d in steps:
            d.start()

    ring.relay()
    for (dz, dl), d in zip(chips_in_sequence(me), kv_copies):
        d.wait_recv()
        source = 2 * lax.rem(me.z - dz + 4, 4) + ((1 - me.xl) if dl else me.xl)
        ref = kvs.at[me.c, source]
        over.append(edges.copy(ref, ref, core))
    for i in range(8):
        wait_got(wo.at[i, spread_rows], orr.at[i])
    ref = wo.at[:, spread_rows]
    wo_copies = [edges.copy(ref, ref, me.at(dz=k)) for k in (1, 3, 2)]
    ring.rest()
    for d in over + pos_copies + wo_copies:
        d.wait_recv()
    for src, sem, stays in blocks:
        wait_sent(src, sem, stays)

    @pl.when(moved)
    def _():
        for d in steps:
            d.wait()

    edges.finish()
    for d in keeps + [wq_save]:
        d.wait()


def begin(tokens, gain, pos, trig, wqkv, wgu, wdn, cot, wout):
    return pl.pallas_call(
        begin_kernel,
        out_shape=(
            shape((1024, Q_DEV)),
            shape((2, 512, 128), F32),
            shape((8, 64, 128), F32),
            shape((8, TOK, D)),
            shape((320, D)),
            shape((8, 8, TOK), jnp.int32),
            shape((2, 8, 512, 128)),
            shape((8, 8, 8, TOK), jnp.int32),
            shape((8, TOK, D)),
            shape((8, 256, Q_DEV)),
            shape((QUARTER, D)),
            shape((2, QUARTER, D)),
        ),
        in_specs=[VMEM, VMEM, VMEM, VMEM] + [ANY] * 5,
        out_specs=(VMEM, VMEM, VMEM) + (ANY,) * 9,
        scratch_shapes=[
            pltpu.VMEM((TOK, D), BF16),
            pltpu.VMEM((8, TOK, D), BF16),
            pltpu.VMEM((320, D), BF16),
            pltpu.VMEM((512, 128), BF16),
        ]
        + sems(7 + 7 + 6 + 2 * GATHER_EDGES + 7 + 7 + 8)
        + sems(5)
        + sems(8)
        + sems(2)
        + sems(2)
        + [pltpu.SemaphoreType.DMA((6,))],
        compiler_params=remote_params(0),
        name="begin",
    )(tokens, gain, pos, trig, wqkv, wgu, wdn, cot, wout)


def split_heads(rows):
    return jnp.concatenate([rows[:, HD * h : HD * (h + 1)] for h in range(4)], axis=0)


def join_heads(rows):
    return jnp.concatenate([rows[64 * h : 64 * (h + 1), :] for h in range(4)], axis=1)


def dot_last(a, b):
    return lax.dot_general(a, b, (((1,), (1,)), ((), ())), preferred_element_type=F32)


def dot_first(a, b):
    return lax.dot_general(a, b, (((0,), (0,)), ((), ())), preferred_element_type=F32)


def dot(a, b):
    return lax.dot_general(a, b, (((1,), (0,)), ((), ())), preferred_element_type=F32)


TILE = 256
WIDE = 4


def sort_keys(runs, seq, kv_ref, keys, values):
    for j in range(32):
        chip, core, u = j // 4, (j // 2) % 2, j % 2
        to = pl.ds(pl.multiple_of(runs[seq * 32 + j] * 64, 64), 64)
        rows, lanes = slice(64 * u, 64 * u + 64), slice(HD * core, HD * core + HD)
        keys[to, :] = kv_ref[0, chip, rows, lanes]
        values[to, :] = kv_ref[1, chip, rows, lanes]


def allowed_tile(tile, run):
    key = lax.broadcasted_iota(jnp.int32, (TILE, 256), 0) + tile * TILE
    query = lax.rem(lax.broadcasted_iota(jnp.int32, (TILE, 256), 1), 64) + run * 64
    return key <= query


def tile_rows(tile):
    return pl.ds(pl.multiple_of(tile * TILE, TILE), TILE)


def attend_kernel(
    key_runs, query_runs, q_ref, kv_ref, att_ref, ot_ref, lse_ref, keys, values, high_ref, total_ref, acc_ref
):
    seq = pl.program_id(0)
    sort_keys(key_runs, seq, kv_ref, keys, values)

    def one_run(r, _):
        run = query_runs[seq * 4 + r]
        rows = pl.ds(pl.multiple_of(r * 64, 64), 64)
        query = split_heads(q_ref[rows, :])
        last = run // 4
        high_ref[...] = jnp.full((1, 256), FILLER, F32)
        total_ref[...] = jnp.zeros((1, 256), F32)
        acc_ref[...] = jnp.zeros((HD, 256), F32)

        def tiles(first, count, masked):
            scores = []
            for k in range(count):
                score = dot_last(keys[tile_rows(first + k), :], query)
                if masked and k == count - 1:
                    score = jnp.where(allowed_tile(first + k, run), score, FILLER)
                scores.append(score)
            high = high_ref[...]
            new_high = high
            for score in scores:
                new_high = jnp.maximum(new_high, jnp.max(score, axis=0, keepdims=True))
            scale = jnp.exp(high - new_high)
            total = total_ref[...] * scale
            acc = acc_ref[...] * scale
            for k, score in enumerate(scores):
                weights = jnp.exp(score - new_high)
                total = total + jnp.sum(weights, axis=0, keepdims=True)
                acc = acc + dot_first(values[tile_rows(first + k), :], weights.astype(BF16))
            high_ref[...] = new_high
            total_ref[...] = total
            acc_ref[...] = acc

        @pl.when(last >= WIDE)
        def _():
            tiles(0, WIDE, False)

        start = (last // WIDE) * WIDE
        for n in range(WIDE):

            @pl.when(last - start == n)
            def _():
                tiles(start, n + 1, True)

        total = total_ref[...]
        out = acc_ref[...] / total
        ot_ref[r] = out
        lse_ref[r] = high_ref[...] + jnp.log(total)
        att_ref[rows, :] = join_heads(out.T).astype(BF16)
        return 0

    lax.fori_loop(0, 4, one_run, 0)


def attend(key_runs, query_runs, q, kv):
    return pl.pallas_call(
        attend_kernel,
        out_shape=(shape((1024, 256)), shape((16, HD, 256), F32), shape((16, 1, 256), F32)),
        grid_spec=pltpu.PrefetchScalarGridSpec(
            num_scalar_prefetch=2,
            grid=(4,),
            in_specs=[
                pl.BlockSpec((256, 256), lambda i, *_: (i, 0)),
                pl.BlockSpec((2, 8, 128, 128), lambda i, *_: (0, 0, i, 0)),
            ],
            out_specs=[
                pl.BlockSpec((256, 256), lambda i, *_: (i, 0)),
                pl.BlockSpec((4, HD, 256), lambda i, *_: (i, 0, 0)),
                pl.BlockSpec((4, 1, 256), lambda i, *_: (i, 0, 0)),
            ],
            scratch_shapes=[
                pltpu.VMEM((2048, HD), BF16),
                pltpu.VMEM((2048, HD), BF16),
                pltpu.VMEM((1, 256), F32),
                pltpu.VMEM((1, 256), F32),
                pltpu.VMEM((HD, 256), F32),
            ],
        ),
        compiler_params=pltpu.CompilerParams(vmem_limit_bytes=40 * 2**20),
        name="attend",
    )(key_runs, query_runs, q, kv)


def attend_back_kernel(
    key_runs, query_runs, q_ref, kv_ref, da_ref, ot_ref, lse_ref, trig_ref,
    dq_ref, dkv_ref, keys, values, dkeys, dvalues, dq_acc,
):
    seq = pl.program_id(0)
    sort_keys(key_runs, seq, kv_ref, keys, values)
    dkeys[...] = jnp.zeros_like(dkeys)
    dvalues[...] = jnp.zeros_like(dvalues)

    def one_run(r, _):
        run = query_runs[seq * 4 + r]
        rows = pl.ds(pl.multiple_of(r * 64, 64), 64)
        query = split_heads(q_ref[rows, :])
        grad = split_heads(da_ref[rows, :])
        lse = lse_ref[r]
        delta = jnp.sum(grad.astype(F32).T * ot_ref[r], axis=0, keepdims=True)
        last = run // 4
        dq_acc[...] = jnp.zeros((HD, 256), F32)

        def tiles(first, count, masked):
            dq = dq_acc[...]
            for k in range(count):
                at = tile_rows(first + k)
                key = keys[at, :]
                probs = jnp.exp(dot_last(key, query) - lse)
                if masked and k == count - 1:
                    probs = jnp.where(allowed_tile(first + k, run), probs, 0.0)
                grad_probs = dot_last(values[at, :], grad)
                grad_scores = (probs * (grad_probs - delta)).astype(BF16)
                dvalues[at, :] += dot(probs.astype(BF16), grad)
                dkeys[at, :] += dot(grad_scores, query)
                dq = dq + dot_first(key, grad_scores)
            dq_acc[...] = dq

        @pl.when(last >= WIDE)
        def _():
            tiles(0, WIDE, False)

        start = (last // WIDE) * WIDE
        for n in range(WIDE):

            @pl.when(last - start == n)
            def _():
                tiles(start, n + 1, True)

        pair_rows = trig_ref[r // 2]
        table = jnp.where(
            lax.rem(r, 2) == 0, rotary_of(pair_rows, 0), rotary_of(pair_rows, 1)
        )
        dq = (dq_acc[...] * 0.125).T
        heads = [rotate(dq[64 * h : 64 * h + 64], table, back=True) for h in range(4)]
        dq_ref[rows, :] = jnp.concatenate(heads, axis=1).astype(BF16)
        return 0

    lax.fori_loop(0, 4, one_run, 0)
    for j in range(32):
        chip, core, u = j // 4, (j // 2) % 2, j % 2
        at = pl.ds(pl.multiple_of(key_runs[seq * 32 + j] * 64, 64), 64)
        rows, lanes = slice(64 * u, 64 * u + 64), slice(HD * core, HD * core + HD)
        dkv_ref[0, chip, rows, lanes] = dkeys[at, :].astype(BF16)
        dkv_ref[1, chip, rows, lanes] = dvalues[at, :].astype(BF16)


def attend_back(key_runs, query_runs, q, kv, grad, ot, lse, trigs):
    return pl.pallas_call(
        attend_back_kernel,
        out_shape=(shape((1024, 256)), shape((2, 8, 512, 128))),
        grid_spec=pltpu.PrefetchScalarGridSpec(
            num_scalar_prefetch=2,
            grid=(4,),
            in_specs=[
                pl.BlockSpec((256, 256), lambda i, *_: (i, 0)),
                pl.BlockSpec((2, 8, 128, 128), lambda i, *_: (0, 0, i, 0)),
                pl.BlockSpec((256, 256), lambda i, *_: (i, 0)),
                pl.BlockSpec((4, HD, 256), lambda i, *_: (i, 0, 0)),
                pl.BlockSpec((4, 1, 256), lambda i, *_: (i, 0, 0)),
                pl.BlockSpec((2, 64, 128), lambda i, *_: (i, 0, 0)),
            ],
            out_specs=[
                pl.BlockSpec((256, 256), lambda i, *_: (i, 0)),
                pl.BlockSpec((2, 8, 128, 128), lambda i, *_: (0, 0, i, 0)),
            ],
            scratch_shapes=[
                pltpu.VMEM((2048, HD), BF16),
                pltpu.VMEM((2048, HD), BF16),
                pltpu.VMEM((2048, HD), F32),
                pltpu.VMEM((2048, HD), F32),
                pltpu.VMEM((HD, 256), F32),
            ],
        ),
        compiler_params=pltpu.CompilerParams(vmem_limit_bytes=40 * 2**20),
        name="attend_back",
    )(key_runs, query_runs, q, kv, grad, ot, lse, trigs)


PART = 3 * FF_DEV // 2
PART_HALF = PART // 2


class RingSum:
    def __init__(self, me, edges, along_z, src, start, rows, width, step, relayed, last):
        self.edges, self.src, self.start, self.width, self.step = edges, src, start, width, step
        self.rows, self.half = rows, rows // 2
        self.relayed, self.last = relayed, last
        self.here = me.z if along_z else x_of(me)
        self.up = around(me, 1, 0) if along_z else around(me, 0, 1)
        self.down = around(me, -1, 0) if along_z else around(me, 0, 3)
        self.a, self.b = pl.ds(0, self.half), pl.ds(self.half, self.half)

    def columns(self, k):
        at = self.width * lax.rem(self.here + k, 4)
        return pl.ds(pl.multiple_of(at, self.width), self.width)

    def piece(self, k, half):
        rows = pl.ds(self.start + self.half * half, self.half)
        return self.src.at[rows, self.columns(k)]

    def far(self):
        self.r_a = self.edges.copy(self.piece(2, 0), self.relayed.at[0], self.up)
        self.r_b = self.edges.copy(self.piece(2, 1), self.relayed.at[1], self.down)

    def near_up(self):
        self.u_b = self.edges.copy(self.piece(1, 1), self.last.at[0, self.b], self.up)

    def near_down(self):
        self.d_a = self.edges.copy(self.piece(3, 0), self.last.at[1, self.a], self.down)

    def add(self, k, half):
        step, start, cols = self.step, self.start + self.half * half, self.columns(k)

        def one(i, _):
            at = pl.ds(pl.multiple_of(start + i * step, 16), step)
            from_ = pl.ds(pl.multiple_of(i * step, 16), step)
            self.src[at, cols] = (
                self.src[at, cols].astype(F32) + self.relayed[half, from_, :].astype(F32)
            ).astype(BF16)
            return 0

        lax.fori_loop(0, self.half // step, one, 0)

    def second(self):
        self.r_a.wait_recv()
        self.add(1, 0)
        self.u_a = self.edges.copy(self.piece(1, 0), self.last.at[0, self.a], self.up)
        self.r_b.wait_recv()
        self.add(3, 1)
        self.d_b = self.edges.copy(self.piece(3, 1), self.last.at[1, self.b], self.down)

    def total(self, out):
        for d in (self.u_b, self.d_a, self.u_a, self.d_b):
            d.wait_recv()
        step, cols = self.step, self.columns(0)

        def one(i, _):
            at = pl.ds(pl.multiple_of(self.start + i * step, 16), step)
            from_ = pl.ds(pl.multiple_of(i * step, 16), step)
            out[from_, :] = (
                self.src[at, cols].astype(F32)
                + self.last[0, from_, :].astype(F32)
                + self.last[1, from_, :].astype(F32)
            ).astype(BF16)
            return 0

        lax.fori_loop(0, self.rows // step, one, 0)


SUM_EDGES = 6


def feed_forward_kernel(
    parts, tokens, gain, cots, wgu, wdn, wswap, wnear,
    output, grad_middle, gain_grad, gbs, z_out, x_out,
    xs, p, c, gp, w, act_t, gate_t, up_t, act, dgate, dup, middle, low,
    g1, b1, r1, l1, g2, b2, r2, l2,
    z_relayed, z_last, x_relayed, x_last, z_q, x_q,
    z_relayed2, z_last2, x_relayed2, x_last2,
    send, recv, fs, fr, local,
):
    me = Place()
    core = me.at(core=1 - me.c)
    greet(
        [core, me.at(dy=1), me.at(dy=-1)]
        + [around(me, k, 0) for k in (1, 2, 3)]
        + [around(me, 0, 1), around(me, 0, 3)]
    )
    edges = Edges(send, recv)
    mine = 2 * me.y + me.c
    moved = me.c != me.xh
    load_p = pltpu.make_async_copy(parts, p, local.at[0])
    load_c = pltpu.make_async_copy(cots, c, local.at[1])
    load_p.start()
    load_c.start()

    def w_rows(dz):
        z = lax.rem(me.z + dz + 4, 4)
        return (
            pl.ds(pl.multiple_of(GU_QUARTER * z, 16), GU_QUARTER),
            pl.ds(pl.multiple_of(2 * FF_DEV + DN_QUARTER * z, 16), DN_QUARTER),
        )

    gu_part, dn_part = pl.ds(0, GU_QUARTER), pl.ds(GU_QUARTER, DN_QUARTER)
    kept = [
        pltpu.make_async_copy(wgu, w.at[pl.ds(0, 2 * FF_DEV)], local.at[2]),
        pltpu.make_async_copy(wdn, w.at[pl.ds(2 * FF_DEV, FF_DEV)], local.at[3]),
    ]
    near_w = []
    for i, (src, dz) in enumerate(((wswap, 0), (wnear.at[0], -1), (wnear.at[1], 1))):
        gu_rows, dn_rows = w_rows(dz)
        near_w.append(pltpu.make_async_copy(src.at[gu_part], w.at[gu_rows], local.at[4 + 2 * i]))
        near_w.append(pltpu.make_async_copy(src.at[dn_part], w.at[dn_rows], local.at[5 + 2 * i]))
    far_w = [
        pltpu.make_async_remote_copy(
            src_ref=wswap.at[part],
            dst_ref=w.at[rows],
            send_sem=fs.at[i],
            recv_sem=fr.at[i],
            device_id=me.at(dz=2),
            device_id_type=pl.DeviceIdType.MESH,
        )
        for i, (part, rows) in enumerate(zip((gu_part, dn_part), w_rows(0)))
    ]

    @pl.when(moved)
    def _():
        for d in far_w + near_w:
            d.start()

    @pl.when(jnp.logical_not(moved))
    def _():
        for d in kept:
            d.start()

    load_p.wait()
    ring = RingScatter(me, edges, p, (g1, b1, r1, l1))
    ring.first()
    ring.second()
    ring.arrived()

    def norm(at):
        rows = tokens[at, :].astype(F32) + ring.rows(at)
        middle[at, :] = rows
        normal = rows * lax.rsqrt(mean_last(rows * rows) + EPSILON)
        low[at, :] = (normal * gain[...]).astype(BF16)

    in_chunks(norm)
    keep = pltpu.make_async_copy(low, xs.at[mine], local.at[10])
    keep.start()
    gather = RingGather(me, edges, low, xs)
    ring.release()

    @pl.when(moved)
    def _():
        for d in near_w:
            d.wait()
        for d in far_w:
            d.wait()

    @pl.when(jnp.logical_not(moved))
    def _():
        for d in kept:
            d.wait()

    load_c.wait()
    keep.wait()

    def compute(pair):
        at = pl.ds(2 * pair, 2)
        x = xs[at].reshape(2 * TOK, D)
        g = c[at].reshape(2 * TOK, D)
        here = pl.ds(pl.multiple_of(2 * TOK * pair, 2 * TOK), 2 * TOK)
        for n0, n1 in ((0, 256), (256, 512), (512, FF_DEV)):
            gate = dot_last(x, w[n0:n1, :])
            upward = dot_last(x, w[FF_DEV + n0 : FF_DEV + n1, :])
            grad = dot_last(g, w[2 * FF_DEV + n0 : 2 * FF_DEV + n1, :])
            sigmoid = 1.0 / (1.0 + jnp.exp(-gate))
            swish = gate * sigmoid
            active = swish * upward
            grad_up = grad * swish
            grad_gate = grad * upward * sigmoid * (1.0 + gate * (1.0 - sigmoid))
            act[:, n0:n1] = active.astype(BF16)
            dup[:, n0:n1] = grad_up.astype(BF16)
            dgate[:, n0:n1] = grad_gate.astype(BF16)
            act_t[n0:n1, here] = active.T.astype(BF16)
            up_t[n0:n1, here] = grad_up.T.astype(BF16)
            gate_t[n0:n1, here] = grad_gate.T.astype(BF16)

        def block(i, _):
            cols = pl.ds(pl.multiple_of(512 * i, 512), 512)
            branch = dot(act[...], w[2 * FF_DEV :, cols])
            p[at, :, cols] = branch.astype(BF16).reshape(2, TOK, 512)
            grads = dot(dgate[...], w[:FF_DEV, cols]) + dot(dup[...], w[FF_DEV : 2 * FF_DEV, cols])
            gp[at, :, cols] = grads.astype(BF16).reshape(2, TOK, 512)
            return 0

        lax.fori_loop(0, 4, block, 0)

    def pair(k):
        return lax.rem(me.y + k, 4)

    two = RingScatter(me, edges, gp, (g1, b1, r1, l1))
    gather.from_core(0, 1)
    compute(pair(0))
    two.send_core(0)
    gather.relay()
    gather.near()
    gather.from_core(1, 5)

    def sides(i, _):
        compute(pair(1 + 2 * i))
        return 0

    lax.fori_loop(0, 2, sides, 0)
    two.send_core(1)
    two.send_core(3)
    gather.far()
    two.near()
    gather.from_core(5, 7)
    compute(pair(2))
    two.send_core(2)
    two.add_core(0)

    z_sum = RingSum(me, edges, True, w, 0, PART, 512, 48, z_relayed, z_last)
    x_sum = RingSum(me, edges, False, w, PART, PART, 512, 48, x_relayed, x_last)
    split = PART - FF_DEV

    def z_task(k):
        cols = z_sum.columns(k)
        x = xs[:, :, cols].reshape(8 * TOK, 512)
        w[:FF_DEV, cols] = dot(gate_t[...], x).astype(BF16)
        w[FF_DEV:PART, cols] = dot(up_t[:split, :], x).astype(BF16)

    def x_task(k):
        cols = x_sum.columns(k)
        x = xs[:, :, cols].reshape(8 * TOK, 512)
        g = c[:, :, cols].reshape(8 * TOK, 512)
        w[PART : 2 * FF_DEV, cols] = dot(up_t[split:, :], x).astype(BF16)
        w[2 * FF_DEV :, cols] = dot(act_t[...], g).astype(BF16)

    two.far()
    z_task(2)
    z_sum.far()
    x_task(2)
    x_sum.far()
    z_task(1)
    z_sum.near_up()
    x_task(1)
    x_sum.near_up()
    two.second()
    z_task(3)
    z_sum.near_down()
    x_task(3)
    x_sum.near_down()
    z_task(0)
    x_task(0)
    two.arrived()
    gain_grad[...] = jnp.zeros_like(gain_grad)

    def back(at):
        rows = middle[at, :]
        inverse = lax.rsqrt(mean_last(rows * rows) + EPSILON)
        normal = rows * inverse
        grad = two.rows(at)
        gain_grad[...] += jnp.sum(normal * grad, axis=0, keepdims=True)
        scaled = grad * gain[...]
        result = c[mine, at].astype(F32) + inverse * (
            scaled - normal * mean_last(scaled * normal)
        )
        grad_middle[at, :] = result
        low[at, :] = result.astype(BF16)

    edges.sent([gather.up_a, gather.up_b, gather.down_a, gather.down_b, gather.to_core[0]])
    in_chunks(back)
    keep = pltpu.make_async_copy(low, gbs.at[mine], local.at[10])
    keep.start()
    gather = RingGather(me, edges, low, gbs)
    branch = RingScatter(me, edges, p, (g2, b2, r2, l2))
    for k in (2, 1, 3, 0):
        branch.send_core(k)
    z_sum.second()
    x_sum.second()
    gather.relay()
    branch.far()
    branch.near()
    branch.add_core(0)
    z_sum.total(z_q)
    z_two = RingSum(me, edges, False, z_q, 0, PART, 128, 176, z_relayed2, z_last2)
    z_two.far()
    z_two.near_up()
    z_two.near_down()
    x_sum.total(x_q)
    x_two = RingSum(me, edges, True, x_q, 0, PART, 128, 176, x_relayed2, x_last2)
    x_two.far()
    x_two.near_up()
    x_two.near_down()
    gather.near()
    gather.far()
    branch.second()
    z_two.second()
    x_two.second()
    gather.from_core(0, 7)
    branch.arrived()

    def out(at):
        output[at, :] = (middle[at, :] + branch.rows(at)).astype(BF16)

    in_chunks(out)
    z_two.total(z_out)
    x_two.total(x_out)
    edges.finish()
    keep.wait()


def feed_forward(parts, tokens, gain, cots, wgu, wdn, wswap, wnear):
    block = pltpu.VMEM((8, TOK, D), BF16)
    turned = pltpu.VMEM((FF_DEV, 8 * TOK), BF16)
    pair = pltpu.VMEM((2 * TOK, FF_DEV), BF16)

    def ring(width):
        return [
            pltpu.VMEM((2, PART_HALF, width), BF16),
            pltpu.VMEM((2, PART, width), BF16),
        ] * 2

    return pl.pallas_call(
        feed_forward_kernel,
        out_shape=(
            shape((TOK, D)),
            shape((TOK, D), F32),
            shape((1, D), F32),
            shape((8, TOK, D)),
            shape((PART, 128)),
            shape((PART, 128)),
        ),
        in_specs=[ANY, VMEM, VMEM] + [ANY] * 5,
        out_specs=(VMEM, VMEM, VMEM, ANY, VMEM, VMEM),
        scratch_shapes=[block] * 4
        + [pltpu.VMEM((3 * FF_DEV, D), BF16)]
        + [turned] * 3
        + [pair] * 3
        + [pltpu.VMEM((TOK, D), F32), pltpu.VMEM((TOK, D), BF16)]
        + scatter_scratch() * 2
        + ring(512)
        + [pltpu.VMEM((PART, 512), BF16)] * 2
        + ring(128)
        + sems(3 * SCATTER_EDGES + 2 * GATHER_EDGES + 4 * SUM_EDGES)
        + sems(2)
        + [pltpu.SemaphoreType.DMA((11,))],
        compiler_params=pltpu.CompilerParams(
            collective_id=2, has_side_effects=True, vmem_limit_bytes=62 * 2**20
        ),
        name="feed_forward",
    )(parts, tokens, gain, cots, wgu, wdn, wswap, wnear)


def columns(width):
    return lambda i: (slice(None), pl.ds(pl.multiple_of(i * width, width), width))


def row_block(height, start=0):
    return lambda i: (pl.ds(pl.multiple_of(start + i * height, height), height), slice(None))


def plane_devices(me):
    found = [me.at(core=1 - me.c)]
    for dz, dx in STEPS:
        z, xl, core, y, xh = around(me, dz, dx)
        found += [(z, xl, core, y, xh), (z, xl, 1 - core, y, xh)]
    return found


def swapped_pairs(rows):
    return jnp.concatenate([halves_swapped(rows[:, :HD]), halves_swapped(rows[:, HD:])], axis=1)


class RingBlocks:
    def __init__(self, me, edges, ref, columns):
        self.me, self.edges, self.ref, self.columns = me, edges, ref, columns
        rows = ref.shape[0]
        self.halves = (pl.ds(0, rows // 2), pl.ds(rows // 2, rows // 2))
        self.up, self.down = me.at(dz=1), me.at(dz=-1)
        self.up_a = self.send(0, 0, self.up)
        self.down_b = self.send(0, 1, self.down)
        self.up_b = self.send(0, 1, self.up)
        self.down_a = self.send(0, 0, self.down)

    def block(self, dz):
        return self.ref.at[:, self.columns(lax.rem(self.me.z + dz + 4, 4))]

    def send(self, dz, half, device):
        cols = self.columns(lax.rem(self.me.z + dz + 4, 4))
        ref = self.ref.at[self.halves[half], cols]
        return self.edges.copy(ref, ref, device)

    def relay(self):
        self.up_a.wait_recv()
        self.on_a = self.send(-1, 0, self.up)
        self.down_b.wait_recv()
        self.on_b = self.send(1, 1, self.down)

    def near(self):
        self.up_b.wait_recv()
        self.down_a.wait_recv()

    def far(self):
        self.on_a.wait_recv()
        self.on_b.wait_recv()


class PlaneGather:
    def __init__(self, me, edges, z_piece, x_piece, z_all, x_all, send, recv):
        self.me, self.edges, self.z_all, self.x_all = me, edges, z_all, x_all
        self.send, self.recv, self.z_piece, self.x_piece = send, recv, z_piece, x_piece
        self.stays = me.c == me.xh
        self.core = me.at(core=1 - me.c)
        self.side = me.at(xl=1 - me.xl)
        across = me.at(core=1 - me.c, xl=1 - me.xl, xh=1 - me.xh)
        x = x_of(me)
        self.held = jnp.where(self.stays, x, 3 - x)
        for i, (piece, ref, at) in enumerate(
            ((z_piece, z_all, 4 * me.z + x), (x_piece, x_all, 4 * x + me.z))
        ):
            dst = ref.at[columns(128)(at)]
            send_block(me, piece, dst, send.at[i], recv.at[i], across, self.stays)

    def z_columns(self, z):
        return pl.ds(pl.multiple_of(512 * z + 256 * self.me.c, 256), 256)

    def x_columns(self, z):
        return pl.ds(pl.multiple_of(512 * self.held + 128 * z, 128), 128)

    def sideways(self):
        own = self.z_all.at[columns(128)(4 * self.me.z + self.held)]
        wait_got(own, self.recv.at[0])
        self.z_side = self.edges.copy(own, own, self.side)
        own = self.x_all.at[:, self.x_columns(self.me.z)]
        wait_got(own, self.recv.at[1])
        self.x_ring = RingBlocks(self.me, self.edges, self.x_all, self.x_columns)
        self.x_side = [self.edges.copy(own, own, self.side)]

    def along(self):
        self.z_side.wait_recv()
        self.z_ring = RingBlocks(self.me, self.edges, self.z_all, self.z_columns)
        own = self.z_ring.block(0)
        self.over = [self.edges.copy(own, own, self.core)]
        self.x_ring.relay()

    def to_side(self, dz):
        ref = self.x_ring.block(dz)
        self.x_side.append(self.edges.copy(ref, ref, self.side))

    def to_core(self, dz):
        ref = self.z_ring.block(dz)
        self.over.append(self.edges.copy(ref, ref, self.core))

    def near(self):
        self.x_ring.near()
        self.to_side(1)
        self.to_side(-1)
        self.z_ring.relay()
        self.x_ring.far()
        self.to_side(2)

    def far(self):
        self.z_ring.near()
        self.to_core(1)
        self.to_core(-1)
        self.z_ring.far()
        self.to_core(2)
        for d in self.x_side:
            d.wait_recv()
        half = self.x_all.at[:, pl.ds(pl.multiple_of(1024 * self.me.c, 1024), 1024)]
        self.over.append(self.edges.copy(half, half, self.core))

    def finish(self):
        for d in self.over:
            d.wait_recv()
        wait_sent(self.z_piece, self.send.at[0], self.stays)
        wait_sent(self.x_piece, self.send.at[1], self.stays)


PLANE_EDGES = 1 + 2 * SUM_EDGES + 4 + 5


class TwoSums:
    def __init__(self, me, edges, src, rows, steps, scratch):
        self.me, self.edges, self.rows, self.steps = me, edges, rows, steps
        self.q, self.out = scratch[4:6], scratch[10:12]
        self.scratch = scratch
        start = (0, rows[0])
        self.one = [
            RingSum(
                me, edges, i == 0, src, start[i], rows[i], 512, steps[0][i],
                scratch[2 * i], scratch[2 * i + 1],
            )
            for i in (0, 1)
        ]
        for ring in self.one:
            ring.far()
            ring.near_up()
            ring.near_down()

    def second(self):
        for ring in self.one:
            ring.second()

    def cross(self):
        self.two = []
        for i in (0, 1):
            self.one[i].total(self.q[i])
            ring = RingSum(
                self.me, self.edges, i == 1, self.q[i], 0, self.rows[i], 128,
                self.steps[1][i], self.scratch[6 + 2 * i], self.scratch[7 + 2 * i],
            )
            ring.far()
            ring.near_up()
            ring.near_down()
            self.two.append(ring)

    def fourth(self):
        for ring in self.two:
            ring.second()

    def total(self):
        for i in (0, 1):
            self.two[i].total(self.out[i])


def two_sums_scratch(rows):
    found = []
    for r in rows:
        found += [pltpu.VMEM((2, r // 2, 512), BF16), pltpu.VMEM((2, r, 512), BF16)]
    found += [pltpu.VMEM((r, 512), BF16) for r in rows]
    for r in rows:
        found += [pltpu.VMEM((2, r // 2, 128), BF16), pltpu.VMEM((2, r, 128), BF16)]
    return found + [pltpu.VMEM((r, 128), BF16) for r in rows]


WQ_ROWS = (128, 192)
WO_ROWS = (128, 128)


def ending_kernel(
    dkv, dq, kv_table, wq, tokens, gain, grad_middle, gain_two, z_piece, x_piece, gwo_in, xs_in,
    grad_tokens, gains, wq_out, wo_out, z_all, x_all,
    kv_got, kv_both, kv_last, dkv_low, xs, grads, grads_t, parts, gwq, gwo,
    got, both, relayed, last, wq_all, wo_all, mine, near, near_sum, owners,
    *rest,
):
    wq_scratch, wo_scratch = rest[:12], rest[12:24]
    (send, recv, ds, dr, es, er, ps, pr, gs, gr, hs, hr, local) = rest[24:]
    me = Place()
    core = me.at(core=1 - me.c)
    far = [
        me.at(dz=dz, xl=(1 - me.xl) if dl else me.xl) for dz, dl in chips_in_sequence(me)
    ]
    greet(plane_devices(me) + group_members(me)[1:])
    edges = Edges(send, recv)
    place = 4 * me.z + x_of(me)
    turned = 4 * x_of(me) + me.z
    rank = 2 * me.y + me.c
    load_x = pltpu.make_async_copy(xs_in, xs, local.at[0])
    load_x.start()
    load_wo = pltpu.make_async_copy(gwo_in, gwo, local.at[1])
    load_wo.start()

    order = []
    for dz, dl in chips_in_sequence(me) + [(0, 0)]:
        chip = 2 * lax.rem(me.z + dz, 4) + ((1 - me.xl) if dl else me.xl)
        order.append((chip, edges.copy(dkv.at[1 - me.c, chip], kv_got.at[chip], core)))
    plane = PlaneGather(me, edges, z_piece, x_piece, z_all, x_all, ps, pr)
    far_copies = []
    for i, (chip, d) in enumerate(order):
        d.wait_recv()
        kv_both[chip] = (dkv[me.c, chip].astype(F32) + kv_got[chip].astype(F32)).astype(BF16)
        if i < 7:
            far_copies.append(edges.copy(kv_both.at[chip], kv_last.at[i], far[i]))
    load_wo.wait()
    wo_sum = TwoSums(me, edges, gwo, WO_ROWS, ((64, 64), (64, 64)), wo_scratch)
    plane.sideways()

    def query_part(i, _):
        at = pl.ds(pl.multiple_of(2 * TOK * i, 2 * TOK), 2 * TOK)
        rows = dq[at, :]
        grads[at, :Q_DEV] = rows
        grads_t[:Q_DEV, at] = rows.astype(F32).T.astype(BF16)
        return 0

    lax.fori_loop(0, 4, query_part, 0)
    plane.along()
    wo_sum.second()
    for d in far_copies:
        d.wait_recv()

    def kv_total(at):
        total = kv_both[2 * me.z + me.xl, at].astype(F32)
        for i in range(7):
            total = total + kv_last[i, at].astype(F32)
        dkv_low[at, :] = (
            total * kv_table[0, at, :] - swapped_pairs(total) * kv_table[1, at, :]
        )

    in_chunks(kv_total, 512)
    for i in range(4):
        for half in (0, 1):
            rows = dkv_low[TOK * i : TOK * (i + 1), HD * half : HD * half + HD]
            at = slice(TOK * (2 * i + half), TOK * (2 * i + half + 1))
            grads[at, Q_DEV:] = rows.astype(BF16)
            grads_t[Q_DEV:, at] = rows.T.astype(BF16)

    load_x.wait()

    def weight_block(i, _):
        cols = pl.ds(pl.multiple_of(512 * i, 512), 512)
        term = dot(grads_t[...], xs[:, :, cols].reshape(8 * TOK, 512))
        gwq[:, cols] = term.astype(BF16)
        return 0

    lax.fori_loop(0, 4, weight_block, 0)
    wq_sum = TwoSums(me, edges, gwq, WQ_ROWS, ((64, 48), (64, 96)), wq_scratch)
    ring = RingScatter(me, edges, parts, (got, both, relayed, last))

    def part(k):
        pair = lax.rem(me.y + k, 4)
        rows = grads[pl.ds(pl.multiple_of(2 * TOK * pair, 2 * TOK), 2 * TOK), :]

        def block(i, _):
            cols = pl.ds(pl.multiple_of(512 * i, 512), 512)
            term = dot(rows, wq[:, cols]).astype(BF16)
            parts[pl.ds(2 * pair, 2), :, cols] = term.reshape(2, TOK, 512)
            return 0

        lax.fori_loop(0, 4, block, 0)
        ring.send_core(k)

    part(2)
    part(1)
    ring.far()
    part(3)
    ring.near()
    part(0)
    ring.add_core(0)
    wq_sum.second()
    wo_sum.cross()
    plane.near()
    ring.second()
    wq_sum.cross()
    wo_sum.fourth()
    wo_sum.total()
    wo_deliver = Deliver(me, es, er)
    for i, at in enumerate((place, turned)):
        dst = wo_all.at[
            pl.ds(pl.multiple_of(Q_DEV * rank + 128 * i, 128), 128),
            pl.ds(pl.multiple_of(128 * lax.rem(at, 2), 128), 128),
        ]
        wo_deliver.to_owner(wo_sum.out[i], dst, me.y // 2, at // 4, lax.rem(at // 2, 2))
    wq_sum.fourth()
    ring.arrived()
    mine[...] = jnp.zeros_like(mine)
    mine[1:2, :] = gain_two[...]

    def back(at):
        rows = tokens[at, :].astype(F32)
        inverse = lax.rsqrt(mean_last(rows * rows) + EPSILON)
        normal = rows * inverse
        grad = ring.rows(at)
        mine[0:1, :] += jnp.sum(normal * grad, axis=0, keepdims=True)
        scaled = grad * gain[...]
        grad_tokens[at, :] = grad_middle[at, :] + inverse * (
            scaled - normal * mean_last(scaled * normal)
        )

    in_chunks(back)

    def slice_of(member):
        return mine.at[:, pl.ds(pl.multiple_of(256 * member, 256), 256)]

    near_copies = []
    for k in range(1, 8):
        dy, other = k // 2, k % 2
        y = lax.rem(me.y + dy, 4)
        to_core = 1 - me.c if other else me.c
        d = pltpu.make_async_remote_copy(
            src_ref=slice_of(2 * y + to_core),
            dst_ref=near.at[k - 1],
            send_sem=gs.at[k - 1],
            recv_sem=gr,
            device_id=me.at(y=y, core=to_core),
            device_id_type=pl.DeviceIdType.MESH,
        )
        d.start()
        near_copies.append(d)
    wq_sum.total()
    wq_deliver = Deliver(me, ds, dr)
    for j in range(5):
        block = own_block(me, j)
        owner, slot = block // 5, lax.rem(block, 5)
        at = place if j < 2 else turned
        piece = wq_sum.out[0] if j < 2 else wq_sum.out[1]
        dst = wq_all.at[
            pl.ds(pl.multiple_of(64 * slot, 64), 64),
            pl.ds(pl.multiple_of(128 * at, 128), 128),
        ]
        src = piece.at[pl.ds(64 * (j if j < 2 else j - 2), 64)]
        wq_deliver.to_owner(src, dst, at // 8, owner // 2, lax.rem(owner, 2))
    own = mine[:, pl.ds(pl.multiple_of(256 * rank, 256), 256)]
    wait_got(near, gr)
    for k in range(7):
        own = own + near[k]
    near_sum[...] = own
    gain_deliver = Deliver(me, hs, hr)
    for to_core in (0, 1):
        gain_deliver.to_owner(near_sum, owners.at[place], to_core, me.y, me.c)
    plane.far()

    half = pl.ds(pl.multiple_of(1024 * me.c, 1024), 1024)
    over = []
    for ref, sem in ((wo_all.at[half], er), (wq_all.at[:, half], dr)):
        wait_got(ref, sem)
        over.append(edges.copy(ref, ref, core))
    wait_got(owners, hr)
    sum_all = owners[0]
    for k in range(1, 16):
        sum_all = sum_all + owners[k]
    gains[...] = sum_all
    for d in over:
        d.wait_recv()
    wo_out[...] = wo_all[...]
    wq_out[...] = wq_all[...]
    plane.finish()
    for d in (wo_deliver, wq_deliver, gain_deliver):
        d.finish()
    for d in near_copies:
        d.wait_send()
    edges.finish()


def ending(dkv, dq, kv_table, wq, tokens, gain, grad_middle, gain_two, z_piece, x_piece, gwo, xs):
    many = pltpu.SemaphoreType.DMA
    return pl.pallas_call(
        ending_kernel,
        out_shape=(
            shape((TOK, D), F32),
            shape((8, 256), F32),
            shape((320, D)),
            shape((D, 256)),
            shape((PART, D)),
            shape((PART, D)),
        ),
        in_specs=[VMEM] * 10 + [ANY] * 2,
        out_specs=(VMEM,) * 4 + (ANY,) * 2,
        scratch_shapes=[
            pltpu.VMEM((8, 512, 128), BF16),
            pltpu.VMEM((8, 512, 128), BF16),
            pltpu.VMEM((7, 512, 128), BF16),
            pltpu.VMEM((512, 128), F32),
            pltpu.VMEM((8, TOK, D), BF16),
            pltpu.VMEM((1024, 320), BF16),
            pltpu.VMEM((320, 1024), BF16),
            pltpu.VMEM((8, TOK, D), BF16),
            pltpu.VMEM((320, D), BF16),
            pltpu.VMEM((256, D), BF16),
        ]
        + scatter_scratch()
        + [
            pltpu.VMEM((320, D), BF16),
            pltpu.VMEM((D, 256), BF16),
            pltpu.VMEM((8, D), F32),
            pltpu.VMEM((7, 8, 256), F32),
            pltpu.VMEM((8, 256), F32),
            pltpu.VMEM((16, 8, 256), F32),
        ]
        + two_sums_scratch(WQ_ROWS)
        + two_sums_scratch(WO_ROWS)
        + sems(15 + SCATTER_EDGES + PLANE_EDGES + 8 * SUM_EDGES + 2)
        + [many((40,)), many, many((16,)), many, many((2,)), many((2,))]
        + [many((7,)), many, many((16,)), many, many((2,))],
        compiler_params=remote_params(3),
        name="ending",
    )(dkv, dq, kv_table, wq, tokens, gain, grad_middle, gain_two, z_piece, x_piece, gwo, xs)


def widen_kernel(z_ref, x_ref, gu_ref, dn_ref):
    i = pl.program_id(0)

    @pl.when(i < 3)
    def _():
        gu_ref[...] = z_ref[...].astype(F32)

    @pl.when(i == 3)
    def _():
        gu_ref[...] = x_ref[...].astype(F32)

    @pl.when(i > 3)
    def _():
        dn_ref[...] = x_ref[...].astype(F32)


def widen(z_all, x_all):
    rows = PART // 3
    return pl.pallas_call(
        widen_kernel,
        out_shape=(shape((2 * FF_DEV, D), F32), shape((FF_DEV, D), F32)),
        grid=(6,),
        in_specs=[
            pl.BlockSpec((rows, D), lambda i: (jnp.minimum(i, 2), 0)),
            pl.BlockSpec((rows, D), lambda i: (jnp.maximum(i - 3, 0), 0)),
        ],
        out_specs=(
            pl.BlockSpec((rows, D), lambda i: (jnp.minimum(i, 3), 0)),
            pl.BlockSpec((rows, D), lambda i: (jnp.maximum(i - 4, 0), 0)),
        ),
        compiler_params=pltpu.CompilerParams(vmem_limit_bytes=40 * 2**20),
        name="widen",
    )(z_all, x_all)


def body(hidden, positions, gain_attn, w_qkv, w_out, gain_mlp, w_gate_up, w_down, cotangent):
    gain_one = gain_attn.astype(F32).reshape(1, D)
    gain_two = gain_mlp.astype(F32).reshape(1, D)
    wgu = w_gate_up.reshape(2 * FF_DEV, D)
    wdn = w_down.T
    query, kv_table, trigs, xs, wq, poss, kvs, places, cots, wo, wswap, wnear = begin(
        hidden[0],
        gain_one,
        jnp.broadcast_to(positions, (8, TOK)),
        rotary_rows(positions[0]),
        w_qkv,
        wgu,
        wdn,
        cotangent[0],
        w_out,
    )
    wo = wo.reshape(D, Q_DEV)
    query_runs = poss[:, 0, ::64].reshape(16) // 64
    key_runs = (
        places[:, :, 0, ::64].reshape(8, 4, 2, 2).transpose(1, 0, 2, 3).reshape(128) // 64
    )
    att, ot, lse = attend(key_runs, query_runs, query, kvs)
    parts = dot_last(att, wo).astype(BF16).reshape(8, TOK, D)
    output, grad_middle, gain_grad, gbs, z_piece, x_piece = feed_forward(
        parts, hidden[0], gain_two, cots, wgu, wdn, wswap, wnear
    )
    gb = gbs.reshape(1024, D)
    grad_att = dot(gb, wo).astype(BF16)
    grad_wo = dot_first(att, gb).astype(BF16)
    dq, dkv = attend_back(key_runs, query_runs, query, kvs, grad_att, ot, lse, trigs)
    grad_tokens, gains, grad_w_qkv, grad_w_out, z_all, x_all = ending(
        dkv,
        dq,
        kv_table,
        wq,
        hidden[0],
        gain_one,
        grad_middle,
        gain_grad,
        z_piece,
        x_piece,
        grad_wo,
        xs,
    )
    grad_gu, grad_dn = widen(z_all, x_all)
    return (
        output[None],
        grad_tokens[None],
        gains[0],
        grad_w_qkv.astype(F32),
        grad_w_out.T.astype(F32),
        gains[1],
        grad_gu.reshape(2, FF_DEV, D),
        grad_dn.T,
    )


def solution(mesh):
    fine = Mesh(mesh.devices.reshape(4, 2, 2, 4, 2), AXES)
    ctx, fsdp = ("z", "xl", "c"), ("y", "xh")
    weight = P(fsdp, None)
    return jax.shard_map(
        body,
        mesh=fine,
        in_specs=(
            P(fsdp, ctx, None),
            P(fsdp, ctx),
            P(),
            weight,
            weight,
            P(),
            P(None, fsdp, None),
            P(None, fsdp),
            P(fsdp, ctx, None),
        ),
        out_specs=(
            P(fsdp, ctx, None),
            P(fsdp, ctx, None),
            P(fsdp),
            weight,
            weight,
            P(fsdp),
            P(None, fsdp, None),
            P(None, fsdp),
        ),
        check_vma=False,
    )
```

```python
import jax
import jax.numpy as jnp
from jax import lax
from jax.experimental import pallas as pl
from jax.experimental.pallas import tpu as pltpu
from jax.sharding import Mesh
from jax.sharding import PartitionSpec as P

D = 2048
H = 32
KV = 4
HD = 64
FF = 5632
TOK = 128
HALF = 64
FF_DEV = 704
Q_DEV = 256
EPSILON = 1e-05
FILLER = -1e30
AXES = ("z", "xl", "c", "y", "xh")
ANY = pl.BlockSpec(memory_space=pl.ANY)
VMEM = pl.BlockSpec(memory_space=pltpu.VMEM)
BF16 = jnp.bfloat16
F32 = jnp.float32


class Place:
    def __init__(self):
        self.z, self.xl, self.c, self.y, self.xh = (lax.axis_index(a) for a in AXES)

    def at(self, dz=0, dy=0, core=None, xl=None, xh=None, y=None):
        z = lax.rem(self.z + dz + 4, 4) if dz else self.z
        y = (lax.rem(self.y + dy + 4, 4) if dy else self.y) if y is None else y
        return (
            z,
            self.xl if xl is None else xl,
            self.c if core is None else core,
            y,
            self.xh if xh is None else xh,
        )


class Edges:
    def __init__(self, send, recv):
        self.send, self.recv, self.count, self.started = send, recv, 0, []

    def copy(self, src, dst, device, start=True):
        i = self.count
        self.count += 1
        d = pltpu.make_async_remote_copy(
            src_ref=src,
            dst_ref=dst,
            send_sem=self.send.at[i],
            recv_sem=self.recv.at[i],
            device_id=device,
            device_id_type=pl.DeviceIdType.MESH,
        )
        self.started.append(d)
        if start:
            d.start()
        return d

    def sent(self, copies):
        for d in copies:
            d.wait_send()
        self.started = [d for d in self.started if all(d is not e for e in copies)]

    def finish(self):
        for d in self.started:
            d.wait_send()


def greet(devices):
    for device in devices:
        pl.semaphore_signal(
            pltpu.get_barrier_semaphore(),
            inc=1,
            device_id=device,
            device_id_type=pl.DeviceIdType.MESH,
        )
    return len(devices)


def met(count):
    pl.semaphore_wait(pltpu.get_barrier_semaphore(), count)


def group_members(me):
    found = [me.at(core=1 - me.c)]
    for dy in (1, 2, 3):
        found += [me.at(dy=dy), me.at(dy=dy, core=1 - me.c)]
    return found


class RingGather:
    def __init__(self, me, edges, own, out):
        self.me, self.edges, self.out = me, edges, out
        self.core = me.at(core=1 - me.c)
        self.up, self.down = me.at(dy=1), me.at(dy=-1)
        a, b = pl.ds(0, HALF), pl.ds(HALF, HALF)
        self.a, self.b = a, b
        mine = self.slot(0)
        self.up_a = edges.copy(own.at[a], out.at[mine, a], self.up)
        self.down_b = edges.copy(own.at[b], out.at[mine, b], self.down)
        self.up_b = edges.copy(own.at[b], out.at[mine, b], self.up)
        self.down_a = edges.copy(own.at[a], out.at[mine, a], self.down)
        self.to_core = [edges.copy(own, out.at[mine], self.core)]

    def slot(self, dy):
        return 2 * lax.rem(self.me.y + dy + 4, 4) + self.me.c

    def pass_core(self, dy, part):
        ref = self.out.at[self.slot(dy), part]
        self.to_core.append(self.edges.copy(ref, ref, self.core))

    def relay(self):
        out = self.out
        self.up_a.wait_recv()
        ref = out.at[self.slot(-1), self.a]
        self.on_a = self.edges.copy(ref, ref, self.up)
        self.down_b.wait_recv()
        ref = out.at[self.slot(1), self.b]
        self.on_b = self.edges.copy(ref, ref, self.down)
        self.pass_core(-1, self.a)
        self.pass_core(1, self.b)

    def near(self):
        self.up_b.wait_recv()
        self.pass_core(-1, self.b)
        self.down_a.wait_recv()
        self.pass_core(1, self.a)

    def far(self):
        self.on_a.wait_recv()
        self.pass_core(2, self.a)
        self.on_b.wait_recv()
        self.pass_core(2, self.b)

    def from_core(self, first, last):
        for d in self.to_core[first:last]:
            d.wait_recv()

    def rest(self):
        self.near()
        self.far()
        self.from_core(0, 7)


GATHER_EDGES = 13


class RingScatter:
    def __init__(self, me, edges, parts, scratch):
        self.me, self.edges, self.parts = me, edges, parts
        self.got, self.both, self.relayed, self.last = scratch
        self.up, self.down = me.at(dy=1), me.at(dy=-1)
        self.cores = {}
        self.a, self.b = pl.ds(0, HALF), pl.ds(HALF, HALF)

    def send_core(self, k):
        row = 2 * lax.rem(self.me.y + k, 4) + 1 - self.me.c
        core = self.me.at(core=1 - self.me.c)
        self.cores[k] = self.edges.copy(self.parts.at[row], self.got.at[k], core)

    def add_core(self, k):
        self.cores[k].wait_recv()
        row = 2 * lax.rem(self.me.y + k, 4) + self.me.c

        def add(at):
            self.both[k, at] = (
                self.parts[row, at].astype(F32) + self.got[k, at].astype(F32)
            ).astype(BF16)

        in_chunks(add)

    def far(self):
        self.add_core(2)
        e, both = self.edges, self.both
        self.r_a = e.copy(both.at[2, self.a], self.relayed.at[0], self.up)
        self.r_b = e.copy(both.at[2, self.b], self.relayed.at[1], self.down)

    def near(self):
        e, both = self.edges, self.both
        self.add_core(1)
        self.u_b = e.copy(both.at[1, self.b], self.last.at[0, self.b], self.up)
        self.add_core(3)
        self.d_a = e.copy(both.at[3, self.a], self.last.at[1, self.a], self.down)

    def first(self):
        for k in (2, 1, 3, 0):
            self.send_core(k)
        self.far()
        self.near()
        self.add_core(0)

    def second(self):
        a, b, e, both = self.a, self.b, self.edges, self.both
        self.r_a.wait_recv()
        both[1, a] = (both[1, a].astype(F32) + self.relayed[0].astype(F32)).astype(BF16)
        self.u_a = e.copy(both.at[1, a], self.last.at[0, a], self.up)
        self.r_b.wait_recv()
        both[3, b] = (both[3, b].astype(F32) + self.relayed[1].astype(F32)).astype(BF16)
        self.d_b = e.copy(both.at[3, b], self.last.at[1, b], self.down)

    def arrived(self):
        for d in (self.u_b, self.d_a, self.u_a, self.d_b):
            d.wait_recv()

    def rows(self, at):
        return (
            self.both[0, at].astype(F32)
            + self.last[0, at].astype(F32)
            + self.last[1, at].astype(F32)
        )

    def release(self):
        ring = [self.r_a, self.r_b, self.u_b, self.d_a, self.u_a, self.d_b]
        self.edges.sent(ring + list(self.cores.values()))


SCATTER_EDGES = 10


def scatter_scratch():
    return [
        pltpu.VMEM((4, TOK, D), BF16),
        pltpu.VMEM((4, TOK, D), BF16),
        pltpu.VMEM((2, HALF, D), BF16),
        pltpu.VMEM((2, TOK, D), BF16),
    ]


def sems(n):
    return [pltpu.SemaphoreType.DMA((n,)), pltpu.SemaphoreType.DMA((n,))]


def shape(dims, dtype=BF16):
    return jax.ShapeDtypeStruct(dims, dtype)


def remote_params(number):
    return pltpu.CompilerParams(
        collective_id=number, has_side_effects=True, vmem_limit_bytes=48 * 2**20
    )


def block_place(block):
    is_kv = block >= 32
    other = block - 32
    rank = block // 4
    y = jnp.where(is_kv, lax.rem(other + 32, 4), rank // 2)
    core = jnp.where(is_kv, other // 4, lax.rem(rank, 2))
    return y, core, jnp.where(is_kv, 4, lax.rem(block, 4))


def own_block(me, j):
    if j == 4:
        return 32 + 4 * me.c + me.y
    return 4 * (2 * me.y + me.c) + j


def send_block(me, src, dst, send_sem, recv_sem, target, stays):
    @pl.when(stays)
    def _():
        pltpu.make_async_copy(src, dst, recv_sem).start()

    @pl.when(jnp.logical_not(stays))
    def _():
        pltpu.make_async_remote_copy(
            src_ref=src,
            dst_ref=dst,
            send_sem=send_sem,
            recv_sem=recv_sem,
            device_id=target,
            device_id_type=pl.DeviceIdType.MESH,
        ).start()


def wait_sent(src, send_sem, stays):
    @pl.when(jnp.logical_not(stays))
    def _():
        pltpu.make_async_copy(src, src, send_sem).wait()


def wait_got(dst, recv_sem):
    pltpu.make_async_copy(dst, dst, recv_sem).wait()


def x_of(me):
    return 2 * me.xh + me.xl


def around(me, dz, dx):
    x = lax.rem(x_of(me) + dx, 4)
    return me.at(dz=dz, xl=lax.rem(x, 2), xh=x // 2)


STEPS = [(dz, dx) for dz in range(4) for dx in range(4)][1:]


class SumOfSixteen:
    def __init__(self, me, src, piece, own, got, send, recv, local):
        self.me, self.src, self.piece, self.own, self.got = me, src, piece, own, got
        self.send, self.recv = send, recv
        self.keep = pltpu.make_async_copy(
            src.at[piece(4 * me.z + x_of(me))], own, local
        )
        self.keep.start()
        for k, (dz, dx) in enumerate(STEPS):
            to = 4 * lax.rem(me.z + dz, 4) + lax.rem(x_of(me) + dx, 4)
            self.copy(src.at[piece(to)], k, around(me, dz, dx)).start()

    def copy(self, src, k, device):
        return pltpu.make_async_remote_copy(
            src_ref=src,
            dst_ref=self.got.at[k],
            send_sem=self.send.at[k],
            recv_sem=self.recv,
            device_id=device,
            device_id_type=pl.DeviceIdType.MESH,
        )

    def total(self):
        self.keep.wait()
        pltpu.make_async_copy(self.got, self.got, self.recv).wait()
        total = self.own[...].astype(F32)
        for k in range(15):
            total = total + self.got[k].astype(F32)
        return total

    def finish(self):
        for k in range(15):
            src = self.src.at[self.piece(0)]
            pltpu.make_async_copy(src, src, self.send.at[k]).wait()


def same(me, z, xl, core, y, xh):
    return (z == me.z) & (xl == me.xl) & (core == me.c) & (y == me.y) & (xh == me.xh)


class Deliver:
    def __init__(self, me, send, recv):
        self.me, self.send, self.recv, self.sent = me, send, recv, []

    def to_owner(self, src, dst, core, y, xh):
        me = self.me
        for dz in range(4):
            for dl in (0, 1):
                z = lax.rem(me.z + dz, 4)
                xl = 1 - me.xl if dl else me.xl
                stays = same(me, z, xl, core, y, xh)
                sem = self.send.at[len(self.sent)]
                send_block(me, src, dst, sem, self.recv, (z, xl, core, y, xh), stays)
                self.sent.append((src, sem, stays))

    def finish(self):
        for src, sem, stays in self.sent:
            wait_sent(src, sem, stays)


def rotary_rows(places):
    steps = jnp.arange(HD // 2, dtype=F32)
    inverse = jnp.power(10000.0, steps * (-2.0 / HD))
    turning = places.astype(F32)[:, None] * inverse[None, :]
    rows = jnp.concatenate([jnp.cos(turning), jnp.sin(turning)], axis=1)
    return rows.reshape(2, 64, HD).transpose(1, 0, 2).reshape(64, 2 * HD)


def halves_swapped(rows):
    return jnp.concatenate([rows[:, HD // 2 :], rows[:, : HD // 2]], axis=1)


def rotate(rows, table, back=False):
    turned = halves_swapped(rows) * table[:, HD:]
    return rows * table[:, :HD] + (-turned if back else turned)


def rotary_of(rows, u):
    cosine = rows[:, HD * u : HD * u + HD // 2]
    sine = rows[:, HD * u + HD // 2 : HD * u + HD]
    return jnp.concatenate([cosine, cosine, -sine, sine], axis=1)


ROWS = 16


def in_chunks(step, rows=TOK):
    def one(i, _):
        step(pl.ds(pl.multiple_of(i * ROWS, ROWS), ROWS))
        return 0

    lax.fori_loop(0, rows // ROWS, one, 0)


def mean_last(rows):
    return jnp.mean(rows, axis=-1, keepdims=True)


GU_QUARTER = 2 * FF_DEV // 4
DN_QUARTER = FF_DEV // 4
QUARTER = GU_QUARTER + DN_QUARTER


def swap_copies(me, wgu, wdn, wswap, send, recv):
    found = []
    across = me.at(core=1 - me.c, xl=1 - me.xl, xh=1 - me.xh)
    for i, (src, rows, start) in enumerate(
        ((wgu, GU_QUARTER, 0), (wdn, DN_QUARTER, GU_QUARTER))
    ):
        found.append(
            pltpu.make_async_remote_copy(
                src_ref=src.at[pl.ds(pl.multiple_of(rows * me.z, 16), rows)],
                dst_ref=wswap.at[pl.ds(start, rows)],
                send_sem=send.at[i],
                recv_sem=recv.at[i],
                device_id=across,
                device_id_type=pl.DeviceIdType.MESH,
            )
        )
    return found


def chips_in_sequence(me):
    return [(dz, dl) for dz in range(4) for dl in (0, 1)][1:]


def begin_kernel(
    tokens, gain, pos, trig, wqkv, wgu, wdn, cot, wout,
    q, kv_table, trigs, xs_out, wq_out, poss, kvs, places, cots, wo, wswap,
    low, xs, wq, kv,
    send, recv, qs, qr, os_, orr, ws, wr, local,
):
    me = Place()
    partner = {"xl": 1 - me.xl, "xh": 1 - me.xh}
    core = me.at(core=1 - me.c)
    members = group_members(me)
    others = [
        me.at(y=lax.rem(me.y + dy, 4), core=c, **partner) for dy in range(4) for c in (0, 1)
    ]
    far = [
        me.at(dz=dz, xl=(1 - me.xl) if dl else me.xl) for dz, dl in chips_in_sequence(me)
    ]
    signalled = greet(members + others + far)
    edges = Edges(send, recv)
    mine = 2 * me.y + me.c
    chip = 2 * me.z + me.xl

    def norm_rows():
        def norm(at):
            rows = tokens[at, :].astype(F32)
            inverse = lax.rsqrt(mean_last(rows * rows) + EPSILON)
            low[at, :] = (rows * inverse * gain[...]).astype(BF16)

        in_chunks(norm)

    spread = pl.ds(pl.multiple_of(512 * me.z, 512), 512)
    spread_rows = pl.ds(pl.multiple_of(64 * me.z, 64), 64)
    own = 2 * me.y + me.xh
    own_column = me.c == 0
    to_xl = jnp.where(own_column, me.xl, 1 - me.xl)
    to_xh = jnp.where(own_column, me.xh, 1 - me.xh)
    norm_rows()
    met(signalled)
    blocks = []
    for i in range(5):
        y, to_core, slot = block_place(5 * own + i)
        stays = own_column & (y == me.y) & (to_core == me.c)
        src = wqkv.at[pl.ds(64 * i, 64), spread]
        dst = wq.at[pl.ds(pl.multiple_of(64 * slot, 64), 64), spread]
        target = (me.z, to_xl, to_core, y, to_xh)
        send_block(me, src, dst, qs.at[i], qr.at[slot], target, stays)
        blocks.append((src, qs.at[i], stays))

    keep = pltpu.make_async_copy(low, xs.at[mine], local.at[0])
    keep.start()
    keep_pos = pltpu.make_async_copy(pos, poss.at[mine], local.at[1])
    keep_pos.start()
    pos_copies = [edges.copy(pos, poss.at[mine], m) for m in members]
    trigs[mine] = trig[...]
    trig_copies = [edges.copy(trig, trigs.at[mine], me.at(dy=k)) for k in (1, 2, 3)]
    trig_over = [edges.copy(trig, trigs.at[mine], core)]
    ring = RingGather(me, edges, low, xs)
    for i in range(8):
        dy, other = i // 2, i % 2
        y = lax.rem(me.y + dy, 4)
        to_core = me.c if other == 0 else 1 - me.c
        stays = own_column if i == 0 else me.c < 0
        cols = pl.ds(pl.multiple_of(Q_DEV * (2 * y + to_core), Q_DEV), Q_DEV)
        src = wout.at[spread_rows, cols]
        dst = wo.at[own, spread_rows]
        target = (me.z, to_xl, to_core, y, to_xh)
        send_block(me, src, dst, os_.at[i], orr.at[own], target, stays)
        blocks.append((src, os_.at[i], stays))
    moved = me.c != me.xh
    swaps = swap_copies(me, wgu, wdn, wswap, ws, wr)

    @pl.when(moved)
    def _():
        for d in swaps:
            d.start()

    for i in range(5):
        wait_got(wq.at[pl.ds(64 * i, 64), spread], qr.at[i])
    wq_copies = [
        edges.copy(wq.at[:, spread], wq.at[:, spread], me.at(dz=k)) for k in (1, 3, 2)
    ]
    for k, d in zip((1, 2, 3), trig_copies):
        d.wait_recv()
        ref = trigs.at[2 * lax.rem(me.y - k + 4, 4) + me.c]
        trig_over.append(edges.copy(ref, ref, core))
    ring.relay()
    for i in range(8):
        wait_got(wo.at[i, spread_rows], orr.at[i])
    ref = wo.at[:, spread_rows]
    wo_copies = [edges.copy(ref, ref, me.at(dz=k)) for k in (1, 3, 2)]
    keep_pos.wait()
    for d in pos_copies + trig_over:
        d.wait_recv()
    keep.wait()
    for d in wq_copies:
        d.wait_recv()
    wq_save = pltpu.make_async_copy(wq, wq_out, local.at[2])
    wq_save.start()
    is_key = me.c == 0

    def compute(pair):
        at = pl.ds(2 * pair, 2)
        projected = dot_last(xs[at].reshape(2 * TOK, D), wq[...])
        for r in range(4):
            half, u = r // 2, r % 2
            rows = rotary_of(trigs[2 * pair + half], u)
            values = projected[64 * r : 64 * r + 64]
            heads = [rotate(values[:, HD * h : HD * h + HD], rows) for h in range(4)]
            query = jnp.concatenate(heads, axis=1).astype(BF16)
            to = pl.ds(pl.multiple_of(2 * TOK * pair + 64 * r, 64), 64)
            q[to, :] = (query.astype(F32) * 0.125).astype(BF16)
            rows = jnp.concatenate(
                [
                    jnp.where(is_key, rows[:, :HD], 1.0),
                    jnp.where(is_key, rows[:, HD:], 0.0),
                ],
                axis=1,
            )
            to = pl.ds(pl.multiple_of(TOK * pair + 64 * u, 64), 64)
            lanes = slice(HD * half, HD * half + HD)
            kv[to, lanes] = rotate(values[:, Q_DEV:], rows).astype(BF16)
            kv_table[0, to, lanes] = rows[:, :HD]
            kv_table[1, to, lanes] = rows[:, HD:]

    def pair(k):
        return lax.rem(me.y + k, 4)

    ring.from_core(0, 1)
    compute(pair(0))
    ring.near()
    ring.from_core(1, 5)

    def sides(i, _):
        compute(pair(1 + 2 * i))
        return 0

    lax.fori_loop(0, 2, sides, 0)
    ring.far()
    ring.from_core(5, 7)
    compute(pair(2))

    keeps = [
        pltpu.make_async_copy(kv, kvs.at[me.c, chip], local.at[0]),
        pltpu.make_async_copy(poss, places.at[chip], local.at[1]),
        pltpu.make_async_copy(xs, xs_out, local.at[4]),
        pltpu.make_async_copy(cot, cots.at[mine], local.at[5]),
    ]
    for d in keeps:
        d.start()
    pos_copies = [edges.copy(poss, places.at[chip], d) for d in far]
    kv_copies = [edges.copy(kv, kvs.at[me.c, chip], d) for d in far]
    over = [edges.copy(kv, kvs.at[me.c, chip], core)]
    ring = RingGather(me, edges, cot, cots)
    ring.relay()
    for (dz, dl), d in zip(chips_in_sequence(me), kv_copies):
        d.wait_recv()
        source = 2 * lax.rem(me.z - dz + 4, 4) + ((1 - me.xl) if dl else me.xl)
        ref = kvs.at[me.c, source]
        over.append(edges.copy(ref, ref, core))
    ring.rest()
    for d in over + pos_copies + wo_copies:
        d.wait_recv()
    for src, sem, stays in blocks:
        wait_sent(src, sem, stays)

    @pl.when(moved)
    def _():
        for d in swaps:
            d.wait()

    edges.finish()
    for d in keeps + [wq_save]:
        d.wait()


def begin(tokens, gain, pos, trig, wqkv, wgu, wdn, cot, wout):
    return pl.pallas_call(
        begin_kernel,
        out_shape=(
            shape((1024, Q_DEV)),
            shape((2, 512, 128), F32),
            shape((8, 64, 128), F32),
            shape((8, TOK, D)),
            shape((320, D)),
            shape((8, 8, TOK), jnp.int32),
            shape((2, 8, 512, 128)),
            shape((8, 8, 8, TOK), jnp.int32),
            shape((8, TOK, D)),
            shape((8, 256, Q_DEV)),
            shape((QUARTER, D)),
        ),
        in_specs=[VMEM, VMEM, VMEM, VMEM] + [ANY] * 5,
        out_specs=(VMEM, VMEM, VMEM) + (ANY,) * 8,
        scratch_shapes=[
            pltpu.VMEM((TOK, D), BF16),
            pltpu.VMEM((8, TOK, D), BF16),
            pltpu.VMEM((320, D), BF16),
            pltpu.VMEM((512, 128), BF16),
        ]
        + sems(7 + 7 + 6 + 2 * GATHER_EDGES + 7 + 7 + 8)
        + sems(5)
        + sems(8)
        + sems(2)
        + [pltpu.SemaphoreType.DMA((6,))],
        compiler_params=remote_params(0),
        name="begin",
    )(tokens, gain, pos, trig, wqkv, wgu, wdn, cot, wout)


def split_heads(rows):
    return jnp.concatenate([rows[:, HD * h : HD * (h + 1)] for h in range(4)], axis=0)


def join_heads(rows):
    return jnp.concatenate([rows[64 * h : 64 * (h + 1), :] for h in range(4)], axis=1)


def dot_last(a, b):
    return lax.dot_general(a, b, (((1,), (1,)), ((), ())), preferred_element_type=F32)


def dot_first(a, b):
    return lax.dot_general(a, b, (((0,), (0,)), ((), ())), preferred_element_type=F32)


def dot(a, b):
    return lax.dot_general(a, b, (((1,), (0,)), ((), ())), preferred_element_type=F32)


TILE = 256
WIDE = 4


def sort_keys(runs, seq, kv_ref, keys, values):
    for j in range(32):
        chip, core, u = j // 4, (j // 2) % 2, j % 2
        to = pl.ds(pl.multiple_of(runs[seq * 32 + j] * 64, 64), 64)
        rows, lanes = slice(64 * u, 64 * u + 64), slice(HD * core, HD * core + HD)
        keys[to, :] = kv_ref[0, chip, rows, lanes]
        values[to, :] = kv_ref[1, chip, rows, lanes]


def turn(rows, turned):
    for i in range(4):
        at = slice(512 * i, 512 * (i + 1))
        turned[:, at] = rows[at, :].astype(F32).T.astype(BF16)


def allowed_tile(tile, run):
    key = lax.broadcasted_iota(jnp.int32, (TILE, 256), 0) + tile * TILE
    query = lax.rem(lax.broadcasted_iota(jnp.int32, (TILE, 256), 1), 64) + run * 64
    return key <= query


def tile_rows(tile):
    return pl.ds(pl.multiple_of(tile * TILE, TILE), TILE)


def attend_kernel(
    key_runs, query_runs, q_ref, kv_ref, att_ref, ot_ref, lse_ref,
    keys, values, values_t, high_ref, total_ref, acc_ref,
):
    seq = pl.program_id(0)
    sort_keys(key_runs, seq, kv_ref, keys, values)
    turn(values, values_t)

    def one_run(r, _):
        run = query_runs[seq * 4 + r]
        rows = pl.ds(pl.multiple_of(r * 64, 64), 64)
        query = split_heads(q_ref[rows, :]).astype(F32).T.astype(BF16)
        last = run // 4
        high_ref[...] = jnp.full((1, 256), FILLER, F32)
        total_ref[...] = jnp.zeros((1, 256), F32)
        acc_ref[...] = jnp.zeros((HD, 256), F32)

        def tiles(first, count, masked):
            scores = []
            for k in range(count):
                score = dot(keys[tile_rows(first + k), :], query)
                if masked and k == count - 1:
                    score = jnp.where(allowed_tile(first + k, run), score, FILLER)
                scores.append(score)
            high = high_ref[...]
            new_high = high
            for score in scores:
                new_high = jnp.maximum(new_high, jnp.max(score, axis=0, keepdims=True))
            scale = jnp.exp(high - new_high)
            total = total_ref[...] * scale
            acc = acc_ref[...] * scale
            for k, score in enumerate(scores):
                weights = jnp.exp(score - new_high)
                total = total + jnp.sum(weights, axis=0, keepdims=True)
                acc = acc + dot(values_t[:, tile_rows(first + k)], weights.astype(BF16))
            high_ref[...] = new_high
            total_ref[...] = total
            acc_ref[...] = acc

        @pl.when(last >= WIDE)
        def _():
            tiles(0, WIDE, False)

        start = (last // WIDE) * WIDE
        for n in range(WIDE):

            @pl.when(last - start == n)
            def _():
                tiles(start, n + 1, True)

        total = total_ref[...]
        out = acc_ref[...] / total
        ot_ref[r] = out
        lse_ref[r] = high_ref[...] + jnp.log(total)
        att_ref[rows, :] = join_heads(out.T).astype(BF16)
        return 0

    lax.fori_loop(0, 4, one_run, 0)


def attend(key_runs, query_runs, q, kv):
    return pl.pallas_call(
        attend_kernel,
        out_shape=(shape((1024, 256)), shape((16, HD, 256), F32), shape((16, 1, 256), F32)),
        grid_spec=pltpu.PrefetchScalarGridSpec(
            num_scalar_prefetch=2,
            grid=(4,),
            in_specs=[
                pl.BlockSpec((256, 256), lambda i, *_: (i, 0)),
                pl.BlockSpec((2, 8, 128, 128), lambda i, *_: (0, 0, i, 0)),
            ],
            out_specs=[
                pl.BlockSpec((256, 256), lambda i, *_: (i, 0)),
                pl.BlockSpec((4, HD, 256), lambda i, *_: (i, 0, 0)),
                pl.BlockSpec((4, 1, 256), lambda i, *_: (i, 0, 0)),
            ],
            scratch_shapes=[
                pltpu.VMEM((2048, HD), BF16),
                pltpu.VMEM((2048, HD), BF16),
                pltpu.VMEM((HD, 2048), BF16),
                pltpu.VMEM((1, 256), F32),
                pltpu.VMEM((1, 256), F32),
                pltpu.VMEM((HD, 256), F32),
            ],
        ),
        compiler_params=pltpu.CompilerParams(vmem_limit_bytes=40 * 2**20),
        name="attend",
    )(key_runs, query_runs, q, kv)


def attend_back_kernel(
    key_runs, query_runs, q_ref, kv_ref, da_ref, ot_ref, lse_ref, trig_ref,
    dq_ref, dkv_ref, keys, values, keys_t, dkeys, dvalues, dq_acc,
):
    seq = pl.program_id(0)
    sort_keys(key_runs, seq, kv_ref, keys, values)
    turn(keys, keys_t)
    dkeys[...] = jnp.zeros_like(dkeys)
    dvalues[...] = jnp.zeros_like(dvalues)

    def one_run(r, _):
        run = query_runs[seq * 4 + r]
        rows = pl.ds(pl.multiple_of(r * 64, 64), 64)
        query = split_heads(q_ref[rows, :])
        grad = split_heads(da_ref[rows, :])
        lse = lse_ref[r]
        query_t = query.astype(F32).T.astype(BF16)
        grad_t = grad.astype(F32).T
        delta = jnp.sum(grad_t * ot_ref[r], axis=0, keepdims=True)
        grad_t = grad_t.astype(BF16)
        last = run // 4
        dq_acc[...] = jnp.zeros((HD, 256), F32)

        def tiles(first, count, masked):
            dq = dq_acc[...]
            for k in range(count):
                at = tile_rows(first + k)
                key = keys[at, :]
                probs = jnp.exp(dot(key, query_t) - lse)
                if masked and k == count - 1:
                    probs = jnp.where(allowed_tile(first + k, run), probs, 0.0)
                grad_probs = dot(values[at, :], grad_t)
                grad_scores = (probs * (grad_probs - delta)).astype(BF16)
                dvalues[at, :] += dot(probs.astype(BF16), grad)
                dkeys[at, :] += dot(grad_scores, query)
                dq = dq + dot(keys_t[:, at], grad_scores)
            dq_acc[...] = dq

        @pl.when(last >= WIDE)
        def _():
            tiles(0, WIDE, False)

        start = (last // WIDE) * WIDE
        for n in range(WIDE):

            @pl.when(last - start == n)
            def _():
                tiles(start, n + 1, True)

        pair_rows = trig_ref[r // 2]
        table = jnp.where(
            lax.rem(r, 2) == 0, rotary_of(pair_rows, 0), rotary_of(pair_rows, 1)
        )
        dq = (dq_acc[...] * 0.125).T
        heads = [rotate(dq[64 * h : 64 * h + 64], table, back=True) for h in range(4)]
        dq_ref[rows, :] = jnp.concatenate(heads, axis=1).astype(BF16)
        return 0

    lax.fori_loop(0, 4, one_run, 0)
    for j in range(32):
        chip, core, u = j // 4, (j // 2) % 2, j % 2
        at = pl.ds(pl.multiple_of(key_runs[seq * 32 + j] * 64, 64), 64)
        rows, lanes = slice(64 * u, 64 * u + 64), slice(HD * core, HD * core + HD)
        dkv_ref[0, chip, rows, lanes] = dkeys[at, :].astype(BF16)
        dkv_ref[1, chip, rows, lanes] = dvalues[at, :].astype(BF16)


def attend_back(key_runs, query_runs, q, kv, grad, ot, lse, trigs):
    return pl.pallas_call(
        attend_back_kernel,
        out_shape=(shape((1024, 256)), shape((2, 8, 512, 128))),
        grid_spec=pltpu.PrefetchScalarGridSpec(
            num_scalar_prefetch=2,
            grid=(4,),
            in_specs=[
                pl.BlockSpec((256, 256), lambda i, *_: (i, 0)),
                pl.BlockSpec((2, 8, 128, 128), lambda i, *_: (0, 0, i, 0)),
                pl.BlockSpec((256, 256), lambda i, *_: (i, 0)),
                pl.BlockSpec((4, HD, 256), lambda i, *_: (i, 0, 0)),
                pl.BlockSpec((4, 1, 256), lambda i, *_: (i, 0, 0)),
                pl.BlockSpec((2, 64, 128), lambda i, *_: (i, 0, 0)),
            ],
            out_specs=[
                pl.BlockSpec((256, 256), lambda i, *_: (i, 0)),
                pl.BlockSpec((2, 8, 128, 128), lambda i, *_: (0, 0, i, 0)),
            ],
            scratch_shapes=[
                pltpu.VMEM((2048, HD), BF16),
                pltpu.VMEM((2048, HD), BF16),
                pltpu.VMEM((HD, 2048), BF16),
                pltpu.VMEM((2048, HD), F32),
                pltpu.VMEM((2048, HD), F32),
                pltpu.VMEM((HD, 256), F32),
            ],
        ),
        compiler_params=pltpu.CompilerParams(vmem_limit_bytes=40 * 2**20),
        name="attend_back",
    )(key_runs, query_runs, q, kv, grad, ot, lse, trigs)


PART = 3 * FF_DEV // 2
PART_HALF = PART // 2


class RingSum:
    def __init__(self, me, edges, along_z, src, start, rows, width, step, relayed, last):
        self.edges, self.src, self.start, self.width, self.step = edges, src, start, width, step
        self.rows, self.half = rows, rows // 2
        self.relayed, self.last = relayed, last
        self.here = me.z if along_z else x_of(me)
        self.up = around(me, 1, 0) if along_z else around(me, 0, 1)
        self.down = around(me, -1, 0) if along_z else around(me, 0, 3)
        self.a, self.b = pl.ds(0, self.half), pl.ds(self.half, self.half)

    def columns(self, k):
        at = self.width * lax.rem(self.here + k, 4)
        return pl.ds(pl.multiple_of(at, self.width), self.width)

    def piece(self, k, half):
        rows = pl.ds(self.start + self.half * half, self.half)
        return self.src.at[rows, self.columns(k)]

    def far(self):
        self.r_a = self.edges.copy(self.piece(2, 0), self.relayed.at[0], self.up)
        self.r_b = self.edges.copy(self.piece(2, 1), self.relayed.at[1], self.down)

    def near_up(self):
        self.u_b = self.edges.copy(self.piece(1, 1), self.last.at[0, self.b], self.up)

    def near_down(self):
        self.d_a = self.edges.copy(self.piece(3, 0), self.last.at[1, self.a], self.down)

    def add(self, k, half):
        step, start, cols = self.step, self.start + self.half * half, self.columns(k)

        def one(i, _):
            at = pl.ds(pl.multiple_of(start + i * step, 16), step)
            from_ = pl.ds(pl.multiple_of(i * step, 16), step)
            self.src[at, cols] = (
                self.src[at, cols].astype(F32) + self.relayed[half, from_, :].astype(F32)
            ).astype(BF16)
            return 0

        lax.fori_loop(0, self.half // step, one, 0)

    def second(self):
        self.r_a.wait_recv()
        self.add(1, 0)
        self.u_a = self.edges.copy(self.piece(1, 0), self.last.at[0, self.a], self.up)
        self.r_b.wait_recv()
        self.add(3, 1)
        self.d_b = self.edges.copy(self.piece(3, 1), self.last.at[1, self.b], self.down)

    def total(self, out):
        for d in (self.u_b, self.d_a, self.u_a, self.d_b):
            d.wait_recv()
        step, cols = self.step, self.columns(0)

        def one(i, _):
            at = pl.ds(pl.multiple_of(self.start + i * step, 16), step)
            from_ = pl.ds(pl.multiple_of(i * step, 16), step)
            out[from_, :] = (
                self.src[at, cols].astype(F32)
                + self.last[0, from_, :].astype(F32)
                + self.last[1, from_, :].astype(F32)
            ).astype(BF16)
            return 0

        lax.fori_loop(0, self.rows // step, one, 0)


SUM_EDGES = 6


def feed_forward_kernel(
    parts, tokens, gain, cots, wgu, wdn, wswap, wnear_up, wnear_down,
    middle, grad_middle, gain_grad, gbs, z_out, x_out, branch,
    xs, p, c, gp, w, act_t, gate_t, up_t, act, dgate, dup, low,
    g1, b1, r1, l1,
    z_relayed, z_last, x_relayed, x_last, z_q, x_q,
    z_relayed2, z_last2, x_relayed2, x_last2,
    send, recv, fs, fr, local,
):
    me = Place()
    core = me.at(core=1 - me.c)
    signalled = greet(
        [core, me.at(dy=1), me.at(dy=-1)]
        + [around(me, k, 0) for k in (1, 2, 3)]
        + [around(me, 0, 1), around(me, 0, 3)]
    )
    edges = Edges(send, recv)
    mine = 2 * me.y + me.c
    moved = me.c != me.xh
    load_p = pltpu.make_async_copy(parts, p, local.at[0])
    load_c = pltpu.make_async_copy(cots, c, local.at[1])
    load_p.start()
    load_c.start()

    def w_rows(dz):
        z = lax.rem(me.z + dz + 4, 4)
        return (
            pl.ds(pl.multiple_of(GU_QUARTER * z, 16), GU_QUARTER),
            pl.ds(pl.multiple_of(2 * FF_DEV + DN_QUARTER * z, 16), DN_QUARTER),
        )

    gu_part, dn_part = pl.ds(0, GU_QUARTER), pl.ds(GU_QUARTER, DN_QUARTER)
    kept = [
        pltpu.make_async_copy(wgu, w.at[pl.ds(0, 2 * FF_DEV)], local.at[2]),
        pltpu.make_async_copy(wdn, w.at[pl.ds(2 * FF_DEV, FF_DEV)], local.at[3]),
    ]
    near_w = []
    for i, (src, dz) in enumerate(((wswap, 0), (wnear_up, -1), (wnear_down, 1))):
        gu_rows, dn_rows = w_rows(dz)
        near_w.append(pltpu.make_async_copy(src.at[gu_part], w.at[gu_rows], local.at[4 + 2 * i]))
        near_w.append(pltpu.make_async_copy(src.at[dn_part], w.at[dn_rows], local.at[5 + 2 * i]))
    far_w = [
        pltpu.make_async_remote_copy(
            src_ref=wswap.at[part],
            dst_ref=w.at[rows],
            send_sem=fs.at[i],
            recv_sem=fr.at[i],
            device_id=me.at(dz=2),
            device_id_type=pl.DeviceIdType.MESH,
        )
        for i, (part, rows) in enumerate(zip((gu_part, dn_part), w_rows(0)))
    ]

    met(signalled)

    @pl.when(moved)
    def _():
        for d in far_w + near_w:
            d.start()

    @pl.when(jnp.logical_not(moved))
    def _():
        for d in kept:
            d.start()

    load_p.wait()
    ring = RingScatter(me, edges, p, (g1, b1, r1, l1))
    ring.first()
    ring.second()
    ring.arrived()

    def norm(at):
        rows = tokens[at, :].astype(F32) + ring.rows(at)
        middle[at, :] = rows
        normal = rows * lax.rsqrt(mean_last(rows * rows) + EPSILON)
        low[at, :] = (normal * gain[...]).astype(BF16)

    in_chunks(norm)
    keep = pltpu.make_async_copy(low, xs.at[mine], local.at[10])
    keep.start()
    gather = RingGather(me, edges, low, xs)
    ring.release()

    @pl.when(moved)
    def _():
        for d in near_w:
            d.wait()
        for d in far_w:
            d.wait()

    @pl.when(jnp.logical_not(moved))
    def _():
        for d in kept:
            d.wait()

    load_c.wait()
    keep.wait()

    def compute(pair):
        at = pl.ds(2 * pair, 2)
        x = xs[at].reshape(2 * TOK, D)
        g = c[at].reshape(2 * TOK, D)
        here = pl.ds(pl.multiple_of(2 * TOK * pair, 2 * TOK), 2 * TOK)
        for n0, n1 in ((0, 256), (256, 512), (512, FF_DEV)):
            gate = dot_last(x, w[n0:n1, :])
            upward = dot_last(x, w[FF_DEV + n0 : FF_DEV + n1, :])
            grad = dot_last(g, w[2 * FF_DEV + n0 : 2 * FF_DEV + n1, :])
            sigmoid = 1.0 / (1.0 + jnp.exp(-gate))
            swish = gate * sigmoid
            active = swish * upward
            grad_up = grad * swish
            grad_gate = grad * upward * sigmoid * (1.0 + gate * (1.0 - sigmoid))
            act[:, n0:n1] = active.astype(BF16)
            dup[:, n0:n1] = grad_up.astype(BF16)
            dgate[:, n0:n1] = grad_gate.astype(BF16)
            act_t[n0:n1, here] = active.T.astype(BF16)
            up_t[n0:n1, here] = grad_up.T.astype(BF16)
            gate_t[n0:n1, here] = grad_gate.T.astype(BF16)

        def block(i, _):
            cols = pl.ds(pl.multiple_of(512 * i, 512), 512)
            term = dot(act[...], w[2 * FF_DEV :, cols])
            p[at, :, cols] = term.astype(BF16).reshape(2, TOK, 512)
            grads = dot(dgate[...], w[:FF_DEV, cols]) + dot(dup[...], w[FF_DEV : 2 * FF_DEV, cols])
            gp[at, :, cols] = grads.astype(BF16).reshape(2, TOK, 512)
            return 0

        lax.fori_loop(0, 4, block, 0)

    def pair(k):
        return lax.rem(me.y + k, 4)

    two = RingScatter(me, edges, gp, (g1, b1, r1, l1))
    gather.from_core(0, 1)
    compute(pair(0))
    two.send_core(0)
    gather.relay()
    gather.near()
    gather.from_core(1, 5)

    def sides(i, _):
        compute(pair(1 + 2 * i))
        return 0

    lax.fori_loop(0, 2, sides, 0)
    two.send_core(1)
    two.send_core(3)
    gather.far()
    two.near()
    gather.from_core(5, 7)
    compute(pair(2))
    two.send_core(2)
    save = pltpu.make_async_copy(p, branch, local.at[0])
    save.start()
    two.add_core(0)

    z_sum = RingSum(me, edges, True, w, 0, PART, 512, 48, z_relayed, z_last)
    x_sum = RingSum(me, edges, False, w, PART, PART, 512, 48, x_relayed, x_last)
    split = PART - FF_DEV

    def z_task(k):
        cols = z_sum.columns(k)
        x = xs[:, :, cols].reshape(8 * TOK, 512)
        w[:FF_DEV, cols] = dot(gate_t[...], x).astype(BF16)
        w[FF_DEV:PART, cols] = dot(up_t[:split, :], x).astype(BF16)

    def x_task(k):
        cols = x_sum.columns(k)
        x = xs[:, :, cols].reshape(8 * TOK, 512)
        g = c[:, :, cols].reshape(8 * TOK, 512)
        w[PART : 2 * FF_DEV, cols] = dot(up_t[split:, :], x).astype(BF16)
        w[2 * FF_DEV :, cols] = dot(act_t[...], g).astype(BF16)

    two.far()
    z_task(2)
    z_sum.far()
    x_task(2)
    x_sum.far()
    z_task(1)
    z_sum.near_up()
    x_task(1)
    x_sum.near_up()
    two.second()
    z_task(3)
    z_sum.near_down()
    x_task(3)
    x_sum.near_down()
    z_task(0)
    x_task(0)
    two.arrived()
    gain_grad[...] = jnp.zeros_like(gain_grad)

    def back(at):
        rows = middle[at, :]
        inverse = lax.rsqrt(mean_last(rows * rows) + EPSILON)
        normal = rows * inverse
        grad = two.rows(at)
        gain_grad[...] += jnp.sum(normal * grad, axis=0, keepdims=True)
        scaled = grad * gain[...]
        result = c[mine, at].astype(F32) + inverse * (
            scaled - normal * mean_last(scaled * normal)
        )
        grad_middle[at, :] = result
        low[at, :] = result.astype(BF16)

    edges.sent([gather.up_a, gather.up_b, gather.down_a, gather.down_b, gather.to_core[0]])
    in_chunks(back)
    keep = pltpu.make_async_copy(low, gbs.at[mine], local.at[10])
    keep.start()
    gather = RingGather(me, edges, low, gbs)
    z_sum.second()
    x_sum.second()
    gather.relay()
    z_sum.total(z_q)
    z_two = RingSum(me, edges, False, z_q, 0, PART, 128, 176, z_relayed2, z_last2)
    z_two.far()
    z_two.near_up()
    z_two.near_down()
    x_sum.total(x_q)
    x_two = RingSum(me, edges, True, x_q, 0, PART, 128, 176, x_relayed2, x_last2)
    x_two.far()
    x_two.near_up()
    x_two.near_down()
    gather.near()
    gather.far()
    z_two.second()
    x_two.second()
    gather.from_core(0, 7)
    z_two.total(z_out)
    x_two.total(x_out)
    edges.finish()
    keep.wait()
    save.wait()


def feed_forward(parts, tokens, gain, cots, wgu, wdn, wswap, wnear_up, wnear_down):
    block = pltpu.VMEM((8, TOK, D), BF16)
    turned = pltpu.VMEM((FF_DEV, 8 * TOK), BF16)
    pair = pltpu.VMEM((2 * TOK, FF_DEV), BF16)

    def ring(width):
        return [
            pltpu.VMEM((2, PART_HALF, width), BF16),
            pltpu.VMEM((2, PART, width), BF16),
        ] * 2

    return pl.pallas_call(
        feed_forward_kernel,
        out_shape=(
            shape((TOK, D), F32),
            shape((TOK, D), F32),
            shape((1, D), F32),
            shape((8, TOK, D)),
            shape((PART, 128)),
            shape((PART, 128)),
            shape((8, TOK, D)),
        ),
        in_specs=[ANY, VMEM, VMEM] + [ANY] * 6,
        out_specs=(VMEM, VMEM, VMEM, ANY, VMEM, VMEM, ANY),
        scratch_shapes=[block] * 4
        + [pltpu.VMEM((3 * FF_DEV, D), BF16)]
        + [turned] * 3
        + [pair] * 3
        + [pltpu.VMEM((TOK, D), BF16)]
        + scatter_scratch()
        + ring(512)
        + [pltpu.VMEM((PART, 512), BF16)] * 2
        + ring(128)
        + sems(2 * SCATTER_EDGES + 2 * GATHER_EDGES + 4 * SUM_EDGES)
        + sems(2)
        + [pltpu.SemaphoreType.DMA((11,))],
        compiler_params=pltpu.CompilerParams(
            collective_id=2, has_side_effects=True, vmem_limit_bytes=62 * 2**20
        ),
        name="feed_forward",
    )(parts, tokens, gain, cots, wgu, wdn, wswap, wnear_up, wnear_down)


def columns(width):
    return lambda i: (slice(None), pl.ds(pl.multiple_of(i * width, width), width))


def row_block(height, start=0):
    return lambda i: (pl.ds(pl.multiple_of(start + i * height, height), height), slice(None))


def plane_devices(me):
    found = [me.at(core=1 - me.c)]
    for dz, dx in STEPS:
        z, xl, core, y, xh = around(me, dz, dx)
        found += [(z, xl, core, y, xh), (z, xl, 1 - core, y, xh)]
    return found


def swapped_pairs(rows):
    return jnp.concatenate([halves_swapped(rows[:, :HD]), halves_swapped(rows[:, HD:])], axis=1)


class RingBlocks:
    def __init__(self, me, edges, ref, columns):
        self.me, self.edges, self.ref, self.columns = me, edges, ref, columns
        rows = ref.shape[0]
        self.halves = (pl.ds(0, rows // 2), pl.ds(rows // 2, rows // 2))
        self.up, self.down = me.at(dz=1), me.at(dz=-1)
        self.up_a = self.send(0, 0, self.up)
        self.down_b = self.send(0, 1, self.down)
        self.up_b = self.send(0, 1, self.up)
        self.down_a = self.send(0, 0, self.down)

    def block(self, dz):
        return self.ref.at[:, self.columns(lax.rem(self.me.z + dz + 4, 4))]

    def send(self, dz, half, device):
        cols = self.columns(lax.rem(self.me.z + dz + 4, 4))
        ref = self.ref.at[self.halves[half], cols]
        return self.edges.copy(ref, ref, device)

    def relay(self):
        self.up_a.wait_recv()
        self.on_a = self.send(-1, 0, self.up)
        self.down_b.wait_recv()
        self.on_b = self.send(1, 1, self.down)

    def near(self):
        self.up_b.wait_recv()
        self.down_a.wait_recv()

    def far(self):
        self.on_a.wait_recv()
        self.on_b.wait_recv()


class PlaneGather:
    def __init__(self, me, edges, z_piece, x_piece, z_all, x_all, send, recv):
        self.me, self.edges, self.z_all, self.x_all = me, edges, z_all, x_all
        self.send, self.recv, self.z_piece, self.x_piece = send, recv, z_piece, x_piece
        self.stays = me.c == me.xh
        self.core = me.at(core=1 - me.c)
        self.side = me.at(xl=1 - me.xl)
        across = me.at(core=1 - me.c, xl=1 - me.xl, xh=1 - me.xh)
        x = x_of(me)
        self.held = jnp.where(self.stays, x, 3 - x)
        for i, (piece, ref, at) in enumerate(
            ((z_piece, z_all, 4 * me.z + x), (x_piece, x_all, 4 * x + me.z))
        ):
            dst = ref.at[columns(128)(at)]
            send_block(me, piece, dst, send.at[i], recv.at[i], across, self.stays)

    def z_columns(self, z):
        return pl.ds(pl.multiple_of(512 * z + 256 * self.me.c, 256), 256)

    def x_columns(self, z):
        return pl.ds(pl.multiple_of(512 * self.held + 128 * z, 128), 128)

    def sideways(self):
        own = self.z_all.at[columns(128)(4 * self.me.z + self.held)]
        wait_got(own, self.recv.at[0])
        self.z_side = self.edges.copy(own, own, self.side)
        own = self.x_all.at[:, self.x_columns(self.me.z)]
        wait_got(own, self.recv.at[1])
        self.x_ring = RingBlocks(self.me, self.edges, self.x_all, self.x_columns)
        self.x_side = [self.edges.copy(own, own, self.side)]

    def along(self):
        self.z_side.wait_recv()
        self.z_ring = RingBlocks(self.me, self.edges, self.z_all, self.z_columns)
        own = self.z_ring.block(0)
        self.over = [self.edges.copy(own, own, self.core)]
        self.x_ring.relay()

    def to_side(self, dz):
        ref = self.x_ring.block(dz)
        self.x_side.append(self.edges.copy(ref, ref, self.side))

    def to_core(self, dz):
        ref = self.z_ring.block(dz)
        self.over.append(self.edges.copy(ref, ref, self.core))

    def near(self):
        self.x_ring.near()
        self.to_side(1)
        self.to_side(-1)
        self.z_ring.relay()
        self.x_ring.far()
        self.to_side(2)

    def far(self):
        self.z_ring.near()
        self.to_core(1)
        self.to_core(-1)
        self.z_ring.far()
        self.to_core(2)
        for d in self.x_side:
            d.wait_recv()
        half = self.x_all.at[:, pl.ds(pl.multiple_of(1024 * self.me.c, 1024), 1024)]
        self.over.append(self.edges.copy(half, half, self.core))

    def finish(self):
        for d in self.over:
            d.wait_recv()
        wait_sent(self.z_piece, self.send.at[0], self.stays)
        wait_sent(self.x_piece, self.send.at[1], self.stays)


PLANE_EDGES = 1 + 2 * SUM_EDGES + 4 + 5


class TwoSums:
    def __init__(self, me, edges, src, rows, steps, scratch):
        self.me, self.edges, self.rows, self.steps = me, edges, rows, steps
        self.q, self.out = scratch[4:6], scratch[10:12]
        self.scratch = scratch
        start = (0, rows[0])
        self.one = [
            RingSum(
                me, edges, i == 0, src, start[i], rows[i], 512, steps[0][i],
                scratch[2 * i], scratch[2 * i + 1],
            )
            for i in (0, 1)
        ]
        for ring in self.one:
            ring.far()
            ring.near_up()
            ring.near_down()

    def second(self):
        for ring in self.one:
            ring.second()

    def cross(self):
        self.two = []
        for i in (0, 1):
            self.one[i].total(self.q[i])
            ring = RingSum(
                self.me, self.edges, i == 1, self.q[i], 0, self.rows[i], 128,
                self.steps[1][i], self.scratch[6 + 2 * i], self.scratch[7 + 2 * i],
            )
            ring.far()
            ring.near_up()
            ring.near_down()
            self.two.append(ring)

    def fourth(self):
        for ring in self.two:
            ring.second()

    def total(self):
        for i in (0, 1):
            self.two[i].total(self.out[i])


def two_sums_scratch(rows):
    found = []
    for r in rows:
        found += [pltpu.VMEM((2, r // 2, 512), BF16), pltpu.VMEM((2, r, 512), BF16)]
    found += [pltpu.VMEM((r, 512), BF16) for r in rows]
    for r in rows:
        found += [pltpu.VMEM((2, r // 2, 128), BF16), pltpu.VMEM((2, r, 128), BF16)]
    return found + [pltpu.VMEM((r, 128), BF16) for r in rows]


EARLY_ROWS = (256, 256)


def ending_kernel(
    dkv, dq, kv_table, wq, tokens, gain, grad_middle, gain_two, z_piece, x_piece, middle,
    gwo, xs_in, branch_in,
    output, grad_tokens, gains, wq_out, wo_out, z_all, x_all,
    kv_got, kv_both, kv_last, dkv_low, xs, grads, grads_t, parts, branch_parts, early, late,
    g1, b1, r1, l1, g2, b2, r2, l2,
    wq_all, wo_all, late_own, late_got, late_piece, mine, near, near_sum, owners,
    *rest,
):
    early_scratch = rest[:12]
    (send, recv, ds, dr, es, er, ps, pr, gs, gr, hs, hr, us, ur, local) = rest[12:]
    me = Place()
    core = me.at(core=1 - me.c)
    far = [
        me.at(dz=dz, xl=(1 - me.xl) if dl else me.xl) for dz, dl in chips_in_sequence(me)
    ]
    signalled = greet(plane_devices(me) + group_members(me)[1:])
    edges = Edges(send, recv)
    place = 4 * me.z + x_of(me)
    turned = 4 * x_of(me) + me.z
    rank = 2 * me.y + me.c
    load_x = pltpu.make_async_copy(xs_in, xs, local.at[0])
    load_branch = pltpu.make_async_copy(branch_in, branch_parts, local.at[1])
    load_wo = [
        pltpu.make_async_copy(
            gwo.at[pl.ds(128 * i, 128)], early.at[pl.ds(256 * i + 128, 128)], local.at[2 + i]
        )
        for i in (0, 1)
    ]
    for d in [load_x, load_branch] + load_wo:
        d.start()

    def query_part(i, _):
        at = pl.ds(pl.multiple_of(2 * TOK * i, 2 * TOK), 2 * TOK)
        rows = dq[at, :]
        grads[at, :Q_DEV] = rows
        grads_t[:Q_DEV, at] = rows.astype(F32).T.astype(BF16)
        return 0

    lax.fori_loop(0, 4, query_part, 0)
    met(signalled)

    order = []
    for dz, dl in chips_in_sequence(me) + [(0, 0)]:
        chip = 2 * lax.rem(me.z + dz, 4) + ((1 - me.xl) if dl else me.xl)
        order.append((chip, edges.copy(dkv.at[1 - me.c, chip], kv_got.at[chip], core)))
    load_branch.wait()
    branch = RingScatter(me, edges, branch_parts, (g2, b2, r2, l2))
    for k in (2, 1, 3, 0):
        branch.send_core(k)
    plane = PlaneGather(me, edges, z_piece, x_piece, z_all, x_all, ps, pr)
    far_copies = []
    for i, (chip, d) in enumerate(order):
        d.wait_recv()
        kv_both[chip] = (dkv[me.c, chip].astype(F32) + kv_got[chip].astype(F32)).astype(BF16)
        if i < 7:
            far_copies.append(edges.copy(kv_both.at[chip], kv_last.at[i], far[i]))
    branch.far()
    branch.near()
    load_x.wait()

    def weight_block(i, _):
        cols = pl.ds(pl.multiple_of(512 * i, 512), 512)
        rows = xs[:, :, cols].reshape(8 * TOK, 512)
        early[:128, cols] = dot(grads_t[:128, :], rows).astype(BF16)
        early[256:384, cols] = dot(grads_t[128:Q_DEV, :], rows).astype(BF16)
        return 0

    lax.fori_loop(0, 4, weight_block, 0)
    for d in load_wo:
        d.wait()
    early_sum = TwoSums(me, edges, early, EARLY_ROWS, ((64, 64), (128, 128)), early_scratch)
    plane.sideways()
    branch.add_core(0)
    branch.second()
    for d in far_copies:
        d.wait_recv()

    def kv_total(at):
        total = kv_both[2 * me.z + me.xl, at].astype(F32)
        for i in range(7):
            total = total + kv_last[i, at].astype(F32)
        dkv_low[at, :] = (
            total * kv_table[0, at, :] - swapped_pairs(total) * kv_table[1, at, :]
        )

    in_chunks(kv_total, 512)
    for i in range(4):
        for half in (0, 1):
            rows = dkv_low[TOK * i : TOK * (i + 1), HD * half : HD * half + HD]
            at = slice(TOK * (2 * i + half), TOK * (2 * i + half + 1))
            grads[at, Q_DEV:] = rows.astype(BF16)
            grads_t[Q_DEV:, at] = rows.T.astype(BF16)
    early_sum.second()
    plane.along()

    ring = RingScatter(me, edges, parts, (g1, b1, r1, l1))

    def part(k):
        pair = lax.rem(me.y + k, 4)
        rows = grads[pl.ds(pl.multiple_of(2 * TOK * pair, 2 * TOK), 2 * TOK), :]

        def block(i, _):
            cols = pl.ds(pl.multiple_of(512 * i, 512), 512)
            term = dot(rows, wq[:, cols]).astype(BF16)
            parts[pl.ds(2 * pair, 2), :, cols] = term.reshape(2, TOK, 512)
            return 0

        lax.fori_loop(0, 4, block, 0)
        ring.send_core(k)

    part(2)
    part(1)
    ring.far()
    part(3)
    ring.near()
    part(0)

    def late_block(i, _):
        cols = pl.ds(pl.multiple_of(512 * i, 512), 512)
        rows = xs[:, :, cols].reshape(8 * TOK, 512)
        late[:, cols] = dot(grads_t[Q_DEV:, :], rows).astype(BF16)
        return 0

    lax.fori_loop(0, 4, late_block, 0)
    late_sum = SumOfSixteen(me, late, columns(128), late_own, late_got, us, ur, local.at[4])
    ring.add_core(0)
    early_sum.cross()
    plane.near()
    ring.second()
    early_sum.fourth()
    branch.arrived()

    def out(at):
        output[at, :] = (middle[at, :] + branch.rows(at)).astype(BF16)

    in_chunks(out)
    late_piece[...] = late_sum.total().astype(BF16)
    wq_deliver = Deliver(me, ds, dr)

    def deliver_block(j, src, at):
        block = own_block(me, j)
        owner, slot = block // 5, lax.rem(block, 5)
        dst = wq_all.at[
            pl.ds(pl.multiple_of(64 * slot, 64), 64),
            pl.ds(pl.multiple_of(128 * at, 128), 128),
        ]
        wq_deliver.to_owner(src, dst, at // 8, owner // 2, lax.rem(owner, 2))

    deliver_block(4, late_piece, place)
    early_sum.total()
    wo_deliver = Deliver(me, es, er)
    for i, at in enumerate((place, turned)):
        for j in (0, 1):
            deliver_block(2 * i + j, early_sum.out[i].at[pl.ds(64 * j, 64)], at)
        dst = wo_all.at[
            pl.ds(pl.multiple_of(Q_DEV * rank + 128 * i, 128), 128),
            pl.ds(pl.multiple_of(128 * lax.rem(at, 2), 128), 128),
        ]
        src = early_sum.out[i].at[pl.ds(128, 128)]
        wo_deliver.to_owner(src, dst, me.y // 2, at // 4, lax.rem(at // 2, 2))
    ring.arrived()
    mine[...] = jnp.zeros_like(mine)
    mine[1:2, :] = gain_two[...]

    def back(at):
        rows = tokens[at, :].astype(F32)
        inverse = lax.rsqrt(mean_last(rows * rows) + EPSILON)
        normal = rows * inverse
        grad = ring.rows(at)
        mine[0:1, :] += jnp.sum(normal * grad, axis=0, keepdims=True)
        scaled = grad * gain[...]
        grad_tokens[at, :] = grad_middle[at, :] + inverse * (
            scaled - normal * mean_last(scaled * normal)
        )

    in_chunks(back)

    def slice_of(member):
        return mine.at[:, pl.ds(pl.multiple_of(256 * member, 256), 256)]

    near_copies = []
    for k in range(1, 8):
        dy, other = k // 2, k % 2
        y = lax.rem(me.y + dy, 4)
        to_core = 1 - me.c if other else me.c
        d = pltpu.make_async_remote_copy(
            src_ref=slice_of(2 * y + to_core),
            dst_ref=near.at[k - 1],
            send_sem=gs.at[k - 1],
            recv_sem=gr,
            device_id=me.at(y=y, core=to_core),
            device_id_type=pl.DeviceIdType.MESH,
        )
        d.start()
        near_copies.append(d)
    plane.far()
    own = mine[:, pl.ds(pl.multiple_of(256 * rank, 256), 256)]
    wait_got(near, gr)
    for k in range(7):
        own = own + near[k]
    near_sum[...] = own
    gain_deliver = Deliver(me, hs, hr)
    for to_core in (0, 1):
        gain_deliver.to_owner(near_sum, owners.at[place], to_core, me.y, me.c)

    half = pl.ds(pl.multiple_of(1024 * me.c, 1024), 1024)
    over = []
    for ref, sem in ((wo_all.at[half], er), (wq_all.at[:, half], dr)):
        wait_got(ref, sem)
        over.append(edges.copy(ref, ref, core))
    wait_got(owners, hr)
    sum_all = owners[0]
    for k in range(1, 16):
        sum_all = sum_all + owners[k]
    gains[...] = sum_all
    for d in over:
        d.wait_recv()
    wo_out[...] = wo_all[...]
    wq_out[...] = wq_all[...]
    plane.finish()
    late_sum.finish()
    for d in (wo_deliver, wq_deliver, gain_deliver):
        d.finish()
    for d in near_copies:
        d.wait_send()
    edges.finish()


def ending(
    dkv, dq, kv_table, wq, tokens, gain, grad_middle, gain_two, z_piece, x_piece, middle,
    gwo, xs, branch,
):
    many = pltpu.SemaphoreType.DMA
    return pl.pallas_call(
        ending_kernel,
        out_shape=(
            shape((TOK, D)),
            shape((TOK, D), F32),
            shape((8, 256), F32),
            shape((320, D)),
            shape((D, 256)),
            shape((PART, D)),
            shape((PART, D)),
        ),
        in_specs=[VMEM] * 11 + [ANY] * 3,
        out_specs=(VMEM,) * 5 + (ANY,) * 2,
        scratch_shapes=[
            pltpu.VMEM((8, 512, 128), BF16),
            pltpu.VMEM((8, 512, 128), BF16),
            pltpu.VMEM((7, 512, 128), BF16),
            pltpu.VMEM((512, 128), F32),
            pltpu.VMEM((8, TOK, D), BF16),
            pltpu.VMEM((1024, 320), BF16),
            pltpu.VMEM((320, 1024), BF16),
            pltpu.VMEM((8, TOK, D), BF16),
            pltpu.VMEM((8, TOK, D), BF16),
            pltpu.VMEM((512, D), BF16),
            pltpu.VMEM((64, D), BF16),
        ]
        + scatter_scratch() * 2
        + [
            pltpu.VMEM((320, D), BF16),
            pltpu.VMEM((D, 256), BF16),
            pltpu.VMEM((64, 128), BF16),
            pltpu.VMEM((15, 64, 128), BF16),
            pltpu.VMEM((64, 128), BF16),
            pltpu.VMEM((8, D), F32),
            pltpu.VMEM((7, 8, 256), F32),
            pltpu.VMEM((8, 256), F32),
            pltpu.VMEM((16, 8, 256), F32),
        ]
        + two_sums_scratch(EARLY_ROWS)
        + sems(15 + 2 * SCATTER_EDGES + PLANE_EDGES + 4 * SUM_EDGES + 2)
        + [many((40,)), many, many((16,)), many, many((2,)), many((2,))]
        + [many((7,)), many, many((16,)), many, many((15,)), many, many((5,))],
        compiler_params=pltpu.CompilerParams(
            collective_id=3, has_side_effects=True, vmem_limit_bytes=60 * 2**20
        ),
        name="ending",
    )(
        dkv, dq, kv_table, wq, tokens, gain, grad_middle, gain_two, z_piece, x_piece, middle,
        gwo, xs, branch,
    )


def widen_kernel(z_ref, x_ref, gu_ref, dn_ref):
    i = pl.program_id(0)

    @pl.when(i < 3)
    def _():
        gu_ref[...] = z_ref[...].astype(F32)

    @pl.when(i == 3)
    def _():
        gu_ref[...] = x_ref[...].astype(F32)

    @pl.when(i > 3)
    def _():
        dn_ref[...] = x_ref[...].astype(F32)


def widen(z_all, x_all):
    rows = PART // 3
    return pl.pallas_call(
        widen_kernel,
        out_shape=(shape((2 * FF_DEV, D), F32), shape((FF_DEV, D), F32)),
        grid=(6,),
        in_specs=[
            pl.BlockSpec((rows, D), lambda i: (jnp.minimum(i, 2), 0)),
            pl.BlockSpec((rows, D), lambda i: (jnp.maximum(i - 3, 0), 0)),
        ],
        out_specs=(
            pl.BlockSpec((rows, D), lambda i: (jnp.minimum(i, 3), 0)),
            pl.BlockSpec((rows, D), lambda i: (jnp.maximum(i - 4, 0), 0)),
        ),
        compiler_params=pltpu.CompilerParams(vmem_limit_bytes=40 * 2**20),
        name="widen",
    )(z_all, x_all)


def route(dz):
    pairs = []
    for i in range(128):
        z, xl, c, y, xh = i // 32, i // 16 % 2, i // 8 % 2, i // 2 % 4, i % 2
        if c != xh:
            pairs.append((i, (((((z + dz) % 4) * 2 + xl) * 2 + c) * 4 + y) * 2 + xh))
    return pairs


def body(hidden, positions, gain_attn, w_qkv, w_out, gain_mlp, w_gate_up, w_down, cotangent):
    gain_one = gain_attn.astype(F32).reshape(1, D)
    gain_two = gain_mlp.astype(F32).reshape(1, D)
    wgu = w_gate_up.reshape(2 * FF_DEV, D)
    wdn = w_down.T
    query, kv_table, trigs, xs, wq, poss, kvs, places, cots, wo, wswap = begin(
        hidden[0],
        gain_one,
        jnp.broadcast_to(positions, (8, TOK)),
        rotary_rows(positions[0]),
        w_qkv,
        wgu,
        wdn,
        cotangent[0],
        w_out,
    )
    wo = wo.reshape(D, Q_DEV)
    query_runs = poss[:, 0, ::64].reshape(16) // 64
    key_runs = (
        places[:, :, 0, ::64].reshape(8, 4, 2, 2).transpose(1, 0, 2, 3).reshape(128) // 64
    )
    wnear_up = lax.ppermute(wswap, AXES, route(1))
    wnear_down = lax.ppermute(wswap, AXES, route(3))
    att, ot, lse = attend(key_runs, query_runs, query, kvs)
    parts = dot_last(att, wo).astype(BF16).reshape(8, TOK, D)
    middle, grad_middle, gain_grad, gbs, z_piece, x_piece, branch = feed_forward(
        parts, hidden[0], gain_two, cots, wgu, wdn, wswap, wnear_up, wnear_down
    )
    gb = gbs.reshape(1024, D)
    grad_att = dot(gb, wo).astype(BF16)
    grad_wo = dot_first(att, gb).astype(BF16)
    dq, dkv = attend_back(key_runs, query_runs, query, kvs, grad_att, ot, lse, trigs)
    output, grad_tokens, gains, grad_w_qkv, grad_w_out, z_all, x_all = ending(
        dkv,
        dq,
        kv_table,
        wq,
        hidden[0],
        gain_one,
        grad_middle,
        gain_grad,
        z_piece,
        x_piece,
        middle,
        grad_wo,
        xs,
        branch,
    )
    grad_gu, grad_dn = widen(z_all, x_all)
    return (
        output[None],
        grad_tokens[None],
        gains[0],
        grad_w_qkv.astype(F32),
        grad_w_out.T.astype(F32),
        gains[1],
        grad_gu.reshape(2, FF_DEV, D),
        grad_dn.T,
    )


def solution(mesh):
    fine = Mesh(mesh.devices.reshape(4, 2, 2, 4, 2), AXES)
    ctx, fsdp = ("z", "xl", "c"), ("y", "xh")
    weight = P(fsdp, None)
    return jax.shard_map(
        body,
        mesh=fine,
        in_specs=(
            P(fsdp, ctx, None),
            P(fsdp, ctx),
            P(),
            weight,
            weight,
            P(),
            P(None, fsdp, None),
            P(None, fsdp),
            P(fsdp, ctx, None),
        ),
        out_specs=(
            P(fsdp, ctx, None),
            P(fsdp, ctx, None),
            P(fsdp),
            weight,
            weight,
            P(fsdp),
            P(None, fsdp, None),
            P(None, fsdp),
        ),
        check_vma=False,
    )
```

```python
import jax
import jax.numpy as jnp
from jax import lax
from jax.experimental import pallas as pl
from jax.experimental.pallas import tpu as pltpu
from jax.sharding import Mesh
from jax.sharding import PartitionSpec as P

D = 2048
H = 32
KV = 4
HD = 64
FF = 5632
TOK = 128
HALF = 64
FF_DEV = 704
Q_DEV = 256
EPSILON = 1e-05
FILLER = -1e30
AXES = ("z", "xl", "c", "y", "xh")
ANY = pl.BlockSpec(memory_space=pl.ANY)
VMEM = pl.BlockSpec(memory_space=pltpu.VMEM)
BF16 = jnp.bfloat16
F32 = jnp.float32


class Place:
    def __init__(self):
        self.z, self.xl, self.c, self.y, self.xh = (lax.axis_index(a) for a in AXES)

    def at(self, dz=0, dy=0, core=None, xl=None, xh=None, y=None):
        z = lax.rem(self.z + dz + 4, 4) if dz else self.z
        y = (lax.rem(self.y + dy + 4, 4) if dy else self.y) if y is None else y
        return (
            z,
            self.xl if xl is None else xl,
            self.c if core is None else core,
            y,
            self.xh if xh is None else xh,
        )


class Edges:
    def __init__(self, send, recv):
        self.send, self.recv, self.count, self.started = send, recv, 0, []

    def copy(self, src, dst, device, start=True):
        i = self.count
        self.count += 1
        d = pltpu.make_async_remote_copy(
            src_ref=src,
            dst_ref=dst,
            send_sem=self.send.at[i],
            recv_sem=self.recv.at[i],
            device_id=device,
            device_id_type=pl.DeviceIdType.MESH,
        )
        self.started.append(d)
        if start:
            d.start()
        return d

    def sent(self, copies):
        for d in copies:
            d.wait_send()
        self.started = [d for d in self.started if all(d is not e for e in copies)]

    def finish(self):
        for d in self.started:
            d.wait_send()


def greet(devices):
    for device in devices:
        pl.semaphore_signal(
            pltpu.get_barrier_semaphore(),
            inc=1,
            device_id=device,
            device_id_type=pl.DeviceIdType.MESH,
        )
    return len(devices)


def met(count):
    pl.semaphore_wait(pltpu.get_barrier_semaphore(), count)


def group_members(me):
    found = [me.at(core=1 - me.c)]
    for dy in (1, 2, 3):
        found += [me.at(dy=dy), me.at(dy=dy, core=1 - me.c)]
    return found


class RingGather:
    def __init__(self, me, edges, own, out, local):
        self.me, self.edges, self.out = me, edges, out
        self.core = me.at(core=1 - me.c)
        self.up, self.down = me.at(dy=1), me.at(dy=-1)
        a, b = own.at[pl.ds(0, HALF)], own.at[pl.ds(HALF, HALF)]
        to_a, to_b = self.block(0, 0), self.block(0, 1)
        self.up_a = edges.copy(a, to_a, self.up)
        self.down_b = edges.copy(b, to_b, self.down)
        self.up_b = edges.copy(b, to_b, self.up)
        self.down_a = edges.copy(a, to_a, self.down)
        self.to_core = [edges.copy(a, to_a, self.core), edges.copy(b, to_b, self.core)]
        self.kept = [
            pltpu.make_async_copy(a, to_a, local.at[0]),
            pltpu.make_async_copy(b, to_b, local.at[1]),
        ]
        for d in self.kept:
            d.start()

    def block(self, dy, half):
        y = lax.rem(self.me.y + dy + 4, 4)
        rows = pl.ds(pl.multiple_of(HALF * self.me.c, HALF), HALF)
        return self.out.at[2 * y + half, rows]

    def pass_core(self, dy, half):
        ref = self.block(dy, half)
        self.to_core.append(self.edges.copy(ref, ref, self.core))

    def own(self):
        for d in self.kept:
            d.wait()
        self.from_core(0, 2)

    def relay(self):
        self.up_a.wait_recv()
        ref = self.block(-1, 0)
        self.on_a = self.edges.copy(ref, ref, self.up)
        self.pass_core(-1, 0)
        self.down_b.wait_recv()
        ref = self.block(1, 1)
        self.on_b = self.edges.copy(ref, ref, self.down)
        self.pass_core(1, 1)

    def near(self):
        self.up_b.wait_recv()
        self.pass_core(-1, 1)
        self.down_a.wait_recv()
        self.pass_core(1, 0)

    def far(self):
        self.on_a.wait_recv()
        self.pass_core(2, 0)
        self.on_b.wait_recv()
        self.pass_core(2, 1)

    def from_core(self, first, last):
        for d in self.to_core[first:last]:
            d.wait_recv()

    def rest(self):
        self.near()
        self.far()
        self.own()
        self.from_core(2, 8)

    def sources(self):
        return [self.up_a, self.up_b, self.down_a, self.down_b] + self.to_core[:2]


GATHER_EDGES = 14
GROUPS = (((0, 0), (0, 1)), ((3, 0), (1, 1)), ((3, 1), (1, 0)), ((2, 0), (2, 1)))


class RingScatter:
    def __init__(self, me, edges, parts, scratch):
        self.me, self.edges, self.parts = me, edges, parts
        self.got, self.both, self.relayed, self.last = scratch
        self.up, self.down = me.at(dy=1), me.at(dy=-1)
        self.cores = {}
        self.a, self.b = pl.ds(0, HALF), pl.ds(HALF, HALF)

    def send_core(self, k):
        row = 2 * lax.rem(self.me.y + k, 4) + 1 - self.me.c
        core = self.me.at(core=1 - self.me.c)
        self.cores[k] = self.edges.copy(self.parts.at[row], self.got.at[k], core)

    def add_core(self, k):
        self.cores[k].wait_recv()
        row = 2 * lax.rem(self.me.y + k, 4) + self.me.c

        def add(at):
            self.both[k, at] = (
                self.parts[row, at].astype(F32) + self.got[k, at].astype(F32)
            ).astype(BF16)

        in_chunks(add)

    def far(self):
        self.add_core(2)
        e, both = self.edges, self.both
        self.r_a = e.copy(both.at[2, self.a], self.relayed.at[0], self.up)
        self.r_b = e.copy(both.at[2, self.b], self.relayed.at[1], self.down)

    def near(self):
        e, both = self.edges, self.both
        self.add_core(1)
        self.u_b = e.copy(both.at[1, self.b], self.last.at[0, self.b], self.up)
        self.add_core(3)
        self.d_a = e.copy(both.at[3, self.a], self.last.at[1, self.a], self.down)

    def first(self):
        for k in (2, 1, 3, 0):
            self.send_core(k)
        self.far()
        self.near()
        self.add_core(0)

    def second(self):
        a, b, e, both = self.a, self.b, self.edges, self.both
        self.r_a.wait_recv()
        both[1, a] = (both[1, a].astype(F32) + self.relayed[0].astype(F32)).astype(BF16)
        self.u_a = e.copy(both.at[1, a], self.last.at[0, a], self.up)
        self.r_b.wait_recv()
        both[3, b] = (both[3, b].astype(F32) + self.relayed[1].astype(F32)).astype(BF16)
        self.d_b = e.copy(both.at[3, b], self.last.at[1, b], self.down)

    def arrived(self):
        for d in (self.u_b, self.d_a, self.u_a, self.d_b):
            d.wait_recv()

    def rows(self, at):
        return (
            self.both[0, at].astype(F32)
            + self.last[0, at].astype(F32)
            + self.last[1, at].astype(F32)
        )

    def release(self):
        ring = [self.r_a, self.r_b, self.u_b, self.d_a, self.u_a, self.d_b]
        self.edges.sent(ring + list(self.cores.values()))


SCATTER_EDGES = 10


def scatter_scratch():
    return [
        pltpu.VMEM((4, TOK, D), BF16),
        pltpu.VMEM((4, TOK, D), BF16),
        pltpu.VMEM((2, HALF, D), BF16),
        pltpu.VMEM((2, TOK, D), BF16),
    ]


def sems(n):
    return [pltpu.SemaphoreType.DMA((n,)), pltpu.SemaphoreType.DMA((n,))]


def shape(dims, dtype=BF16):
    return jax.ShapeDtypeStruct(dims, dtype)


def remote_params(number):
    return pltpu.CompilerParams(
        collective_id=number, has_side_effects=True, vmem_limit_bytes=48 * 2**20
    )


def block_place(block):
    is_kv = block >= 32
    other = block - 32
    rank = block // 4
    y = jnp.where(is_kv, lax.rem(other + 32, 4), rank // 2)
    core = jnp.where(is_kv, other // 4, lax.rem(rank, 2))
    return y, core, jnp.where(is_kv, 4, lax.rem(block, 4))


def own_block(me, j):
    if j == 4:
        return 32 + 4 * me.c + me.y
    return 4 * (2 * me.y + me.c) + j


def send_block(me, src, dst, send_sem, recv_sem, target, stays):
    @pl.when(stays)
    def _():
        pltpu.make_async_copy(src, dst, recv_sem).start()

    @pl.when(jnp.logical_not(stays))
    def _():
        pltpu.make_async_remote_copy(
            src_ref=src,
            dst_ref=dst,
            send_sem=send_sem,
            recv_sem=recv_sem,
            device_id=target,
            device_id_type=pl.DeviceIdType.MESH,
        ).start()


def wait_sent(src, send_sem, stays):
    @pl.when(jnp.logical_not(stays))
    def _():
        pltpu.make_async_copy(src, src, send_sem).wait()


def wait_got(dst, recv_sem):
    pltpu.make_async_copy(dst, dst, recv_sem).wait()


def x_of(me):
    return 2 * me.xh + me.xl


def around(me, dz, dx):
    x = lax.rem(x_of(me) + dx, 4)
    return me.at(dz=dz, xl=lax.rem(x, 2), xh=x // 2)


STEPS = [(dz, dx) for dz in range(4) for dx in range(4)][1:]


class SumOfSixteen:
    def __init__(self, me, src, piece, own, got, send, recv, local):
        self.me, self.src, self.piece, self.own, self.got = me, src, piece, own, got
        self.send, self.recv = send, recv
        self.keep = pltpu.make_async_copy(
            src.at[piece(4 * me.z + x_of(me))], own, local
        )
        self.keep.start()
        for k, (dz, dx) in enumerate(STEPS):
            to = 4 * lax.rem(me.z + dz, 4) + lax.rem(x_of(me) + dx, 4)
            self.copy(src.at[piece(to)], k, around(me, dz, dx)).start()

    def copy(self, src, k, device):
        return pltpu.make_async_remote_copy(
            src_ref=src,
            dst_ref=self.got.at[k],
            send_sem=self.send.at[k],
            recv_sem=self.recv,
            device_id=device,
            device_id_type=pl.DeviceIdType.MESH,
        )

    def total(self):
        self.keep.wait()
        pltpu.make_async_copy(self.got, self.got, self.recv).wait()
        total = self.own[...].astype(F32)
        for k in range(15):
            total = total + self.got[k].astype(F32)
        return total

    def finish(self):
        for k in range(15):
            src = self.src.at[self.piece(0)]
            pltpu.make_async_copy(src, src, self.send.at[k]).wait()


def same(me, z, xl, core, y, xh):
    return (z == me.z) & (xl == me.xl) & (core == me.c) & (y == me.y) & (xh == me.xh)


class Deliver:
    def __init__(self, me, send, recv):
        self.me, self.send, self.recv, self.sent = me, send, recv, []

    def to_owner(self, src, dst, core, y, xh):
        me = self.me
        for dz in range(4):
            for dl in (0, 1):
                z = lax.rem(me.z + dz, 4)
                xl = 1 - me.xl if dl else me.xl
                stays = same(me, z, xl, core, y, xh)
                sem = self.send.at[len(self.sent)]
                send_block(me, src, dst, sem, self.recv, (z, xl, core, y, xh), stays)
                self.sent.append((src, sem, stays))

    def finish(self):
        for src, sem, stays in self.sent:
            wait_sent(src, sem, stays)


def rotary_rows(places):
    steps = jnp.arange(HD // 2, dtype=F32)
    inverse = jnp.power(10000.0, steps * (-2.0 / HD))
    turning = places.astype(F32)[:, None] * inverse[None, :]
    rows = jnp.concatenate([jnp.cos(turning), jnp.sin(turning)], axis=1)
    return rows.reshape(2, 64, HD).transpose(1, 0, 2).reshape(64, 2 * HD)


def halves_swapped(rows):
    return jnp.concatenate([rows[:, HD // 2 :], rows[:, : HD // 2]], axis=1)


def rotate(rows, table, back=False):
    turned = halves_swapped(rows) * table[:, HD:]
    return rows * table[:, :HD] + (-turned if back else turned)


def rotary_of(rows, u):
    cosine = rows[:, HD * u : HD * u + HD // 2]
    sine = rows[:, HD * u + HD // 2 : HD * u + HD]
    return jnp.concatenate([cosine, cosine, -sine, sine], axis=1)


ROWS = 16


def in_chunks(step, rows=TOK):
    def one(i, _):
        step(pl.ds(pl.multiple_of(i * ROWS, ROWS), ROWS))
        return 0

    lax.fori_loop(0, rows // ROWS, one, 0)


def mean_last(rows):
    return jnp.mean(rows, axis=-1, keepdims=True)


GU_QUARTER = 2 * FF_DEV // 4
DN_QUARTER = FF_DEV // 4
QUARTER = GU_QUARTER + DN_QUARTER


def swap_copies(me, wgu, wdn, wswap, send, recv):
    found = []
    across = me.at(core=1 - me.c, xl=1 - me.xl, xh=1 - me.xh)
    for i, (src, rows, start) in enumerate(
        ((wgu, GU_QUARTER, 0), (wdn, DN_QUARTER, GU_QUARTER))
    ):
        found.append(
            pltpu.make_async_remote_copy(
                src_ref=src.at[pl.ds(pl.multiple_of(rows * me.z, 16), rows)],
                dst_ref=wswap.at[pl.ds(start, rows)],
                send_sem=send.at[i],
                recv_sem=recv.at[i],
                device_id=across,
                device_id_type=pl.DeviceIdType.MESH,
            )
        )
    return found


def chips_in_sequence(me):
    return [(dz, dl) for dz in range(4) for dl in (0, 1)][1:]


def begin_kernel(
    tokens, gain, pos, trig, wqkv, wgu, wdn, cot, wout,
    q, kv_table, trigs, xs_out, wq_out, poss, kvs, places, cots, wo, wswap,
    low, xs, wq, kv,
    send, recv, qs, qr, os_, orr, ws, wr, local,
):
    me = Place()
    partner = {"xl": 1 - me.xl, "xh": 1 - me.xh}
    core = me.at(core=1 - me.c)
    members = group_members(me)
    others = [
        me.at(y=lax.rem(me.y + dy, 4), core=c, **partner) for dy in range(4) for c in (0, 1)
    ]
    far = [
        me.at(dz=dz, xl=(1 - me.xl) if dl else me.xl) for dz, dl in chips_in_sequence(me)
    ]
    signalled = greet(members + others + far)
    edges = Edges(send, recv)
    mine = 2 * me.y + me.c
    chip = 2 * me.z + me.xl

    def norm_rows():
        def norm(at):
            rows = tokens[at, :].astype(F32)
            inverse = lax.rsqrt(mean_last(rows * rows) + EPSILON)
            low[at, :] = (rows * inverse * gain[...]).astype(BF16)

        in_chunks(norm)

    spread = pl.ds(pl.multiple_of(512 * me.z, 512), 512)
    spread_rows = pl.ds(pl.multiple_of(64 * me.z, 64), 64)
    own = 2 * me.y + me.xh
    own_column = me.c == 0
    to_xl = jnp.where(own_column, me.xl, 1 - me.xl)
    to_xh = jnp.where(own_column, me.xh, 1 - me.xh)
    norm_rows()
    met(signalled)
    blocks = []
    for i in range(5):
        y, to_core, slot = block_place(5 * own + i)
        stays = own_column & (y == me.y) & (to_core == me.c)
        src = wqkv.at[pl.ds(64 * i, 64), spread]
        dst = wq.at[pl.ds(pl.multiple_of(64 * slot, 64), 64), spread]
        target = (me.z, to_xl, to_core, y, to_xh)
        send_block(me, src, dst, qs.at[i], qr.at[slot], target, stays)
        blocks.append((src, qs.at[i], stays))

    keep_pos = pltpu.make_async_copy(pos, poss.at[mine], local.at[1])
    keep_pos.start()
    pos_copies = [edges.copy(pos, poss.at[mine], m) for m in members]
    trigs[mine] = trig[...]
    trig_copies = [edges.copy(trig, trigs.at[mine], me.at(dy=k)) for k in (1, 2, 3)]
    trig_over = [edges.copy(trig, trigs.at[mine], core)]
    ring = RingGather(me, edges, low, xs, local.at[pl.ds(6, 2)])
    for i in range(8):
        dy, other = i // 2, i % 2
        y = lax.rem(me.y + dy, 4)
        to_core = me.c if other == 0 else 1 - me.c
        stays = own_column if i == 0 else me.c < 0
        cols = pl.ds(pl.multiple_of(Q_DEV * (2 * y + to_core), Q_DEV), Q_DEV)
        src = wout.at[spread_rows, cols]
        dst = wo.at[own, spread_rows]
        target = (me.z, to_xl, to_core, y, to_xh)
        send_block(me, src, dst, os_.at[i], orr.at[own], target, stays)
        blocks.append((src, os_.at[i], stays))
    moved = me.c != me.xh
    swaps = swap_copies(me, wgu, wdn, wswap, ws, wr)

    @pl.when(moved)
    def _():
        for d in swaps:
            d.start()

    for i in range(5):
        wait_got(wq.at[pl.ds(64 * i, 64), spread], qr.at[i])
    wq_copies = [
        edges.copy(wq.at[:, spread], wq.at[:, spread], me.at(dz=k)) for k in (1, 3, 2)
    ]
    for k, d in zip((1, 2, 3), trig_copies):
        d.wait_recv()
        ref = trigs.at[2 * lax.rem(me.y - k + 4, 4) + me.c]
        trig_over.append(edges.copy(ref, ref, core))
    ring.relay()
    for i in range(8):
        wait_got(wo.at[i, spread_rows], orr.at[i])
    ref = wo.at[:, spread_rows]
    wo_copies = [edges.copy(ref, ref, me.at(dz=k)) for k in (1, 3, 2)]
    keep_pos.wait()
    for d in pos_copies + trig_over:
        d.wait_recv()
    for d in wq_copies:
        d.wait_recv()
    wq_save = pltpu.make_async_copy(wq, wq_out, local.at[2])
    wq_save.start()
    is_key = me.c == 0

    def compute(group):
        ys = [lax.rem(me.y + dy, 4) for dy, _ in group]
        rows = [xs[2 * y + u] for y, (_, u) in zip(ys, group)]
        projected = dot_last(jnp.concatenate(rows, axis=0), wq[...])
        for i, (y, (_, u)) in enumerate(zip(ys, group)):
            for half in (0, 1):
                rows = rotary_of(trigs[2 * y + half], u)
                at = TOK * i + 64 * half
                values = projected[at : at + 64]
                heads = [rotate(values[:, HD * h : HD * h + HD], rows) for h in range(4)]
                query = jnp.concatenate(heads, axis=1).astype(BF16)
                to = pl.ds(pl.multiple_of(2 * TOK * y + TOK * u + 64 * half, 64), 64)
                q[to, :] = (query.astype(F32) * 0.125).astype(BF16)
                rows = jnp.concatenate(
                    [
                        jnp.where(is_key, rows[:, :HD], 1.0),
                        jnp.where(is_key, rows[:, HD:], 0.0),
                    ],
                    axis=1,
                )
                to = pl.ds(pl.multiple_of(TOK * y + 64 * u, 64), 64)
                lanes = slice(HD * half, HD * half + HD)
                kv[to, lanes] = rotate(values[:, Q_DEV:], rows).astype(BF16)
                kv_table[0, to, lanes] = rows[:, :HD]
                kv_table[1, to, lanes] = rows[:, HD:]

    ring.own()
    compute(GROUPS[0])
    ring.near()
    ring.from_core(2, 4)
    compute(GROUPS[1])
    ring.from_core(4, 6)
    ring.far()
    compute(GROUPS[2])
    ring.from_core(6, 8)
    compute(GROUPS[3])

    keeps = [
        pltpu.make_async_copy(kv, kvs.at[me.c, chip], local.at[0]),
        pltpu.make_async_copy(poss, places.at[chip], local.at[1]),
        pltpu.make_async_copy(xs, xs_out, local.at[4]),
    ]
    for d in keeps:
        d.start()
    pos_copies = [edges.copy(poss, places.at[chip], d) for d in far]
    kv_copies = [edges.copy(kv, kvs.at[me.c, chip], d) for d in far]
    over = [edges.copy(kv, kvs.at[me.c, chip], core)]
    ring = RingGather(me, edges, cot, cots, local.at[pl.ds(6, 2)])
    ring.relay()
    for (dz, dl), d in zip(chips_in_sequence(me), kv_copies):
        d.wait_recv()
        source = 2 * lax.rem(me.z - dz + 4, 4) + ((1 - me.xl) if dl else me.xl)
        ref = kvs.at[me.c, source]
        over.append(edges.copy(ref, ref, core))
    ring.rest()
    for d in over + pos_copies + wo_copies:
        d.wait_recv()
    for src, sem, stays in blocks:
        wait_sent(src, sem, stays)

    @pl.when(moved)
    def _():
        for d in swaps:
            d.wait()

    edges.finish()
    for d in keeps + [wq_save]:
        d.wait()


def begin(tokens, gain, pos, trig, wqkv, wgu, wdn, cot, wout):
    return pl.pallas_call(
        begin_kernel,
        out_shape=(
            shape((1024, Q_DEV)),
            shape((2, 512, 128), F32),
            shape((8, 64, 128), F32),
            shape((8, TOK, D)),
            shape((320, D)),
            shape((8, 8, TOK), jnp.int32),
            shape((2, 8, 512, 128)),
            shape((8, 8, 8, TOK), jnp.int32),
            shape((8, TOK, D)),
            shape((8, 256, Q_DEV)),
            shape((QUARTER, D)),
        ),
        in_specs=[VMEM, VMEM, VMEM, VMEM] + [ANY] * 5,
        out_specs=(VMEM, VMEM, VMEM) + (ANY,) * 8,
        scratch_shapes=[
            pltpu.VMEM((TOK, D), BF16),
            pltpu.VMEM((8, TOK, D), BF16),
            pltpu.VMEM((320, D), BF16),
            pltpu.VMEM((512, 128), BF16),
        ]
        + sems(7 + 7 + 6 + 2 * GATHER_EDGES + 7 + 7 + 8)
        + sems(5)
        + sems(8)
        + sems(2)
        + [pltpu.SemaphoreType.DMA((8,))],
        compiler_params=remote_params(0),
        name="begin",
    )(tokens, gain, pos, trig, wqkv, wgu, wdn, cot, wout)


def split_heads(rows):
    return jnp.concatenate([rows[:, HD * h : HD * (h + 1)] for h in range(4)], axis=0)


def join_heads(rows):
    return jnp.concatenate([rows[64 * h : 64 * (h + 1), :] for h in range(4)], axis=1)


def dot_last(a, b):
    return lax.dot_general(a, b, (((1,), (1,)), ((), ())), preferred_element_type=F32)


def dot_first(a, b):
    return lax.dot_general(a, b, (((0,), (0,)), ((), ())), preferred_element_type=F32)


def dot(a, b):
    return lax.dot_general(a, b, (((1,), (0,)), ((), ())), preferred_element_type=F32)


TILE = 256
WIDE = 4


def sort_keys(runs, seq, kv_ref, keys, values):
    for j in range(32):
        chip, core, u = j // 4, (j // 2) % 2, j % 2
        to = pl.ds(pl.multiple_of(runs[seq * 32 + j] * 64, 64), 64)
        rows, lanes = slice(64 * u, 64 * u + 64), slice(HD * core, HD * core + HD)
        keys[to, :] = kv_ref[0, chip, rows, lanes]
        values[to, :] = kv_ref[1, chip, rows, lanes]


def turn(rows, turned):
    for i in range(4):
        at = slice(512 * i, 512 * (i + 1))
        turned[:, at] = rows[at, :].astype(F32).T.astype(BF16)


def allowed_tile(tile, run):
    key = lax.broadcasted_iota(jnp.int32, (TILE, 256), 0) + tile * TILE
    query = lax.rem(lax.broadcasted_iota(jnp.int32, (TILE, 256), 1), 64) + run * 64
    return key <= query


def tile_rows(tile):
    return pl.ds(pl.multiple_of(tile * TILE, TILE), TILE)


def attend_kernel(
    key_runs, query_runs, q_ref, kv_ref, att_ref, ot_ref, lse_ref,
    keys, values, values_t, high_ref, total_ref, acc_ref,
):
    seq = pl.program_id(0)
    sort_keys(key_runs, seq, kv_ref, keys, values)
    turn(values, values_t)

    def one_run(r, _):
        run = query_runs[seq * 4 + r]
        rows = pl.ds(pl.multiple_of(r * 64, 64), 64)
        query = split_heads(q_ref[rows, :]).astype(F32).T.astype(BF16)
        last = run // 4
        high_ref[...] = jnp.full((1, 256), FILLER, F32)
        total_ref[...] = jnp.zeros((1, 256), F32)
        acc_ref[...] = jnp.zeros((HD, 256), F32)

        def tiles(first, count, masked):
            scores = []
            for k in range(count):
                score = dot(keys[tile_rows(first + k), :], query)
                if masked and k == count - 1:
                    score = jnp.where(allowed_tile(first + k, run), score, FILLER)
                scores.append(score)
            high = high_ref[...]
            new_high = high
            for score in scores:
                new_high = jnp.maximum(new_high, jnp.max(score, axis=0, keepdims=True))
            scale = jnp.exp(high - new_high)
            total = total_ref[...] * scale
            acc = acc_ref[...] * scale
            for k, score in enumerate(scores):
                weights = jnp.exp(score - new_high)
                total = total + jnp.sum(weights, axis=0, keepdims=True)
                acc = acc + dot(values_t[:, tile_rows(first + k)], weights.astype(BF16))
            high_ref[...] = new_high
            total_ref[...] = total
            acc_ref[...] = acc

        @pl.when(last >= WIDE)
        def _():
            tiles(0, WIDE, False)

        start = (last // WIDE) * WIDE
        for n in range(WIDE):

            @pl.when(last - start == n)
            def _():
                tiles(start, n + 1, True)

        total = total_ref[...]
        out = acc_ref[...] / total
        ot_ref[r] = out
        lse_ref[r] = high_ref[...] + jnp.log(total)
        att_ref[rows, :] = join_heads(out.T).astype(BF16)
        return 0

    lax.fori_loop(0, 4, one_run, 0)


def attend(key_runs, query_runs, q, kv):
    return pl.pallas_call(
        attend_kernel,
        out_shape=(shape((1024, 256)), shape((16, HD, 256), F32), shape((16, 1, 256), F32)),
        grid_spec=pltpu.PrefetchScalarGridSpec(
            num_scalar_prefetch=2,
            grid=(4,),
            in_specs=[
                pl.BlockSpec((256, 256), lambda i, *_: (i, 0)),
                pl.BlockSpec((2, 8, 128, 128), lambda i, *_: (0, 0, i, 0)),
            ],
            out_specs=[
                pl.BlockSpec((256, 256), lambda i, *_: (i, 0)),
                pl.BlockSpec((4, HD, 256), lambda i, *_: (i, 0, 0)),
                pl.BlockSpec((4, 1, 256), lambda i, *_: (i, 0, 0)),
            ],
            scratch_shapes=[
                pltpu.VMEM((2048, HD), BF16),
                pltpu.VMEM((2048, HD), BF16),
                pltpu.VMEM((HD, 2048), BF16),
                pltpu.VMEM((1, 256), F32),
                pltpu.VMEM((1, 256), F32),
                pltpu.VMEM((HD, 256), F32),
            ],
        ),
        compiler_params=pltpu.CompilerParams(vmem_limit_bytes=61 * 2**20),
        name="attend",
    )(key_runs, query_runs, q, kv)


def attend_back_kernel(
    key_runs, query_runs, q_ref, kv_ref, da_ref, ot_ref, lse_ref, trig_ref,
    dq_ref, dkv_ref, keys, values, keys_t, dkeys, dvalues, dq_acc,
):
    seq = pl.program_id(0)
    sort_keys(key_runs, seq, kv_ref, keys, values)
    turn(keys, keys_t)
    dkeys[...] = jnp.zeros_like(dkeys)
    dvalues[...] = jnp.zeros_like(dvalues)

    def one_run(r, _):
        run = query_runs[seq * 4 + r]
        rows = pl.ds(pl.multiple_of(r * 64, 64), 64)
        query = split_heads(q_ref[rows, :])
        grad = split_heads(da_ref[rows, :])
        lse = lse_ref[r]
        query_t = query.astype(F32).T.astype(BF16)
        grad_t = grad.astype(F32).T
        delta = jnp.sum(grad_t * ot_ref[r], axis=0, keepdims=True)
        grad_t = grad_t.astype(BF16)
        last = run // 4
        dq_acc[...] = jnp.zeros((HD, 256), F32)

        def tiles(first, count, masked):
            dq = dq_acc[...]
            for k in range(count):
                at = tile_rows(first + k)
                key = keys[at, :]
                probs = jnp.exp(dot(key, query_t) - lse)
                if masked and k == count - 1:
                    probs = jnp.where(allowed_tile(first + k, run), probs, 0.0)
                grad_probs = dot(values[at, :], grad_t)
                grad_scores = (probs * (grad_probs - delta)).astype(BF16)
                dvalues[at, :] += dot(probs.astype(BF16), grad)
                dkeys[at, :] += dot(grad_scores, query)
                dq = dq + dot(keys_t[:, at], grad_scores)
            dq_acc[...] = dq

        @pl.when(last >= WIDE)
        def _():
            tiles(0, WIDE, False)

        start = (last // WIDE) * WIDE
        for n in range(WIDE):

            @pl.when(last - start == n)
            def _():
                tiles(start, n + 1, True)

        pair_rows = trig_ref[lax.rem(r, 2)]
        table = jnp.where(r < 2, rotary_of(pair_rows, 0), rotary_of(pair_rows, 1))
        dq = (dq_acc[...] * 0.125).T
        heads = [rotate(dq[64 * h : 64 * h + 64], table, back=True) for h in range(4)]
        dq_ref[rows, :] = jnp.concatenate(heads, axis=1).astype(BF16)
        return 0

    lax.fori_loop(0, 4, one_run, 0)
    for j in range(32):
        chip, core, u = j // 4, (j // 2) % 2, j % 2
        at = pl.ds(pl.multiple_of(key_runs[seq * 32 + j] * 64, 64), 64)
        rows, lanes = slice(64 * u, 64 * u + 64), slice(HD * core, HD * core + HD)
        dkv_ref[0, chip, rows, lanes] = dkeys[at, :].astype(BF16)
        dkv_ref[1, chip, rows, lanes] = dvalues[at, :].astype(BF16)


def attend_back(key_runs, query_runs, q, kv, grad, ot, lse, trigs):
    return pl.pallas_call(
        attend_back_kernel,
        out_shape=(shape((1024, 256)), shape((2, 8, 512, 128))),
        grid_spec=pltpu.PrefetchScalarGridSpec(
            num_scalar_prefetch=2,
            grid=(4,),
            in_specs=[
                pl.BlockSpec((256, 256), lambda i, *_: (i, 0)),
                pl.BlockSpec((2, 8, 128, 128), lambda i, *_: (0, 0, i, 0)),
                pl.BlockSpec((256, 256), lambda i, *_: (i, 0)),
                pl.BlockSpec((4, HD, 256), lambda i, *_: (i, 0, 0)),
                pl.BlockSpec((4, 1, 256), lambda i, *_: (i, 0, 0)),
                pl.BlockSpec((2, 64, 128), lambda i, *_: (i, 0, 0)),
            ],
            out_specs=[
                pl.BlockSpec((256, 256), lambda i, *_: (i, 0)),
                pl.BlockSpec((2, 8, 128, 128), lambda i, *_: (0, 0, i, 0)),
            ],
            scratch_shapes=[
                pltpu.VMEM((2048, HD), BF16),
                pltpu.VMEM((2048, HD), BF16),
                pltpu.VMEM((HD, 2048), BF16),
                pltpu.VMEM((2048, HD), F32),
                pltpu.VMEM((2048, HD), F32),
                pltpu.VMEM((HD, 256), F32),
            ],
        ),
        compiler_params=pltpu.CompilerParams(vmem_limit_bytes=61 * 2**20),
        name="attend_back",
    )(key_runs, query_runs, q, kv, grad, ot, lse, trigs)


PART = 3 * FF_DEV // 2
PART_HALF = PART // 2


class RingSum:
    def __init__(
        self, me, edges, along_z, src, start, rows, width, step, relayed, last, shift=0
    ):
        self.edges, self.src, self.start, self.width, self.step = edges, src, start, width, step
        self.rows, self.half = rows, rows // 2
        self.relayed, self.last, self.shift = relayed, last, shift
        self.here = me.z if along_z else x_of(me)
        self.up = around(me, 1, 0) if along_z else around(me, 0, 1)
        self.down = around(me, -1, 0) if along_z else around(me, 0, 3)
        self.a, self.b = pl.ds(0, self.half), pl.ds(self.half, self.half)

    def columns(self, k):
        at = self.width * lax.rem(self.here + k + self.shift, 4)
        return pl.ds(pl.multiple_of(at, self.width), self.width)

    def piece(self, k, half):
        rows = pl.ds(self.start + self.half * half, self.half)
        return self.src.at[rows, self.columns(k)]

    def far(self):
        self.r_a = self.edges.copy(self.piece(2, 0), self.relayed.at[0], self.up)
        self.r_b = self.edges.copy(self.piece(2, 1), self.relayed.at[1], self.down)

    def near_up(self):
        self.u_b = self.edges.copy(self.piece(1, 1), self.last.at[0, self.b], self.up)

    def near_down(self):
        self.d_a = self.edges.copy(self.piece(3, 0), self.last.at[1, self.a], self.down)

    def add(self, k, half):
        step, start, cols = self.step, self.start + self.half * half, self.columns(k)

        def one(i, _):
            at = pl.ds(pl.multiple_of(start + i * step, 16), step)
            from_ = pl.ds(pl.multiple_of(i * step, 16), step)
            self.src[at, cols] = (
                self.src[at, cols].astype(F32) + self.relayed[half, from_, :].astype(F32)
            ).astype(BF16)
            return 0

        lax.fori_loop(0, self.half // step, one, 0)

    def second(self):
        self.r_a.wait_recv()
        self.add(1, 0)
        self.u_a = self.edges.copy(self.piece(1, 0), self.last.at[0, self.a], self.up)
        self.r_b.wait_recv()
        self.add(3, 1)
        self.d_b = self.edges.copy(self.piece(3, 1), self.last.at[1, self.b], self.down)

    def total(self, out):
        for d in (self.u_b, self.d_a, self.u_a, self.d_b):
            d.wait_recv()
        step, cols = self.step, self.columns(0)

        def one(i, _):
            at = pl.ds(pl.multiple_of(self.start + i * step, 16), step)
            from_ = pl.ds(pl.multiple_of(i * step, 16), step)
            out[from_, :] = (
                self.src[at, cols].astype(F32)
                + self.last[0, from_, :].astype(F32)
                + self.last[1, from_, :].astype(F32)
            ).astype(BF16)
            return 0

        lax.fori_loop(0, self.rows // step, one, 0)


SUM_EDGES = 6


def to_chunks(ref, ys, halves, cols, rows):
    for i, (y, half) in enumerate(zip(ys, halves)):
        for core in (0, 1):
            at = TOK * i + HALF * core
            ref[2 * y + core, HALF * half : HALF * half + HALF, cols] = rows[at : at + HALF]


def feed_forward_kernel(
    att, wo, tokens, cot, gain, cots, wgu, wdn, wswap, wnear_up, wnear_down,
    middle, grad_middle, gain_grad, grad_att, grad_wo, z_out, x_out, branch,
    xs, p, c, gp, gb, att_t, w, act_t, gate_t, up_t, act, dgate, dup, low,
    g1, b1, r1, l1,
    z_relayed, z_last, x_relayed, x_last, z_q, x_q,
    z_relayed2, z_last2, x_relayed2, x_last2,
    send, recv, fs, fr, local,
):
    me = Place()
    core = me.at(core=1 - me.c)
    signalled = greet(
        [core, me.at(dy=1), me.at(dy=-1)]
        + [around(me, k, 0) for k in (1, 2, 3)]
        + [around(me, 0, 1), around(me, 0, 3)]
    )
    edges = Edges(send, recv)
    moved = me.c != me.xh
    load_c = pltpu.make_async_copy(cots, c, local.at[1])
    load_c.start()

    def w_rows(dz):
        z = lax.rem(me.z + dz + 4, 4)
        return (
            pl.ds(pl.multiple_of(GU_QUARTER * z, 16), GU_QUARTER),
            pl.ds(pl.multiple_of(2 * FF_DEV + DN_QUARTER * z, 16), DN_QUARTER),
        )

    gu_part, dn_part = pl.ds(0, GU_QUARTER), pl.ds(GU_QUARTER, DN_QUARTER)
    kept = [
        pltpu.make_async_copy(wgu, w.at[pl.ds(0, 2 * FF_DEV)], local.at[2]),
        pltpu.make_async_copy(wdn, w.at[pl.ds(2 * FF_DEV, FF_DEV)], local.at[3]),
    ]
    near_w = []
    for i, (src, dz) in enumerate(((wswap, 0), (wnear_up, -1), (wnear_down, 1))):
        gu_rows, dn_rows = w_rows(dz)
        near_w.append(pltpu.make_async_copy(src.at[gu_part], w.at[gu_rows], local.at[4 + 2 * i]))
        near_w.append(pltpu.make_async_copy(src.at[dn_part], w.at[dn_rows], local.at[5 + 2 * i]))
    far_w = [
        pltpu.make_async_remote_copy(
            src_ref=wswap.at[part],
            dst_ref=w.at[rows],
            send_sem=fs.at[i],
            recv_sem=fr.at[i],
            device_id=me.at(dz=2),
            device_id_type=pl.DeviceIdType.MESH,
        )
        for i, (part, rows) in enumerate(zip((gu_part, dn_part), w_rows(0)))
    ]

    met(signalled)

    @pl.when(moved)
    def _():
        for d in far_w + near_w:
            d.start()

    @pl.when(jnp.logical_not(moved))
    def _():
        for d in kept:
            d.start()

    ring = RingScatter(me, edges, p, (g1, b1, r1, l1))

    def attended_part(k):
        y = lax.rem(me.y + k, 4)
        rows = att[pl.ds(pl.multiple_of(2 * TOK * y, 2 * TOK), 2 * TOK), :]

        def block(i, _):
            cols = pl.ds(pl.multiple_of(512 * i, 512), 512)
            term = dot_last(rows, wo[cols, :]).astype(BF16)
            to_chunks(p, (y, y), (0, 1), cols, term)
            return 0

        lax.fori_loop(0, 4, block, 0)
        ring.send_core(k)

    attended_part(2)
    attended_part(1)
    ring.far()
    attended_part(3)
    ring.near()
    attended_part(0)
    ring.add_core(0)

    def turn_block(i, _):
        at = pl.ds(pl.multiple_of(2 * TOK * i, 2 * TOK), 2 * TOK)
        att_t[:, at] = att[at, :].astype(F32).T.astype(BF16)
        return 0

    lax.fori_loop(0, 4, turn_block, 0)
    ring.second()
    ring.arrived()

    def norm(at):
        rows = tokens[at, :].astype(F32) + ring.rows(at)
        middle[at, :] = rows
        normal = rows * lax.rsqrt(mean_last(rows * rows) + EPSILON)
        low[at, :] = (normal * gain[...]).astype(BF16)

    in_chunks(norm)
    gather = RingGather(me, edges, low, xs, local.at[pl.ds(10, 2)])
    ring.release()

    @pl.when(moved)
    def _():
        for d in near_w:
            d.wait()
        for d in far_w:
            d.wait()

    @pl.when(jnp.logical_not(moved))
    def _():
        for d in kept:
            d.wait()

    load_c.wait()

    def compute(group):
        ys = [lax.rem(me.y + dy, 4) for dy, _ in group]
        halves = [half for _, half in group]
        blocks = [2 * y + half for y, half in zip(ys, halves)]
        x = jnp.concatenate([xs[b] for b in blocks], axis=0)
        g = jnp.concatenate([c[b] for b in blocks], axis=0)
        here = [pl.ds(pl.multiple_of(TOK * b, TOK), TOK) for b in blocks]
        for n0, n1 in ((0, 256), (256, 512), (512, FF_DEV)):
            gate = dot_last(x, w[n0:n1, :])
            upward = dot_last(x, w[FF_DEV + n0 : FF_DEV + n1, :])
            grad = dot_last(g, w[2 * FF_DEV + n0 : 2 * FF_DEV + n1, :])
            sigmoid = 1.0 / (1.0 + jnp.exp(-gate))
            swish = gate * sigmoid
            active = swish * upward
            grad_up = grad * swish
            grad_gate = grad * upward * sigmoid * (1.0 + gate * (1.0 - sigmoid))
            act[:, n0:n1] = active.astype(BF16)
            dup[:, n0:n1] = grad_up.astype(BF16)
            dgate[:, n0:n1] = grad_gate.astype(BF16)
            for ref, value in ((act_t, active), (up_t, grad_up), (gate_t, grad_gate)):
                value = value.T.astype(BF16)
                ref[n0:n1, here[0]] = value[:, :TOK]
                ref[n0:n1, here[1]] = value[:, TOK:]

        def block(i, _):
            cols = pl.ds(pl.multiple_of(512 * i, 512), 512)
            term = dot(act[...], w[2 * FF_DEV :, cols])
            to_chunks(p, ys, halves, cols, term.astype(BF16))
            grads = dot(dgate[...], w[:FF_DEV, cols]) + dot(dup[...], w[FF_DEV : 2 * FF_DEV, cols])
            to_chunks(gp, ys, halves, cols, grads.astype(BF16))
            return 0

        lax.fori_loop(0, 4, block, 0)

    two = RingScatter(me, edges, gp, (g1, b1, r1, l1))
    gather.own()
    compute(GROUPS[0])
    two.send_core(0)
    gather.relay()
    gather.near()
    gather.from_core(2, 4)
    compute(GROUPS[1])
    gather.from_core(4, 6)
    gather.far()
    compute(GROUPS[2])
    two.send_core(1)
    two.send_core(3)
    two.near()
    gather.from_core(6, 8)
    compute(GROUPS[3])
    two.send_core(2)
    save = pltpu.make_async_copy(p, branch, local.at[0])
    save.start()
    two.add_core(0)

    z_sum = RingSum(me, edges, True, w, 0, PART, 512, 48, z_relayed, z_last)
    x_sum = RingSum(me, edges, False, w, PART, PART, 512, 48, x_relayed, x_last)
    split = PART - FF_DEV

    def z_task(k):
        cols = z_sum.columns(k)
        x = xs[:, :, cols].reshape(8 * TOK, 512)
        w[:FF_DEV, cols] = dot(gate_t[...], x).astype(BF16)
        w[FF_DEV:PART, cols] = dot(up_t[:split, :], x).astype(BF16)

    def x_task(k):
        cols = x_sum.columns(k)
        x = xs[:, :, cols].reshape(8 * TOK, 512)
        g = c[:, :, cols].reshape(8 * TOK, 512)
        w[PART : 2 * FF_DEV, cols] = dot(up_t[split:, :], x).astype(BF16)
        w[2 * FF_DEV :, cols] = dot(act_t[...], g).astype(BF16)

    two.far()
    z_task(2)
    z_sum.far()
    x_task(2)
    x_sum.far()
    z_task(1)
    z_sum.near_up()
    x_task(1)
    x_sum.near_up()
    two.second()
    z_task(3)
    z_sum.near_down()
    x_task(3)
    x_sum.near_down()
    z_task(0)
    x_task(0)
    two.arrived()
    gain_grad[...] = jnp.zeros_like(gain_grad)

    def back(at):
        rows = middle[at, :]
        inverse = lax.rsqrt(mean_last(rows * rows) + EPSILON)
        normal = rows * inverse
        grad = two.rows(at)
        gain_grad[...] += jnp.sum(normal * grad, axis=0, keepdims=True)
        scaled = grad * gain[...]
        result = cot[at, :].astype(F32) + inverse * (
            scaled - normal * mean_last(scaled * normal)
        )
        grad_middle[at, :] = result
        low[at, :] = result.astype(BF16)

    edges.sent(gather.sources())
    in_chunks(back)
    gather = RingGather(me, edges, low, gb, local.at[pl.ds(10, 2)])
    z_sum.second()
    x_sum.second()
    gather.relay()
    z_sum.total(z_q)
    z_two = RingSum(me, edges, False, z_q, 0, PART, 128, 176, z_relayed2, z_last2)
    z_two.far()
    z_two.near_up()
    z_two.near_down()
    x_sum.total(x_q)
    x_two = RingSum(me, edges, True, x_q, 0, PART, 128, 176, x_relayed2, x_last2)
    x_two.far()
    x_two.near_up()
    x_two.near_down()
    gather.near()
    gather.far()
    gather.own()
    gather.from_core(2, 8)

    def attended_grad(i, _):
        at = pl.ds(pl.multiple_of(2 * TOK * i, 2 * TOK), 2 * TOK)
        rows = gb[pl.ds(2 * i, 2)].reshape(2 * TOK, D)
        grad_att[at, :] = dot(rows, wo[...]).astype(BF16)
        cols = pl.ds(pl.multiple_of(512 * i, 512), 512)
        rows = gb[:, :, cols].reshape(8 * TOK, 512)
        grad_wo[:, cols] = dot(att_t[...], rows).astype(BF16)
        return 0

    lax.fori_loop(0, 4, attended_grad, 0)
    z_two.second()
    x_two.second()
    z_two.total(z_out)
    x_two.total(x_out)
    edges.finish()
    save.wait()


def feed_forward(att, wo, tokens, cot, gain, cots, wgu, wdn, wswap, wnear_up, wnear_down):
    block = pltpu.VMEM((8, TOK, D), BF16)
    turned = pltpu.VMEM((FF_DEV, 8 * TOK), BF16)
    pair = pltpu.VMEM((2 * TOK, FF_DEV), BF16)

    def ring(width):
        return [
            pltpu.VMEM((2, PART_HALF, width), BF16),
            pltpu.VMEM((2, PART, width), BF16),
        ] * 2

    return pl.pallas_call(
        feed_forward_kernel,
        out_shape=(
            shape((TOK, D), F32),
            shape((TOK, D), F32),
            shape((1, D), F32),
            shape((1024, Q_DEV)),
            shape((Q_DEV, D)),
            shape((PART, 128)),
            shape((PART, 128)),
            shape((8, TOK, D)),
        ),
        in_specs=[VMEM] * 5 + [ANY] * 6,
        out_specs=(VMEM,) * 7 + (ANY,),
        scratch_shapes=[block] * 5
        + [pltpu.VMEM((Q_DEV, 8 * TOK), BF16)]
        + [pltpu.VMEM((3 * FF_DEV, D), BF16)]
        + [turned] * 3
        + [pair] * 3
        + [pltpu.VMEM((TOK, D), BF16)]
        + scatter_scratch()
        + ring(512)
        + [pltpu.VMEM((PART, 512), BF16)] * 2
        + ring(128)
        + sems(2 * SCATTER_EDGES + 2 * GATHER_EDGES + 4 * SUM_EDGES)
        + sems(2)
        + [pltpu.SemaphoreType.DMA((12,))],
        compiler_params=pltpu.CompilerParams(
            collective_id=2, has_side_effects=True, vmem_limit_bytes=62 * 2**20
        ),
        name="feed_forward",
    )(att, wo, tokens, cot, gain, cots, wgu, wdn, wswap, wnear_up, wnear_down)


def columns(width):
    return lambda i: (slice(None), pl.ds(pl.multiple_of(i * width, width), width))


def row_block(height, start=0):
    return lambda i: (pl.ds(pl.multiple_of(start + i * height, height), height), slice(None))


def plane_devices(me):
    found = [me.at(core=1 - me.c)]
    for dz, dx in STEPS:
        z, xl, core, y, xh = around(me, dz, dx)
        found += [(z, xl, core, y, xh), (z, xl, 1 - core, y, xh)]
    return found


def swapped_pairs(rows):
    return jnp.concatenate([halves_swapped(rows[:, :HD]), halves_swapped(rows[:, HD:])], axis=1)


class RingBlocks:
    def __init__(self, me, edges, ref, columns):
        self.me, self.edges, self.ref, self.columns = me, edges, ref, columns
        rows = ref.shape[0]
        self.halves = (pl.ds(0, rows // 2), pl.ds(rows // 2, rows // 2))
        self.up, self.down = me.at(dz=1), me.at(dz=-1)
        self.up_a = self.send(0, 0, self.up)
        self.down_b = self.send(0, 1, self.down)
        self.up_b = self.send(0, 1, self.up)
        self.down_a = self.send(0, 0, self.down)

    def block(self, dz):
        return self.ref.at[:, self.columns(lax.rem(self.me.z + dz + 4, 4))]

    def send(self, dz, half, device):
        cols = self.columns(lax.rem(self.me.z + dz + 4, 4))
        ref = self.ref.at[self.halves[half], cols]
        return self.edges.copy(ref, ref, device)

    def relay(self):
        self.up_a.wait_recv()
        self.on_a = self.send(-1, 0, self.up)
        self.down_b.wait_recv()
        self.on_b = self.send(1, 1, self.down)

    def near(self):
        self.up_b.wait_recv()
        self.down_a.wait_recv()

    def far(self):
        self.on_a.wait_recv()
        self.on_b.wait_recv()


class PlaneGather:
    def __init__(self, me, edges, z_piece, x_piece, z_all, x_all, send, recv):
        self.me, self.edges, self.z_all, self.x_all = me, edges, z_all, x_all
        self.send, self.recv, self.z_piece, self.x_piece = send, recv, z_piece, x_piece
        self.stays = me.c == me.xh
        self.core = me.at(core=1 - me.c)
        self.side = me.at(xl=1 - me.xl)
        across = me.at(core=1 - me.c, xl=1 - me.xl, xh=1 - me.xh)
        x = x_of(me)
        self.held = jnp.where(self.stays, x, 3 - x)
        for i, (piece, ref, at) in enumerate(
            ((z_piece, z_all, 4 * me.z + x), (x_piece, x_all, 4 * x + me.z))
        ):
            dst = ref.at[columns(128)(at)]
            send_block(me, piece, dst, send.at[i], recv.at[i], across, self.stays)

    def z_columns(self, z):
        return pl.ds(pl.multiple_of(512 * z + 256 * self.me.c, 256), 256)

    def x_columns(self, z):
        return pl.ds(pl.multiple_of(512 * self.held + 128 * z, 128), 128)

    def sideways(self):
        own = self.z_all.at[columns(128)(4 * self.me.z + self.held)]
        wait_got(own, self.recv.at[0])
        self.z_side = self.edges.copy(own, own, self.side)
        own = self.x_all.at[:, self.x_columns(self.me.z)]
        wait_got(own, self.recv.at[1])
        self.x_ring = RingBlocks(self.me, self.edges, self.x_all, self.x_columns)
        self.x_side = [self.edges.copy(own, own, self.side)]

    def along(self):
        self.z_side.wait_recv()
        self.z_ring = RingBlocks(self.me, self.edges, self.z_all, self.z_columns)
        own = self.z_ring.block(0)
        self.over = [self.edges.copy(own, own, self.core)]
        self.x_ring.relay()

    def to_side(self, dz):
        ref = self.x_ring.block(dz)
        self.x_side.append(self.edges.copy(ref, ref, self.side))

    def to_core(self, dz):
        ref = self.z_ring.block(dz)
        self.over.append(self.edges.copy(ref, ref, self.core))

    def near(self):
        self.x_ring.near()
        self.to_side(1)
        self.to_side(-1)
        self.z_ring.relay()
        self.x_ring.far()
        self.to_side(2)

    def far(self):
        self.z_ring.near()
        self.to_core(1)
        self.to_core(-1)
        self.z_ring.far()
        self.to_core(2)
        for d in self.x_side:
            d.wait_recv()
        half = self.x_all.at[:, pl.ds(pl.multiple_of(1024 * self.me.c, 1024), 1024)]
        self.over.append(self.edges.copy(half, half, self.core))

    def finish(self):
        for d in self.over:
            d.wait_recv()
        wait_sent(self.z_piece, self.send.at[0], self.stays)
        wait_sent(self.x_piece, self.send.at[1], self.stays)


PLANE_EDGES = 1 + 2 * SUM_EDGES + 4 + 5


class TwoSums:
    def __init__(self, me, edges, src, rows, steps, scratch):
        self.me, self.edges, self.rows, self.steps = me, edges, rows, steps
        self.q, self.out = scratch[4:6], scratch[10:12]
        self.scratch = scratch
        start = (0, rows[0])
        self.one = [
            RingSum(
                me, edges, i == 0, src, start[i], rows[i], 512, steps[0][i],
                scratch[2 * i], scratch[2 * i + 1], me.y,
            )
            for i in (0, 1)
        ]
        for ring in self.one:
            ring.far()
            ring.near_up()
            ring.near_down()

    def second(self):
        for ring in self.one:
            ring.second()

    def cross(self):
        self.two = []
        for i in (0, 1):
            self.one[i].total(self.q[i])
            ring = RingSum(
                self.me, self.edges, i == 1, self.q[i], 0, self.rows[i], 128,
                self.steps[1][i], self.scratch[6 + 2 * i], self.scratch[7 + 2 * i],
            )
            ring.far()
            ring.near_up()
            ring.near_down()
            self.two.append(ring)

    def fourth(self):
        for ring in self.two:
            ring.second()

    def total(self):
        for i in (0, 1):
            self.two[i].total(self.out[i])


def two_sums_scratch(rows):
    found = []
    for r in rows:
        found += [pltpu.VMEM((2, r // 2, 512), BF16), pltpu.VMEM((2, r, 512), BF16)]
    found += [pltpu.VMEM((r, 512), BF16) for r in rows]
    for r in rows:
        found += [pltpu.VMEM((2, r // 2, 128), BF16), pltpu.VMEM((2, r, 128), BF16)]
    return found + [pltpu.VMEM((r, 128), BF16) for r in rows]


EARLY_ROWS = (256, 256)


def ending_kernel(
    dkv, dq, kv_table, wq, tokens, gain, grad_middle, gain_two, z_piece, x_piece, middle,
    gwo, xs_in, branch_in,
    output, grad_tokens, gains, wq_out, wo_out, z_all, x_all,
    kv_got, kv_both, kv_last, dkv_low, xs, grads, grads_t, parts, branch_parts, early, late,
    g1, b1, r1, l1, g2, b2, r2, l2,
    wq_all, wo_all, late_own, late_got, late_piece, mine, near, near_sum, owners,
    *rest,
):
    early_scratch = rest[:12]
    (send, recv, ds, dr, es, er, ps, pr, gs, gr, hs, hr, us, ur, local) = rest[12:]
    me = Place()
    core = me.at(core=1 - me.c)
    far = [
        me.at(dz=dz, xl=(1 - me.xl) if dl else me.xl) for dz, dl in chips_in_sequence(me)
    ]
    signalled = greet(plane_devices(me) + group_members(me)[1:])
    edges = Edges(send, recv)
    place = 4 * me.z + x_of(me)
    rank = 2 * me.y + me.c
    load_x = pltpu.make_async_copy(xs_in, xs, local.at[0])
    load_branch = pltpu.make_async_copy(branch_in, branch_parts, local.at[1])
    load_wo = [
        pltpu.make_async_copy(
            gwo.at[pl.ds(128 * i, 128)], early.at[pl.ds(256 * i + 128, 128)], local.at[2 + i]
        )
        for i in (0, 1)
    ]
    for d in [load_x, load_branch] + load_wo:
        d.start()

    def query_part(i, _):
        at = pl.ds(pl.multiple_of(2 * TOK * i, 2 * TOK), 2 * TOK)
        rows = dq[at, :]
        grads[at, :Q_DEV] = rows
        grads_t[:Q_DEV, at] = rows.astype(F32).T.astype(BF16)
        return 0

    lax.fori_loop(0, 4, query_part, 0)
    met(signalled)

    order = []
    for dz, dl in chips_in_sequence(me) + [(0, 0)]:
        chip = 2 * lax.rem(me.z + dz, 4) + ((1 - me.xl) if dl else me.xl)
        order.append((chip, edges.copy(dkv.at[1 - me.c, chip], kv_got.at[chip], core)))
    load_branch.wait()
    branch = RingScatter(me, edges, branch_parts, (g2, b2, r2, l2))
    for k in (2, 1, 3, 0):
        branch.send_core(k)
    far_copies = []
    for i, (chip, d) in enumerate(order):
        d.wait_recv()
        kv_both[chip] = (dkv[me.c, chip].astype(F32) + kv_got[chip].astype(F32)).astype(BF16)
        if i < 7:
            far_copies.append(edges.copy(kv_both.at[chip], kv_last.at[i], far[i]))
    plane = PlaneGather(me, edges, z_piece, x_piece, z_all, x_all, ps, pr)
    load_x.wait()

    def weight_block(i, _):
        cols = pl.ds(pl.multiple_of(512 * i, 512), 512)
        rows = xs[:, :, cols].reshape(8 * TOK, 512)
        early[:128, cols] = dot(grads_t[:128, :], rows).astype(BF16)
        early[256:384, cols] = dot(grads_t[128:Q_DEV, :], rows).astype(BF16)
        return 0

    lax.fori_loop(0, 4, weight_block, 0)
    for d in load_wo:
        d.wait()
    early_sum = TwoSums(me, edges, early, EARLY_ROWS, ((64, 64), (128, 128)), early_scratch)
    branch.far()
    branch.near()
    plane.sideways()
    branch.add_core(0)
    early_sum.second()
    branch.second()
    for d in far_copies:
        d.wait_recv()

    def kv_total(at):
        total = kv_both[2 * me.z + me.xl, at].astype(F32)
        for i in range(7):
            total = total + kv_last[i, at].astype(F32)
        dkv_low[at, :] = (
            total * kv_table[0, at, :] - swapped_pairs(total) * kv_table[1, at, :]
        )

    in_chunks(kv_total, 512)
    for i in range(8):
        rows = dkv_low[64 * i : 64 * (i + 1), :]
        rows = jnp.concatenate([rows[:, :HD], rows[:, HD:]], axis=0)
        at = slice(TOK * i, TOK * (i + 1))
        grads[at, Q_DEV:] = rows.astype(BF16)
        grads_t[Q_DEV:, at] = rows.T.astype(BF16)

    plane.along()

    def late_block(i, _):
        cols = pl.ds(pl.multiple_of(512 * i, 512), 512)
        rows = xs[:, :, cols].reshape(8 * TOK, 512)
        late[:, cols] = dot(grads_t[Q_DEV:, :], rows).astype(BF16)
        return 0

    ring = RingScatter(me, edges, parts, (g1, b1, r1, l1))

    def part(k):
        y = lax.rem(me.y + k, 4)
        rows = grads[pl.ds(pl.multiple_of(2 * TOK * y, 2 * TOK), 2 * TOK), :]

        def block(i, _):
            cols = pl.ds(pl.multiple_of(512 * i, 512), 512)
            to_chunks(parts, (y, y), (0, 1), cols, dot(rows, wq[:, cols]).astype(BF16))
            return 0

        lax.fori_loop(0, 4, block, 0)
        ring.send_core(k)

    part(2)
    part(1)
    ring.far()
    part(3)
    early_sum.cross()
    ring.near()
    lax.fori_loop(0, 4, late_block, 0)
    late_sum = SumOfSixteen(me, late, columns(128), late_own, late_got, us, ur, local.at[4])
    part(0)
    ring.add_core(0)
    early_sum.fourth()
    early_sum.total()
    plane.near()
    ring.second()
    wq_deliver = Deliver(me, ds, dr)

    def deliver_block(j, src, at):
        block = own_block(me, j)
        owner, slot = block // 5, lax.rem(block, 5)
        dst = wq_all.at[
            pl.ds(pl.multiple_of(64 * slot, 64), 64),
            pl.ds(pl.multiple_of(128 * at, 128), 128),
        ]
        wq_deliver.to_owner(src, dst, at // 8, owner // 2, lax.rem(owner, 2))

    wo_deliver = Deliver(me, es, er)
    early_place = 4 * lax.rem(me.z + me.y, 4) + x_of(me)
    early_turned = 4 * lax.rem(x_of(me) + me.y, 4) + me.z
    for i, at in enumerate((early_place, early_turned)):
        for j in (0, 1):
            deliver_block(2 * i + j, early_sum.out[i].at[pl.ds(64 * j, 64)], at)
        dst = wo_all.at[
            pl.ds(pl.multiple_of(Q_DEV * rank + 128 * i, 128), 128),
            pl.ds(pl.multiple_of(128 * lax.rem(at, 2), 128), 128),
        ]
        src = early_sum.out[i].at[pl.ds(128, 128)]
        wo_deliver.to_owner(src, dst, me.y // 2, at // 4, lax.rem(at // 2, 2))
    late_piece[...] = late_sum.total().astype(BF16)
    deliver_block(4, late_piece, place)
    branch.arrived()

    def out(at):
        output[at, :] = (middle[at, :] + branch.rows(at)).astype(BF16)

    in_chunks(out)
    ring.arrived()
    mine[...] = jnp.zeros_like(mine)
    mine[1:2, :] = gain_two[...]

    def back(at):
        rows = tokens[at, :].astype(F32)
        inverse = lax.rsqrt(mean_last(rows * rows) + EPSILON)
        normal = rows * inverse
        grad = ring.rows(at)
        mine[0:1, :] += jnp.sum(normal * grad, axis=0, keepdims=True)
        scaled = grad * gain[...]
        grad_tokens[at, :] = grad_middle[at, :] + inverse * (
            scaled - normal * mean_last(scaled * normal)
        )

    in_chunks(back)

    def slice_of(member):
        return mine.at[:, pl.ds(pl.multiple_of(256 * member, 256), 256)]

    near_copies = []
    for k in range(1, 8):
        dy, other = k // 2, k % 2
        y = lax.rem(me.y + dy, 4)
        to_core = 1 - me.c if other else me.c
        d = pltpu.make_async_remote_copy(
            src_ref=slice_of(2 * y + to_core),
            dst_ref=near.at[k - 1],
            send_sem=gs.at[k - 1],
            recv_sem=gr,
            device_id=me.at(y=y, core=to_core),
            device_id_type=pl.DeviceIdType.MESH,
        )
        d.start()
        near_copies.append(d)
    plane.far()
    own = mine[:, pl.ds(pl.multiple_of(256 * rank, 256), 256)]
    wait_got(near, gr)
    for k in range(7):
        own = own + near[k]
    near_sum[...] = own
    gain_deliver = Deliver(me, hs, hr)
    for to_core in (0, 1):
        gain_deliver.to_owner(near_sum, owners.at[place], to_core, me.y, me.c)

    half = pl.ds(pl.multiple_of(1024 * me.c, 1024), 1024)
    over = []
    for ref, sem in ((wo_all.at[half], er), (wq_all.at[:, half], dr)):
        wait_got(ref, sem)
        over.append(edges.copy(ref, ref, core))
    wait_got(owners, hr)
    sum_all = owners[0]
    for k in range(1, 16):
        sum_all = sum_all + owners[k]
    gains[...] = sum_all
    for d in over:
        d.wait_recv()
    wo_out[...] = wo_all[...]
    wq_out[...] = wq_all[...]
    plane.finish()
    late_sum.finish()
    for d in (wo_deliver, wq_deliver, gain_deliver):
        d.finish()
    for d in near_copies:
        d.wait_send()
    edges.finish()


def ending(
    dkv, dq, kv_table, wq, tokens, gain, grad_middle, gain_two, z_piece, x_piece, middle,
    gwo, xs, branch,
):
    many = pltpu.SemaphoreType.DMA
    return pl.pallas_call(
        ending_kernel,
        out_shape=(
            shape((TOK, D)),
            shape((TOK, D), F32),
            shape((8, 256), F32),
            shape((320, D)),
            shape((D, 256)),
            shape((PART, D)),
            shape((PART, D)),
        ),
        in_specs=[VMEM] * 11 + [ANY] * 3,
        out_specs=(VMEM,) * 5 + (ANY,) * 2,
        scratch_shapes=[
            pltpu.VMEM((8, 512, 128), BF16),
            pltpu.VMEM((8, 512, 128), BF16),
            pltpu.VMEM((7, 512, 128), BF16),
            pltpu.VMEM((512, 128), F32),
            pltpu.VMEM((8, TOK, D), BF16),
            pltpu.VMEM((1024, 320), BF16),
            pltpu.VMEM((320, 1024), BF16),
            pltpu.VMEM((8, TOK, D), BF16),
            pltpu.VMEM((8, TOK, D), BF16),
            pltpu.VMEM((512, D), BF16),
            pltpu.VMEM((64, D), BF16),
        ]
        + scatter_scratch() * 2
        + [
            pltpu.VMEM((320, D), BF16),
            pltpu.VMEM((D, 256), BF16),
            pltpu.VMEM((64, 128), BF16),
            pltpu.VMEM((15, 64, 128), BF16),
            pltpu.VMEM((64, 128), BF16),
            pltpu.VMEM((8, D), F32),
            pltpu.VMEM((7, 8, 256), F32),
            pltpu.VMEM((8, 256), F32),
            pltpu.VMEM((16, 8, 256), F32),
        ]
        + two_sums_scratch(EARLY_ROWS)
        + sems(15 + 2 * SCATTER_EDGES + PLANE_EDGES + 4 * SUM_EDGES + 2)
        + [many((40,)), many, many((16,)), many, many((2,)), many((2,))]
        + [many((7,)), many, many((16,)), many, many((15,)), many, many((5,))],
        compiler_params=pltpu.CompilerParams(
            collective_id=3, has_side_effects=True, vmem_limit_bytes=60 * 2**20
        ),
        name="ending",
    )(
        dkv, dq, kv_table, wq, tokens, gain, grad_middle, gain_two, z_piece, x_piece, middle,
        gwo, xs, branch,
    )


def widen_kernel(z_ref, x_ref, wq_ref, wo_ref, gu_ref, dn_ref, gq_ref, go_ref):
    i = pl.program_id(0)

    @pl.when(i < 3)
    def _():
        gu_ref[...] = z_ref[...].astype(F32)

    @pl.when(i == 3)
    def _():
        gu_ref[...] = x_ref[...].astype(F32)

    @pl.when(i > 3)
    def _():
        dn_ref[...] = x_ref[...].astype(F32)

    gq_ref[...] = wq_ref[...].astype(F32)
    go_ref[...] = wo_ref[...].astype(F32).T


def widen(z_all, x_all, wq, wo):
    rows = PART // 3
    return pl.pallas_call(
        widen_kernel,
        out_shape=(
            shape((2 * FF_DEV, D), F32),
            shape((FF_DEV, D), F32),
            shape((320, D), F32),
            shape((256, D), F32),
        ),
        grid=(6,),
        in_specs=[
            pl.BlockSpec((rows, D), lambda i: (jnp.minimum(i, 2), 0)),
            pl.BlockSpec((rows, D), lambda i: (jnp.maximum(i - 3, 0), 0)),
            pl.BlockSpec((64, D), lambda i: (jnp.minimum(i, 4), 0)),
            pl.BlockSpec((512, 256), lambda i: (jnp.minimum(i, 3), 0)),
        ],
        out_specs=(
            pl.BlockSpec((rows, D), lambda i: (jnp.minimum(i, 3), 0)),
            pl.BlockSpec((rows, D), lambda i: (jnp.maximum(i - 4, 0), 0)),
            pl.BlockSpec((64, D), lambda i: (jnp.minimum(i, 4), 0)),
            pl.BlockSpec((256, 512), lambda i: (0, jnp.minimum(i, 3))),
        ),
        compiler_params=pltpu.CompilerParams(vmem_limit_bytes=61 * 2**20),
        name="widen",
    )(z_all, x_all, wq, wo)


def route(dz):
    pairs = []
    for i in range(128):
        z, xl, c, y, xh = i // 32, i // 16 % 2, i // 8 % 2, i // 2 % 4, i % 2
        if c != xh:
            pairs.append((i, (((((z + dz) % 4) * 2 + xl) * 2 + c) * 4 + y) * 2 + xh))
    return pairs


def body(hidden, positions, gain_attn, w_qkv, w_out, gain_mlp, w_gate_up, w_down, cotangent):
    gain_one = gain_attn.astype(F32).reshape(1, D)
    gain_two = gain_mlp.astype(F32).reshape(1, D)
    wgu = w_gate_up.reshape(2 * FF_DEV, D)
    wdn = w_down.T
    query, kv_table, trigs, xs, wq, poss, kvs, places, cots, wo, wswap = begin(
        hidden[0],
        gain_one,
        jnp.broadcast_to(positions, (8, TOK)),
        rotary_rows(positions[0]),
        w_qkv,
        wgu,
        wdn,
        cotangent[0],
        w_out,
    )
    wo = wo.reshape(D, Q_DEV)
    query_runs = poss[:, 0, ::64].reshape(4, 2, 2).transpose(0, 2, 1).reshape(16) // 64
    key_runs = (
        places[:, :, 0, ::64].reshape(8, 4, 2, 2).transpose(1, 0, 2, 3).reshape(128) // 64
    )
    wnear_up = lax.ppermute(wswap, AXES, route(1))
    wnear_down = lax.ppermute(wswap, AXES, route(3))
    att, ot, lse = attend(key_runs, query_runs, query, kvs)
    middle, grad_middle, gain_grad, grad_att, grad_wo, z_piece, x_piece, branch = feed_forward(
        att, wo, hidden[0], cotangent[0], gain_two, cots, wgu, wdn, wswap, wnear_up, wnear_down
    )
    dq, dkv = attend_back(key_runs, query_runs, query, kvs, grad_att, ot, lse, trigs)
    output, grad_tokens, gains, grad_w_qkv, grad_w_out, z_all, x_all = ending(
        dkv,
        dq,
        kv_table,
        wq,
        hidden[0],
        gain_one,
        grad_middle,
        gain_grad,
        z_piece,
        x_piece,
        middle,
        grad_wo,
        xs,
        branch,
    )
    grad_gu, grad_dn, grad_w_qkv, grad_w_out = widen(z_all, x_all, grad_w_qkv, grad_w_out)
    return (
        output[None],
        grad_tokens[None],
        gains[0],
        grad_w_qkv,
        grad_w_out,
        gains[1],
        grad_gu.reshape(2, FF_DEV, D),
        grad_dn.T,
    )


def solution(mesh):
    fine = Mesh(mesh.devices.reshape(4, 2, 2, 4, 2), AXES)
    ctx, fsdp = ("z", "xl", "c"), ("y", "xh")
    weight = P(fsdp, None)
    return jax.shard_map(
        body,
        mesh=fine,
        in_specs=(
            P(fsdp, ctx, None),
            P(fsdp, ctx),
            P(),
            weight,
            weight,
            P(),
            P(None, fsdp, None),
            P(None, fsdp),
            P(fsdp, ctx, None),
        ),
        out_specs=(
            P(fsdp, ctx, None),
            P(fsdp, ctx, None),
            P(fsdp),
            weight,
            weight,
            P(fsdp),
            P(None, fsdp, None),
            P(None, fsdp),
        ),
        check_vma=False,
    )
```

```python
import jax
import jax.numpy as jnp
from jax import lax
from jax.experimental import pallas as pl
from jax.experimental.pallas import tpu as pltpu
from jax.sharding import Mesh
from jax.sharding import PartitionSpec as P

D = 2048
H = 32
KV = 4
HD = 64
FF = 5632
TOK = 128
HALF = 64
FF_DEV = 704
Q_DEV = 256
EPSILON = 1e-05
FILLER = -1e30
AXES = ("z", "xl", "c", "y", "xh")
ANY = pl.BlockSpec(memory_space=pl.ANY)
VMEM = pl.BlockSpec(memory_space=pltpu.VMEM)
BF16 = jnp.bfloat16
F32 = jnp.float32


class Place:
    def __init__(self):
        self.z, self.xl, self.c, self.y, self.xh = (lax.axis_index(a) for a in AXES)

    def at(self, dz=0, dy=0, core=None, xl=None, xh=None, y=None):
        z = lax.rem(self.z + dz + 4, 4) if dz else self.z
        y = (lax.rem(self.y + dy + 4, 4) if dy else self.y) if y is None else y
        return (
            z,
            self.xl if xl is None else xl,
            self.c if core is None else core,
            y,
            self.xh if xh is None else xh,
        )


class Edges:
    def __init__(self, send, recv):
        self.send, self.recv, self.count, self.started = send, recv, 0, []

    def copy(self, src, dst, device, start=True):
        i = self.count
        self.count += 1
        d = pltpu.make_async_remote_copy(
            src_ref=src,
            dst_ref=dst,
            send_sem=self.send.at[i],
            recv_sem=self.recv.at[i],
            device_id=device,
            device_id_type=pl.DeviceIdType.MESH,
        )
        self.started.append(d)
        if start:
            d.start()
        return d

    def sent(self, copies):
        for d in copies:
            d.wait_send()
        self.started = [d for d in self.started if all(d is not e for e in copies)]

    def finish(self):
        for d in self.started:
            d.wait_send()


def greet(devices):
    for device in devices:
        pl.semaphore_signal(
            pltpu.get_barrier_semaphore(),
            inc=1,
            device_id=device,
            device_id_type=pl.DeviceIdType.MESH,
        )
    return len(devices)


def met(count):
    pl.semaphore_wait(pltpu.get_barrier_semaphore(), count)


def group_members(me):
    found = [me.at(core=1 - me.c)]
    for dy in (1, 2, 3):
        found += [me.at(dy=dy), me.at(dy=dy, core=1 - me.c)]
    return found


class RingGather:
    def __init__(self, me, edges, own, out, local):
        self.me, self.edges, self.out = me, edges, out
        self.core = me.at(core=1 - me.c)
        self.up, self.down = me.at(dy=1), me.at(dy=-1)
        a, b = own.at[pl.ds(0, HALF)], own.at[pl.ds(HALF, HALF)]
        to_a, to_b = self.block(0, 0), self.block(0, 1)
        self.up_a = edges.copy(a, to_a, self.up)
        self.down_b = edges.copy(b, to_b, self.down)
        self.up_b = edges.copy(b, to_b, self.up)
        self.down_a = edges.copy(a, to_a, self.down)
        self.to_core = [edges.copy(a, to_a, self.core), edges.copy(b, to_b, self.core)]
        self.kept = [
            pltpu.make_async_copy(a, to_a, local.at[0]),
            pltpu.make_async_copy(b, to_b, local.at[1]),
        ]
        for d in self.kept:
            d.start()

    def block(self, dy, half):
        y = lax.rem(self.me.y + dy + 4, 4)
        rows = pl.ds(pl.multiple_of(HALF * self.me.c, HALF), HALF)
        return self.out.at[2 * y + half, rows]

    def pass_core(self, dy, half):
        ref = self.block(dy, half)
        self.to_core.append(self.edges.copy(ref, ref, self.core))

    def own(self):
        for d in self.kept:
            d.wait()
        self.from_core(0, 2)

    def relay(self):
        self.up_a.wait_recv()
        ref = self.block(-1, 0)
        self.on_a = self.edges.copy(ref, ref, self.up)
        self.pass_core(-1, 0)
        self.down_b.wait_recv()
        ref = self.block(1, 1)
        self.on_b = self.edges.copy(ref, ref, self.down)
        self.pass_core(1, 1)

    def near(self):
        self.up_b.wait_recv()
        self.pass_core(-1, 1)
        self.down_a.wait_recv()
        self.pass_core(1, 0)

    def far(self):
        self.on_a.wait_recv()
        self.pass_core(2, 0)
        self.on_b.wait_recv()
        self.pass_core(2, 1)

    def from_core(self, first, last):
        for d in self.to_core[first:last]:
            d.wait_recv()

    def rest(self):
        self.near()
        self.far()
        self.own()
        self.from_core(2, 8)

    def sources(self):
        return [self.up_a, self.up_b, self.down_a, self.down_b] + self.to_core[:2]


GATHER_EDGES = 14
GROUPS = (((0, 0), (0, 1)), ((3, 0), (1, 1)), ((3, 1), (1, 0)), ((2, 0), (2, 1)))


class RingScatter:
    def __init__(self, me, edges, parts, scratch):
        self.me, self.edges, self.parts = me, edges, parts
        self.got, self.both, self.relayed, self.last = scratch
        self.up, self.down = me.at(dy=1), me.at(dy=-1)
        self.cores = {}
        self.a, self.b = pl.ds(0, HALF), pl.ds(HALF, HALF)

    def send_core(self, k):
        row = 2 * lax.rem(self.me.y + k, 4) + 1 - self.me.c
        core = self.me.at(core=1 - self.me.c)
        self.cores[k] = self.edges.copy(self.parts.at[row], self.got.at[k], core)

    def add_core(self, k):
        self.cores[k].wait_recv()
        row = 2 * lax.rem(self.me.y + k, 4) + self.me.c

        def add(at):
            self.both[k, at] = (
                self.parts[row, at].astype(F32) + self.got[k, at].astype(F32)
            ).astype(BF16)

        in_chunks(add)

    def far(self):
        self.add_core(2)
        e, both = self.edges, self.both
        self.r_a = e.copy(both.at[2, self.a], self.relayed.at[0], self.up)
        self.r_b = e.copy(both.at[2, self.b], self.relayed.at[1], self.down)

    def near(self):
        e, both = self.edges, self.both
        self.add_core(1)
        self.u_b = e.copy(both.at[1, self.b], self.last.at[0, self.b], self.up)
        self.add_core(3)
        self.d_a = e.copy(both.at[3, self.a], self.last.at[1, self.a], self.down)

    def first(self):
        for k in (2, 1, 3, 0):
            self.send_core(k)
        self.far()
        self.near()
        self.add_core(0)

    def second(self):
        a, b, e, both = self.a, self.b, self.edges, self.both
        self.r_a.wait_recv()
        both[1, a] = (both[1, a].astype(F32) + self.relayed[0].astype(F32)).astype(BF16)
        self.u_a = e.copy(both.at[1, a], self.last.at[0, a], self.up)
        self.r_b.wait_recv()
        both[3, b] = (both[3, b].astype(F32) + self.relayed[1].astype(F32)).astype(BF16)
        self.d_b = e.copy(both.at[3, b], self.last.at[1, b], self.down)

    def arrived(self):
        for d in (self.u_b, self.d_a, self.u_a, self.d_b):
            d.wait_recv()

    def rows(self, at):
        return (
            self.both[0, at].astype(F32)
            + self.last[0, at].astype(F32)
            + self.last[1, at].astype(F32)
        )

    def release(self):
        ring = [self.r_a, self.r_b, self.u_b, self.d_a, self.u_a, self.d_b]
        self.edges.sent(ring + list(self.cores.values()))


SCATTER_EDGES = 10


def scatter_scratch():
    return [
        pltpu.VMEM((4, TOK, D), BF16),
        pltpu.VMEM((4, TOK, D), BF16),
        pltpu.VMEM((2, HALF, D), BF16),
        pltpu.VMEM((2, TOK, D), BF16),
    ]


def sems(n):
    return [pltpu.SemaphoreType.DMA((n,)), pltpu.SemaphoreType.DMA((n,))]


def shape(dims, dtype=BF16):
    return jax.ShapeDtypeStruct(dims, dtype)


def remote_params(number):
    return pltpu.CompilerParams(
        collective_id=number, has_side_effects=True, vmem_limit_bytes=61 * 2**20
    )


def block_place(block):
    is_kv = block >= 32
    other = block - 32
    rank = block // 4
    y = jnp.where(is_kv, lax.rem(other + 32, 4), rank // 2)
    core = jnp.where(is_kv, other // 4, lax.rem(rank, 2))
    return y, core, jnp.where(is_kv, 4, lax.rem(block, 4))


def own_block(me, j):
    if j == 4:
        return 32 + 4 * me.c + me.y
    return 4 * (2 * me.y + me.c) + j


def send_block(me, src, dst, send_sem, recv_sem, target, stays):
    @pl.when(stays)
    def _():
        pltpu.make_async_copy(src, dst, recv_sem).start()

    @pl.when(jnp.logical_not(stays))
    def _():
        pltpu.make_async_remote_copy(
            src_ref=src,
            dst_ref=dst,
            send_sem=send_sem,
            recv_sem=recv_sem,
            device_id=target,
            device_id_type=pl.DeviceIdType.MESH,
        ).start()


def wait_sent(src, send_sem, stays):
    @pl.when(jnp.logical_not(stays))
    def _():
        pltpu.make_async_copy(src, src, send_sem).wait()


def wait_got(dst, recv_sem):
    pltpu.make_async_copy(dst, dst, recv_sem).wait()


def x_of(me):
    return 2 * me.xh + me.xl


def around(me, dz, dx):
    x = lax.rem(x_of(me) + dx, 4)
    return me.at(dz=dz, xl=lax.rem(x, 2), xh=x // 2)


STEPS = [(dz, dx) for dz in range(4) for dx in range(4)][1:]


class SumOfSixteen:
    def __init__(self, me, src, piece, own, got, send, recv, local):
        self.me, self.src, self.piece, self.own, self.got = me, src, piece, own, got
        self.send, self.recv = send, recv
        self.keep = pltpu.make_async_copy(
            src.at[piece(4 * me.z + x_of(me))], own, local
        )
        self.keep.start()
        for k, (dz, dx) in enumerate(STEPS):
            to = 4 * lax.rem(me.z + dz, 4) + lax.rem(x_of(me) + dx, 4)
            self.copy(src.at[piece(to)], k, around(me, dz, dx)).start()

    def copy(self, src, k, device):
        return pltpu.make_async_remote_copy(
            src_ref=src,
            dst_ref=self.got.at[k],
            send_sem=self.send.at[k],
            recv_sem=self.recv,
            device_id=device,
            device_id_type=pl.DeviceIdType.MESH,
        )

    def total(self):
        self.keep.wait()
        pltpu.make_async_copy(self.got, self.got, self.recv).wait()
        total = self.own[...].astype(F32)
        for k in range(15):
            total = total + self.got[k].astype(F32)
        return total

    def finish(self):
        for k in range(15):
            src = self.src.at[self.piece(0)]
            pltpu.make_async_copy(src, src, self.send.at[k]).wait()


def same(me, z, xl, core, y, xh):
    return (z == me.z) & (xl == me.xl) & (core == me.c) & (y == me.y) & (xh == me.xh)


class Deliver:
    def __init__(self, me, send, recv):
        self.me, self.send, self.recv, self.sent = me, send, recv, []

    def to_owner(self, src, dst, core, y, xh):
        me = self.me
        for dz in range(4):
            for dl in (0, 1):
                z = lax.rem(me.z + dz, 4)
                xl = 1 - me.xl if dl else me.xl
                stays = same(me, z, xl, core, y, xh)
                sem = self.send.at[len(self.sent)]
                send_block(me, src, dst, sem, self.recv, (z, xl, core, y, xh), stays)
                self.sent.append((src, sem, stays))

    def finish(self):
        for src, sem, stays in self.sent:
            wait_sent(src, sem, stays)


def rotary_rows(places):
    steps = jnp.arange(HD // 2, dtype=F32)
    inverse = jnp.power(10000.0, steps * (-2.0 / HD))
    turning = places.astype(F32)[:, None] * inverse[None, :]
    rows = jnp.concatenate([jnp.cos(turning), jnp.sin(turning)], axis=1)
    return rows.reshape(2, 64, HD).transpose(1, 0, 2).reshape(64, 2 * HD)


def halves_swapped(rows):
    return jnp.concatenate([rows[:, HD // 2 :], rows[:, : HD // 2]], axis=1)


def rotate(rows, table, back=False):
    turned = halves_swapped(rows) * table[:, HD:]
    return rows * table[:, :HD] + (-turned if back else turned)


def rotary_of(rows, u):
    cosine = rows[:, HD * u : HD * u + HD // 2]
    sine = rows[:, HD * u + HD // 2 : HD * u + HD]
    return jnp.concatenate([cosine, cosine, -sine, sine], axis=1)


ROWS = 16


def in_chunks(step, rows=TOK):
    def one(i, _):
        step(pl.ds(pl.multiple_of(i * ROWS, ROWS), ROWS))
        return 0

    lax.fori_loop(0, rows // ROWS, one, 0)


def mean_last(rows):
    return jnp.mean(rows, axis=-1, keepdims=True)


GU_QUARTER = 2 * FF_DEV // 4
DN_QUARTER = FF_DEV // 4
QUARTER = GU_QUARTER + DN_QUARTER


def swap_copies(me, wgu, wdn, wswap, send, recv):
    found = []
    across = me.at(core=1 - me.c, xl=1 - me.xl, xh=1 - me.xh)
    for i, (src, rows, start) in enumerate(
        ((wgu, GU_QUARTER, 0), (wdn, DN_QUARTER, GU_QUARTER))
    ):
        found.append(
            pltpu.make_async_remote_copy(
                src_ref=src.at[pl.ds(pl.multiple_of(rows * me.z, 16), rows)],
                dst_ref=wswap.at[pl.ds(start, rows)],
                send_sem=send.at[i],
                recv_sem=recv.at[i],
                device_id=across,
                device_id_type=pl.DeviceIdType.MESH,
            )
        )
    return found


def chips_in_sequence(me):
    return [(dz, dl) for dz in range(4) for dl in (0, 1)][1:]


def begin_kernel(
    tokens, gain, pos, trig, wqkv, wgu, wdn, cot, wout,
    q, kv_table, trigs, runs, xs_out, wq_out, kvs, places, cots, wo, wswap,
    low, xs, wq, kv, poss, own_runs,
    send, recv, qs, qr, os_, orr, ws, wr, local,
):
    me = Place()
    partner = {"xl": 1 - me.xl, "xh": 1 - me.xh}
    core = me.at(core=1 - me.c)
    members = group_members(me)
    others = [
        me.at(y=lax.rem(me.y + dy, 4), core=c, **partner) for dy in range(4) for c in (0, 1)
    ]
    far = [
        me.at(dz=dz, xl=(1 - me.xl) if dl else me.xl) for dz, dl in chips_in_sequence(me)
    ]
    signalled = greet(members + others + far)
    edges = Edges(send, recv)
    mine = 2 * me.y + me.c
    chip = 2 * me.z + me.xl

    def norm_rows():
        def norm(at):
            rows = tokens[at, :].astype(F32)
            inverse = lax.rsqrt(mean_last(rows * rows) + EPSILON)
            low[at, :] = (rows * inverse * gain[...]).astype(BF16)

        in_chunks(norm)

    spread = pl.ds(pl.multiple_of(512 * me.z, 512), 512)
    spread_rows = pl.ds(pl.multiple_of(64 * me.z, 64), 64)
    own = 2 * me.y + me.xh
    own_column = me.c == 0
    to_xl = jnp.where(own_column, me.xl, 1 - me.xl)
    to_xh = jnp.where(own_column, me.xh, 1 - me.xh)
    norm_rows()
    met(signalled)
    blocks = []
    for i in range(5):
        y, to_core, slot = block_place(5 * own + i)
        stays = own_column & (y == me.y) & (to_core == me.c)
        src = wqkv.at[pl.ds(64 * i, 64), spread]
        dst = wq.at[pl.ds(pl.multiple_of(64 * slot, 64), 64), spread]
        target = (me.z, to_xl, to_core, y, to_xh)
        send_block(me, src, dst, qs.at[i], qr.at[slot], target, stays)
        blocks.append((src, qs.at[i], stays))

    lane = lax.broadcasted_iota(jnp.int32, (8, TOK), 1)
    first = 4 * me.y + me.c
    run_numbers = jnp.where(
        lane == first,
        jnp.broadcast_to(pos[:, 0:1], (8, TOK)),
        jnp.where(lane == first + 2, jnp.broadcast_to(pos[:, 64:65], (8, TOK)), 0),
    )
    own_runs[...] = lax.shift_right_logical(run_numbers, 6)
    keep_pos = pltpu.make_async_copy(own_runs, poss.at[mine], local.at[1])
    keep_pos.start()
    pos_copies = [edges.copy(own_runs, poss.at[mine], m) for m in members]
    trigs[mine] = trig[...]
    trig_copies = [edges.copy(trig, trigs.at[mine], me.at(dy=k)) for k in (1, 2, 3)]
    trig_over = [edges.copy(trig, trigs.at[mine], core)]
    ring = RingGather(me, edges, low, xs, local.at[pl.ds(6, 2)])
    for i in range(8):
        dy, other = i // 2, i % 2
        y = lax.rem(me.y + dy, 4)
        to_core = me.c if other == 0 else 1 - me.c
        stays = own_column if i == 0 else me.c < 0
        cols = pl.ds(pl.multiple_of(Q_DEV * (2 * y + to_core), Q_DEV), Q_DEV)
        src = wout.at[spread_rows, cols]
        dst = wo.at[own, spread_rows]
        target = (me.z, to_xl, to_core, y, to_xh)
        send_block(me, src, dst, os_.at[i], orr.at[own], target, stays)
        blocks.append((src, os_.at[i], stays))
    moved = me.c != me.xh
    swaps = swap_copies(me, wgu, wdn, wswap, ws, wr)

    @pl.when(moved)
    def _():
        for d in swaps:
            d.start()

    for i in range(5):
        wait_got(wq.at[pl.ds(64 * i, 64), spread], qr.at[i])
    wq_copies = [
        edges.copy(wq.at[:, spread], wq.at[:, spread], me.at(dz=k)) for k in (1, 3, 2)
    ]
    for k, d in zip((1, 2, 3), trig_copies):
        d.wait_recv()
        ref = trigs.at[2 * lax.rem(me.y - k + 4, 4) + me.c]
        trig_over.append(edges.copy(ref, ref, core))
    ring.relay()
    for i in range(8):
        wait_got(wo.at[i, spread_rows], orr.at[i])
    ref = wo.at[:, spread_rows]
    wo_copies = [edges.copy(ref, ref, me.at(dz=k)) for k in (1, 3, 2)]
    keep_pos.wait()
    for d in pos_copies + trig_over:
        d.wait_recv()
    combined = poss[0]
    for i in range(1, 8):
        combined = combined + poss[i]
    runs[...] = combined
    for d in wq_copies:
        d.wait_recv()
    wq_save = pltpu.make_async_copy(wq, wq_out, local.at[2])
    wq_save.start()
    is_key = me.c == 0

    def compute(group):
        ys = [lax.rem(me.y + dy, 4) for dy, _ in group]
        rows = [xs[2 * y + u] for y, (_, u) in zip(ys, group)]
        projected = dot_last(jnp.concatenate(rows, axis=0), wq[...])
        for i, (y, (_, u)) in enumerate(zip(ys, group)):
            for half in (0, 1):
                rows = rotary_of(trigs[2 * y + half], u)
                at = TOK * i + 64 * half
                values = projected[at : at + 64]
                heads = [rotate(values[:, HD * h : HD * h + HD], rows) for h in range(4)]
                query = jnp.concatenate(heads, axis=1).astype(BF16)
                to = pl.ds(pl.multiple_of(2 * TOK * y + TOK * u + 64 * half, 64), 64)
                q[to, :] = (query.astype(F32) * 0.125).astype(BF16)
                rows = jnp.concatenate(
                    [
                        jnp.where(is_key, rows[:, :HD], 1.0),
                        jnp.where(is_key, rows[:, HD:], 0.0),
                    ],
                    axis=1,
                )
                to = pl.ds(pl.multiple_of(TOK * y + 64 * u, 64), 64)
                lanes = slice(HD * half, HD * half + HD)
                kv[to, lanes] = rotate(values[:, Q_DEV:], rows).astype(BF16)
                kv_table[0, to, lanes] = rows[:, :HD]
                kv_table[1, to, lanes] = rows[:, HD:]

    ring.own()
    compute(GROUPS[0])
    ring.near()
    ring.from_core(2, 4)
    compute(GROUPS[1])
    ring.from_core(4, 6)
    ring.far()
    compute(GROUPS[2])
    ring.from_core(6, 8)
    compute(GROUPS[3])

    keeps = [
        pltpu.make_async_copy(kv, kvs.at[me.c, chip], local.at[0]),
        pltpu.make_async_copy(runs, places.at[chip], local.at[1]),
        pltpu.make_async_copy(xs, xs_out, local.at[4]),
    ]
    for d in keeps:
        d.start()
    pos_copies = [edges.copy(runs, places.at[chip], d) for d in far]
    kv_copies = [edges.copy(kv, kvs.at[me.c, chip], d) for d in far]
    over = [edges.copy(kv, kvs.at[me.c, chip], core)]
    ring = RingGather(me, edges, cot, cots, local.at[pl.ds(6, 2)])
    ring.relay()
    for (dz, dl), d in zip(chips_in_sequence(me), kv_copies):
        d.wait_recv()
        source = 2 * lax.rem(me.z - dz + 4, 4) + ((1 - me.xl) if dl else me.xl)
        ref = kvs.at[me.c, source]
        over.append(edges.copy(ref, ref, core))
    ring.rest()
    for d in over + pos_copies + wo_copies:
        d.wait_recv()
    for src, sem, stays in blocks:
        wait_sent(src, sem, stays)

    @pl.when(moved)
    def _():
        for d in swaps:
            d.wait()

    edges.finish()
    for d in keeps + [wq_save]:
        d.wait()


def begin(tokens, gain, pos, trig, wqkv, wgu, wdn, cot, wout):
    return pl.pallas_call(
        begin_kernel,
        out_shape=(
            shape((1024, Q_DEV)),
            shape((2, 512, 128), F32),
            shape((8, 64, 128), F32),
            shape((8, TOK), jnp.int32),
            shape((8, TOK, D)),
            shape((320, D)),
            shape((2, 8, 512, 128)),
            shape((8, 8, TOK), jnp.int32),
            shape((8, TOK, D)),
            shape((8, 256, Q_DEV)),
            shape((QUARTER, D)),
        ),
        in_specs=[VMEM, VMEM, VMEM, VMEM] + [ANY] * 5,
        out_specs=(VMEM, VMEM, VMEM, VMEM) + (ANY,) * 7,
        scratch_shapes=[
            pltpu.VMEM((TOK, D), BF16),
            pltpu.VMEM((8, TOK, D), BF16),
            pltpu.VMEM((320, D), BF16),
            pltpu.VMEM((512, 128), BF16),
            pltpu.VMEM((8, 8, TOK), jnp.int32),
            pltpu.VMEM((8, TOK), jnp.int32),
        ]
        + sems(7 + 7 + 6 + 2 * GATHER_EDGES + 7 + 7 + 8)
        + sems(5)
        + sems(8)
        + sems(2)
        + [pltpu.SemaphoreType.DMA((8,))],
        compiler_params=remote_params(0),
        name="begin",
    )(tokens, gain, pos, trig, wqkv, wgu, wdn, cot, wout)


def split_heads(rows):
    return jnp.concatenate([rows[:, HD * h : HD * (h + 1)] for h in range(4)], axis=0)


def join_heads(rows):
    return jnp.concatenate([rows[64 * h : 64 * (h + 1), :] for h in range(4)], axis=1)


def dot_last(a, b):
    return lax.dot_general(a, b, (((1,), (1,)), ((), ())), preferred_element_type=F32)


def dot_first(a, b):
    return lax.dot_general(a, b, (((0,), (0,)), ((), ())), preferred_element_type=F32)


def dot(a, b):
    return lax.dot_general(a, b, (((1,), (0,)), ((), ())), preferred_element_type=F32)


TILE = 256
WIDE = 8


def run_rows(runs, seq, chip, core, u):
    run = runs[16 * chip + 4 * seq + 2 * u + core]
    return pl.ds(pl.multiple_of(run * 64, 64), 64)


def sort_keys(runs, seq, kv_ref, sorted_kv):
    for j in range(32):
        chip, core, u = j // 4, (j // 2) % 2, j % 2
        to = run_rows(runs, seq, chip, core, u)
        rows, lanes = slice(64 * u, 64 * u + 64), slice(HD * core, HD * core + HD)
        both = [kv_ref[0, chip, rows, lanes], kv_ref[1, chip, rows, lanes]]
        sorted_kv[to, :] = jnp.concatenate(both, axis=1)


def turn(rows, lanes, turned):
    for i in range(4):
        at = slice(512 * i, 512 * (i + 1))
        turned[:, at] = rows[at, lanes].astype(F32).T.astype(BF16)


def allowed_tile(tile, run):
    key = lax.broadcasted_iota(jnp.int32, (TILE, 256), 0) + tile * TILE
    query = lax.rem(lax.broadcasted_iota(jnp.int32, (TILE, 256), 1), 64) + run * 64
    return key <= query


def tile_rows(tile):
    return pl.ds(pl.multiple_of(tile * TILE, TILE), TILE)


def attend_kernel(
    key_runs, query_runs, q_ref, kv_ref, att_ref, ot_ref, lse_ref,
    sorted_kv, values_t, high_ref, total_ref, acc_ref,
):
    seq = pl.program_id(0)
    sort_keys(key_runs, seq, kv_ref, sorted_kv)
    turn(sorted_kv, slice(HD, 2 * HD), values_t)
    empty = jnp.zeros((HD, 256), BF16)

    def one_run(r, _):
        run = query_runs[seq * 4 + r]
        rows = pl.ds(pl.multiple_of(r * 64, 64), 64)
        query = split_heads(q_ref[rows, :]).astype(F32).T.astype(BF16)
        query = jnp.concatenate([query, empty], axis=0)
        last = run // 4
        high_ref[...] = jnp.full((1, 256), FILLER, F32)
        total_ref[...] = jnp.zeros((1, 256), F32)
        acc_ref[...] = jnp.zeros((HD, 256), F32)

        def tiles(first, count, masked):
            scores = []
            for k in range(count):
                score = dot(sorted_kv[tile_rows(first + k), :], query)
                if masked and k == count - 1:
                    score = jnp.where(allowed_tile(first + k, run), score, FILLER)
                scores.append(score)
            high = high_ref[...]
            new_high = high
            for score in scores:
                new_high = jnp.maximum(new_high, jnp.max(score, axis=0, keepdims=True))
            scale = jnp.exp(high - new_high)
            total = total_ref[...] * scale
            acc = acc_ref[...] * scale
            for k, score in enumerate(scores):
                weights = jnp.exp(score - new_high)
                total = total + jnp.sum(weights, axis=0, keepdims=True)
                acc = acc + dot(values_t[:, tile_rows(first + k)], weights.astype(BF16))
            high_ref[...] = new_high
            total_ref[...] = total
            acc_ref[...] = acc

        for n in range(WIDE):

            @pl.when(last == n)
            def _():
                tiles(0, n + 1, True)

        total = total_ref[...]
        out = acc_ref[...] / total
        ot_ref[r] = out
        lse_ref[r] = high_ref[...] + jnp.log(total)
        att_ref[rows, :] = join_heads(out.T).astype(BF16)
        return 0

    lax.fori_loop(0, 4, one_run, 0)


def attend(key_runs, query_runs, q, kv):
    return pl.pallas_call(
        attend_kernel,
        out_shape=(shape((1024, 256)), shape((16, HD, 256), F32), shape((16, 1, 256), F32)),
        grid_spec=pltpu.PrefetchScalarGridSpec(
            num_scalar_prefetch=2,
            grid=(4,),
            in_specs=[
                pl.BlockSpec((256, 256), lambda i, *_: (i, 0)),
                pl.BlockSpec((2, 8, 128, 128), lambda i, *_: (0, 0, i, 0)),
            ],
            out_specs=[
                pl.BlockSpec((256, 256), lambda i, *_: (i, 0)),
                pl.BlockSpec((4, HD, 256), lambda i, *_: (i, 0, 0)),
                pl.BlockSpec((4, 1, 256), lambda i, *_: (i, 0, 0)),
            ],
            scratch_shapes=[
                pltpu.VMEM((2048, 2 * HD), BF16),
                pltpu.VMEM((HD, 2048), BF16),
                pltpu.VMEM((1, 256), F32),
                pltpu.VMEM((1, 256), F32),
                pltpu.VMEM((HD, 256), F32),
            ],
        ),
        compiler_params=pltpu.CompilerParams(vmem_limit_bytes=61 * 2**20),
        name="attend",
    )(key_runs, query_runs, q, kv)


def attend_back_kernel(
    key_runs, query_runs, q_ref, kv_ref, da_ref, ot_ref, lse_ref, trig_ref,
    dq_ref, dkv_ref, sorted_kv, keys_t, grad_kv, dq_acc,
):
    seq = pl.program_id(0)
    sort_keys(key_runs, seq, kv_ref, sorted_kv)
    turn(sorted_kv, slice(0, HD), keys_t)
    grad_kv[...] = jnp.zeros_like(grad_kv)
    empty = jnp.zeros((HD, 256), BF16)
    blank = jnp.zeros((256, HD), BF16)

    def one_run(r, _):
        run = query_runs[seq * 4 + r]
        rows = pl.ds(pl.multiple_of(r * 64, 64), 64)
        query = split_heads(q_ref[rows, :])
        grad = split_heads(da_ref[rows, :])
        lse = lse_ref[r]
        query_t = query.astype(F32).T.astype(BF16)
        grad_t = grad.astype(F32).T
        delta = jnp.sum(grad_t * ot_ref[r], axis=0, keepdims=True)
        query_t = jnp.concatenate([query_t, empty], axis=0)
        grad_t = jnp.concatenate([empty, grad_t.astype(BF16)], axis=0)
        right = jnp.concatenate(
            [
                jnp.concatenate([query, blank], axis=1),
                jnp.concatenate([blank, grad], axis=1),
            ],
            axis=0,
        )
        last = run // 4
        dq_acc[...] = jnp.zeros((HD, 256), F32)

        def tiles(first, count, masked):
            dq = dq_acc[...]
            for k in range(count):
                at = tile_rows(first + k)
                both = sorted_kv[at, :]
                probs = jnp.exp(dot(both, query_t) - lse)
                if masked and k == count - 1:
                    probs = jnp.where(allowed_tile(first + k, run), probs, 0.0)
                grad_probs = dot(both, grad_t)
                grad_scores = (probs * (grad_probs - delta)).astype(BF16)
                left = jnp.concatenate([grad_scores, probs.astype(BF16)], axis=1)
                grad_kv[at, :] += dot(left, right)
                dq = dq + dot(keys_t[:, at], grad_scores)
            dq_acc[...] = dq

        for n in range(WIDE):

            @pl.when(last == n)
            def _():
                tiles(0, n + 1, True)

        pair_rows = trig_ref[lax.rem(r, 2)]
        table = jnp.where(r < 2, rotary_of(pair_rows, 0), rotary_of(pair_rows, 1))
        dq = (dq_acc[...] * 0.125).T
        heads = [rotate(dq[64 * h : 64 * h + 64], table, back=True) for h in range(4)]
        dq_ref[rows, :] = jnp.concatenate(heads, axis=1).astype(BF16)
        return 0

    lax.fori_loop(0, 4, one_run, 0)
    for j in range(32):
        chip, core, u = j // 4, (j // 2) % 2, j % 2
        at = run_rows(key_runs, seq, chip, core, u)
        rows, lanes = slice(64 * u, 64 * u + 64), slice(HD * core, HD * core + HD)
        both = grad_kv[at, :].astype(BF16)
        dkv_ref[0, chip, rows, lanes] = both[:, :HD]
        dkv_ref[1, chip, rows, lanes] = both[:, HD:]


def attend_back(key_runs, query_runs, q, kv, grad, ot, lse, trigs):
    return pl.pallas_call(
        attend_back_kernel,
        out_shape=(shape((1024, 256)), shape((2, 8, 512, 128))),
        grid_spec=pltpu.PrefetchScalarGridSpec(
            num_scalar_prefetch=2,
            grid=(4,),
            in_specs=[
                pl.BlockSpec((256, 256), lambda i, *_: (i, 0)),
                pl.BlockSpec((2, 8, 128, 128), lambda i, *_: (0, 0, i, 0)),
                pl.BlockSpec((256, 256), lambda i, *_: (i, 0)),
                pl.BlockSpec((4, HD, 256), lambda i, *_: (i, 0, 0)),
                pl.BlockSpec((4, 1, 256), lambda i, *_: (i, 0, 0)),
                pl.BlockSpec((2, 64, 128), lambda i, *_: (i, 0, 0)),
            ],
            out_specs=[
                pl.BlockSpec((256, 256), lambda i, *_: (i, 0)),
                pl.BlockSpec((2, 8, 128, 128), lambda i, *_: (0, 0, i, 0)),
            ],
            scratch_shapes=[
                pltpu.VMEM((2048, 2 * HD), BF16),
                pltpu.VMEM((HD, 2048), BF16),
                pltpu.VMEM((2048, 2 * HD), F32),
                pltpu.VMEM((HD, 256), F32),
            ],
        ),
        compiler_params=pltpu.CompilerParams(vmem_limit_bytes=61 * 2**20),
        name="attend_back",
    )(key_runs, query_runs, q, kv, grad, ot, lse, trigs)


PART = 3 * FF_DEV // 2
PART_HALF = PART // 2


class RingSum:
    def __init__(
        self, me, edges, along_z, src, start, rows, width, step, relayed, last, shift=0
    ):
        self.edges, self.src, self.start, self.width, self.step = edges, src, start, width, step
        self.rows, self.half = rows, rows // 2
        self.relayed, self.last, self.shift = relayed, last, shift
        self.here = me.z if along_z else x_of(me)
        self.up = around(me, 1, 0) if along_z else around(me, 0, 1)
        self.down = around(me, -1, 0) if along_z else around(me, 0, 3)
        self.a, self.b = pl.ds(0, self.half), pl.ds(self.half, self.half)

    def columns(self, k):
        at = self.width * lax.rem(self.here + k + self.shift, 4)
        return pl.ds(pl.multiple_of(at, self.width), self.width)

    def piece(self, k, half):
        rows = pl.ds(self.start + self.half * half, self.half)
        return self.src.at[rows, self.columns(k)]

    def far(self):
        self.r_a = self.edges.copy(self.piece(2, 0), self.relayed.at[0], self.up)
        self.r_b = self.edges.copy(self.piece(2, 1), self.relayed.at[1], self.down)

    def near_up(self):
        self.u_b = self.edges.copy(self.piece(1, 1), self.last.at[0, self.b], self.up)

    def near_down(self):
        self.d_a = self.edges.copy(self.piece(3, 0), self.last.at[1, self.a], self.down)

    def add(self, k, half):
        step, start, cols = self.step, self.start + self.half * half, self.columns(k)

        def one(i, _):
            at = pl.ds(pl.multiple_of(start + i * step, 16), step)
            from_ = pl.ds(pl.multiple_of(i * step, 16), step)
            self.src[at, cols] = (
                self.src[at, cols].astype(F32) + self.relayed[half, from_, :].astype(F32)
            ).astype(BF16)
            return 0

        lax.fori_loop(0, self.half // step, one, 0)

    def second(self):
        self.r_a.wait_recv()
        self.add(1, 0)
        self.u_a = self.edges.copy(self.piece(1, 0), self.last.at[0, self.a], self.up)
        self.r_b.wait_recv()
        self.add(3, 1)
        self.d_b = self.edges.copy(self.piece(3, 1), self.last.at[1, self.b], self.down)

    def total(self, out):
        for d in (self.u_b, self.d_a, self.u_a, self.d_b):
            d.wait_recv()
        step, cols = self.step, self.columns(0)

        def one(i, _):
            at = pl.ds(pl.multiple_of(self.start + i * step, 16), step)
            from_ = pl.ds(pl.multiple_of(i * step, 16), step)
            out[from_, :] = (
                self.src[at, cols].astype(F32)
                + self.last[0, from_, :].astype(F32)
                + self.last[1, from_, :].astype(F32)
            ).astype(BF16)
            return 0

        lax.fori_loop(0, self.rows // step, one, 0)


SUM_EDGES = 6


def to_chunks(ref, ys, halves, cols, rows):
    for i, (y, half) in enumerate(zip(ys, halves)):
        for core in (0, 1):
            at = TOK * i + HALF * core
            ref[2 * y + core, HALF * half : HALF * half + HALF, cols] = rows[at : at + HALF]


def feed_forward_kernel(
    att, wo, tokens, cot, gain, cots, wgu, wdn, wswap, wnear_up, wnear_down,
    middle, grad_middle, gain_grad, grad_att, grad_wo, z_out, x_out, branch,
    xs, p, c, gp, gb, att_t, w, act_t, gate_t, up_t, act, dgate, dup, low,
    g1, b1, r1, l1,
    z_relayed, z_last, x_relayed, x_last, z_q, x_q,
    z_relayed2, z_last2, x_relayed2, x_last2,
    send, recv, fs, fr, local,
):
    me = Place()
    core = me.at(core=1 - me.c)
    signalled = greet(
        [core, me.at(dy=1), me.at(dy=-1)]
        + [around(me, k, 0) for k in (1, 2, 3)]
        + [around(me, 0, 1), around(me, 0, 3)]
    )
    edges = Edges(send, recv)
    moved = me.c != me.xh
    load_c = pltpu.make_async_copy(cots, c, local.at[1])
    load_c.start()

    def w_rows(dz):
        z = lax.rem(me.z + dz + 4, 4)
        return (
            pl.ds(pl.multiple_of(GU_QUARTER * z, 16), GU_QUARTER),
            pl.ds(pl.multiple_of(2 * FF_DEV + DN_QUARTER * z, 16), DN_QUARTER),
        )

    gu_part, dn_part = pl.ds(0, GU_QUARTER), pl.ds(GU_QUARTER, DN_QUARTER)
    kept = [
        pltpu.make_async_copy(wgu, w.at[pl.ds(0, 2 * FF_DEV)], local.at[2]),
        pltpu.make_async_copy(wdn, w.at[pl.ds(2 * FF_DEV, FF_DEV)], local.at[3]),
    ]
    near_w = []
    for i, (src, dz) in enumerate(((wswap, 0), (wnear_up, -1), (wnear_down, 1))):
        gu_rows, dn_rows = w_rows(dz)
        near_w.append(pltpu.make_async_copy(src.at[gu_part], w.at[gu_rows], local.at[4 + 2 * i]))
        near_w.append(pltpu.make_async_copy(src.at[dn_part], w.at[dn_rows], local.at[5 + 2 * i]))
    far_w = [
        pltpu.make_async_remote_copy(
            src_ref=wswap.at[part],
            dst_ref=w.at[rows],
            send_sem=fs.at[i],
            recv_sem=fr.at[i],
            device_id=me.at(dz=2),
            device_id_type=pl.DeviceIdType.MESH,
        )
        for i, (part, rows) in enumerate(zip((gu_part, dn_part), w_rows(0)))
    ]

    met(signalled)

    @pl.when(moved)
    def _():
        for d in far_w + near_w:
            d.start()

    @pl.when(jnp.logical_not(moved))
    def _():
        for d in kept:
            d.start()

    ring = RingScatter(me, edges, p, (g1, b1, r1, l1))

    def attended_part(k):
        y = lax.rem(me.y + k, 4)
        rows = att[pl.ds(pl.multiple_of(2 * TOK * y, 2 * TOK), 2 * TOK), :]

        def block(i, _):
            cols = pl.ds(pl.multiple_of(512 * i, 512), 512)
            term = dot_last(rows, wo[cols, :]).astype(BF16)
            to_chunks(p, (y, y), (0, 1), cols, term)
            return 0

        lax.fori_loop(0, 4, block, 0)
        ring.send_core(k)

    attended_part(2)
    attended_part(1)
    ring.far()
    attended_part(3)
    ring.near()
    attended_part(0)
    ring.add_core(0)

    def turn_block(i, _):
        at = pl.ds(pl.multiple_of(2 * TOK * i, 2 * TOK), 2 * TOK)
        att_t[:, at] = att[at, :].astype(F32).T.astype(BF16)
        return 0

    lax.fori_loop(0, 4, turn_block, 0)
    ring.second()
    ring.arrived()

    def norm(at):
        rows = tokens[at, :].astype(F32) + ring.rows(at)
        middle[at, :] = rows
        normal = rows * lax.rsqrt(mean_last(rows * rows) + EPSILON)
        low[at, :] = (normal * gain[...]).astype(BF16)

    in_chunks(norm)
    gather = RingGather(me, edges, low, xs, local.at[pl.ds(10, 2)])
    ring.release()

    @pl.when(moved)
    def _():
        for d in near_w:
            d.wait()
        for d in far_w:
            d.wait()

    @pl.when(jnp.logical_not(moved))
    def _():
        for d in kept:
            d.wait()

    load_c.wait()

    def compute(group):
        ys = [lax.rem(me.y + dy, 4) for dy, _ in group]
        halves = [half for _, half in group]
        blocks = [2 * y + half for y, half in zip(ys, halves)]
        x = jnp.concatenate([xs[b] for b in blocks], axis=0)
        g = jnp.concatenate([c[b] for b in blocks], axis=0)
        here = [pl.ds(pl.multiple_of(TOK * b, TOK), TOK) for b in blocks]
        for n0, n1 in ((0, 256), (256, 512), (512, FF_DEV)):
            gate = dot_last(x, w[n0:n1, :])
            upward = dot_last(x, w[FF_DEV + n0 : FF_DEV + n1, :])
            grad = dot_last(g, w[2 * FF_DEV + n0 : 2 * FF_DEV + n1, :])
            sigmoid = 1.0 / (1.0 + jnp.exp(-gate))
            swish = gate * sigmoid
            active = swish * upward
            grad_up = grad * swish
            grad_gate = grad * upward * sigmoid * (1.0 + gate * (1.0 - sigmoid))
            act[:, n0:n1] = active.astype(BF16)
            dup[:, n0:n1] = grad_up.astype(BF16)
            dgate[:, n0:n1] = grad_gate.astype(BF16)
            for ref, value in ((act_t, active), (up_t, grad_up), (gate_t, grad_gate)):
                value = value.T.astype(BF16)
                ref[n0:n1, here[0]] = value[:, :TOK]
                ref[n0:n1, here[1]] = value[:, TOK:]

        def block(i, _):
            cols = pl.ds(pl.multiple_of(512 * i, 512), 512)
            term = dot(act[...], w[2 * FF_DEV :, cols])
            to_chunks(p, ys, halves, cols, term.astype(BF16))
            grads = dot(dgate[...], w[:FF_DEV, cols]) + dot(dup[...], w[FF_DEV : 2 * FF_DEV, cols])
            to_chunks(gp, ys, halves, cols, grads.astype(BF16))
            return 0

        lax.fori_loop(0, 4, block, 0)

    two = RingScatter(me, edges, gp, (g1, b1, r1, l1))
    gather.own()
    compute(GROUPS[0])
    two.send_core(0)
    gather.relay()
    gather.near()
    gather.from_core(2, 4)
    compute(GROUPS[1])
    gather.from_core(4, 6)
    gather.far()
    compute(GROUPS[2])
    two.send_core(1)
    two.send_core(3)
    two.near()
    gather.from_core(6, 8)
    compute(GROUPS[3])
    two.send_core(2)
    save = pltpu.make_async_copy(p, branch, local.at[0])
    save.start()
    two.add_core(0)

    z_sum = RingSum(me, edges, True, w, 0, PART, 512, 48, z_relayed, z_last)
    x_sum = RingSum(me, edges, False, w, PART, PART, 512, 48, x_relayed, x_last)
    split = PART - FF_DEV

    def z_task(k):
        cols = z_sum.columns(k)
        x = xs[:, :, cols].reshape(8 * TOK, 512)
        w[:FF_DEV, cols] = dot(gate_t[...], x).astype(BF16)
        w[FF_DEV:PART, cols] = dot(up_t[:split, :], x).astype(BF16)

    def x_task(k):
        cols = x_sum.columns(k)
        x = xs[:, :, cols].reshape(8 * TOK, 512)
        g = c[:, :, cols].reshape(8 * TOK, 512)
        w[PART : 2 * FF_DEV, cols] = dot(up_t[split:, :], x).astype(BF16)
        w[2 * FF_DEV :, cols] = dot(act_t[...], g).astype(BF16)

    two.far()
    z_task(2)
    z_sum.far()
    x_task(2)
    x_sum.far()
    z_task(1)
    z_sum.near_up()
    x_task(1)
    x_sum.near_up()
    two.second()
    z_task(3)
    z_sum.near_down()
    x_task(3)
    x_sum.near_down()
    z_task(0)
    x_task(0)
    two.arrived()
    gain_grad[...] = jnp.zeros_like(gain_grad)

    def back(at):
        rows = middle[at, :]
        inverse = lax.rsqrt(mean_last(rows * rows) + EPSILON)
        normal = rows * inverse
        grad = two.rows(at)
        gain_grad[...] += jnp.sum(normal * grad, axis=0, keepdims=True)
        scaled = grad * gain[...]
        result = cot[at, :].astype(F32) + inverse * (
            scaled - normal * mean_last(scaled * normal)
        )
        grad_middle[at, :] = result
        low[at, :] = result.astype(BF16)

    edges.sent(gather.sources())
    in_chunks(back)
    gather = RingGather(me, edges, low, gb, local.at[pl.ds(10, 2)])
    z_sum.second()
    x_sum.second()
    gather.relay()
    z_sum.total(z_q)
    z_two = RingSum(me, edges, False, z_q, 0, PART, 128, 176, z_relayed2, z_last2)
    z_two.far()
    z_two.near_up()
    z_two.near_down()
    x_sum.total(x_q)
    x_two = RingSum(me, edges, True, x_q, 0, PART, 128, 176, x_relayed2, x_last2)
    x_two.far()
    x_two.near_up()
    x_two.near_down()
    gather.near()
    gather.far()
    gather.own()
    gather.from_core(2, 8)

    def attended_grad(i, _):
        at = pl.ds(pl.multiple_of(2 * TOK * i, 2 * TOK), 2 * TOK)
        rows = gb[pl.ds(2 * i, 2)].reshape(2 * TOK, D)
        grad_att[at, :] = dot(rows, wo[...]).astype(BF16)
        cols = pl.ds(pl.multiple_of(512 * i, 512), 512)
        rows = gb[:, :, cols].reshape(8 * TOK, 512)
        grad_wo[:, cols] = dot(att_t[...], rows).astype(BF16)
        return 0

    lax.fori_loop(0, 4, attended_grad, 0)
    z_two.second()
    x_two.second()
    z_two.total(z_out)
    x_two.total(x_out)
    edges.finish()
    save.wait()


def feed_forward(att, wo, tokens, cot, gain, cots, wgu, wdn, wswap, wnear_up, wnear_down):
    block = pltpu.VMEM((8, TOK, D), BF16)
    turned = pltpu.VMEM((FF_DEV, 8 * TOK), BF16)
    pair = pltpu.VMEM((2 * TOK, FF_DEV), BF16)

    def ring(width):
        return [
            pltpu.VMEM((2, PART_HALF, width), BF16),
            pltpu.VMEM((2, PART, width), BF16),
        ] * 2

    return pl.pallas_call(
        feed_forward_kernel,
        out_shape=(
            shape((TOK, D), F32),
            shape((TOK, D), F32),
            shape((1, D), F32),
            shape((1024, Q_DEV)),
            shape((Q_DEV, D)),
            shape((PART, 128)),
            shape((PART, 128)),
            shape((8, TOK, D)),
        ),
        in_specs=[VMEM] * 5 + [ANY] * 6,
        out_specs=(VMEM,) * 7 + (ANY,),
        scratch_shapes=[block] * 5
        + [pltpu.VMEM((Q_DEV, 8 * TOK), BF16)]
        + [pltpu.VMEM((3 * FF_DEV, D), BF16)]
        + [turned] * 3
        + [pair] * 3
        + [pltpu.VMEM((TOK, D), BF16)]
        + scatter_scratch()
        + ring(512)
        + [pltpu.VMEM((PART, 512), BF16)] * 2
        + ring(128)
        + sems(2 * SCATTER_EDGES + 2 * GATHER_EDGES + 4 * SUM_EDGES)
        + sems(2)
        + [pltpu.SemaphoreType.DMA((12,))],
        compiler_params=pltpu.CompilerParams(
            collective_id=2, has_side_effects=True, vmem_limit_bytes=61 * 2**20
        ),
        name="feed_forward",
    )(att, wo, tokens, cot, gain, cots, wgu, wdn, wswap, wnear_up, wnear_down)


def columns(width):
    return lambda i: (slice(None), pl.ds(pl.multiple_of(i * width, width), width))


def row_block(height, start=0):
    return lambda i: (pl.ds(pl.multiple_of(start + i * height, height), height), slice(None))


def plane_devices(me):
    found = [me.at(core=1 - me.c)]
    for dz, dx in STEPS:
        z, xl, core, y, xh = around(me, dz, dx)
        found += [(z, xl, core, y, xh), (z, xl, 1 - core, y, xh)]
    return found


def swapped_pairs(rows):
    return jnp.concatenate([halves_swapped(rows[:, :HD]), halves_swapped(rows[:, HD:])], axis=1)


class RingBlocks:
    def __init__(self, me, edges, ref, columns):
        self.me, self.edges, self.ref, self.columns = me, edges, ref, columns
        rows = ref.shape[0]
        self.halves = (pl.ds(0, rows // 2), pl.ds(rows // 2, rows // 2))
        self.up, self.down = me.at(dz=1), me.at(dz=-1)
        self.up_a = self.send(0, 0, self.up)
        self.down_b = self.send(0, 1, self.down)
        self.up_b = self.send(0, 1, self.up)
        self.down_a = self.send(0, 0, self.down)

    def block(self, dz):
        return self.ref.at[:, self.columns(lax.rem(self.me.z + dz + 4, 4))]

    def send(self, dz, half, device):
        cols = self.columns(lax.rem(self.me.z + dz + 4, 4))
        ref = self.ref.at[self.halves[half], cols]
        return self.edges.copy(ref, ref, device)

    def relay(self):
        self.up_a.wait_recv()
        self.on_a = self.send(-1, 0, self.up)
        self.down_b.wait_recv()
        self.on_b = self.send(1, 1, self.down)

    def near(self):
        self.up_b.wait_recv()
        self.down_a.wait_recv()

    def far(self):
        self.on_a.wait_recv()
        self.on_b.wait_recv()


class PlaneGather:
    def __init__(self, me, edges, z_piece, x_piece, z_all, x_all, send, recv):
        self.me, self.edges, self.z_all, self.x_all = me, edges, z_all, x_all
        self.send, self.recv, self.z_piece, self.x_piece = send, recv, z_piece, x_piece
        self.stays = me.c == me.xh
        self.core = me.at(core=1 - me.c)
        self.side = me.at(xl=1 - me.xl)
        across = me.at(core=1 - me.c, xl=1 - me.xl, xh=1 - me.xh)
        x = x_of(me)
        self.held = jnp.where(self.stays, x, 3 - x)
        for i, (piece, ref, at) in enumerate(
            ((z_piece, z_all, 4 * me.z + x), (x_piece, x_all, 4 * x + me.z))
        ):
            dst = ref.at[columns(128)(at)]
            send_block(me, piece, dst, send.at[i], recv.at[i], across, self.stays)

    def z_columns(self, z):
        return pl.ds(pl.multiple_of(512 * z + 256 * self.me.c, 256), 256)

    def x_columns(self, z):
        return pl.ds(pl.multiple_of(512 * self.held + 128 * z, 128), 128)

    def side_block(self, dz):
        held = self.held + 1 - 2 * lax.rem(self.held, 2)
        z = lax.rem(self.me.z + dz + 4, 4)
        return self.x_all.at[columns(128)(4 * held + z)]

    def pass_core(self, ref):
        self.over.append(self.edges.copy(ref, ref, self.core))

    def sideways(self):
        own = self.z_all.at[columns(128)(4 * self.me.z + self.held)]
        wait_got(own, self.recv.at[0])
        self.z_side = self.edges.copy(own, own, self.side)
        own = self.x_all.at[:, self.x_columns(self.me.z)]
        wait_got(own, self.recv.at[1])
        self.x_ring = RingBlocks(self.me, self.edges, self.x_all, self.x_columns)
        self.x_side = [self.edges.copy(own, own, self.side)]
        self.over = []
        self.pass_core(own)

    def along(self):
        self.z_side.wait_recv()
        self.z_ring = RingBlocks(self.me, self.edges, self.z_all, self.z_columns)
        self.pass_core(self.z_ring.block(0))
        self.x_ring.relay()

    def to_side(self, dz):
        ref = self.x_ring.block(dz)
        self.x_side.append(self.edges.copy(ref, ref, self.side))

    def near(self):
        self.x_ring.near()
        self.to_side(1)
        self.to_side(-1)
        self.z_ring.relay()
        self.x_ring.far()
        self.to_side(2)
        for dz in (1, -1, 2):
            self.pass_core(self.x_ring.block(dz))

    def far(self):
        self.z_ring.near()
        self.pass_core(self.z_ring.block(1))
        self.pass_core(self.z_ring.block(-1))
        self.z_ring.far()
        self.pass_core(self.z_ring.block(2))
        for d, dz in zip(self.x_side, (0, 1, -1, 2)):
            d.wait_recv()
            self.pass_core(self.side_block(dz))

    def finish(self):
        for d in self.over:
            d.wait_recv()
        wait_sent(self.z_piece, self.send.at[0], self.stays)
        wait_sent(self.x_piece, self.send.at[1], self.stays)


PLANE_EDGES = 1 + 2 * SUM_EDGES + 4 + 12


class TwoSums:
    def __init__(self, me, edges, src, rows, steps, scratch):
        self.me, self.edges, self.rows, self.steps = me, edges, rows, steps
        self.q, self.out = scratch[4:6], scratch[10:12]
        self.scratch = scratch
        start = (0, rows[0])
        self.one = [
            RingSum(
                me, edges, i == 0, src, start[i], rows[i], 512, steps[0][i],
                scratch[2 * i], scratch[2 * i + 1], me.y,
            )
            for i in (0, 1)
        ]
        for ring in self.one:
            ring.far()
            ring.near_up()
            ring.near_down()

    def second(self):
        for ring in self.one:
            ring.second()

    def cross(self):
        self.two = []
        for i in (0, 1):
            self.one[i].total(self.q[i])
            ring = RingSum(
                self.me, self.edges, i == 1, self.q[i], 0, self.rows[i], 128,
                self.steps[1][i], self.scratch[6 + 2 * i], self.scratch[7 + 2 * i],
            )
            ring.far()
            ring.near_up()
            ring.near_down()
            self.two.append(ring)

    def fourth(self):
        for ring in self.two:
            ring.second()

    def total(self):
        for i in (0, 1):
            self.two[i].total(self.out[i])


def two_sums_scratch(rows):
    found = []
    for r in rows:
        found += [pltpu.VMEM((2, r // 2, 512), BF16), pltpu.VMEM((2, r, 512), BF16)]
    found += [pltpu.VMEM((r, 512), BF16) for r in rows]
    for r in rows:
        found += [pltpu.VMEM((2, r // 2, 128), BF16), pltpu.VMEM((2, r, 128), BF16)]
    return found + [pltpu.VMEM((r, 128), BF16) for r in rows]


EARLY_ROWS = (256, 256)


def ending_kernel(
    dkv, dq, kv_table, wq, tokens, gain, grad_middle, gain_two, z_piece, x_piece, middle,
    gwo, xs_in, branch_in,
    output, grad_tokens, gains, wq_out, wo_out, z_all, x_all,
    kv_got, kv_both, kv_last, dkv_low, xs, grads, grads_t, parts, branch_parts, early, late,
    g1, b1, r1, l1, g2, b2, r2, l2,
    wq_all, wo_all, late_own, late_got, late_piece, mine, near, near_sum, owners,
    *rest,
):
    early_scratch = rest[:12]
    (send, recv, ds, dr, es, er, ps, pr, gs, gr, hs, hr, us, ur, local) = rest[12:]
    me = Place()
    core = me.at(core=1 - me.c)
    far = [
        me.at(dz=dz, xl=(1 - me.xl) if dl else me.xl) for dz, dl in chips_in_sequence(me)
    ]
    signalled = greet(plane_devices(me) + group_members(me)[1:])
    edges = Edges(send, recv)
    place = 4 * me.z + x_of(me)
    rank = 2 * me.y + me.c
    load_x = pltpu.make_async_copy(xs_in, xs, local.at[0])
    load_branch = pltpu.make_async_copy(branch_in, branch_parts, local.at[1])
    load_wo = [
        pltpu.make_async_copy(
            gwo.at[pl.ds(128 * i, 128)], early.at[pl.ds(256 * i + 128, 128)], local.at[2 + i]
        )
        for i in (0, 1)
    ]
    for d in [load_x, load_branch] + load_wo:
        d.start()

    def query_part(i, _):
        at = pl.ds(pl.multiple_of(2 * TOK * i, 2 * TOK), 2 * TOK)
        rows = dq[at, :]
        grads[at, :Q_DEV] = rows
        grads_t[:Q_DEV, at] = rows.astype(F32).T.astype(BF16)
        return 0

    lax.fori_loop(0, 4, query_part, 0)
    met(signalled)

    order = []
    for dz, dl in chips_in_sequence(me) + [(0, 0)]:
        chip = 2 * lax.rem(me.z + dz, 4) + ((1 - me.xl) if dl else me.xl)
        order.append((chip, edges.copy(dkv.at[1 - me.c, chip], kv_got.at[chip], core)))
    load_branch.wait()
    branch = RingScatter(me, edges, branch_parts, (g2, b2, r2, l2))
    for k in (2, 1, 3, 0):
        branch.send_core(k)
    far_copies = []
    for i, (chip, d) in enumerate(order):
        d.wait_recv()
        kv_both[chip] = (dkv[me.c, chip].astype(F32) + kv_got[chip].astype(F32)).astype(BF16)
        if i < 7:
            far_copies.append(edges.copy(kv_both.at[chip], kv_last.at[i], far[i]))
    plane = PlaneGather(me, edges, z_piece, x_piece, z_all, x_all, ps, pr)
    load_x.wait()

    def weight_block(i, _):
        cols = pl.ds(pl.multiple_of(512 * i, 512), 512)
        rows = xs[:, :, cols].reshape(8 * TOK, 512)
        early[:128, cols] = dot(grads_t[:128, :], rows).astype(BF16)
        early[256:384, cols] = dot(grads_t[128:Q_DEV, :], rows).astype(BF16)
        return 0

    lax.fori_loop(0, 4, weight_block, 0)
    for d in load_wo:
        d.wait()
    early_sum = TwoSums(me, edges, early, EARLY_ROWS, ((64, 64), (128, 128)), early_scratch)
    branch.far()
    branch.near()
    branch.add_core(0)
    for d in far_copies:
        d.wait_recv()

    def kv_total(at):
        total = kv_both[2 * me.z + me.xl, at].astype(F32)
        for i in range(7):
            total = total + kv_last[i, at].astype(F32)
        dkv_low[at, :] = (
            total * kv_table[0, at, :] - swapped_pairs(total) * kv_table[1, at, :]
        )

    in_chunks(kv_total, 512)
    for i in range(8):
        rows = dkv_low[64 * i : 64 * (i + 1), :]
        rows = jnp.concatenate([rows[:, :HD], rows[:, HD:]], axis=0)
        at = slice(TOK * i, TOK * (i + 1))
        grads[at, Q_DEV:] = rows.astype(BF16)
        grads_t[Q_DEV:, at] = rows.T.astype(BF16)

    early_sum.second()
    branch.second()
    def late_block(i, _):
        cols = pl.ds(pl.multiple_of(512 * i, 512), 512)
        rows = xs[:, :, cols].reshape(8 * TOK, 512)
        late[:, cols] = dot(grads_t[Q_DEV:, :], rows).astype(BF16)
        return 0

    ring = RingScatter(me, edges, parts, (g1, b1, r1, l1))

    def part(k):
        y = lax.rem(me.y + k, 4)
        rows = grads[pl.ds(pl.multiple_of(2 * TOK * y, 2 * TOK), 2 * TOK), :]

        def block(i, _):
            cols = pl.ds(pl.multiple_of(512 * i, 512), 512)
            to_chunks(parts, (y, y), (0, 1), cols, dot(rows, wq[:, cols]).astype(BF16))
            return 0

        lax.fori_loop(0, 4, block, 0)
        ring.send_core(k)

    part(2)
    part(1)
    ring.far()
    early_sum.cross()
    part(3)
    ring.near()
    part(0)
    ring.add_core(0)
    early_sum.fourth()
    plane.sideways()
    lax.fori_loop(0, 4, late_block, 0)
    late_sum = SumOfSixteen(me, late, columns(128), late_own, late_got, us, ur, local.at[4])
    early_sum.total()
    wq_deliver = Deliver(me, ds, dr)

    def deliver_block(j, src, at):
        block = own_block(me, j)
        owner, slot = block // 5, lax.rem(block, 5)
        dst = wq_all.at[
            pl.ds(pl.multiple_of(64 * slot, 64), 64),
            pl.ds(pl.multiple_of(128 * at, 128), 128),
        ]
        wq_deliver.to_owner(src, dst, at // 8, owner // 2, lax.rem(owner, 2))

    wo_deliver = Deliver(me, es, er)
    early_place = 4 * lax.rem(me.z + me.y, 4) + x_of(me)
    early_turned = 4 * lax.rem(x_of(me) + me.y, 4) + me.z
    for i, at in enumerate((early_place, early_turned)):
        for j in (0, 1):
            deliver_block(2 * i + j, early_sum.out[i].at[pl.ds(64 * j, 64)], at)
        dst = wo_all.at[
            pl.ds(pl.multiple_of(Q_DEV * rank + 128 * i, 128), 128),
            pl.ds(pl.multiple_of(128 * lax.rem(at, 2), 128), 128),
        ]
        src = early_sum.out[i].at[pl.ds(128, 128)]
        wo_deliver.to_owner(src, dst, me.y // 2, at // 4, lax.rem(at // 2, 2))
    plane.along()
    late_piece[...] = late_sum.total().astype(BF16)
    deliver_block(4, late_piece, place)
    ring.second()
    plane.near()
    branch.arrived()

    def out(at):
        output[at, :] = (middle[at, :] + branch.rows(at)).astype(BF16)

    in_chunks(out)
    ring.arrived()
    mine[...] = jnp.zeros_like(mine)
    mine[1:2, :] = gain_two[...]

    def back(at):
        rows = tokens[at, :].astype(F32)
        inverse = lax.rsqrt(mean_last(rows * rows) + EPSILON)
        normal = rows * inverse
        grad = ring.rows(at)
        mine[0:1, :] += jnp.sum(normal * grad, axis=0, keepdims=True)
        scaled = grad * gain[...]
        grad_tokens[at, :] = grad_middle[at, :] + inverse * (
            scaled - normal * mean_last(scaled * normal)
        )

    in_chunks(back)

    def slice_of(member):
        return mine.at[:, pl.ds(pl.multiple_of(256 * member, 256), 256)]

    near_copies = []
    for k in range(1, 8):
        dy, other = k // 2, k % 2
        y = lax.rem(me.y + dy, 4)
        to_core = 1 - me.c if other else me.c
        d = pltpu.make_async_remote_copy(
            src_ref=slice_of(2 * y + to_core),
            dst_ref=near.at[k - 1],
            send_sem=gs.at[k - 1],
            recv_sem=gr,
            device_id=me.at(y=y, core=to_core),
            device_id_type=pl.DeviceIdType.MESH,
        )
        d.start()
        near_copies.append(d)
    plane.far()
    own = mine[:, pl.ds(pl.multiple_of(256 * rank, 256), 256)]
    wait_got(near, gr)
    for k in range(7):
        own = own + near[k]
    near_sum[...] = own
    gain_deliver = Deliver(me, hs, hr)
    for to_core in (0, 1):
        gain_deliver.to_owner(near_sum, owners.at[place], to_core, me.y, me.c)

    half = pl.ds(pl.multiple_of(1024 * me.c, 1024), 1024)
    over = []
    for ref, sem in ((wo_all.at[half], er), (wq_all.at[:, half], dr)):
        wait_got(ref, sem)
        over.append(edges.copy(ref, ref, core))
    wait_got(owners, hr)
    sum_all = owners[0]
    for k in range(1, 16):
        sum_all = sum_all + owners[k]
    gains[...] = sum_all
    for d in over:
        d.wait_recv()
    wo_out[...] = wo_all[...]
    wq_out[...] = wq_all[...]
    plane.finish()
    late_sum.finish()
    for d in (wo_deliver, wq_deliver, gain_deliver):
        d.finish()
    for d in near_copies:
        d.wait_send()
    edges.finish()


def ending(
    dkv, dq, kv_table, wq, tokens, gain, grad_middle, gain_two, z_piece, x_piece, middle,
    gwo, xs, branch,
):
    many = pltpu.SemaphoreType.DMA
    return pl.pallas_call(
        ending_kernel,
        out_shape=(
            shape((TOK, D)),
            shape((TOK, D), F32),
            shape((8, 256), F32),
            shape((320, D)),
            shape((D, 256)),
            shape((PART, D)),
            shape((PART, D)),
        ),
        in_specs=[VMEM] * 11 + [ANY] * 3,
        out_specs=(VMEM,) * 5 + (ANY,) * 2,
        scratch_shapes=[
            pltpu.VMEM((8, 512, 128), BF16),
            pltpu.VMEM((8, 512, 128), BF16),
            pltpu.VMEM((7, 512, 128), BF16),
            pltpu.VMEM((512, 128), F32),
            pltpu.VMEM((8, TOK, D), BF16),
            pltpu.VMEM((1024, 320), BF16),
            pltpu.VMEM((320, 1024), BF16),
            pltpu.VMEM((8, TOK, D), BF16),
            pltpu.VMEM((8, TOK, D), BF16),
            pltpu.VMEM((512, D), BF16),
            pltpu.VMEM((64, D), BF16),
        ]
        + scatter_scratch() * 2
        + [
            pltpu.VMEM((320, D), BF16),
            pltpu.VMEM((D, 256), BF16),
            pltpu.VMEM((64, 128), BF16),
            pltpu.VMEM((15, 64, 128), BF16),
            pltpu.VMEM((64, 128), BF16),
            pltpu.VMEM((8, D), F32),
            pltpu.VMEM((7, 8, 256), F32),
            pltpu.VMEM((8, 256), F32),
            pltpu.VMEM((16, 8, 256), F32),
        ]
        + two_sums_scratch(EARLY_ROWS)
        + sems(15 + 2 * SCATTER_EDGES + PLANE_EDGES + 4 * SUM_EDGES + 2)
        + [many((40,)), many, many((16,)), many, many((2,)), many((2,))]
        + [many((7,)), many, many((16,)), many, many((15,)), many, many((5,))],
        compiler_params=pltpu.CompilerParams(
            collective_id=3, has_side_effects=True, vmem_limit_bytes=61 * 2**20
        ),
        name="ending",
    )(
        dkv, dq, kv_table, wq, tokens, gain, grad_middle, gain_two, z_piece, x_piece, middle,
        gwo, xs, branch,
    )


def widen_kernel(z_ref, x_ref, wq_ref, wo_ref, gu_ref, dn_ref, gq_ref, go_ref):
    i = pl.program_id(0)

    @pl.when(i < 3)
    def _():
        gu_ref[...] = z_ref[...].astype(F32)

    @pl.when(i == 3)
    def _():
        gu_ref[...] = x_ref[...].astype(F32)

    @pl.when(i > 3)
    def _():
        dn_ref[...] = x_ref[...].astype(F32)

    gq_ref[...] = wq_ref[...].astype(F32)
    go_ref[...] = wo_ref[...].astype(F32).T


def widen(z_all, x_all, wq, wo):
    rows = PART // 3
    return pl.pallas_call(
        widen_kernel,
        out_shape=(
            shape((2 * FF_DEV, D), F32),
            shape((FF_DEV, D), F32),
            shape((320, D), F32),
            shape((256, D), F32),
        ),
        grid=(6,),
        in_specs=[
            pl.BlockSpec((rows, D), lambda i: (jnp.minimum(i, 2), 0)),
            pl.BlockSpec((rows, D), lambda i: (jnp.maximum(i - 3, 0), 0)),
            pl.BlockSpec((64, D), lambda i: (jnp.minimum(i, 4), 0)),
            pl.BlockSpec((512, 256), lambda i: (jnp.minimum(i, 3), 0)),
        ],
        out_specs=(
            pl.BlockSpec((rows, D), lambda i: (jnp.minimum(i, 3), 0)),
            pl.BlockSpec((rows, D), lambda i: (jnp.maximum(i - 4, 0), 0)),
            pl.BlockSpec((64, D), lambda i: (jnp.minimum(i, 4), 0)),
            pl.BlockSpec((256, 512), lambda i: (0, jnp.minimum(i, 3))),
        ),
        compiler_params=pltpu.CompilerParams(vmem_limit_bytes=61 * 2**20),
        name="widen",
    )(z_all, x_all, wq, wo)


def route(dz):
    pairs = []
    for i in range(128):
        z, xl, c, y, xh = i // 32, i // 16 % 2, i // 8 % 2, i // 2 % 4, i % 2
        if c != xh:
            pairs.append((i, (((((z + dz) % 4) * 2 + xl) * 2 + c) * 4 + y) * 2 + xh))
    return pairs


def body(hidden, positions, gain_attn, w_qkv, w_out, gain_mlp, w_gate_up, w_down, cotangent):
    gain_one = gain_attn.astype(F32).reshape(1, D)
    gain_two = gain_mlp.astype(F32).reshape(1, D)
    wgu = w_gate_up.reshape(2 * FF_DEV, D)
    wdn = w_down.T
    query, kv_table, trigs, runs, xs, wq, kvs, places, cots, wo, wswap = begin(
        hidden[0],
        gain_one,
        jnp.broadcast_to(positions, (8, TOK)),
        rotary_rows(positions[0]),
        w_qkv,
        wgu,
        wdn,
        cotangent[0],
        w_out,
    )
    wo = wo.reshape(D, Q_DEV)
    query_runs = runs[0, :16]
    key_runs = places[:, 0, :16].reshape(128)
    wnear_up = lax.ppermute(wswap, AXES, route(1))
    wnear_down = lax.ppermute(wswap, AXES, route(3))
    att, ot, lse = attend(key_runs, query_runs, query, kvs)
    middle, grad_middle, gain_grad, grad_att, grad_wo, z_piece, x_piece, branch = feed_forward(
        att, wo, hidden[0], cotangent[0], gain_two, cots, wgu, wdn, wswap, wnear_up, wnear_down
    )
    dq, dkv = attend_back(key_runs, query_runs, query, kvs, grad_att, ot, lse, trigs)
    output, grad_tokens, gains, grad_w_qkv, grad_w_out, z_all, x_all = ending(
        dkv,
        dq,
        kv_table,
        wq,
        hidden[0],
        gain_one,
        grad_middle,
        gain_grad,
        z_piece,
        x_piece,
        middle,
        grad_wo,
        xs,
        branch,
    )
    grad_gu, grad_dn, grad_w_qkv, grad_w_out = widen(z_all, x_all, grad_w_qkv, grad_w_out)
    return (
        output[None],
        grad_tokens[None],
        gains[0],
        grad_w_qkv,
        grad_w_out,
        gains[1],
        grad_gu.reshape(2, FF_DEV, D),
        grad_dn.T,
    )


def solution(mesh):
    fine = Mesh(mesh.devices.reshape(4, 2, 2, 4, 2), AXES)
    ctx, fsdp = ("z", "xl", "c"), ("y", "xh")
    weight = P(fsdp, None)
    return jax.shard_map(
        body,
        mesh=fine,
        in_specs=(
            P(fsdp, ctx, None),
            P(fsdp, ctx),
            P(),
            weight,
            weight,
            P(),
            P(None, fsdp, None),
            P(None, fsdp),
            P(fsdp, ctx, None),
        ),
        out_specs=(
            P(fsdp, ctx, None),
            P(fsdp, ctx, None),
            P(fsdp),
            weight,
            weight,
            P(fsdp),
            P(None, fsdp, None),
            P(None, fsdp),
        ),
        check_vma=False,
    )
```

```python
import jax
import jax.numpy as jnp
from jax import lax
from jax.experimental import pallas as pl
from jax.experimental.pallas import tpu as pltpu
from jax.sharding import Mesh
from jax.sharding import PartitionSpec as P

D = 2048
H = 32
KV = 4
HD = 64
FF = 5632
TOK = 128
HALF = 64
FF_DEV = 704
Q_DEV = 256
EPSILON = 1e-05
FILLER = -1e30
AXES = ("z", "xl", "c", "y", "xh")
ANY = pl.BlockSpec(memory_space=pl.ANY)
VMEM = pl.BlockSpec(memory_space=pltpu.VMEM)
BF16 = jnp.bfloat16
F32 = jnp.float32


class Place:
    def __init__(self):
        self.z, self.xl, self.c, self.y, self.xh = (lax.axis_index(a) for a in AXES)

    def at(self, dz=0, dy=0, core=None, xl=None, xh=None, y=None):
        z = lax.rem(self.z + dz + 4, 4) if dz else self.z
        y = (lax.rem(self.y + dy + 4, 4) if dy else self.y) if y is None else y
        return (
            z,
            self.xl if xl is None else xl,
            self.c if core is None else core,
            y,
            self.xh if xh is None else xh,
        )


class Edges:
    def __init__(self, send, recv):
        self.send, self.recv, self.count, self.started = send, recv, 0, []

    def copy(self, src, dst, device, start=True):
        i = self.count
        self.count += 1
        d = pltpu.make_async_remote_copy(
            src_ref=src,
            dst_ref=dst,
            send_sem=self.send.at[i],
            recv_sem=self.recv.at[i],
            device_id=device,
            device_id_type=pl.DeviceIdType.MESH,
        )
        self.started.append(d)
        if start:
            d.start()
        return d

    def sent(self, copies):
        for d in copies:
            d.wait_send()
        self.started = [d for d in self.started if all(d is not e for e in copies)]

    def finish(self):
        for d in self.started:
            d.wait_send()


def greet(devices):
    for device in devices:
        pl.semaphore_signal(
            pltpu.get_barrier_semaphore(),
            inc=1,
            device_id=device,
            device_id_type=pl.DeviceIdType.MESH,
        )
    return len(devices)


def met(count):
    pl.semaphore_wait(pltpu.get_barrier_semaphore(), count)


def group_members(me):
    found = [me.at(core=1 - me.c)]
    for dy in (1, 2, 3):
        found += [me.at(dy=dy), me.at(dy=dy, core=1 - me.c)]
    return found


class RingGather:
    def __init__(self, me, edges, own, out, local):
        self.me, self.edges, self.out = me, edges, out
        self.core = me.at(core=1 - me.c)
        self.up, self.down = me.at(dy=1), me.at(dy=-1)
        a, b = own.at[pl.ds(0, HALF)], own.at[pl.ds(HALF, HALF)]
        to_a, to_b = self.block(0, 0), self.block(0, 1)
        self.up_a = edges.copy(a, to_a, self.up)
        self.down_b = edges.copy(b, to_b, self.down)
        self.up_b = edges.copy(b, to_b, self.up)
        self.down_a = edges.copy(a, to_a, self.down)
        self.to_core = [edges.copy(a, to_a, self.core), edges.copy(b, to_b, self.core)]
        self.kept = [
            pltpu.make_async_copy(a, to_a, local.at[0]),
            pltpu.make_async_copy(b, to_b, local.at[1]),
        ]
        for d in self.kept:
            d.start()

    def block(self, dy, half):
        y = lax.rem(self.me.y + dy + 4, 4)
        rows = pl.ds(pl.multiple_of(HALF * self.me.c, HALF), HALF)
        return self.out.at[2 * y + half, rows]

    def pass_core(self, dy, half):
        ref = self.block(dy, half)
        self.to_core.append(self.edges.copy(ref, ref, self.core))

    def own(self):
        for d in self.kept:
            d.wait()
        self.from_core(0, 2)

    def relay(self):
        self.up_a.wait_recv()
        ref = self.block(-1, 0)
        self.on_a = self.edges.copy(ref, ref, self.up)
        self.pass_core(-1, 0)
        self.down_b.wait_recv()
        ref = self.block(1, 1)
        self.on_b = self.edges.copy(ref, ref, self.down)
        self.pass_core(1, 1)

    def near(self):
        self.up_b.wait_recv()
        self.pass_core(-1, 1)
        self.down_a.wait_recv()
        self.pass_core(1, 0)

    def far(self):
        self.on_a.wait_recv()
        self.pass_core(2, 0)
        self.on_b.wait_recv()
        self.pass_core(2, 1)

    def from_core(self, first, last):
        for d in self.to_core[first:last]:
            d.wait_recv()

    def rest(self):
        self.near()
        self.far()
        self.own()
        self.from_core(2, 8)

    def sources(self):
        return [self.up_a, self.up_b, self.down_a, self.down_b] + self.to_core[:2]


GATHER_EDGES = 14
GROUPS = (((0, 0), (0, 1)), ((3, 0), (1, 1)), ((3, 1), (1, 0)), ((2, 0), (2, 1)))


class RingScatter:
    def __init__(self, me, edges, parts, scratch):
        self.me, self.edges, self.parts = me, edges, parts
        self.got, self.both, self.relayed, self.last = scratch
        self.up, self.down = me.at(dy=1), me.at(dy=-1)
        self.cores = {}
        self.a, self.b = pl.ds(0, HALF), pl.ds(HALF, HALF)

    def send_core(self, k):
        row = 2 * lax.rem(self.me.y + k, 4) + 1 - self.me.c
        core = self.me.at(core=1 - self.me.c)
        self.cores[k] = self.edges.copy(self.parts.at[row], self.got.at[k], core)

    def add_core(self, k):
        self.cores[k].wait_recv()
        row = 2 * lax.rem(self.me.y + k, 4) + self.me.c

        def add(at):
            self.both[k, at] = (
                self.parts[row, at].astype(F32) + self.got[k, at].astype(F32)
            ).astype(BF16)

        in_chunks(add)

    def far(self):
        self.add_core(2)
        e, both = self.edges, self.both
        self.r_a = e.copy(both.at[2, self.a], self.relayed.at[0], self.up)
        self.r_b = e.copy(both.at[2, self.b], self.relayed.at[1], self.down)

    def near(self):
        e, both = self.edges, self.both
        self.add_core(1)
        self.u_b = e.copy(both.at[1, self.b], self.last.at[0, self.b], self.up)
        self.add_core(3)
        self.d_a = e.copy(both.at[3, self.a], self.last.at[1, self.a], self.down)

    def first(self):
        for k in (2, 1, 3, 0):
            self.send_core(k)
        self.far()
        self.near()
        self.add_core(0)

    def second(self):
        a, b, e, both = self.a, self.b, self.edges, self.both
        self.r_a.wait_recv()
        both[1, a] = (both[1, a].astype(F32) + self.relayed[0].astype(F32)).astype(BF16)
        self.u_a = e.copy(both.at[1, a], self.last.at[0, a], self.up)
        self.r_b.wait_recv()
        both[3, b] = (both[3, b].astype(F32) + self.relayed[1].astype(F32)).astype(BF16)
        self.d_b = e.copy(both.at[3, b], self.last.at[1, b], self.down)

    def arrived(self):
        for d in (self.u_b, self.d_a, self.u_a, self.d_b):
            d.wait_recv()

    def rows(self, at):
        return (
            self.both[0, at].astype(F32)
            + self.last[0, at].astype(F32)
            + self.last[1, at].astype(F32)
        )

    def release(self):
        ring = [self.r_a, self.r_b, self.u_b, self.d_a, self.u_a, self.d_b]
        self.edges.sent(ring + list(self.cores.values()))


SCATTER_EDGES = 10


def scatter_scratch():
    return [
        pltpu.VMEM((4, TOK, D), BF16),
        pltpu.VMEM((4, TOK, D), BF16),
        pltpu.VMEM((2, HALF, D), BF16),
        pltpu.VMEM((2, TOK, D), BF16),
    ]


def sems(n):
    return [pltpu.SemaphoreType.DMA((n,)), pltpu.SemaphoreType.DMA((n,))]


def shape(dims, dtype=BF16):
    return jax.ShapeDtypeStruct(dims, dtype)


def remote_params(number):
    return pltpu.CompilerParams(
        collective_id=number, has_side_effects=True, vmem_limit_bytes=61 * 2**20
    )


def block_place(block):
    is_kv = block >= 32
    other = block - 32
    rank = block // 4
    y = jnp.where(is_kv, lax.rem(other + 32, 4), rank // 2)
    core = jnp.where(is_kv, other // 4, lax.rem(rank, 2))
    return y, core, jnp.where(is_kv, 4, lax.rem(block, 4))


def own_block(me, j):
    if j == 4:
        return 32 + 4 * me.c + me.y
    return 4 * (2 * me.y + me.c) + j


def send_block(me, src, dst, send_sem, recv_sem, target, stays):
    @pl.when(stays)
    def _():
        pltpu.make_async_copy(src, dst, recv_sem).start()

    @pl.when(jnp.logical_not(stays))
    def _():
        pltpu.make_async_remote_copy(
            src_ref=src,
            dst_ref=dst,
            send_sem=send_sem,
            recv_sem=recv_sem,
            device_id=target,
            device_id_type=pl.DeviceIdType.MESH,
        ).start()


def wait_sent(src, send_sem, stays):
    @pl.when(jnp.logical_not(stays))
    def _():
        pltpu.make_async_copy(src, src, send_sem).wait()


def wait_got(dst, recv_sem):
    pltpu.make_async_copy(dst, dst, recv_sem).wait()


def x_of(me):
    return 2 * me.xh + me.xl


def around(me, dz, dx):
    x = lax.rem(x_of(me) + dx, 4)
    return me.at(dz=dz, xl=lax.rem(x, 2), xh=x // 2)


STEPS = [(dz, dx) for dz in range(4) for dx in range(4)][1:]


class SumOfSixteen:
    def __init__(self, me, src, piece, own, got, send, recv, local):
        self.me, self.src, self.piece, self.own, self.got = me, src, piece, own, got
        self.send, self.recv = send, recv
        self.keep = pltpu.make_async_copy(
            src.at[piece(4 * me.z + x_of(me))], own, local
        )
        self.keep.start()
        for k, (dz, dx) in enumerate(STEPS):
            to = 4 * lax.rem(me.z + dz, 4) + lax.rem(x_of(me) + dx, 4)
            self.copy(src.at[piece(to)], k, around(me, dz, dx)).start()

    def copy(self, src, k, device):
        return pltpu.make_async_remote_copy(
            src_ref=src,
            dst_ref=self.got.at[k],
            send_sem=self.send.at[k],
            recv_sem=self.recv,
            device_id=device,
            device_id_type=pl.DeviceIdType.MESH,
        )

    def total(self):
        self.keep.wait()
        pltpu.make_async_copy(self.got, self.got, self.recv).wait()
        total = self.own[...].astype(F32)
        for k in range(15):
            total = total + self.got[k].astype(F32)
        return total

    def finish(self):
        for k in range(15):
            src = self.src.at[self.piece(0)]
            pltpu.make_async_copy(src, src, self.send.at[k]).wait()


def same(me, z, xl, core, y, xh):
    return (z == me.z) & (xl == me.xl) & (core == me.c) & (y == me.y) & (xh == me.xh)


class Deliver:
    def __init__(self, me, send, recv):
        self.me, self.send, self.recv, self.sent = me, send, recv, []

    def to_owner(self, src, dst, core, y, xh):
        me = self.me
        for dz in range(4):
            for dl in (0, 1):
                z = lax.rem(me.z + dz, 4)
                xl = 1 - me.xl if dl else me.xl
                stays = same(me, z, xl, core, y, xh)
                sem = self.send.at[len(self.sent)]
                send_block(me, src, dst, sem, self.recv, (z, xl, core, y, xh), stays)
                self.sent.append((src, sem, stays))

    def finish(self):
        for src, sem, stays in self.sent:
            wait_sent(src, sem, stays)


def rotary_rows(places):
    steps = jnp.arange(HD // 2, dtype=F32)
    inverse = jnp.power(10000.0, steps * (-2.0 / HD))
    turning = places.astype(F32)[:, None] * inverse[None, :]
    rows = jnp.concatenate([jnp.cos(turning), jnp.sin(turning)], axis=1)
    return rows.reshape(2, 64, HD).transpose(1, 0, 2).reshape(64, 2 * HD)


def halves_swapped(rows):
    return jnp.concatenate([rows[:, HD // 2 :], rows[:, : HD // 2]], axis=1)


def rotate(rows, table, back=False):
    turned = halves_swapped(rows) * table[:, HD:]
    return rows * table[:, :HD] + (-turned if back else turned)


def rotary_of(rows, u):
    cosine = rows[:, HD * u : HD * u + HD // 2]
    sine = rows[:, HD * u + HD // 2 : HD * u + HD]
    return jnp.concatenate([cosine, cosine, -sine, sine], axis=1)


ROWS = 32


def in_chunks(step, rows=TOK, chunk=ROWS):
    def one(i, _):
        step(pl.ds(pl.multiple_of(i * chunk, chunk), chunk))
        return 0

    lax.fori_loop(0, rows // chunk, one, 0)


def mean_last(rows):
    return jnp.mean(rows, axis=-1, keepdims=True)


GU_QUARTER = 2 * FF_DEV // 4
DN_QUARTER = FF_DEV // 4
QUARTER = GU_QUARTER + DN_QUARTER


def swap_copies(me, wgu, wdn, wswap, send, recv):
    found = []
    across = me.at(core=1 - me.c, xl=1 - me.xl, xh=1 - me.xh)
    for i, (src, rows, start) in enumerate(
        ((wgu, GU_QUARTER, 0), (wdn, DN_QUARTER, GU_QUARTER))
    ):
        found.append(
            pltpu.make_async_remote_copy(
                src_ref=src.at[pl.ds(pl.multiple_of(rows * me.z, 16), rows)],
                dst_ref=wswap.at[pl.ds(start, rows)],
                send_sem=send.at[i],
                recv_sem=recv.at[i],
                device_id=across,
                device_id_type=pl.DeviceIdType.MESH,
            )
        )
    return found


def chips_in_sequence(me):
    return [(dz, dl) for dz in range(4) for dl in (0, 1)][1:]


def begin_kernel(
    tokens, gain, pos, trig, wqkv, wgu, wdn, cot, wout,
    q, kv_table, trigs, runs, xs_out, wq_out, kvs, places, cots, wo, wswap,
    low, xs, wq, kv, poss, own_runs,
    send, recv, qs, qr, os_, orr, ws, wr, local,
):
    me = Place()
    partner = {"xl": 1 - me.xl, "xh": 1 - me.xh}
    core = me.at(core=1 - me.c)
    members = group_members(me)
    others = [
        me.at(y=lax.rem(me.y + dy, 4), core=c, **partner) for dy in range(4) for c in (0, 1)
    ]
    far = [
        me.at(dz=dz, xl=(1 - me.xl) if dl else me.xl) for dz, dl in chips_in_sequence(me)
    ]
    signalled = greet(members + others + far)
    edges = Edges(send, recv)
    mine = 2 * me.y + me.c
    chip = 2 * me.z + me.xl

    def norm_rows():
        def norm(at):
            rows = tokens[at, :].astype(F32)
            inverse = lax.rsqrt(mean_last(rows * rows) + EPSILON)
            low[at, :] = (rows * inverse * gain[...]).astype(BF16)

        in_chunks(norm)

    spread = pl.ds(pl.multiple_of(512 * me.z, 512), 512)
    spread_rows = pl.ds(pl.multiple_of(64 * me.z, 64), 64)
    own = 2 * me.y + me.xh
    own_column = me.c == 0
    to_xl = jnp.where(own_column, me.xl, 1 - me.xl)
    to_xh = jnp.where(own_column, me.xh, 1 - me.xh)
    norm_rows()
    met(signalled)
    blocks = []
    for i in range(5):
        y, to_core, slot = block_place(5 * own + i)
        stays = own_column & (y == me.y) & (to_core == me.c)
        src = wqkv.at[pl.ds(64 * i, 64), spread]
        dst = wq.at[pl.ds(pl.multiple_of(64 * slot, 64), 64), spread]
        target = (me.z, to_xl, to_core, y, to_xh)
        send_block(me, src, dst, qs.at[i], qr.at[slot], target, stays)
        blocks.append((src, qs.at[i], stays))

    lane = lax.broadcasted_iota(jnp.int32, (8, TOK), 1)
    first = 4 * me.y + me.c
    run_numbers = jnp.where(
        lane == first,
        jnp.broadcast_to(pos[:, 0:1], (8, TOK)),
        jnp.where(lane == first + 2, jnp.broadcast_to(pos[:, 64:65], (8, TOK)), 0),
    )
    own_runs[...] = lax.shift_right_logical(run_numbers, 6)
    keep_pos = pltpu.make_async_copy(own_runs, poss.at[mine], local.at[1])
    keep_pos.start()
    pos_copies = [edges.copy(own_runs, poss.at[mine], m) for m in members]
    trigs[mine] = trig[...]
    trig_copies = [edges.copy(trig, trigs.at[mine], me.at(dy=k)) for k in (1, 2, 3)]
    trig_over = [edges.copy(trig, trigs.at[mine], core)]
    ring = RingGather(me, edges, low, xs, local.at[pl.ds(6, 2)])
    for i in range(8):
        dy, other = i // 2, i % 2
        y = lax.rem(me.y + dy, 4)
        to_core = me.c if other == 0 else 1 - me.c
        stays = own_column if i == 0 else me.c < 0
        cols = pl.ds(pl.multiple_of(Q_DEV * (2 * y + to_core), Q_DEV), Q_DEV)
        src = wout.at[spread_rows, cols]
        dst = wo.at[own, spread_rows]
        target = (me.z, to_xl, to_core, y, to_xh)
        send_block(me, src, dst, os_.at[i], orr.at[own], target, stays)
        blocks.append((src, os_.at[i], stays))
    moved = me.c != me.xh
    swaps = swap_copies(me, wgu, wdn, wswap, ws, wr)

    @pl.when(moved)
    def _():
        for d in swaps:
            d.start()

    for i in range(5):
        wait_got(wq.at[pl.ds(64 * i, 64), spread], qr.at[i])
    wq_copies = [
        edges.copy(wq.at[:, spread], wq.at[:, spread], me.at(dz=k)) for k in (1, 3, 2)
    ]
    for k, d in zip((1, 2, 3), trig_copies):
        d.wait_recv()
        ref = trigs.at[2 * lax.rem(me.y - k + 4, 4) + me.c]
        trig_over.append(edges.copy(ref, ref, core))
    ring.relay()
    for i in range(8):
        wait_got(wo.at[i, spread_rows], orr.at[i])
    ref = wo.at[:, spread_rows]
    wo_copies = [edges.copy(ref, ref, me.at(dz=k)) for k in (1, 3, 2)]
    keep_pos.wait()
    for d in pos_copies + trig_over:
        d.wait_recv()
    combined = poss[0]
    for i in range(1, 8):
        combined = combined + poss[i]
    runs[...] = combined
    for d in wq_copies:
        d.wait_recv()
    wq_save = pltpu.make_async_copy(wq, wq_out, local.at[2])
    wq_save.start()
    is_key = me.c == 0

    def compute(group):
        ys = [lax.rem(me.y + dy, 4) for dy, _ in group]
        rows = [xs[2 * y + u] for y, (_, u) in zip(ys, group)]
        projected = dot_last(jnp.concatenate(rows, axis=0), wq[...])
        for i, (y, (_, u)) in enumerate(zip(ys, group)):
            for half in (0, 1):
                rows = rotary_of(trigs[2 * y + half], u)
                at = TOK * i + 64 * half
                values = projected[at : at + 64]
                heads = [rotate(values[:, HD * h : HD * h + HD], rows) for h in range(4)]
                query = jnp.concatenate(heads, axis=1).astype(BF16)
                to = pl.ds(pl.multiple_of(2 * TOK * y + TOK * u + 64 * half, 64), 64)
                q[to, :] = (query.astype(F32) * 0.125).astype(BF16)
                rows = jnp.concatenate(
                    [
                        jnp.where(is_key, rows[:, :HD], 1.0),
                        jnp.where(is_key, rows[:, HD:], 0.0),
                    ],
                    axis=1,
                )
                to = pl.ds(pl.multiple_of(TOK * y + 64 * u, 64), 64)
                lanes = slice(HD * half, HD * half + HD)
                kv[to, lanes] = rotate(values[:, Q_DEV:], rows).astype(BF16)
                kv_table[0, to, lanes] = rows[:, :HD]
                kv_table[1, to, lanes] = rows[:, HD:]

    ring.own()
    compute(GROUPS[0])
    ring.near()
    ring.from_core(2, 4)
    compute(GROUPS[1])
    ring.from_core(4, 6)
    ring.far()
    compute(GROUPS[2])
    ring.from_core(6, 8)
    compute(GROUPS[3])

    keeps = [
        pltpu.make_async_copy(kv, kvs.at[me.c, chip], local.at[0]),
        pltpu.make_async_copy(runs, places.at[chip], local.at[1]),
        pltpu.make_async_copy(xs, xs_out, local.at[4]),
    ]
    for d in keeps:
        d.start()
    pos_copies = [edges.copy(runs, places.at[chip], d) for d in far]
    kv_copies = [edges.copy(kv, kvs.at[me.c, chip], d) for d in far]
    over = [edges.copy(kv, kvs.at[me.c, chip], core)]
    ring = RingGather(me, edges, cot, cots, local.at[pl.ds(6, 2)])
    ring.relay()
    for (dz, dl), d in zip(chips_in_sequence(me), kv_copies):
        d.wait_recv()
        source = 2 * lax.rem(me.z - dz + 4, 4) + ((1 - me.xl) if dl else me.xl)
        ref = kvs.at[me.c, source]
        over.append(edges.copy(ref, ref, core))
    ring.rest()
    for d in over + pos_copies + wo_copies:
        d.wait_recv()
    for src, sem, stays in blocks:
        wait_sent(src, sem, stays)

    @pl.when(moved)
    def _():
        for d in swaps:
            d.wait()

    edges.finish()
    for d in keeps + [wq_save]:
        d.wait()


def begin(tokens, gain, pos, trig, wqkv, wgu, wdn, cot, wout):
    return pl.pallas_call(
        begin_kernel,
        out_shape=(
            shape((1024, Q_DEV)),
            shape((2, 512, 128), F32),
            shape((8, 64, 128), F32),
            shape((8, TOK), jnp.int32),
            shape((8, TOK, D)),
            shape((320, D)),
            shape((2, 8, 512, 128)),
            shape((8, 8, TOK), jnp.int32),
            shape((8, TOK, D)),
            shape((8, 256, Q_DEV)),
            shape((QUARTER, D)),
        ),
        in_specs=[VMEM, VMEM, VMEM, VMEM] + [ANY] * 5,
        out_specs=(VMEM, VMEM, VMEM, VMEM) + (ANY,) * 7,
        scratch_shapes=[
            pltpu.VMEM((TOK, D), BF16),
            pltpu.VMEM((8, TOK, D), BF16),
            pltpu.VMEM((320, D), BF16),
            pltpu.VMEM((512, 128), BF16),
            pltpu.VMEM((8, 8, TOK), jnp.int32),
            pltpu.VMEM((8, TOK), jnp.int32),
        ]
        + sems(7 + 7 + 6 + 2 * GATHER_EDGES + 7 + 7 + 8)
        + sems(5)
        + sems(8)
        + sems(2)
        + [pltpu.SemaphoreType.DMA((8,))],
        compiler_params=remote_params(0),
        name="begin",
    )(tokens, gain, pos, trig, wqkv, wgu, wdn, cot, wout)


def split_heads(rows):
    return jnp.concatenate([rows[:, HD * h : HD * (h + 1)] for h in range(4)], axis=0)


def join_heads(rows):
    return jnp.concatenate([rows[64 * h : 64 * (h + 1), :] for h in range(4)], axis=1)


def dot_last(a, b):
    return lax.dot_general(a, b, (((1,), (1,)), ((), ())), preferred_element_type=F32)


def dot_first(a, b):
    return lax.dot_general(a, b, (((0,), (0,)), ((), ())), preferred_element_type=F32)


def dot(a, b):
    return lax.dot_general(a, b, (((1,), (0,)), ((), ())), preferred_element_type=F32)


TILE = 256
WIDE = 8


def run_rows(runs, seq, chip, core, u):
    run = runs[16 * chip + 4 * seq + 2 * u + core]
    return pl.ds(pl.multiple_of(run * 64, 64), 64)


def sort_keys(runs, seq, kv_ref, sorted_kv):
    for j in range(32):
        chip, core, u = j // 4, (j // 2) % 2, j % 2
        to = run_rows(runs, seq, chip, core, u)
        rows, lanes = slice(64 * u, 64 * u + 64), slice(HD * core, HD * core + HD)
        both = [kv_ref[0, chip, rows, lanes], kv_ref[1, chip, rows, lanes]]
        sorted_kv[to, :] = jnp.concatenate(both, axis=1)


def turn(rows, lanes, turned):
    for i in range(4):
        at = slice(512 * i, 512 * (i + 1))
        turned[:, at] = rows[at, lanes].astype(F32).T.astype(BF16)


def allowed_tile(tile, run):
    key = lax.broadcasted_iota(jnp.int32, (TILE, 256), 0) + tile * TILE
    query = lax.rem(lax.broadcasted_iota(jnp.int32, (TILE, 256), 1), 64) + run * 64
    return key <= query


def tile_rows(tile):
    return pl.ds(pl.multiple_of(tile * TILE, TILE), TILE)


def attend_kernel(
    key_runs, query_runs, q_ref, kv_ref, att_ref, ot_ref, lse_ref,
    sorted_kv, values_t, high_ref, total_ref, acc_ref,
):
    seq = pl.program_id(0)
    sort_keys(key_runs, seq, kv_ref, sorted_kv)
    turn(sorted_kv, slice(HD, 2 * HD), values_t)
    empty = jnp.zeros((HD, 256), BF16)

    def one_run(r, _):
        run = query_runs[seq * 4 + r]
        rows = pl.ds(pl.multiple_of(r * 64, 64), 64)
        query = split_heads(q_ref[rows, :]).astype(F32).T.astype(BF16)
        query = jnp.concatenate([query, empty], axis=0)
        last = run // 4
        high_ref[...] = jnp.full((1, 256), FILLER, F32)
        total_ref[...] = jnp.zeros((1, 256), F32)
        acc_ref[...] = jnp.zeros((HD, 256), F32)

        def tiles(first, count, masked):
            scores = []
            for k in range(count):
                score = dot(sorted_kv[tile_rows(first + k), :], query)
                if masked and k == count - 1:
                    score = jnp.where(allowed_tile(first + k, run), score, FILLER)
                scores.append(score)
            high = high_ref[...]
            new_high = high
            for score in scores:
                new_high = jnp.maximum(new_high, jnp.max(score, axis=0, keepdims=True))
            scale = jnp.exp(high - new_high)
            total = total_ref[...] * scale
            acc = acc_ref[...] * scale
            for k, score in enumerate(scores):
                weights = jnp.exp(score - new_high)
                total = total + jnp.sum(weights, axis=0, keepdims=True)
                acc = acc + dot(values_t[:, tile_rows(first + k)], weights.astype(BF16))
            high_ref[...] = new_high
            total_ref[...] = total
            acc_ref[...] = acc

        for n in range(WIDE):

            @pl.when(last == n)
            def _():
                tiles(0, n + 1, True)

        total = total_ref[...]
        out = acc_ref[...] / total
        ot_ref[r] = out
        lse_ref[r] = high_ref[...] + jnp.log(total)
        att_ref[rows, :] = join_heads(out.T).astype(BF16)
        return 0

    lax.fori_loop(0, 4, one_run, 0)


def attend(key_runs, query_runs, q, kv):
    return pl.pallas_call(
        attend_kernel,
        out_shape=(shape((1024, 256)), shape((16, HD, 256), F32), shape((16, 1, 256), F32)),
        grid_spec=pltpu.PrefetchScalarGridSpec(
            num_scalar_prefetch=2,
            grid=(4,),
            in_specs=[
                pl.BlockSpec((256, 256), lambda i, *_: (i, 0)),
                pl.BlockSpec((2, 8, 128, 128), lambda i, *_: (0, 0, i, 0)),
            ],
            out_specs=[
                pl.BlockSpec((256, 256), lambda i, *_: (i, 0)),
                pl.BlockSpec((4, HD, 256), lambda i, *_: (i, 0, 0)),
                pl.BlockSpec((4, 1, 256), lambda i, *_: (i, 0, 0)),
            ],
            scratch_shapes=[
                pltpu.VMEM((2048, 2 * HD), BF16),
                pltpu.VMEM((HD, 2048), BF16),
                pltpu.VMEM((1, 256), F32),
                pltpu.VMEM((1, 256), F32),
                pltpu.VMEM((HD, 256), F32),
            ],
        ),
        compiler_params=pltpu.CompilerParams(vmem_limit_bytes=61 * 2**20),
        name="attend",
    )(key_runs, query_runs, q, kv)


def attend_back_kernel(
    key_runs, query_runs, q_ref, kv_ref, da_ref, ot_ref, lse_ref, trig_ref,
    dq_ref, dkv_ref, sorted_kv, keys_t, grad_kv, dq_acc,
):
    seq = pl.program_id(0)
    sort_keys(key_runs, seq, kv_ref, sorted_kv)
    turn(sorted_kv, slice(0, HD), keys_t)
    grad_kv[...] = jnp.zeros_like(grad_kv)
    empty = jnp.zeros((HD, 256), BF16)
    blank = jnp.zeros((256, HD), BF16)

    def one_run(r, _):
        run = query_runs[seq * 4 + r]
        rows = pl.ds(pl.multiple_of(r * 64, 64), 64)
        query = split_heads(q_ref[rows, :])
        grad = split_heads(da_ref[rows, :])
        lse = lse_ref[r]
        query_t = query.astype(F32).T.astype(BF16)
        grad_t = grad.astype(F32).T
        delta = jnp.sum(grad_t * ot_ref[r], axis=0, keepdims=True)
        query_t = jnp.concatenate([query_t, empty], axis=0)
        grad_t = jnp.concatenate([empty, grad_t.astype(BF16)], axis=0)
        right = jnp.concatenate(
            [
                jnp.concatenate([query, blank], axis=1),
                jnp.concatenate([blank, grad], axis=1),
            ],
            axis=0,
        )
        last = run // 4
        dq_acc[...] = jnp.zeros((HD, 256), F32)

        def tiles(first, count, masked):
            dq = dq_acc[...]
            for k in range(count):
                at = tile_rows(first + k)
                both = sorted_kv[at, :]
                probs = jnp.exp(dot(both, query_t) - lse)
                if masked and k == count - 1:
                    probs = jnp.where(allowed_tile(first + k, run), probs, 0.0)
                grad_probs = dot(both, grad_t)
                grad_scores = (probs * (grad_probs - delta)).astype(BF16)
                left = jnp.concatenate([grad_scores, probs.astype(BF16)], axis=1)
                grad_kv[at, :] += dot(left, right)
                dq = dq + dot(keys_t[:, at], grad_scores)
            dq_acc[...] = dq

        for n in range(WIDE):

            @pl.when(last == n)
            def _():
                tiles(0, n + 1, True)

        pair_rows = trig_ref[lax.rem(r, 2)]
        table = jnp.where(r < 2, rotary_of(pair_rows, 0), rotary_of(pair_rows, 1))
        dq = (dq_acc[...] * 0.125).T
        heads = [rotate(dq[64 * h : 64 * h + 64], table, back=True) for h in range(4)]
        dq_ref[rows, :] = jnp.concatenate(heads, axis=1).astype(BF16)
        return 0

    lax.fori_loop(0, 4, one_run, 0)
    for j in range(32):
        chip, core, u = j // 4, (j // 2) % 2, j % 2
        at = run_rows(key_runs, seq, chip, core, u)
        rows, lanes = slice(64 * u, 64 * u + 64), slice(HD * core, HD * core + HD)
        both = grad_kv[at, :].astype(BF16)
        dkv_ref[0, chip, rows, lanes] = both[:, :HD]
        dkv_ref[1, chip, rows, lanes] = both[:, HD:]


def attend_back(key_runs, query_runs, q, kv, grad, ot, lse, trigs):
    return pl.pallas_call(
        attend_back_kernel,
        out_shape=(shape((1024, 256)), shape((2, 8, 512, 128))),
        grid_spec=pltpu.PrefetchScalarGridSpec(
            num_scalar_prefetch=2,
            grid=(4,),
            in_specs=[
                pl.BlockSpec((256, 256), lambda i, *_: (i, 0)),
                pl.BlockSpec((2, 8, 128, 128), lambda i, *_: (0, 0, i, 0)),
                pl.BlockSpec((256, 256), lambda i, *_: (i, 0)),
                pl.BlockSpec((4, HD, 256), lambda i, *_: (i, 0, 0)),
                pl.BlockSpec((4, 1, 256), lambda i, *_: (i, 0, 0)),
                pl.BlockSpec((2, 64, 128), lambda i, *_: (i, 0, 0)),
            ],
            out_specs=[
                pl.BlockSpec((256, 256), lambda i, *_: (i, 0)),
                pl.BlockSpec((2, 8, 128, 128), lambda i, *_: (0, 0, i, 0)),
            ],
            scratch_shapes=[
                pltpu.VMEM((2048, 2 * HD), BF16),
                pltpu.VMEM((HD, 2048), BF16),
                pltpu.VMEM((2048, 2 * HD), F32),
                pltpu.VMEM((HD, 256), F32),
            ],
        ),
        compiler_params=pltpu.CompilerParams(vmem_limit_bytes=61 * 2**20),
        name="attend_back",
    )(key_runs, query_runs, q, kv, grad, ot, lse, trigs)


PART = 3 * FF_DEV // 2
PART_HALF = PART // 2


class RingSum:
    def __init__(
        self, me, edges, along_z, src, start, rows, width, step, relayed, last, shift=0
    ):
        self.edges, self.src, self.start, self.width, self.step = edges, src, start, width, step
        self.rows, self.half = rows, rows // 2
        self.relayed, self.last, self.shift = relayed, last, shift
        self.here = me.z if along_z else x_of(me)
        self.up = around(me, 1, 0) if along_z else around(me, 0, 1)
        self.down = around(me, -1, 0) if along_z else around(me, 0, 3)
        self.a, self.b = pl.ds(0, self.half), pl.ds(self.half, self.half)

    def columns(self, k):
        at = self.width * lax.rem(self.here + k + self.shift, 4)
        return pl.ds(pl.multiple_of(at, self.width), self.width)

    def piece(self, k, half):
        rows = pl.ds(self.start + self.half * half, self.half)
        return self.src.at[rows, self.columns(k)]

    def far(self):
        self.r_a = self.edges.copy(self.piece(2, 0), self.relayed.at[0], self.up)
        self.r_b = self.edges.copy(self.piece(2, 1), self.relayed.at[1], self.down)

    def near_up(self):
        self.u_b = self.edges.copy(self.piece(1, 1), self.last.at[0, self.b], self.up)

    def near_down(self):
        self.d_a = self.edges.copy(self.piece(3, 0), self.last.at[1, self.a], self.down)

    def add(self, k, half):
        step, start, cols = self.step, self.start + self.half * half, self.columns(k)

        def one(i, _):
            at = pl.ds(pl.multiple_of(start + i * step, 16), step)
            from_ = pl.ds(pl.multiple_of(i * step, 16), step)
            self.src[at, cols] = (
                self.src[at, cols].astype(F32) + self.relayed[half, from_, :].astype(F32)
            ).astype(BF16)
            return 0

        lax.fori_loop(0, self.half // step, one, 0)

    def second(self):
        self.r_a.wait_recv()
        self.add(1, 0)
        self.u_a = self.edges.copy(self.piece(1, 0), self.last.at[0, self.a], self.up)
        self.r_b.wait_recv()
        self.add(3, 1)
        self.d_b = self.edges.copy(self.piece(3, 1), self.last.at[1, self.b], self.down)

    def total(self, out):
        for d in (self.u_b, self.d_a, self.u_a, self.d_b):
            d.wait_recv()
        step, cols = self.step, self.columns(0)

        def one(i, _):
            at = pl.ds(pl.multiple_of(self.start + i * step, 16), step)
            from_ = pl.ds(pl.multiple_of(i * step, 16), step)
            out[from_, :] = (
                self.src[at, cols].astype(F32)
                + self.last[0, from_, :].astype(F32)
                + self.last[1, from_, :].astype(F32)
            ).astype(BF16)
            return 0

        lax.fori_loop(0, self.rows // step, one, 0)


SUM_EDGES = 6


def to_chunks(ref, ys, halves, cols, rows):
    for i, (y, half) in enumerate(zip(ys, halves)):
        for core in (0, 1):
            at = TOK * i + HALF * core
            ref[2 * y + core, HALF * half : HALF * half + HALF, cols] = rows[at : at + HALF]


def feed_forward_kernel(
    att, wo, tokens, cot, gain, cots, wgu, wdn, wswap, wnear_up, wnear_down,
    middle, grad_middle, gain_grad, grad_att, grad_wo, z_out, x_out, branch,
    xs, p, c, gp, gb, att_t, w, act_t, gate_t, up_t, act, dgate, dup, low,
    g1, b1, r1, l1,
    z_relayed, z_last, x_relayed, x_last, z_q, x_q,
    z_relayed2, z_last2, x_relayed2, x_last2,
    send, recv, fs, fr, local,
):
    me = Place()
    core = me.at(core=1 - me.c)
    signalled = greet(
        [core, me.at(dy=1), me.at(dy=-1)]
        + [around(me, k, 0) for k in (1, 2, 3)]
        + [around(me, 0, 1), around(me, 0, 3)]
    )
    edges = Edges(send, recv)
    moved = me.c != me.xh
    load_c = pltpu.make_async_copy(cots, c, local.at[1])
    load_c.start()

    def w_rows(dz):
        z = lax.rem(me.z + dz + 4, 4)
        return (
            pl.ds(pl.multiple_of(GU_QUARTER * z, 16), GU_QUARTER),
            pl.ds(pl.multiple_of(2 * FF_DEV + DN_QUARTER * z, 16), DN_QUARTER),
        )

    gu_part, dn_part = pl.ds(0, GU_QUARTER), pl.ds(GU_QUARTER, DN_QUARTER)
    kept = [
        pltpu.make_async_copy(wgu, w.at[pl.ds(0, 2 * FF_DEV)], local.at[2]),
        pltpu.make_async_copy(wdn, w.at[pl.ds(2 * FF_DEV, FF_DEV)], local.at[3]),
    ]
    near_w = []
    for i, (src, dz) in enumerate(((wswap, 0), (wnear_up, -1), (wnear_down, 1))):
        gu_rows, dn_rows = w_rows(dz)
        near_w.append(pltpu.make_async_copy(src.at[gu_part], w.at[gu_rows], local.at[4 + 2 * i]))
        near_w.append(pltpu.make_async_copy(src.at[dn_part], w.at[dn_rows], local.at[5 + 2 * i]))
    far_w = [
        pltpu.make_async_remote_copy(
            src_ref=wswap.at[part],
            dst_ref=w.at[rows],
            send_sem=fs.at[i],
            recv_sem=fr.at[i],
            device_id=me.at(dz=2),
            device_id_type=pl.DeviceIdType.MESH,
        )
        for i, (part, rows) in enumerate(zip((gu_part, dn_part), w_rows(0)))
    ]

    met(signalled)

    @pl.when(moved)
    def _():
        for d in far_w + near_w:
            d.start()

    @pl.when(jnp.logical_not(moved))
    def _():
        for d in kept:
            d.start()

    ring = RingScatter(me, edges, p, (g1, b1, r1, l1))

    def attended_part(k):
        y = lax.rem(me.y + k, 4)
        rows = att[pl.ds(pl.multiple_of(2 * TOK * y, 2 * TOK), 2 * TOK), :]

        def block(i, _):
            cols = pl.ds(pl.multiple_of(512 * i, 512), 512)
            term = dot_last(rows, wo[cols, :]).astype(BF16)
            to_chunks(p, (y, y), (0, 1), cols, term)
            return 0

        lax.fori_loop(0, 4, block, 0)
        ring.send_core(k)

    attended_part(2)
    attended_part(1)
    ring.far()
    attended_part(3)
    ring.near()
    attended_part(0)
    ring.add_core(0)

    def turn_block(i, _):
        at = pl.ds(pl.multiple_of(2 * TOK * i, 2 * TOK), 2 * TOK)
        att_t[:, at] = att[at, :].astype(F32).T.astype(BF16)
        return 0

    lax.fori_loop(0, 4, turn_block, 0)
    ring.second()
    ring.arrived()

    def norm(at):
        rows = tokens[at, :].astype(F32) + ring.rows(at)
        middle[at, :] = rows
        normal = rows * lax.rsqrt(mean_last(rows * rows) + EPSILON)
        low[at, :] = (normal * gain[...]).astype(BF16)

    in_chunks(norm)
    gather = RingGather(me, edges, low, xs, local.at[pl.ds(10, 2)])
    ring.release()

    @pl.when(moved)
    def _():
        for d in near_w:
            d.wait()
        for d in far_w:
            d.wait()

    @pl.when(jnp.logical_not(moved))
    def _():
        for d in kept:
            d.wait()

    load_c.wait()

    def compute(group):
        ys = [lax.rem(me.y + dy, 4) for dy, _ in group]
        halves = [half for _, half in group]
        blocks = [2 * y + half for y, half in zip(ys, halves)]
        x = jnp.concatenate([xs[b] for b in blocks], axis=0)
        g = jnp.concatenate([c[b] for b in blocks], axis=0)
        here = [pl.ds(pl.multiple_of(TOK * b, TOK), TOK) for b in blocks]
        for n0, n1 in ((0, 256), (256, 512), (512, FF_DEV)):
            gate = dot_last(x, w[n0:n1, :])
            upward = dot_last(x, w[FF_DEV + n0 : FF_DEV + n1, :])
            grad = dot_last(g, w[2 * FF_DEV + n0 : 2 * FF_DEV + n1, :])
            sigmoid = 1.0 / (1.0 + jnp.exp(-gate))
            swish = gate * sigmoid
            active = swish * upward
            grad_up = grad * swish
            grad_gate = grad * upward * sigmoid * (1.0 + gate * (1.0 - sigmoid))
            act[:, n0:n1] = active.astype(BF16)
            dup[:, n0:n1] = grad_up.astype(BF16)
            dgate[:, n0:n1] = grad_gate.astype(BF16)
            for ref, value in ((act_t, active), (up_t, grad_up), (gate_t, grad_gate)):
                value = value.T.astype(BF16)
                ref[n0:n1, here[0]] = value[:, :TOK]
                ref[n0:n1, here[1]] = value[:, TOK:]

        def block(i, _):
            cols = pl.ds(pl.multiple_of(512 * i, 512), 512)
            term = dot(act[...], w[2 * FF_DEV :, cols])
            to_chunks(p, ys, halves, cols, term.astype(BF16))
            grads = dot(dgate[...], w[:FF_DEV, cols]) + dot(dup[...], w[FF_DEV : 2 * FF_DEV, cols])
            to_chunks(gp, ys, halves, cols, grads.astype(BF16))
            return 0

        lax.fori_loop(0, 4, block, 0)

    two = RingScatter(me, edges, gp, (g1, b1, r1, l1))
    gather.own()
    compute(GROUPS[0])
    two.send_core(0)
    gather.relay()
    gather.near()
    gather.from_core(2, 4)
    compute(GROUPS[1])
    gather.from_core(4, 6)
    gather.far()
    compute(GROUPS[2])
    two.send_core(1)
    two.send_core(3)
    two.near()
    gather.from_core(6, 8)
    compute(GROUPS[3])
    two.send_core(2)
    save = pltpu.make_async_copy(p, branch, local.at[0])
    save.start()
    two.add_core(0)

    z_sum = RingSum(me, edges, True, w, 0, PART, 512, 48, z_relayed, z_last)
    x_sum = RingSum(me, edges, False, w, PART, PART, 512, 48, x_relayed, x_last)
    split = PART - FF_DEV

    def z_task(k):
        cols = z_sum.columns(k)
        x = xs[:, :, cols].reshape(8 * TOK, 512)
        w[:FF_DEV, cols] = dot(gate_t[...], x).astype(BF16)
        w[FF_DEV:PART, cols] = dot(up_t[:split, :], x).astype(BF16)

    def x_task(k):
        cols = x_sum.columns(k)
        x = xs[:, :, cols].reshape(8 * TOK, 512)
        g = c[:, :, cols].reshape(8 * TOK, 512)
        w[PART : 2 * FF_DEV, cols] = dot(up_t[split:, :], x).astype(BF16)
        w[2 * FF_DEV :, cols] = dot(act_t[...], g).astype(BF16)

    two.far()
    z_task(2)
    z_sum.far()
    x_task(2)
    x_sum.far()
    z_task(1)
    z_sum.near_up()
    x_task(1)
    x_sum.near_up()
    two.second()
    z_task(3)
    z_sum.near_down()
    x_task(3)
    x_sum.near_down()
    z_task(0)
    x_task(0)
    two.arrived()
    gain_grad[...] = jnp.zeros_like(gain_grad)

    def back(at):
        rows = middle[at, :]
        inverse = lax.rsqrt(mean_last(rows * rows) + EPSILON)
        normal = rows * inverse
        grad = two.rows(at)
        gain_grad[...] += jnp.sum(normal * grad, axis=0, keepdims=True)
        scaled = grad * gain[...]
        result = cot[at, :].astype(F32) + inverse * (
            scaled - normal * mean_last(scaled * normal)
        )
        grad_middle[at, :] = result
        low[at, :] = result.astype(BF16)

    edges.sent(gather.sources())
    in_chunks(back)
    gather = RingGather(me, edges, low, gb, local.at[pl.ds(10, 2)])
    z_sum.second()
    x_sum.second()
    gather.relay()
    z_sum.total(z_q)
    z_two = RingSum(me, edges, False, z_q, 0, PART, 128, 176, z_relayed2, z_last2)
    z_two.far()
    z_two.near_up()
    z_two.near_down()
    x_sum.total(x_q)
    x_two = RingSum(me, edges, True, x_q, 0, PART, 128, 176, x_relayed2, x_last2)
    x_two.far()
    x_two.near_up()
    x_two.near_down()
    gather.near()
    gather.far()
    gather.own()
    gather.from_core(2, 8)

    def attended_grad(i, _):
        at = pl.ds(pl.multiple_of(2 * TOK * i, 2 * TOK), 2 * TOK)
        rows = gb[pl.ds(2 * i, 2)].reshape(2 * TOK, D)
        grad_att[at, :] = dot(rows, wo[...]).astype(BF16)
        cols = pl.ds(pl.multiple_of(512 * i, 512), 512)
        rows = gb[:, :, cols].reshape(8 * TOK, 512)
        grad_wo[:, cols] = dot(att_t[...], rows).astype(BF16)
        return 0

    lax.fori_loop(0, 4, attended_grad, 0)
    z_two.second()
    x_two.second()
    z_two.total(z_out)
    x_two.total(x_out)
    edges.finish()
    save.wait()


def feed_forward(att, wo, tokens, cot, gain, cots, wgu, wdn, wswap, wnear_up, wnear_down):
    block = pltpu.VMEM((8, TOK, D), BF16)
    turned = pltpu.VMEM((FF_DEV, 8 * TOK), BF16)
    pair = pltpu.VMEM((2 * TOK, FF_DEV), BF16)

    def ring(width):
        return [
            pltpu.VMEM((2, PART_HALF, width), BF16),
            pltpu.VMEM((2, PART, width), BF16),
        ] * 2

    return pl.pallas_call(
        feed_forward_kernel,
        out_shape=(
            shape((TOK, D), F32),
            shape((TOK, D), F32),
            shape((1, D), F32),
            shape((1024, Q_DEV)),
            shape((Q_DEV, D)),
            shape((PART, 128)),
            shape((PART, 128)),
            shape((8, TOK, D)),
        ),
        in_specs=[VMEM] * 5 + [ANY] * 6,
        out_specs=(VMEM,) * 7 + (ANY,),
        scratch_shapes=[block] * 5
        + [pltpu.VMEM((Q_DEV, 8 * TOK), BF16)]
        + [pltpu.VMEM((3 * FF_DEV, D), BF16)]
        + [turned] * 3
        + [pair] * 3
        + [pltpu.VMEM((TOK, D), BF16)]
        + scatter_scratch()
        + ring(512)
        + [pltpu.VMEM((PART, 512), BF16)] * 2
        + ring(128)
        + sems(2 * SCATTER_EDGES + 2 * GATHER_EDGES + 4 * SUM_EDGES)
        + sems(2)
        + [pltpu.SemaphoreType.DMA((12,))],
        compiler_params=pltpu.CompilerParams(
            collective_id=2, has_side_effects=True, vmem_limit_bytes=61 * 2**20
        ),
        name="feed_forward",
    )(att, wo, tokens, cot, gain, cots, wgu, wdn, wswap, wnear_up, wnear_down)


def columns(width):
    return lambda i: (slice(None), pl.ds(pl.multiple_of(i * width, width), width))


def row_block(height, start=0):
    return lambda i: (pl.ds(pl.multiple_of(start + i * height, height), height), slice(None))


def plane_devices(me):
    found = [me.at(core=1 - me.c)]
    for dz, dx in STEPS:
        z, xl, core, y, xh = around(me, dz, dx)
        found += [(z, xl, core, y, xh), (z, xl, 1 - core, y, xh)]
    return found


def swapped_pairs(rows):
    return jnp.concatenate([halves_swapped(rows[:, :HD]), halves_swapped(rows[:, HD:])], axis=1)


class RingBlocks:
    def __init__(self, me, edges, ref, columns):
        self.me, self.edges, self.ref, self.columns = me, edges, ref, columns
        rows = ref.shape[0]
        self.halves = (pl.ds(0, rows // 2), pl.ds(rows // 2, rows // 2))
        self.up, self.down = me.at(dz=1), me.at(dz=-1)
        self.up_a = self.send(0, 0, self.up)
        self.down_b = self.send(0, 1, self.down)
        self.up_b = self.send(0, 1, self.up)
        self.down_a = self.send(0, 0, self.down)

    def block(self, dz):
        return self.ref.at[:, self.columns(lax.rem(self.me.z + dz + 4, 4))]

    def send(self, dz, half, device):
        cols = self.columns(lax.rem(self.me.z + dz + 4, 4))
        ref = self.ref.at[self.halves[half], cols]
        return self.edges.copy(ref, ref, device)

    def relay(self):
        self.up_a.wait_recv()
        self.on_a = self.send(-1, 0, self.up)
        self.down_b.wait_recv()
        self.on_b = self.send(1, 1, self.down)

    def near(self):
        self.up_b.wait_recv()
        self.down_a.wait_recv()

    def far(self):
        self.on_a.wait_recv()
        self.on_b.wait_recv()


class PlaneGather:
    def __init__(self, me, edges, z_piece, x_piece, z_all, x_all, send, recv):
        self.me, self.edges, self.z_all, self.x_all = me, edges, z_all, x_all
        self.send, self.recv, self.z_piece, self.x_piece = send, recv, z_piece, x_piece
        self.stays = me.c == me.xh
        self.core = me.at(core=1 - me.c)
        self.side = me.at(xl=1 - me.xl)
        across = me.at(core=1 - me.c, xl=1 - me.xl, xh=1 - me.xh)
        x = x_of(me)
        self.held = jnp.where(self.stays, x, 3 - x)
        for i, (piece, ref, at) in enumerate(
            ((z_piece, z_all, 4 * me.z + x), (x_piece, x_all, 4 * x + me.z))
        ):
            dst = ref.at[columns(128)(at)]
            send_block(me, piece, dst, send.at[i], recv.at[i], across, self.stays)

    def z_columns(self, z):
        return pl.ds(pl.multiple_of(512 * z + 256 * self.me.c, 256), 256)

    def x_columns(self, z):
        return pl.ds(pl.multiple_of(512 * self.held + 128 * z, 128), 128)

    def side_block(self, dz):
        held = self.held + 1 - 2 * lax.rem(self.held, 2)
        z = lax.rem(self.me.z + dz + 4, 4)
        return self.x_all.at[columns(128)(4 * held + z)]

    def pass_core(self, ref):
        self.over.append(self.edges.copy(ref, ref, self.core))

    def sideways(self):
        own = self.z_all.at[columns(128)(4 * self.me.z + self.held)]
        wait_got(own, self.recv.at[0])
        self.z_side = self.edges.copy(own, own, self.side)
        own = self.x_all.at[:, self.x_columns(self.me.z)]
        wait_got(own, self.recv.at[1])
        self.x_ring = RingBlocks(self.me, self.edges, self.x_all, self.x_columns)
        self.x_side = [self.edges.copy(own, own, self.side)]
        self.over = []
        self.pass_core(own)

    def along(self):
        self.z_side.wait_recv()
        self.z_ring = RingBlocks(self.me, self.edges, self.z_all, self.z_columns)
        self.pass_core(self.z_ring.block(0))
        self.x_ring.relay()

    def to_side(self, dz):
        ref = self.x_ring.block(dz)
        self.x_side.append(self.edges.copy(ref, ref, self.side))

    def near(self):
        self.x_ring.near()
        self.to_side(1)
        self.to_side(-1)
        self.z_ring.relay()
        self.x_ring.far()
        self.to_side(2)
        for dz in (1, -1, 2):
            self.pass_core(self.x_ring.block(dz))

    def far(self):
        self.z_ring.near()
        self.pass_core(self.z_ring.block(1))
        self.pass_core(self.z_ring.block(-1))
        self.z_ring.far()
        self.pass_core(self.z_ring.block(2))
        for d, dz in zip(self.x_side, (0, 1, -1, 2)):
            d.wait_recv()
            self.pass_core(self.side_block(dz))

    def finish(self):
        for d in self.over:
            d.wait_recv()
        wait_sent(self.z_piece, self.send.at[0], self.stays)
        wait_sent(self.x_piece, self.send.at[1], self.stays)


PLANE_EDGES = 1 + 2 * SUM_EDGES + 4 + 12


class TwoSums:
    def __init__(self, me, edges, src, rows, steps, scratch):
        self.me, self.edges, self.rows, self.steps = me, edges, rows, steps
        self.q, self.out = scratch[4:6], scratch[10:12]
        self.scratch = scratch
        start = (0, rows[0])
        self.one = [
            RingSum(
                me, edges, i == 0, src, start[i], rows[i], 512, steps[0][i],
                scratch[2 * i], scratch[2 * i + 1], me.y,
            )
            for i in (0, 1)
        ]
        for ring in self.one:
            ring.far()
            ring.near_up()
            ring.near_down()

    def second(self):
        for ring in self.one:
            ring.second()

    def cross(self):
        self.two = []
        for i in (0, 1):
            self.one[i].total(self.q[i])
            ring = RingSum(
                self.me, self.edges, i == 1, self.q[i], 0, self.rows[i], 128,
                self.steps[1][i], self.scratch[6 + 2 * i], self.scratch[7 + 2 * i],
            )
            ring.far()
            ring.near_up()
            ring.near_down()
            self.two.append(ring)

    def fourth(self):
        for ring in self.two:
            ring.second()

    def total(self):
        for i in (0, 1):
            self.two[i].total(self.out[i])


def two_sums_scratch(rows):
    found = []
    for r in rows:
        found += [pltpu.VMEM((2, r // 2, 512), BF16), pltpu.VMEM((2, r, 512), BF16)]
    found += [pltpu.VMEM((r, 512), BF16) for r in rows]
    for r in rows:
        found += [pltpu.VMEM((2, r // 2, 128), BF16), pltpu.VMEM((2, r, 128), BF16)]
    return found + [pltpu.VMEM((r, 128), BF16) for r in rows]


EARLY_ROWS = (256, 256)


def ending_kernel(
    dkv, dq, kv_table, wq, tokens, gain, grad_middle, gain_two, z_piece, x_piece, middle,
    gwo, xs_in, branch_in,
    output, grad_tokens, gains, wq_out, wo_out, z_all, x_all,
    kv_got, kv_both, kv_last, dkv_low, xs, grads, grads_t, parts, branch_parts, early, late,
    g1, b1, r1, l1, g2, b2, r2, l2,
    wq_all, wo_all, late_own, late_got, late_piece, mine, near, near_sum, owners,
    *rest,
):
    early_scratch = rest[:12]
    (send, recv, ds, dr, es, er, ps, pr, gs, gr, hs, hr, us, ur, local) = rest[12:]
    me = Place()
    core = me.at(core=1 - me.c)
    far = [
        me.at(dz=dz, xl=(1 - me.xl) if dl else me.xl) for dz, dl in chips_in_sequence(me)
    ]
    signalled = greet(plane_devices(me) + group_members(me)[1:])
    edges = Edges(send, recv)
    place = 4 * me.z + x_of(me)
    rank = 2 * me.y + me.c
    load_x = pltpu.make_async_copy(xs_in, xs, local.at[0])
    load_branch = pltpu.make_async_copy(branch_in, branch_parts, local.at[1])
    load_wo = [
        pltpu.make_async_copy(
            gwo.at[pl.ds(128 * i, 128)], early.at[pl.ds(256 * i + 128, 128)], local.at[2 + i]
        )
        for i in (0, 1)
    ]
    for d in [load_x, load_branch] + load_wo:
        d.start()

    def query_part(i, _):
        at = pl.ds(pl.multiple_of(2 * TOK * i, 2 * TOK), 2 * TOK)
        rows = dq[at, :]
        grads[at, :Q_DEV] = rows
        grads_t[:Q_DEV, at] = rows.astype(F32).T.astype(BF16)
        return 0

    lax.fori_loop(0, 4, query_part, 0)
    met(signalled)

    order = []
    for dz, dl in chips_in_sequence(me) + [(0, 0)]:
        chip = 2 * lax.rem(me.z + dz, 4) + ((1 - me.xl) if dl else me.xl)
        order.append((chip, edges.copy(dkv.at[1 - me.c, chip], kv_got.at[chip], core)))
    load_branch.wait()
    branch = RingScatter(me, edges, branch_parts, (g2, b2, r2, l2))
    for k in (2, 1, 3, 0):
        branch.send_core(k)
    far_copies = []
    for i, (chip, d) in enumerate(order):
        d.wait_recv()
        kv_both[chip] = (dkv[me.c, chip].astype(F32) + kv_got[chip].astype(F32)).astype(BF16)
        if i < 7:
            far_copies.append(edges.copy(kv_both.at[chip], kv_last.at[i], far[i]))
    plane = PlaneGather(me, edges, z_piece, x_piece, z_all, x_all, ps, pr)
    load_x.wait()

    def weight_block(i, _):
        cols = pl.ds(pl.multiple_of(512 * i, 512), 512)
        rows = xs[:, :, cols].reshape(8 * TOK, 512)
        early[:128, cols] = dot(grads_t[:128, :], rows).astype(BF16)
        early[256:384, cols] = dot(grads_t[128:Q_DEV, :], rows).astype(BF16)
        return 0

    lax.fori_loop(0, 4, weight_block, 0)
    for d in load_wo:
        d.wait()
    early_sum = TwoSums(me, edges, early, EARLY_ROWS, ((64, 64), (128, 128)), early_scratch)
    branch.far()
    branch.near()
    branch.add_core(0)
    for d in far_copies:
        d.wait_recv()

    def kv_total(at):
        total = kv_both[2 * me.z + me.xl, at].astype(F32)
        for i in range(7):
            total = total + kv_last[i, at].astype(F32)
        dkv_low[at, :] = (
            total * kv_table[0, at, :] - swapped_pairs(total) * kv_table[1, at, :]
        )

    in_chunks(kv_total, 512, 128)
    for i in range(8):
        rows = dkv_low[64 * i : 64 * (i + 1), :]
        rows = jnp.concatenate([rows[:, :HD], rows[:, HD:]], axis=0)
        at = slice(TOK * i, TOK * (i + 1))
        grads[at, Q_DEV:] = rows.astype(BF16)
        grads_t[Q_DEV:, at] = rows.T.astype(BF16)

    early_sum.second()
    branch.second()
    def late_block(i, _):
        cols = pl.ds(pl.multiple_of(512 * i, 512), 512)
        rows = xs[:, :, cols].reshape(8 * TOK, 512)
        late[:, cols] = dot(grads_t[Q_DEV:, :], rows).astype(BF16)
        return 0

    ring = RingScatter(me, edges, parts, (g1, b1, r1, l1))

    def part(k):
        y = lax.rem(me.y + k, 4)
        rows = grads[pl.ds(pl.multiple_of(2 * TOK * y, 2 * TOK), 2 * TOK), :]

        def block(i, _):
            cols = pl.ds(pl.multiple_of(512 * i, 512), 512)
            to_chunks(parts, (y, y), (0, 1), cols, dot(rows, wq[:, cols]).astype(BF16))
            return 0

        lax.fori_loop(0, 4, block, 0)
        ring.send_core(k)

    part(2)
    part(1)
    ring.far()
    early_sum.cross()
    part(3)
    ring.near()
    part(0)
    ring.add_core(0)
    early_sum.fourth()
    plane.sideways()
    lax.fori_loop(0, 4, late_block, 0)
    late_sum = SumOfSixteen(me, late, columns(128), late_own, late_got, us, ur, local.at[4])
    early_sum.total()
    wq_deliver = Deliver(me, ds, dr)

    def deliver_block(j, src, at):
        block = own_block(me, j)
        owner, slot = block // 5, lax.rem(block, 5)
        dst = wq_all.at[
            pl.ds(pl.multiple_of(64 * slot, 64), 64),
            pl.ds(pl.multiple_of(128 * at, 128), 128),
        ]
        wq_deliver.to_owner(src, dst, at // 8, owner // 2, lax.rem(owner, 2))

    wo_deliver = Deliver(me, es, er)
    early_place = 4 * lax.rem(me.z + me.y, 4) + x_of(me)
    early_turned = 4 * lax.rem(x_of(me) + me.y, 4) + me.z
    for i, at in enumerate((early_place, early_turned)):
        for j in (0, 1):
            deliver_block(2 * i + j, early_sum.out[i].at[pl.ds(64 * j, 64)], at)
        dst = wo_all.at[
            pl.ds(pl.multiple_of(Q_DEV * rank + 128 * i, 128), 128),
            pl.ds(pl.multiple_of(128 * lax.rem(at, 2), 128), 128),
        ]
        src = early_sum.out[i].at[pl.ds(128, 128)]
        wo_deliver.to_owner(src, dst, me.y // 2, at // 4, lax.rem(at // 2, 2))
    plane.along()
    late_piece[...] = late_sum.total().astype(BF16)
    deliver_block(4, late_piece, place)
    ring.second()
    plane.near()
    branch.arrived()

    def out(at):
        output[at, :] = (middle[at, :] + branch.rows(at)).astype(BF16)

    in_chunks(out)
    ring.arrived()
    mine[...] = jnp.zeros_like(mine)
    mine[1:2, :] = gain_two[...]

    def back(at):
        rows = tokens[at, :].astype(F32)
        inverse = lax.rsqrt(mean_last(rows * rows) + EPSILON)
        normal = rows * inverse
        grad = ring.rows(at)
        mine[0:1, :] += jnp.sum(normal * grad, axis=0, keepdims=True)
        scaled = grad * gain[...]
        grad_tokens[at, :] = grad_middle[at, :] + inverse * (
            scaled - normal * mean_last(scaled * normal)
        )

    in_chunks(back)

    def slice_of(member):
        return mine.at[:, pl.ds(pl.multiple_of(256 * member, 256), 256)]

    near_copies = []
    for k in range(1, 8):
        dy, other = k // 2, k % 2
        y = lax.rem(me.y + dy, 4)
        to_core = 1 - me.c if other else me.c
        d = pltpu.make_async_remote_copy(
            src_ref=slice_of(2 * y + to_core),
            dst_ref=near.at[k - 1],
            send_sem=gs.at[k - 1],
            recv_sem=gr,
            device_id=me.at(y=y, core=to_core),
            device_id_type=pl.DeviceIdType.MESH,
        )
        d.start()
        near_copies.append(d)
    plane.far()
    own = mine[:, pl.ds(pl.multiple_of(256 * rank, 256), 256)]
    wait_got(near, gr)
    for k in range(7):
        own = own + near[k]
    near_sum[...] = own
    gain_deliver = Deliver(me, hs, hr)
    for to_core in (0, 1):
        gain_deliver.to_owner(near_sum, owners.at[place], to_core, me.y, me.c)

    half = pl.ds(pl.multiple_of(1024 * me.c, 1024), 1024)
    over = []
    for ref, sem in ((wo_all.at[half], er), (wq_all.at[:, half], dr)):
        wait_got(ref, sem)
        over.append(edges.copy(ref, ref, core))
    wait_got(owners, hr)
    sum_all = owners[0]
    for k in range(1, 16):
        sum_all = sum_all + owners[k]
    gains[...] = sum_all
    for d in over:
        d.wait_recv()
    wo_out[...] = wo_all[...]
    wq_out[...] = wq_all[...]
    plane.finish()
    late_sum.finish()
    for d in (wo_deliver, wq_deliver, gain_deliver):
        d.finish()
    for d in near_copies:
        d.wait_send()
    edges.finish()


def ending(
    dkv, dq, kv_table, wq, tokens, gain, grad_middle, gain_two, z_piece, x_piece, middle,
    gwo, xs, branch,
):
    many = pltpu.SemaphoreType.DMA
    return pl.pallas_call(
        ending_kernel,
        out_shape=(
            shape((TOK, D)),
            shape((TOK, D), F32),
            shape((8, 256), F32),
            shape((320, D)),
            shape((D, 256)),
            shape((PART, D)),
            shape((PART, D)),
        ),
        in_specs=[VMEM] * 11 + [ANY] * 3,
        out_specs=(VMEM,) * 5 + (ANY,) * 2,
        scratch_shapes=[
            pltpu.VMEM((8, 512, 128), BF16),
            pltpu.VMEM((8, 512, 128), BF16),
            pltpu.VMEM((7, 512, 128), BF16),
            pltpu.VMEM((512, 128), F32),
            pltpu.VMEM((8, TOK, D), BF16),
            pltpu.VMEM((1024, 320), BF16),
            pltpu.VMEM((320, 1024), BF16),
            pltpu.VMEM((8, TOK, D), BF16),
            pltpu.VMEM((8, TOK, D), BF16),
            pltpu.VMEM((512, D), BF16),
            pltpu.VMEM((64, D), BF16),
        ]
        + scatter_scratch() * 2
        + [
            pltpu.VMEM((320, D), BF16),
            pltpu.VMEM((D, 256), BF16),
            pltpu.VMEM((64, 128), BF16),
            pltpu.VMEM((15, 64, 128), BF16),
            pltpu.VMEM((64, 128), BF16),
            pltpu.VMEM((8, D), F32),
            pltpu.VMEM((7, 8, 256), F32),
            pltpu.VMEM((8, 256), F32),
            pltpu.VMEM((16, 8, 256), F32),
        ]
        + two_sums_scratch(EARLY_ROWS)
        + sems(15 + 2 * SCATTER_EDGES + PLANE_EDGES + 4 * SUM_EDGES + 2)
        + [many((40,)), many, many((16,)), many, many((2,)), many((2,))]
        + [many((7,)), many, many((16,)), many, many((15,)), many, many((5,))],
        compiler_params=pltpu.CompilerParams(
            collective_id=3, has_side_effects=True, vmem_limit_bytes=61 * 2**20
        ),
        name="ending",
    )(
        dkv, dq, kv_table, wq, tokens, gain, grad_middle, gain_two, z_piece, x_piece, middle,
        gwo, xs, branch,
    )


def widen_kernel(z_ref, x_ref, wq_ref, wo_ref, gu_ref, dn_ref, gq_ref, go_ref):
    i = pl.program_id(0)

    @pl.when(i < 3)
    def _():
        gu_ref[...] = z_ref[...].astype(F32)

    @pl.when(i == 3)
    def _():
        gu_ref[...] = x_ref[...].astype(F32)

    @pl.when(i > 3)
    def _():
        dn_ref[...] = x_ref[...].astype(F32)

    gq_ref[...] = wq_ref[...].astype(F32)
    go_ref[...] = wo_ref[...].astype(F32).T


def widen(z_all, x_all, wq, wo):
    rows = PART // 3
    return pl.pallas_call(
        widen_kernel,
        out_shape=(
            shape((2 * FF_DEV, D), F32),
            shape((FF_DEV, D), F32),
            shape((320, D), F32),
            shape((256, D), F32),
        ),
        grid=(6,),
        in_specs=[
            pl.BlockSpec((rows, D), lambda i: (jnp.minimum(i, 2), 0)),
            pl.BlockSpec((rows, D), lambda i: (jnp.maximum(i - 3, 0), 0)),
            pl.BlockSpec((64, D), lambda i: (jnp.minimum(i, 4), 0)),
            pl.BlockSpec((512, 256), lambda i: (jnp.minimum(i, 3), 0)),
        ],
        out_specs=(
            pl.BlockSpec((rows, D), lambda i: (jnp.minimum(i, 3), 0)),
            pl.BlockSpec((rows, D), lambda i: (jnp.maximum(i - 4, 0), 0)),
            pl.BlockSpec((64, D), lambda i: (jnp.minimum(i, 4), 0)),
            pl.BlockSpec((256, 512), lambda i: (0, jnp.minimum(i, 3))),
        ),
        compiler_params=pltpu.CompilerParams(vmem_limit_bytes=61 * 2**20),
        name="widen",
    )(z_all, x_all, wq, wo)


def route(dz):
    pairs = []
    for i in range(128):
        z, xl, c, y, xh = i // 32, i // 16 % 2, i // 8 % 2, i // 2 % 4, i % 2
        if c != xh:
            pairs.append((i, (((((z + dz) % 4) * 2 + xl) * 2 + c) * 4 + y) * 2 + xh))
    return pairs


def body(hidden, positions, gain_attn, w_qkv, w_out, gain_mlp, w_gate_up, w_down, cotangent):
    gain_one = gain_attn.astype(F32).reshape(1, D)
    gain_two = gain_mlp.astype(F32).reshape(1, D)
    wgu = w_gate_up.reshape(2 * FF_DEV, D)
    wdn = w_down.T
    query, kv_table, trigs, runs, xs, wq, kvs, places, cots, wo, wswap = begin(
        hidden[0],
        gain_one,
        jnp.broadcast_to(positions, (8, TOK)),
        rotary_rows(positions[0]),
        w_qkv,
        wgu,
        wdn,
        cotangent[0],
        w_out,
    )
    wo = wo.reshape(D, Q_DEV)
    query_runs = runs[0, :16]
    key_runs = places[:, 0, :16].reshape(128)
    wnear_up = lax.ppermute(wswap, AXES, route(1))
    wnear_down = lax.ppermute(wswap, AXES, route(3))
    att, ot, lse = attend(key_runs, query_runs, query, kvs)
    middle, grad_middle, gain_grad, grad_att, grad_wo, z_piece, x_piece, branch = feed_forward(
        att, wo, hidden[0], cotangent[0], gain_two, cots, wgu, wdn, wswap, wnear_up, wnear_down
    )
    dq, dkv = attend_back(key_runs, query_runs, query, kvs, grad_att, ot, lse, trigs)
    output, grad_tokens, gains, grad_w_qkv, grad_w_out, z_all, x_all = ending(
        dkv,
        dq,
        kv_table,
        wq,
        hidden[0],
        gain_one,
        grad_middle,
        gain_grad,
        z_piece,
        x_piece,
        middle,
        grad_wo,
        xs,
        branch,
    )
    grad_gu, grad_dn, grad_w_qkv, grad_w_out = widen(z_all, x_all, grad_w_qkv, grad_w_out)
    return (
        output[None],
        grad_tokens[None],
        gains[0],
        grad_w_qkv,
        grad_w_out,
        gains[1],
        grad_gu.reshape(2, FF_DEV, D),
        grad_dn.T,
    )


def solution(mesh):
    fine = Mesh(mesh.devices.reshape(4, 2, 2, 4, 2), AXES)
    ctx, fsdp = ("z", "xl", "c"), ("y", "xh")
    weight = P(fsdp, None)
    return jax.shard_map(
        body,
        mesh=fine,
        in_specs=(
            P(fsdp, ctx, None),
            P(fsdp, ctx),
            P(),
            weight,
            weight,
            P(),
            P(None, fsdp, None),
            P(None, fsdp),
            P(fsdp, ctx, None),
        ),
        out_specs=(
            P(fsdp, ctx, None),
            P(fsdp, ctx, None),
            P(fsdp),
            weight,
            weight,
            P(fsdp),
            P(None, fsdp, None),
            P(None, fsdp),
        ),
        check_vma=False,
    )
```

```python
import jax
import jax.numpy as jnp
from jax import lax
from jax.experimental import pallas as pl
from jax.experimental.pallas import tpu as pltpu
from jax.sharding import Mesh
from jax.sharding import PartitionSpec as P

D = 2048
H = 32
KV = 4
HD = 64
FF = 5632
TOK = 128
HALF = 64
FF_DEV = 704
Q_DEV = 256
EPSILON = 1e-05
FILLER = -1e30
AXES = ("z", "xl", "c", "y", "xh")
ANY = pl.BlockSpec(memory_space=pl.ANY)
VMEM = pl.BlockSpec(memory_space=pltpu.VMEM)
BF16 = jnp.bfloat16
F32 = jnp.float32


class Place:
    def __init__(self):
        self.z, self.xl, self.c, self.y, self.xh = (lax.axis_index(a) for a in AXES)

    def at(self, dz=0, dy=0, core=None, xl=None, xh=None, y=None):
        z = lax.rem(self.z + dz + 4, 4) if dz else self.z
        y = (lax.rem(self.y + dy + 4, 4) if dy else self.y) if y is None else y
        return (
            z,
            self.xl if xl is None else xl,
            self.c if core is None else core,
            y,
            self.xh if xh is None else xh,
        )


class Edges:
    def __init__(self, send, recv):
        self.send, self.recv, self.count, self.started = send, recv, 0, []

    def copy(self, src, dst, device, start=True):
        i = self.count
        self.count += 1
        d = pltpu.make_async_remote_copy(
            src_ref=src,
            dst_ref=dst,
            send_sem=self.send.at[i],
            recv_sem=self.recv.at[i],
            device_id=device,
            device_id_type=pl.DeviceIdType.MESH,
        )
        self.started.append(d)
        if start:
            d.start()
        return d

    def sent(self, copies):
        for d in copies:
            d.wait_send()
        self.started = [d for d in self.started if all(d is not e for e in copies)]

    def finish(self):
        for d in self.started:
            d.wait_send()


def greet(devices):
    for device in devices:
        pl.semaphore_signal(
            pltpu.get_barrier_semaphore(),
            inc=1,
            device_id=device,
            device_id_type=pl.DeviceIdType.MESH,
        )
    return len(devices)


def met(count):
    pl.semaphore_wait(pltpu.get_barrier_semaphore(), count)


def group_members(me):
    found = [me.at(core=1 - me.c)]
    for dy in (1, 2, 3):
        found += [me.at(dy=dy), me.at(dy=dy, core=1 - me.c)]
    return found


class RingGather:
    def __init__(self, me, edges, own, out, local):
        self.me, self.edges, self.out = me, edges, out
        self.core = me.at(core=1 - me.c)
        self.up, self.down = me.at(dy=1), me.at(dy=-1)
        a, b = own.at[pl.ds(0, HALF)], own.at[pl.ds(HALF, HALF)]
        to_a, to_b = self.block(0, 0), self.block(0, 1)
        self.up_a = edges.copy(a, to_a, self.up)
        self.down_b = edges.copy(b, to_b, self.down)
        self.up_b = edges.copy(b, to_b, self.up)
        self.down_a = edges.copy(a, to_a, self.down)
        self.to_core = [edges.copy(a, to_a, self.core), edges.copy(b, to_b, self.core)]
        self.kept = [
            pltpu.make_async_copy(a, to_a, local.at[0]),
            pltpu.make_async_copy(b, to_b, local.at[1]),
        ]
        for d in self.kept:
            d.start()

    def block(self, dy, half):
        y = lax.rem(self.me.y + dy + 4, 4)
        rows = pl.ds(pl.multiple_of(HALF * self.me.c, HALF), HALF)
        return self.out.at[2 * y + half, rows]

    def pass_core(self, dy, half):
        ref = self.block(dy, half)
        self.to_core.append(self.edges.copy(ref, ref, self.core))

    def own(self):
        for d in self.kept:
            d.wait()
        self.from_core(0, 2)

    def relay(self):
        self.up_a.wait_recv()
        ref = self.block(-1, 0)
        self.on_a = self.edges.copy(ref, ref, self.up)
        self.pass_core(-1, 0)
        self.down_b.wait_recv()
        ref = self.block(1, 1)
        self.on_b = self.edges.copy(ref, ref, self.down)
        self.pass_core(1, 1)

    def near(self):
        self.up_b.wait_recv()
        self.pass_core(-1, 1)
        self.down_a.wait_recv()
        self.pass_core(1, 0)

    def far(self):
        self.on_a.wait_recv()
        self.pass_core(2, 0)
        self.on_b.wait_recv()
        self.pass_core(2, 1)

    def from_core(self, first, last):
        for d in self.to_core[first:last]:
            d.wait_recv()

    def rest(self):
        self.near()
        self.far()
        self.own()
        self.from_core(2, 8)

    def sources(self):
        return [self.up_a, self.up_b, self.down_a, self.down_b] + self.to_core[:2]


GATHER_EDGES = 14
GROUPS = (((0, 0), (0, 1)), ((3, 0), (1, 1)), ((3, 1), (1, 0)), ((2, 0), (2, 1)))


class RingScatter:
    def __init__(self, me, edges, parts, scratch):
        self.me, self.edges, self.parts = me, edges, parts
        self.got, self.both, self.relayed, self.last = scratch
        self.up, self.down = me.at(dy=1), me.at(dy=-1)
        self.cores = {}
        self.a, self.b = pl.ds(0, HALF), pl.ds(HALF, HALF)

    def send_core(self, k):
        row = 2 * lax.rem(self.me.y + k, 4) + 1 - self.me.c
        core = self.me.at(core=1 - self.me.c)
        self.cores[k] = self.edges.copy(self.parts.at[row], self.got.at[k], core)

    def add_core(self, k):
        self.cores[k].wait_recv()
        row = 2 * lax.rem(self.me.y + k, 4) + self.me.c

        def add(at):
            self.both[k, at] = (
                self.parts[row, at].astype(F32) + self.got[k, at].astype(F32)
            ).astype(BF16)

        in_chunks(add)

    def far(self):
        self.add_core(2)
        e, both = self.edges, self.both
        self.r_a = e.copy(both.at[2, self.a], self.relayed.at[0], self.up)
        self.r_b = e.copy(both.at[2, self.b], self.relayed.at[1], self.down)

    def near(self):
        e, both = self.edges, self.both
        self.add_core(1)
        self.u_b = e.copy(both.at[1, self.b], self.last.at[0, self.b], self.up)
        self.add_core(3)
        self.d_a = e.copy(both.at[3, self.a], self.last.at[1, self.a], self.down)

    def first(self):
        for k in (2, 1, 3, 0):
            self.send_core(k)
        self.far()
        self.near()
        self.add_core(0)

    def second(self):
        a, b, e, both = self.a, self.b, self.edges, self.both
        self.r_a.wait_recv()
        both[1, a] = (both[1, a].astype(F32) + self.relayed[0].astype(F32)).astype(BF16)
        self.u_a = e.copy(both.at[1, a], self.last.at[0, a], self.up)
        self.r_b.wait_recv()
        both[3, b] = (both[3, b].astype(F32) + self.relayed[1].astype(F32)).astype(BF16)
        self.d_b = e.copy(both.at[3, b], self.last.at[1, b], self.down)

    def arrived(self):
        for d in (self.u_b, self.d_a, self.u_a, self.d_b):
            d.wait_recv()

    def rows(self, at):
        return (
            self.both[0, at].astype(F32)
            + self.last[0, at].astype(F32)
            + self.last[1, at].astype(F32)
        )

    def release(self):
        ring = [self.r_a, self.r_b, self.u_b, self.d_a, self.u_a, self.d_b]
        self.edges.sent(ring + list(self.cores.values()))


SCATTER_EDGES = 10


def scatter_scratch():
    return [
        pltpu.VMEM((4, TOK, D), BF16),
        pltpu.VMEM((4, TOK, D), BF16),
        pltpu.VMEM((2, HALF, D), BF16),
        pltpu.VMEM((2, TOK, D), BF16),
    ]


def sems(n):
    return [pltpu.SemaphoreType.DMA((n,)), pltpu.SemaphoreType.DMA((n,))]


def shape(dims, dtype=BF16):
    return jax.ShapeDtypeStruct(dims, dtype)


def remote_params(number):
    return pltpu.CompilerParams(
        collective_id=number, has_side_effects=True, vmem_limit_bytes=61 * 2**20
    )


def block_place(block):
    is_kv = block >= 32
    other = block - 32
    rank = block // 4
    y = jnp.where(is_kv, lax.rem(other + 32, 4), rank // 2)
    core = jnp.where(is_kv, other // 4, lax.rem(rank, 2))
    return y, core, jnp.where(is_kv, 4, lax.rem(block, 4))


def own_block(me, j):
    if j == 4:
        return 32 + 4 * me.c + me.y
    return 4 * (2 * me.y + me.c) + j


def send_block(me, src, dst, send_sem, recv_sem, target, stays):
    @pl.when(stays)
    def _():
        pltpu.make_async_copy(src, dst, recv_sem).start()

    @pl.when(jnp.logical_not(stays))
    def _():
        pltpu.make_async_remote_copy(
            src_ref=src,
            dst_ref=dst,
            send_sem=send_sem,
            recv_sem=recv_sem,
            device_id=target,
            device_id_type=pl.DeviceIdType.MESH,
        ).start()


def wait_sent(src, send_sem, stays):
    @pl.when(jnp.logical_not(stays))
    def _():
        pltpu.make_async_copy(src, src, send_sem).wait()


def wait_got(dst, recv_sem):
    pltpu.make_async_copy(dst, dst, recv_sem).wait()


def x_of(me):
    return 2 * me.xh + me.xl


def around(me, dz, dx):
    x = lax.rem(x_of(me) + dx, 4)
    return me.at(dz=dz, xl=lax.rem(x, 2), xh=x // 2)


STEPS = [(dz, dx) for dz in range(4) for dx in range(4)][1:]


class SumOfSixteen:
    def __init__(self, me, src, piece, own, got, send, recv, local):
        self.me, self.src, self.piece, self.own, self.got = me, src, piece, own, got
        self.send, self.recv = send, recv
        self.keep = pltpu.make_async_copy(
            src.at[piece(4 * me.z + x_of(me))], own, local
        )
        self.keep.start()
        for k, (dz, dx) in enumerate(STEPS):
            to = 4 * lax.rem(me.z + dz, 4) + lax.rem(x_of(me) + dx, 4)
            self.copy(src.at[piece(to)], k, around(me, dz, dx)).start()

    def copy(self, src, k, device):
        return pltpu.make_async_remote_copy(
            src_ref=src,
            dst_ref=self.got.at[k],
            send_sem=self.send.at[k],
            recv_sem=self.recv,
            device_id=device,
            device_id_type=pl.DeviceIdType.MESH,
        )

    def total(self):
        self.keep.wait()
        pltpu.make_async_copy(self.got, self.got, self.recv).wait()
        total = self.own[...].astype(F32)
        for k in range(15):
            total = total + self.got[k].astype(F32)
        return total

    def finish(self):
        for k in range(15):
            src = self.src.at[self.piece(0)]
            pltpu.make_async_copy(src, src, self.send.at[k]).wait()


def same(me, z, xl, core, y, xh):
    return (z == me.z) & (xl == me.xl) & (core == me.c) & (y == me.y) & (xh == me.xh)


class Deliver:
    def __init__(self, me, send, recv):
        self.me, self.send, self.recv, self.sent = me, send, recv, []

    def to_owner(self, src, dst, core, y, xh):
        me = self.me
        for dz in range(4):
            for dl in (0, 1):
                z = lax.rem(me.z + dz, 4)
                xl = 1 - me.xl if dl else me.xl
                stays = same(me, z, xl, core, y, xh)
                sem = self.send.at[len(self.sent)]
                send_block(me, src, dst, sem, self.recv, (z, xl, core, y, xh), stays)
                self.sent.append((src, sem, stays))

    def finish(self):
        for src, sem, stays in self.sent:
            wait_sent(src, sem, stays)


def rotary_rows(places):
    steps = jnp.arange(HD // 2, dtype=F32)
    inverse = jnp.power(10000.0, steps * (-2.0 / HD))
    turning = places.astype(F32)[:, None] * inverse[None, :]
    rows = jnp.concatenate([jnp.cos(turning), jnp.sin(turning)], axis=1)
    return rows.reshape(2, 64, HD).transpose(1, 0, 2).reshape(64, 2 * HD)


def halves_swapped(rows):
    return jnp.concatenate([rows[:, HD // 2 :], rows[:, : HD // 2]], axis=1)


def rotate(rows, table, back=False):
    turned = halves_swapped(rows) * table[:, HD:]
    return rows * table[:, :HD] + (-turned if back else turned)


def rotary_of(rows, u):
    cosine = rows[:, HD * u : HD * u + HD // 2]
    sine = rows[:, HD * u + HD // 2 : HD * u + HD]
    return jnp.concatenate([cosine, cosine, -sine, sine], axis=1)


ROWS = 32


def in_chunks(step, rows=TOK, chunk=ROWS):
    def one(i, _):
        step(pl.ds(pl.multiple_of(i * chunk, chunk), chunk))
        return 0

    lax.fori_loop(0, rows // chunk, one, 0)


def mean_last(rows):
    return jnp.mean(rows, axis=-1, keepdims=True)


GU_QUARTER = 2 * FF_DEV // 4
DN_QUARTER = FF_DEV // 4
QUARTER = GU_QUARTER + DN_QUARTER


def swap_copies(me, wgu, wdn, wswap, send, recv):
    found = []
    across = me.at(core=1 - me.c, xl=1 - me.xl, xh=1 - me.xh)
    for i, (src, rows, start) in enumerate(
        ((wgu, GU_QUARTER, 0), (wdn, DN_QUARTER, GU_QUARTER))
    ):
        found.append(
            pltpu.make_async_remote_copy(
                src_ref=src.at[pl.ds(pl.multiple_of(rows * me.z, 16), rows)],
                dst_ref=wswap.at[pl.ds(start, rows)],
                send_sem=send.at[i],
                recv_sem=recv.at[i],
                device_id=across,
                device_id_type=pl.DeviceIdType.MESH,
            )
        )
    return found


def chips_in_sequence(me):
    return [(dz, dl) for dz in range(4) for dl in (0, 1)][1:]


def begin_kernel(
    tokens, gain, pos, trig, wqkv, wgu, wdn, cot, wout,
    q, kv_table, trigs, runs, xs_out, wq_out, kvs, places, cots, wo, wswap,
    low, xs, wq, kv, poss, own_runs,
    send, recv, qs, qr, os_, orr, ws, wr, local,
):
    me = Place()
    partner = {"xl": 1 - me.xl, "xh": 1 - me.xh}
    core = me.at(core=1 - me.c)
    members = group_members(me)
    others = [
        me.at(y=lax.rem(me.y + dy, 4), core=c, **partner) for dy in range(4) for c in (0, 1)
    ]
    far = [
        me.at(dz=dz, xl=(1 - me.xl) if dl else me.xl) for dz, dl in chips_in_sequence(me)
    ]
    signalled = greet(members + others + far)
    edges = Edges(send, recv)
    mine = 2 * me.y + me.c
    chip = 2 * me.z + me.xl

    def norm_rows():
        def norm(at):
            rows = tokens[at, :].astype(F32)
            inverse = lax.rsqrt(mean_last(rows * rows) + EPSILON)
            low[at, :] = (rows * inverse * gain[...]).astype(BF16)

        in_chunks(norm)

    spread = pl.ds(pl.multiple_of(512 * me.z, 512), 512)
    spread_rows = pl.ds(pl.multiple_of(64 * me.z, 64), 64)
    own = 2 * me.y + me.xh
    own_column = me.c == 0
    to_xl = jnp.where(own_column, me.xl, 1 - me.xl)
    to_xh = jnp.where(own_column, me.xh, 1 - me.xh)
    norm_rows()
    met(signalled)
    blocks = []
    for i in range(5):
        y, to_core, slot = block_place(5 * own + i)
        stays = own_column & (y == me.y) & (to_core == me.c)
        src = wqkv.at[pl.ds(64 * i, 64), spread]
        dst = wq.at[pl.ds(pl.multiple_of(64 * slot, 64), 64), spread]
        target = (me.z, to_xl, to_core, y, to_xh)
        send_block(me, src, dst, qs.at[i], qr.at[slot], target, stays)
        blocks.append((src, qs.at[i], stays))

    lane = lax.broadcasted_iota(jnp.int32, (8, TOK), 1)
    first = 4 * me.y + me.c
    run_numbers = jnp.where(
        lane == first,
        jnp.broadcast_to(pos[:, 0:1], (8, TOK)),
        jnp.where(lane == first + 2, jnp.broadcast_to(pos[:, 64:65], (8, TOK)), 0),
    )
    own_runs[...] = lax.shift_right_logical(run_numbers, 6)
    keep_pos = pltpu.make_async_copy(own_runs, poss.at[mine], local.at[1])
    keep_pos.start()
    pos_copies = [edges.copy(own_runs, poss.at[mine], m) for m in members]
    trigs[mine] = trig[...]
    trig_copies = [edges.copy(trig, trigs.at[mine], me.at(dy=k)) for k in (1, 2, 3)]
    trig_over = [edges.copy(trig, trigs.at[mine], core)]
    ring = RingGather(me, edges, low, xs, local.at[pl.ds(6, 2)])
    for i in range(8):
        dy, other = i // 2, i % 2
        y = lax.rem(me.y + dy, 4)
        to_core = me.c if other == 0 else 1 - me.c
        stays = own_column if i == 0 else me.c < 0
        cols = pl.ds(pl.multiple_of(Q_DEV * (2 * y + to_core), Q_DEV), Q_DEV)
        src = wout.at[spread_rows, cols]
        dst = wo.at[own, spread_rows]
        target = (me.z, to_xl, to_core, y, to_xh)
        send_block(me, src, dst, os_.at[i], orr.at[own], target, stays)
        blocks.append((src, os_.at[i], stays))
    moved = me.c != me.xh
    swaps = swap_copies(me, wgu, wdn, wswap, ws, wr)

    @pl.when(moved)
    def _():
        for d in swaps:
            d.start()

    for i in range(5):
        wait_got(wq.at[pl.ds(64 * i, 64), spread], qr.at[i])
    wq_copies = [
        edges.copy(wq.at[:, spread], wq.at[:, spread], me.at(dz=k)) for k in (1, 3, 2)
    ]
    for k, d in zip((1, 2, 3), trig_copies):
        d.wait_recv()
        ref = trigs.at[2 * lax.rem(me.y - k + 4, 4) + me.c]
        trig_over.append(edges.copy(ref, ref, core))
    ring.relay()
    for i in range(8):
        wait_got(wo.at[i, spread_rows], orr.at[i])
    ref = wo.at[:, spread_rows]
    wo_copies = [edges.copy(ref, ref, me.at(dz=k)) for k in (1, 3, 2)]
    keep_pos.wait()
    for d in pos_copies + trig_over:
        d.wait_recv()
    combined = poss[0]
    for i in range(1, 8):
        combined = combined + poss[i]
    runs[...] = combined
    for d in wq_copies:
        d.wait_recv()
    wq_save = pltpu.make_async_copy(wq, wq_out, local.at[2])
    wq_save.start()
    is_key = me.c == 0

    def compute(group):
        ys = [lax.rem(me.y + dy, 4) for dy, _ in group]
        rows = [xs[2 * y + u] for y, (_, u) in zip(ys, group)]
        projected = dot_last(jnp.concatenate(rows, axis=0), wq[...])
        for i, (y, (_, u)) in enumerate(zip(ys, group)):
            for half in (0, 1):
                rows = rotary_of(trigs[2 * y + half], u)
                at = TOK * i + 64 * half
                values = projected[at : at + 64]
                heads = [rotate(values[:, HD * h : HD * h + HD], rows) for h in range(4)]
                query = jnp.concatenate(heads, axis=1).astype(BF16)
                to = pl.ds(pl.multiple_of(2 * TOK * y + TOK * u + 64 * half, 64), 64)
                q[to, :] = (query.astype(F32) * 0.125).astype(BF16)
                rows = jnp.concatenate(
                    [
                        jnp.where(is_key, rows[:, :HD], 1.0),
                        jnp.where(is_key, rows[:, HD:], 0.0),
                    ],
                    axis=1,
                )
                to = pl.ds(pl.multiple_of(TOK * y + 64 * u, 64), 64)
                lanes = slice(HD * half, HD * half + HD)
                kv[to, lanes] = rotate(values[:, Q_DEV:], rows).astype(BF16)
                kv_table[0, to, lanes] = rows[:, :HD]
                kv_table[1, to, lanes] = rows[:, HD:]

    ring.own()
    compute(GROUPS[0])
    ring.near()
    ring.from_core(2, 4)
    compute(GROUPS[1])
    ring.from_core(4, 6)
    ring.far()
    compute(GROUPS[2])
    ring.from_core(6, 8)
    compute(GROUPS[3])

    keeps = [
        pltpu.make_async_copy(kv, kvs.at[me.c, chip], local.at[0]),
        pltpu.make_async_copy(runs, places.at[chip], local.at[1]),
        pltpu.make_async_copy(xs, xs_out, local.at[4]),
    ]
    for d in keeps:
        d.start()
    pos_copies = [edges.copy(runs, places.at[chip], d) for d in far]
    kv_copies = [edges.copy(kv, kvs.at[me.c, chip], d) for d in far]
    over = [edges.copy(kv, kvs.at[me.c, chip], core)]
    ring = RingGather(me, edges, cot, cots, local.at[pl.ds(6, 2)])
    ring.relay()
    for (dz, dl), d in zip(chips_in_sequence(me), kv_copies):
        d.wait_recv()
        source = 2 * lax.rem(me.z - dz + 4, 4) + ((1 - me.xl) if dl else me.xl)
        ref = kvs.at[me.c, source]
        over.append(edges.copy(ref, ref, core))
    ring.rest()
    for d in over + pos_copies + wo_copies:
        d.wait_recv()
    for src, sem, stays in blocks:
        wait_sent(src, sem, stays)

    @pl.when(moved)
    def _():
        for d in swaps:
            d.wait()

    edges.finish()
    for d in keeps + [wq_save]:
        d.wait()


def begin(tokens, gain, pos, trig, wqkv, wgu, wdn, cot, wout):
    return pl.pallas_call(
        begin_kernel,
        out_shape=(
            shape((1024, Q_DEV)),
            shape((2, 512, 128), F32),
            shape((8, 64, 128), F32),
            shape((8, TOK), jnp.int32),
            shape((8, TOK, D)),
            shape((320, D)),
            shape((2, 8, 512, 128)),
            shape((8, 8, TOK), jnp.int32),
            shape((8, TOK, D)),
            shape((8, 256, Q_DEV)),
            shape((QUARTER, D)),
        ),
        in_specs=[VMEM, VMEM, VMEM, VMEM] + [ANY] * 5,
        out_specs=(VMEM, VMEM, VMEM, VMEM) + (ANY,) * 7,
        scratch_shapes=[
            pltpu.VMEM((TOK, D), BF16),
            pltpu.VMEM((8, TOK, D), BF16),
            pltpu.VMEM((320, D), BF16),
            pltpu.VMEM((512, 128), BF16),
            pltpu.VMEM((8, 8, TOK), jnp.int32),
            pltpu.VMEM((8, TOK), jnp.int32),
        ]
        + sems(7 + 7 + 6 + 2 * GATHER_EDGES + 7 + 7 + 8)
        + sems(5)
        + sems(8)
        + sems(2)
        + [pltpu.SemaphoreType.DMA((8,))],
        compiler_params=remote_params(0),
        name="begin",
    )(tokens, gain, pos, trig, wqkv, wgu, wdn, cot, wout)


def split_heads(rows):
    return jnp.concatenate([rows[:, HD * h : HD * (h + 1)] for h in range(4)], axis=0)


def join_heads(rows):
    return jnp.concatenate([rows[64 * h : 64 * (h + 1), :] for h in range(4)], axis=1)


def dot_last(a, b):
    return lax.dot_general(a, b, (((1,), (1,)), ((), ())), preferred_element_type=F32)


def dot_first(a, b):
    return lax.dot_general(a, b, (((0,), (0,)), ((), ())), preferred_element_type=F32)


def dot(a, b):
    return lax.dot_general(a, b, (((1,), (0,)), ((), ())), preferred_element_type=F32)


TILE = 256
WIDE = 8


def run_rows(runs, seq, chip, core, u):
    run = runs[16 * chip + 4 * seq + 2 * u + core]
    return pl.ds(pl.multiple_of(run * 64, 64), 64)


def sort_keys(runs, seq, kv_ref, sorted_kv):
    for j in range(32):
        chip, core, u = j // 4, (j // 2) % 2, j % 2
        to = run_rows(runs, seq, chip, core, u)
        rows, lanes = slice(64 * u, 64 * u + 64), slice(HD * core, HD * core + HD)
        both = [kv_ref[0, chip, rows, lanes], kv_ref[1, chip, rows, lanes]]
        sorted_kv[to, :] = jnp.concatenate(both, axis=1)


def turn(rows, lanes, turned):
    for i in range(4):
        at = slice(512 * i, 512 * (i + 1))
        turned[:, at] = rows[at, lanes].astype(F32).T.astype(BF16)


def allowed_tile(tile, run):
    key = lax.broadcasted_iota(jnp.int32, (TILE, 256), 0) + tile * TILE
    query = lax.rem(lax.broadcasted_iota(jnp.int32, (TILE, 256), 1), 64) + run * 64
    return key <= query


def tile_rows(tile):
    return pl.ds(pl.multiple_of(tile * TILE, TILE), TILE)


def attend_kernel(
    key_runs, query_runs, q_ref, kv_ref, att_ref, ot_ref, lse_ref,
    sorted_kv, values_t, high_ref, total_ref, acc_ref,
):
    seq = pl.program_id(0)
    sort_keys(key_runs, seq, kv_ref, sorted_kv)
    turn(sorted_kv, slice(HD, 2 * HD), values_t)
    empty = jnp.zeros((HD, 256), BF16)

    def one_run(r, _):
        run = query_runs[seq * 4 + r]
        rows = pl.ds(pl.multiple_of(r * 64, 64), 64)
        query = split_heads(q_ref[rows, :]).astype(F32).T.astype(BF16)
        query = jnp.concatenate([query, empty], axis=0)
        last = run // 4
        high_ref[...] = jnp.full((1, 256), FILLER, F32)
        total_ref[...] = jnp.zeros((1, 256), F32)
        acc_ref[...] = jnp.zeros((HD, 256), F32)

        def tiles(first, count, masked):
            scores = []
            for k in range(count):
                score = dot(sorted_kv[tile_rows(first + k), :], query)
                if masked and k == count - 1:
                    score = jnp.where(allowed_tile(first + k, run), score, FILLER)
                scores.append(score)
            high = high_ref[...]
            new_high = high
            for score in scores:
                new_high = jnp.maximum(new_high, jnp.max(score, axis=0, keepdims=True))
            scale = jnp.exp(high - new_high)
            total = total_ref[...] * scale
            acc = acc_ref[...] * scale
            for k, score in enumerate(scores):
                weights = jnp.exp(score - new_high)
                total = total + jnp.sum(weights, axis=0, keepdims=True)
                acc = acc + dot(values_t[:, tile_rows(first + k)], weights.astype(BF16))
            high_ref[...] = new_high
            total_ref[...] = total
            acc_ref[...] = acc

        for n in range(WIDE):

            @pl.when(last == n)
            def _():
                tiles(0, n + 1, True)

        total = total_ref[...]
        out = acc_ref[...] / total
        ot_ref[r] = out
        lse_ref[r] = high_ref[...] + jnp.log(total)
        att_ref[rows, :] = join_heads(out.T).astype(BF16)
        return 0

    lax.fori_loop(0, 4, one_run, 0)


def attend(key_runs, query_runs, q, kv):
    return pl.pallas_call(
        attend_kernel,
        out_shape=(shape((1024, 256)), shape((16, HD, 256), F32), shape((16, 1, 256), F32)),
        grid_spec=pltpu.PrefetchScalarGridSpec(
            num_scalar_prefetch=2,
            grid=(4,),
            in_specs=[
                pl.BlockSpec((256, 256), lambda i, *_: (i, 0)),
                pl.BlockSpec((2, 8, 128, 128), lambda i, *_: (0, 0, i, 0)),
            ],
            out_specs=[
                pl.BlockSpec((256, 256), lambda i, *_: (i, 0)),
                pl.BlockSpec((4, HD, 256), lambda i, *_: (i, 0, 0)),
                pl.BlockSpec((4, 1, 256), lambda i, *_: (i, 0, 0)),
            ],
            scratch_shapes=[
                pltpu.VMEM((2048, 2 * HD), BF16),
                pltpu.VMEM((HD, 2048), BF16),
                pltpu.VMEM((1, 256), F32),
                pltpu.VMEM((1, 256), F32),
                pltpu.VMEM((HD, 256), F32),
            ],
        ),
        compiler_params=pltpu.CompilerParams(vmem_limit_bytes=61 * 2**20),
        name="attend",
    )(key_runs, query_runs, q, kv)


def attend_back_kernel(
    key_runs, query_runs, q_ref, kv_ref, da_ref, ot_ref, lse_ref, trig_ref,
    dq_ref, dkv_ref, sorted_kv, keys_t, grad_kv, dq_acc,
):
    seq = pl.program_id(0)
    sort_keys(key_runs, seq, kv_ref, sorted_kv)
    turn(sorted_kv, slice(0, HD), keys_t)
    grad_kv[...] = jnp.zeros_like(grad_kv)
    empty = jnp.zeros((HD, 256), BF16)
    blank = jnp.zeros((256, HD), BF16)

    def one_run(r, _):
        run = query_runs[seq * 4 + r]
        rows = pl.ds(pl.multiple_of(r * 64, 64), 64)
        query = split_heads(q_ref[rows, :])
        grad = split_heads(da_ref[rows, :])
        lse = lse_ref[r]
        query_t = query.astype(F32).T.astype(BF16)
        grad_t = grad.astype(F32).T
        delta = jnp.sum(grad_t * ot_ref[r], axis=0, keepdims=True)
        query_t = jnp.concatenate([query_t, empty], axis=0)
        grad_t = jnp.concatenate([empty, grad_t.astype(BF16)], axis=0)
        right = jnp.concatenate(
            [
                jnp.concatenate([query, blank], axis=1),
                jnp.concatenate([blank, grad], axis=1),
            ],
            axis=0,
        )
        last = run // 4
        dq_acc[...] = jnp.zeros((HD, 256), F32)

        def tiles(first, count, masked):
            dq = dq_acc[...]
            for k in range(count):
                at = tile_rows(first + k)
                both = sorted_kv[at, :]
                probs = jnp.exp(dot(both, query_t) - lse)
                if masked and k == count - 1:
                    probs = jnp.where(allowed_tile(first + k, run), probs, 0.0)
                grad_probs = dot(both, grad_t)
                grad_scores = (probs * (grad_probs - delta)).astype(BF16)
                left = jnp.concatenate([grad_scores, probs.astype(BF16)], axis=1)
                grad_kv[at, :] += dot(left, right)
                dq = dq + dot(keys_t[:, at], grad_scores)
            dq_acc[...] = dq

        for n in range(WIDE):

            @pl.when(last == n)
            def _():
                tiles(0, n + 1, True)

        pair_rows = trig_ref[lax.rem(r, 2)]
        table = jnp.where(r < 2, rotary_of(pair_rows, 0), rotary_of(pair_rows, 1))
        dq = (dq_acc[...] * 0.125).T
        heads = [rotate(dq[64 * h : 64 * h + 64], table, back=True) for h in range(4)]
        dq_ref[rows, :] = jnp.concatenate(heads, axis=1).astype(BF16)
        return 0

    lax.fori_loop(0, 4, one_run, 0)
    for j in range(32):
        chip, core, u = j // 4, (j // 2) % 2, j % 2
        at = run_rows(key_runs, seq, chip, core, u)
        rows, lanes = slice(64 * u, 64 * u + 64), slice(HD * core, HD * core + HD)
        both = grad_kv[at, :].astype(BF16)
        dkv_ref[0, chip, rows, lanes] = both[:, :HD]
        dkv_ref[1, chip, rows, lanes] = both[:, HD:]


def attend_back(key_runs, query_runs, q, kv, grad, ot, lse, trigs):
    return pl.pallas_call(
        attend_back_kernel,
        out_shape=(shape((1024, 256)), shape((2, 8, 512, 128))),
        grid_spec=pltpu.PrefetchScalarGridSpec(
            num_scalar_prefetch=2,
            grid=(4,),
            in_specs=[
                pl.BlockSpec((256, 256), lambda i, *_: (i, 0)),
                pl.BlockSpec((2, 8, 128, 128), lambda i, *_: (0, 0, i, 0)),
                pl.BlockSpec((256, 256), lambda i, *_: (i, 0)),
                pl.BlockSpec((4, HD, 256), lambda i, *_: (i, 0, 0)),
                pl.BlockSpec((4, 1, 256), lambda i, *_: (i, 0, 0)),
                pl.BlockSpec((2, 64, 128), lambda i, *_: (i, 0, 0)),
            ],
            out_specs=[
                pl.BlockSpec((256, 256), lambda i, *_: (i, 0)),
                pl.BlockSpec((2, 8, 128, 128), lambda i, *_: (0, 0, i, 0)),
            ],
            scratch_shapes=[
                pltpu.VMEM((2048, 2 * HD), BF16),
                pltpu.VMEM((HD, 2048), BF16),
                pltpu.VMEM((2048, 2 * HD), F32),
                pltpu.VMEM((HD, 256), F32),
            ],
        ),
        compiler_params=pltpu.CompilerParams(vmem_limit_bytes=61 * 2**20),
        name="attend_back",
    )(key_runs, query_runs, q, kv, grad, ot, lse, trigs)


PART = 3 * FF_DEV // 2
PART_HALF = PART // 2


class RingSum:
    def __init__(
        self, me, edges, along_z, src, start, rows, width, step, relayed, last, shift=0
    ):
        self.edges, self.src, self.start, self.width, self.step = edges, src, start, width, step
        self.rows, self.half = rows, rows // 2
        self.relayed, self.last, self.shift = relayed, last, shift
        self.here = me.z if along_z else x_of(me)
        self.up = around(me, 1, 0) if along_z else around(me, 0, 1)
        self.down = around(me, -1, 0) if along_z else around(me, 0, 3)
        self.a, self.b = pl.ds(0, self.half), pl.ds(self.half, self.half)

    def columns(self, k):
        at = self.width * lax.rem(self.here + k + self.shift, 4)
        return pl.ds(pl.multiple_of(at, self.width), self.width)

    def piece(self, k, half):
        rows = pl.ds(self.start + self.half * half, self.half)
        return self.src.at[rows, self.columns(k)]

    def far(self):
        self.r_a = self.edges.copy(self.piece(2, 0), self.relayed.at[0], self.up)
        self.r_b = self.edges.copy(self.piece(2, 1), self.relayed.at[1], self.down)

    def near_up(self):
        self.u_b = self.edges.copy(self.piece(1, 1), self.last.at[0, self.b], self.up)

    def near_down(self):
        self.d_a = self.edges.copy(self.piece(3, 0), self.last.at[1, self.a], self.down)

    def add(self, k, half):
        step, start, cols = self.step, self.start + self.half * half, self.columns(k)

        def one(i, _):
            at = pl.ds(pl.multiple_of(start + i * step, 16), step)
            from_ = pl.ds(pl.multiple_of(i * step, 16), step)
            self.src[at, cols] = (
                self.src[at, cols].astype(F32) + self.relayed[half, from_, :].astype(F32)
            ).astype(BF16)
            return 0

        lax.fori_loop(0, self.half // step, one, 0)

    def second(self):
        self.r_a.wait_recv()
        self.add(1, 0)
        self.u_a = self.edges.copy(self.piece(1, 0), self.last.at[0, self.a], self.up)
        self.r_b.wait_recv()
        self.add(3, 1)
        self.d_b = self.edges.copy(self.piece(3, 1), self.last.at[1, self.b], self.down)

    def total(self, out):
        for d in (self.u_b, self.d_a, self.u_a, self.d_b):
            d.wait_recv()
        step, cols = self.step, self.columns(0)

        def one(i, _):
            at = pl.ds(pl.multiple_of(self.start + i * step, 16), step)
            from_ = pl.ds(pl.multiple_of(i * step, 16), step)
            out[from_, :] = (
                self.src[at, cols].astype(F32)
                + self.last[0, from_, :].astype(F32)
                + self.last[1, from_, :].astype(F32)
            ).astype(BF16)
            return 0

        lax.fori_loop(0, self.rows // step, one, 0)


SUM_EDGES = 6


def to_chunks(ref, ys, halves, cols, rows):
    for i, (y, half) in enumerate(zip(ys, halves)):
        for core in (0, 1):
            at = TOK * i + HALF * core
            ref[2 * y + core, HALF * half : HALF * half + HALF, cols] = rows[at : at + HALF]


def feed_forward_kernel(
    att, wo, tokens, cot, gain, cots, wgu, wdn, wswap, wnear_up, wnear_down,
    middle, grad_middle, gain_grad, grad_att, grad_wo, z_out, x_out, branch,
    xs, p, c, gp, gb, att_t, w, act_t, gate_t, up_t, act, dgate, dup, low,
    g1, b1, r1, l1,
    z_relayed, z_last, x_relayed, x_last, z_q, x_q,
    z_relayed2, z_last2, x_relayed2, x_last2,
    send, recv, fs, fr, local,
):
    me = Place()
    core = me.at(core=1 - me.c)
    signalled = greet(
        [core, me.at(dy=1), me.at(dy=-1)]
        + [around(me, k, 0) for k in (1, 2, 3)]
        + [around(me, 0, 1), around(me, 0, 3)]
    )
    edges = Edges(send, recv)
    moved = me.c != me.xh
    load_c = pltpu.make_async_copy(cots, c, local.at[1])
    load_c.start()

    def w_rows(dz):
        z = lax.rem(me.z + dz + 4, 4)
        return (
            pl.ds(pl.multiple_of(GU_QUARTER * z, 16), GU_QUARTER),
            pl.ds(pl.multiple_of(2 * FF_DEV + DN_QUARTER * z, 16), DN_QUARTER),
        )

    gu_part, dn_part = pl.ds(0, GU_QUARTER), pl.ds(GU_QUARTER, DN_QUARTER)
    kept = [
        pltpu.make_async_copy(wgu, w.at[pl.ds(0, 2 * FF_DEV)], local.at[2]),
        pltpu.make_async_copy(wdn, w.at[pl.ds(2 * FF_DEV, FF_DEV)], local.at[3]),
    ]
    near_w = []
    for i, (src, dz) in enumerate(((wswap, 0), (wnear_up, -1), (wnear_down, 1))):
        gu_rows, dn_rows = w_rows(dz)
        near_w.append(pltpu.make_async_copy(src.at[gu_part], w.at[gu_rows], local.at[4 + 2 * i]))
        near_w.append(pltpu.make_async_copy(src.at[dn_part], w.at[dn_rows], local.at[5 + 2 * i]))
    far_w = [
        pltpu.make_async_remote_copy(
            src_ref=wswap.at[part],
            dst_ref=w.at[rows],
            send_sem=fs.at[i],
            recv_sem=fr.at[i],
            device_id=me.at(dz=2),
            device_id_type=pl.DeviceIdType.MESH,
        )
        for i, (part, rows) in enumerate(zip((gu_part, dn_part), w_rows(0)))
    ]

    met(signalled)

    @pl.when(moved)
    def _():
        for d in far_w + near_w:
            d.start()

    @pl.when(jnp.logical_not(moved))
    def _():
        for d in kept:
            d.start()

    ring = RingScatter(me, edges, p, (g1, b1, r1, l1))

    def attended_part(k):
        y = lax.rem(me.y + k, 4)
        rows = att[pl.ds(pl.multiple_of(2 * TOK * y, 2 * TOK), 2 * TOK), :]

        def block(i, _):
            cols = pl.ds(pl.multiple_of(512 * i, 512), 512)
            term = dot_last(rows, wo[cols, :]).astype(BF16)
            to_chunks(p, (y, y), (0, 1), cols, term)
            return 0

        lax.fori_loop(0, 4, block, 0)
        ring.send_core(k)

    attended_part(2)
    attended_part(1)
    ring.far()
    attended_part(3)
    ring.near()
    attended_part(0)
    ring.add_core(0)

    def turn_block(i, _):
        at = pl.ds(pl.multiple_of(2 * TOK * i, 2 * TOK), 2 * TOK)
        att_t[:, at] = att[at, :].astype(F32).T.astype(BF16)
        return 0

    lax.fori_loop(0, 4, turn_block, 0)
    ring.second()
    ring.arrived()

    def norm(at):
        rows = tokens[at, :].astype(F32) + ring.rows(at)
        middle[at, :] = rows
        normal = rows * lax.rsqrt(mean_last(rows * rows) + EPSILON)
        low[at, :] = (normal * gain[...]).astype(BF16)

    in_chunks(norm)
    gather = RingGather(me, edges, low, xs, local.at[pl.ds(10, 2)])
    ring.release()

    @pl.when(moved)
    def _():
        for d in near_w:
            d.wait()
        for d in far_w:
            d.wait()

    @pl.when(jnp.logical_not(moved))
    def _():
        for d in kept:
            d.wait()

    load_c.wait()

    def compute(group):
        ys = [lax.rem(me.y + dy, 4) for dy, _ in group]
        halves = [half for _, half in group]
        blocks = [2 * y + half for y, half in zip(ys, halves)]
        x = jnp.concatenate([xs[b] for b in blocks], axis=0)
        g = jnp.concatenate([c[b] for b in blocks], axis=0)
        here = [pl.ds(pl.multiple_of(TOK * b, TOK), TOK) for b in blocks]
        for n0, n1 in ((0, 256), (256, 512), (512, FF_DEV)):
            gate = dot_last(x, w[n0:n1, :])
            upward = dot_last(x, w[FF_DEV + n0 : FF_DEV + n1, :])
            grad = dot_last(g, w[2 * FF_DEV + n0 : 2 * FF_DEV + n1, :])
            sigmoid = 1.0 / (1.0 + jnp.exp(-gate))
            swish = gate * sigmoid
            active = swish * upward
            grad_up = grad * swish
            grad_gate = grad * upward * sigmoid * (1.0 + gate * (1.0 - sigmoid))
            act[:, n0:n1] = active.astype(BF16)
            dup[:, n0:n1] = grad_up.astype(BF16)
            dgate[:, n0:n1] = grad_gate.astype(BF16)
            for ref, value in ((act_t, active), (up_t, grad_up), (gate_t, grad_gate)):
                value = value.T.astype(BF16)
                ref[n0:n1, here[0]] = value[:, :TOK]
                ref[n0:n1, here[1]] = value[:, TOK:]

        def block(i, _):
            cols = pl.ds(pl.multiple_of(512 * i, 512), 512)
            term = dot(act[...], w[2 * FF_DEV :, cols])
            to_chunks(p, ys, halves, cols, term.astype(BF16))
            grads = dot(dgate[...], w[:FF_DEV, cols]) + dot(dup[...], w[FF_DEV : 2 * FF_DEV, cols])
            to_chunks(gp, ys, halves, cols, grads.astype(BF16))
            return 0

        lax.fori_loop(0, 4, block, 0)

    two = RingScatter(me, edges, gp, (g1, b1, r1, l1))
    gather.own()
    compute(GROUPS[0])
    two.send_core(0)
    gather.relay()
    gather.near()
    gather.from_core(2, 4)
    compute(GROUPS[1])
    gather.from_core(4, 6)
    gather.far()
    compute(GROUPS[2])
    two.send_core(1)
    two.send_core(3)
    two.near()
    gather.from_core(6, 8)
    compute(GROUPS[3])
    two.send_core(2)
    save = pltpu.make_async_copy(p, branch, local.at[0])
    save.start()
    two.add_core(0)

    z_sum = RingSum(me, edges, True, w, 0, PART, 512, 48, z_relayed, z_last)
    x_sum = RingSum(me, edges, False, w, PART, PART, 512, 48, x_relayed, x_last)
    split = PART - FF_DEV

    def z_task(k):
        cols = z_sum.columns(k)
        x = xs[:, :, cols].reshape(8 * TOK, 512)
        w[:FF_DEV, cols] = dot(gate_t[...], x).astype(BF16)
        w[FF_DEV:PART, cols] = dot(up_t[:split, :], x).astype(BF16)

    def x_task(k):
        cols = x_sum.columns(k)
        x = xs[:, :, cols].reshape(8 * TOK, 512)
        g = c[:, :, cols].reshape(8 * TOK, 512)
        w[PART : 2 * FF_DEV, cols] = dot(up_t[split:, :], x).astype(BF16)
        w[2 * FF_DEV :, cols] = dot(act_t[...], g).astype(BF16)

    two.far()
    z_task(2)
    z_sum.far()
    x_task(2)
    x_sum.far()
    z_task(1)
    z_sum.near_up()
    x_task(1)
    x_sum.near_up()
    two.second()
    z_task(3)
    z_sum.near_down()
    x_task(3)
    x_sum.near_down()
    z_task(0)
    x_task(0)
    two.arrived()
    gain_grad[...] = jnp.zeros_like(gain_grad)

    def back(at):
        rows = middle[at, :]
        inverse = lax.rsqrt(mean_last(rows * rows) + EPSILON)
        normal = rows * inverse
        grad = two.rows(at)
        gain_grad[...] += jnp.sum(normal * grad, axis=0, keepdims=True)
        scaled = grad * gain[...]
        result = cot[at, :].astype(F32) + inverse * (
            scaled - normal * mean_last(scaled * normal)
        )
        grad_middle[at, :] = result
        low[at, :] = result.astype(BF16)

    edges.sent(gather.sources())
    in_chunks(back)
    gather = RingGather(me, edges, low, gb, local.at[pl.ds(10, 2)])
    z_sum.second()
    x_sum.second()
    gather.relay()
    z_sum.total(z_q)
    z_two = RingSum(me, edges, False, z_q, 0, PART, 128, 176, z_relayed2, z_last2)
    z_two.far()
    z_two.near_up()
    z_two.near_down()
    x_sum.total(x_q)
    x_two = RingSum(me, edges, True, x_q, 0, PART, 128, 176, x_relayed2, x_last2)
    x_two.far()
    x_two.near_up()
    x_two.near_down()
    gather.near()
    gather.far()
    gather.own()
    gather.from_core(2, 8)

    def attended_grad(i, _):
        at = pl.ds(pl.multiple_of(2 * TOK * i, 2 * TOK), 2 * TOK)
        rows = gb[pl.ds(2 * i, 2)].reshape(2 * TOK, D)
        grad_att[at, :] = dot(rows, wo[...]).astype(BF16)
        cols = pl.ds(pl.multiple_of(512 * i, 512), 512)
        rows = gb[:, :, cols].reshape(8 * TOK, 512)
        grad_wo[:, cols] = dot(att_t[...], rows).astype(BF16)
        return 0

    lax.fori_loop(0, 4, attended_grad, 0)
    z_two.second()
    x_two.second()
    z_two.total(z_out)
    x_two.total(x_out)
    edges.finish()
    save.wait()


def feed_forward(att, wo, tokens, cot, gain, cots, wgu, wdn, wswap, wnear_up, wnear_down):
    block = pltpu.VMEM((8, TOK, D), BF16)
    turned = pltpu.VMEM((FF_DEV, 8 * TOK), BF16)
    pair = pltpu.VMEM((2 * TOK, FF_DEV), BF16)

    def ring(width):
        return [
            pltpu.VMEM((2, PART_HALF, width), BF16),
            pltpu.VMEM((2, PART, width), BF16),
        ] * 2

    return pl.pallas_call(
        feed_forward_kernel,
        out_shape=(
            shape((TOK, D), F32),
            shape((TOK, D), F32),
            shape((1, D), F32),
            shape((1024, Q_DEV)),
            shape((Q_DEV, D)),
            shape((PART, 128)),
            shape((PART, 128)),
            shape((8, TOK, D)),
        ),
        in_specs=[VMEM] * 5 + [ANY] * 6,
        out_specs=(VMEM,) * 7 + (ANY,),
        scratch_shapes=[block] * 5
        + [pltpu.VMEM((Q_DEV, 8 * TOK), BF16)]
        + [pltpu.VMEM((3 * FF_DEV, D), BF16)]
        + [turned] * 3
        + [pair] * 3
        + [pltpu.VMEM((TOK, D), BF16)]
        + scatter_scratch()
        + ring(512)
        + [pltpu.VMEM((PART, 512), BF16)] * 2
        + ring(128)
        + sems(2 * SCATTER_EDGES + 2 * GATHER_EDGES + 4 * SUM_EDGES)
        + sems(2)
        + [pltpu.SemaphoreType.DMA((12,))],
        compiler_params=pltpu.CompilerParams(
            collective_id=2, has_side_effects=True, vmem_limit_bytes=61 * 2**20
        ),
        name="feed_forward",
    )(att, wo, tokens, cot, gain, cots, wgu, wdn, wswap, wnear_up, wnear_down)


def columns(width):
    return lambda i: (slice(None), pl.ds(pl.multiple_of(i * width, width), width))


def row_block(height, start=0):
    return lambda i: (pl.ds(pl.multiple_of(start + i * height, height), height), slice(None))


def plane_devices(me):
    found = [me.at(core=1 - me.c)]
    for dz, dx in STEPS:
        z, xl, core, y, xh = around(me, dz, dx)
        found += [(z, xl, core, y, xh), (z, xl, 1 - core, y, xh)]
    return found


def swapped_pairs(rows):
    return jnp.concatenate([halves_swapped(rows[:, :HD]), halves_swapped(rows[:, HD:])], axis=1)


class RingBlocks:
    def __init__(self, me, edges, ref, columns):
        self.me, self.edges, self.ref, self.columns = me, edges, ref, columns
        rows = ref.shape[0]
        self.halves = (pl.ds(0, rows // 2), pl.ds(rows // 2, rows // 2))
        self.up, self.down = me.at(dz=1), me.at(dz=-1)
        self.up_a = self.send(0, 0, self.up)
        self.down_b = self.send(0, 1, self.down)
        self.up_b = self.send(0, 1, self.up)
        self.down_a = self.send(0, 0, self.down)

    def block(self, dz):
        return self.ref.at[:, self.columns(lax.rem(self.me.z + dz + 4, 4))]

    def send(self, dz, half, device):
        cols = self.columns(lax.rem(self.me.z + dz + 4, 4))
        ref = self.ref.at[self.halves[half], cols]
        return self.edges.copy(ref, ref, device)

    def relay(self):
        self.up_a.wait_recv()
        self.on_a = self.send(-1, 0, self.up)
        self.down_b.wait_recv()
        self.on_b = self.send(1, 1, self.down)

    def near(self):
        self.up_b.wait_recv()
        self.down_a.wait_recv()

    def far(self):
        self.on_a.wait_recv()
        self.on_b.wait_recv()


class PlaneGather:
    def __init__(self, me, edges, z_piece, x_piece, z_all, x_all, send, recv):
        self.me, self.edges, self.z_all, self.x_all = me, edges, z_all, x_all
        self.send, self.recv, self.z_piece, self.x_piece = send, recv, z_piece, x_piece
        self.stays = me.c == me.xh
        self.core = me.at(core=1 - me.c)
        self.side = me.at(xl=1 - me.xl)
        across = me.at(core=1 - me.c, xl=1 - me.xl, xh=1 - me.xh)
        x = x_of(me)
        self.held = jnp.where(self.stays, x, 3 - x)
        for i, (piece, ref, at) in enumerate(
            ((z_piece, z_all, 4 * me.z + x), (x_piece, x_all, 4 * x + me.z))
        ):
            dst = ref.at[columns(128)(at)]
            send_block(me, piece, dst, send.at[i], recv.at[i], across, self.stays)

    def z_columns(self, z):
        return pl.ds(pl.multiple_of(512 * z + 256 * self.me.c, 256), 256)

    def x_columns(self, z):
        return pl.ds(pl.multiple_of(512 * self.held + 128 * z, 128), 128)

    def side_block(self, dz):
        held = self.held + 1 - 2 * lax.rem(self.held, 2)
        z = lax.rem(self.me.z + dz + 4, 4)
        return self.x_all.at[columns(128)(4 * held + z)]

    def pass_core(self, ref):
        self.over.append(self.edges.copy(ref, ref, self.core))

    def sideways(self):
        own = self.z_all.at[columns(128)(4 * self.me.z + self.held)]
        wait_got(own, self.recv.at[0])
        self.z_side = self.edges.copy(own, own, self.side)
        own = self.x_all.at[:, self.x_columns(self.me.z)]
        wait_got(own, self.recv.at[1])
        self.x_ring = RingBlocks(self.me, self.edges, self.x_all, self.x_columns)
        self.x_side = [self.edges.copy(own, own, self.side)]
        self.over = []
        self.pass_core(own)

    def along(self):
        self.z_side.wait_recv()
        self.z_ring = RingBlocks(self.me, self.edges, self.z_all, self.z_columns)
        self.pass_core(self.z_ring.block(0))
        self.x_ring.relay()

    def to_side(self, dz):
        ref = self.x_ring.block(dz)
        self.x_side.append(self.edges.copy(ref, ref, self.side))

    def near(self):
        self.x_ring.near()
        self.to_side(1)
        self.to_side(-1)
        self.z_ring.relay()
        self.x_ring.far()
        self.to_side(2)
        for dz in (1, -1, 2):
            self.pass_core(self.x_ring.block(dz))

    def far(self):
        self.z_ring.near()
        self.pass_core(self.z_ring.block(1))
        self.pass_core(self.z_ring.block(-1))
        self.z_ring.far()
        self.pass_core(self.z_ring.block(2))
        for d, dz in zip(self.x_side, (0, 1, -1, 2)):
            d.wait_recv()
            self.pass_core(self.side_block(dz))

    def finish(self):
        for d in self.over:
            d.wait_recv()
        wait_sent(self.z_piece, self.send.at[0], self.stays)
        wait_sent(self.x_piece, self.send.at[1], self.stays)


PLANE_EDGES = 1 + 2 * SUM_EDGES + 4 + 12


class TwoSums:
    def __init__(self, me, edges, src, rows, steps, scratch):
        self.me, self.edges, self.rows, self.steps = me, edges, rows, steps
        self.q, self.out = scratch[4:6], scratch[10:12]
        self.scratch = scratch
        start = (0, rows[0])
        self.one = [
            RingSum(
                me, edges, i == 0, src, start[i], rows[i], 512, steps[0][i],
                scratch[2 * i], scratch[2 * i + 1], me.y,
            )
            for i in (0, 1)
        ]
        for ring in self.one:
            ring.far()
            ring.near_up()
            ring.near_down()

    def second(self):
        for ring in self.one:
            ring.second()

    def cross(self):
        self.two = []
        for i in (0, 1):
            self.one[i].total(self.q[i])
            ring = RingSum(
                self.me, self.edges, i == 1, self.q[i], 0, self.rows[i], 128,
                self.steps[1][i], self.scratch[6 + 2 * i], self.scratch[7 + 2 * i],
            )
            ring.far()
            ring.near_up()
            ring.near_down()
            self.two.append(ring)

    def fourth(self):
        for ring in self.two:
            ring.second()

    def total(self):
        for i in (0, 1):
            self.two[i].total(self.out[i])


def two_sums_scratch(rows):
    found = []
    for r in rows:
        found += [pltpu.VMEM((2, r // 2, 512), BF16), pltpu.VMEM((2, r, 512), BF16)]
    found += [pltpu.VMEM((r, 512), BF16) for r in rows]
    for r in rows:
        found += [pltpu.VMEM((2, r // 2, 128), BF16), pltpu.VMEM((2, r, 128), BF16)]
    return found + [pltpu.VMEM((r, 128), BF16) for r in rows]


EARLY_ROWS = (256, 256)


def ending_kernel(
    dkv, dq, kv_table, wq, tokens, gain, grad_middle, gain_two, z_piece, x_piece, middle,
    gwo, xs_in, branch_in,
    output, grad_tokens, gains, wq_out, wo_out, z_all, x_all,
    kv_got, kv_both, kv_last, dkv_low, xs, grads, grads_t, parts, branch_parts, early, late,
    g1, b1, r1, l1, g2, b2, r2, l2,
    wq_all, wo_all, late_own, late_got, late_piece, mine, near, near_sum, owners,
    *rest,
):
    early_scratch = rest[:12]
    (send, recv, ds, dr, es, er, ps, pr, gs, gr, hs, hr, us, ur, local) = rest[12:]
    me = Place()
    core = me.at(core=1 - me.c)
    far = [
        me.at(dz=dz, xl=(1 - me.xl) if dl else me.xl) for dz, dl in chips_in_sequence(me)
    ]
    signalled = greet(plane_devices(me) + group_members(me)[1:])
    edges = Edges(send, recv)
    place = 4 * me.z + x_of(me)
    rank = 2 * me.y + me.c
    load_x = pltpu.make_async_copy(xs_in, xs, local.at[0])
    load_branch = pltpu.make_async_copy(branch_in, branch_parts, local.at[1])
    load_wo = [
        pltpu.make_async_copy(
            gwo.at[pl.ds(128 * i, 128)], early.at[pl.ds(256 * i + 128, 128)], local.at[2 + i]
        )
        for i in (0, 1)
    ]
    for d in [load_x, load_branch] + load_wo:
        d.start()

    def query_part(i, _):
        at = pl.ds(pl.multiple_of(2 * TOK * i, 2 * TOK), 2 * TOK)
        rows = dq[at, :]
        grads[at, :Q_DEV] = rows
        grads_t[:Q_DEV, at] = rows.astype(F32).T.astype(BF16)
        return 0

    lax.fori_loop(0, 4, query_part, 0)
    met(signalled)

    order = []
    for dz, dl in chips_in_sequence(me) + [(0, 0)]:
        chip = 2 * lax.rem(me.z + dz, 4) + ((1 - me.xl) if dl else me.xl)
        order.append((chip, edges.copy(dkv.at[1 - me.c, chip], kv_got.at[chip], core)))
    load_branch.wait()
    branch = RingScatter(me, edges, branch_parts, (g2, b2, r2, l2))
    for k in (2, 1, 3, 0):
        branch.send_core(k)
    far_copies = []
    for i, (chip, d) in enumerate(order):
        d.wait_recv()
        kv_both[chip] = (dkv[me.c, chip].astype(F32) + kv_got[chip].astype(F32)).astype(BF16)
        if i < 7:
            far_copies.append(edges.copy(kv_both.at[chip], kv_last.at[i], far[i]))
    plane = PlaneGather(me, edges, z_piece, x_piece, z_all, x_all, ps, pr)
    load_x.wait()

    def weight_block(i, _):
        cols = pl.ds(pl.multiple_of(512 * i, 512), 512)
        rows = xs[:, :, cols].reshape(8 * TOK, 512)
        early[:128, cols] = dot(grads_t[:128, :], rows).astype(BF16)
        early[256:384, cols] = dot(grads_t[128:Q_DEV, :], rows).astype(BF16)
        return 0

    lax.fori_loop(0, 4, weight_block, 0)
    for d in load_wo:
        d.wait()
    early_sum = TwoSums(me, edges, early, EARLY_ROWS, ((64, 64), (128, 128)), early_scratch)
    branch.far()
    branch.near()
    branch.add_core(0)
    for d in far_copies:
        d.wait_recv()

    def kv_total(at):
        total = kv_both[2 * me.z + me.xl, at].astype(F32)
        for i in range(7):
            total = total + kv_last[i, at].astype(F32)
        dkv_low[at, :] = (
            total * kv_table[0, at, :] - swapped_pairs(total) * kv_table[1, at, :]
        )

    in_chunks(kv_total, 512, 128)
    for i in range(8):
        rows = dkv_low[64 * i : 64 * (i + 1), :]
        rows = jnp.concatenate([rows[:, :HD], rows[:, HD:]], axis=0)
        at = slice(TOK * i, TOK * (i + 1))
        grads[at, Q_DEV:] = rows.astype(BF16)
        grads_t[Q_DEV:, at] = rows.T.astype(BF16)

    early_sum.second()
    branch.second()
    def late_block(i, _):
        cols = pl.ds(pl.multiple_of(512 * i, 512), 512)
        rows = xs[:, :, cols].reshape(8 * TOK, 512)
        late[:, cols] = dot(grads_t[Q_DEV:, :], rows).astype(BF16)
        return 0

    ring = RingScatter(me, edges, parts, (g1, b1, r1, l1))

    def part(k):
        y = lax.rem(me.y + k, 4)
        rows = grads[pl.ds(pl.multiple_of(2 * TOK * y, 2 * TOK), 2 * TOK), :]

        def block(i, _):
            cols = pl.ds(pl.multiple_of(512 * i, 512), 512)
            to_chunks(parts, (y, y), (0, 1), cols, dot(rows, wq[:, cols]).astype(BF16))
            return 0

        lax.fori_loop(0, 4, block, 0)
        ring.send_core(k)

    part(2)
    part(1)
    ring.far()
    early_sum.cross()
    part(3)
    ring.near()
    part(0)
    ring.add_core(0)
    early_sum.fourth()
    plane.sideways()
    lax.fori_loop(0, 4, late_block, 0)
    late_sum = SumOfSixteen(me, late, columns(128), late_own, late_got, us, ur, local.at[4])
    early_sum.total()
    wq_deliver = Deliver(me, ds, dr)

    def deliver_block(j, src, at):
        block = own_block(me, j)
        owner, slot = block // 5, lax.rem(block, 5)
        dst = wq_all.at[
            pl.ds(pl.multiple_of(64 * slot, 64), 64),
            pl.ds(pl.multiple_of(128 * at, 128), 128),
        ]
        wq_deliver.to_owner(src, dst, at // 8, owner // 2, lax.rem(owner, 2))

    wo_deliver = Deliver(me, es, er)
    early_place = 4 * lax.rem(me.z + me.y, 4) + x_of(me)
    early_turned = 4 * lax.rem(x_of(me) + me.y, 4) + me.z
    for i, at in enumerate((early_place, early_turned)):
        for j in (0, 1):
            deliver_block(2 * i + j, early_sum.out[i].at[pl.ds(64 * j, 64)], at)
        dst = wo_all.at[
            pl.ds(pl.multiple_of(Q_DEV * rank + 128 * i, 128), 128),
            pl.ds(pl.multiple_of(128 * lax.rem(at, 2), 128), 128),
        ]
        src = early_sum.out[i].at[pl.ds(128, 128)]
        wo_deliver.to_owner(src, dst, me.y // 2, at // 4, lax.rem(at // 2, 2))
    plane.along()
    late_piece[...] = late_sum.total().astype(BF16)
    deliver_block(4, late_piece, place)
    ring.second()
    plane.near()
    branch.arrived()

    def out(at):
        output[at, :] = (middle[at, :] + branch.rows(at)).astype(BF16)

    in_chunks(out)
    ring.arrived()
    mine[...] = jnp.zeros_like(mine)
    mine[1:2, :] = gain_two[...]

    def back(at):
        rows = tokens[at, :].astype(F32)
        inverse = lax.rsqrt(mean_last(rows * rows) + EPSILON)
        normal = rows * inverse
        grad = ring.rows(at)
        mine[0:1, :] += jnp.sum(normal * grad, axis=0, keepdims=True)
        scaled = grad * gain[...]
        grad_tokens[at, :] = grad_middle[at, :] + inverse * (
            scaled - normal * mean_last(scaled * normal)
        )

    in_chunks(back)

    def slice_of(member):
        return mine.at[:, pl.ds(pl.multiple_of(256 * member, 256), 256)]

    near_copies = []
    for k in range(1, 8):
        dy, other = k // 2, k % 2
        y = lax.rem(me.y + dy, 4)
        to_core = 1 - me.c if other else me.c
        d = pltpu.make_async_remote_copy(
            src_ref=slice_of(2 * y + to_core),
            dst_ref=near.at[k - 1],
            send_sem=gs.at[k - 1],
            recv_sem=gr,
            device_id=me.at(y=y, core=to_core),
            device_id_type=pl.DeviceIdType.MESH,
        )
        d.start()
        near_copies.append(d)
    plane.far()
    own = mine[:, pl.ds(pl.multiple_of(256 * rank, 256), 256)]
    wait_got(near, gr)
    for k in range(7):
        own = own + near[k]
    near_sum[...] = own
    gain_deliver = Deliver(me, hs, hr)
    for to_core in (0, 1):
        gain_deliver.to_owner(near_sum, owners.at[place], to_core, me.y, me.c)

    half = pl.ds(pl.multiple_of(1024 * me.c, 1024), 1024)
    over = []
    for ref, sem in ((wo_all.at[half], er), (wq_all.at[:, half], dr)):
        wait_got(ref, sem)
        over.append(edges.copy(ref, ref, core))
    wait_got(owners, hr)
    sum_all = owners[0]
    for k in range(1, 16):
        sum_all = sum_all + owners[k]
    gains[...] = sum_all
    for d in over:
        d.wait_recv()
    wo_out[...] = wo_all[...]
    wq_out[...] = wq_all[...]
    plane.finish()
    late_sum.finish()
    for d in (wo_deliver, wq_deliver, gain_deliver):
        d.finish()
    for d in near_copies:
        d.wait_send()
    edges.finish()


def ending(
    dkv, dq, kv_table, wq, tokens, gain, grad_middle, gain_two, z_piece, x_piece, middle,
    gwo, xs, branch,
):
    many = pltpu.SemaphoreType.DMA
    return pl.pallas_call(
        ending_kernel,
        out_shape=(
            shape((TOK, D)),
            shape((TOK, D), F32),
            shape((8, 256), F32),
            shape((320, D)),
            shape((D, 256)),
            shape((PART, D)),
            shape((PART, D)),
        ),
        in_specs=[VMEM] * 11 + [ANY] * 3,
        out_specs=(VMEM,) * 5 + (ANY,) * 2,
        scratch_shapes=[
            pltpu.VMEM((8, 512, 128), BF16),
            pltpu.VMEM((8, 512, 128), BF16),
            pltpu.VMEM((7, 512, 128), BF16),
            pltpu.VMEM((512, 128), F32),
            pltpu.VMEM((8, TOK, D), BF16),
            pltpu.VMEM((1024, 320), BF16),
            pltpu.VMEM((320, 1024), BF16),
            pltpu.VMEM((8, TOK, D), BF16),
            pltpu.VMEM((8, TOK, D), BF16),
            pltpu.VMEM((512, D), BF16),
            pltpu.VMEM((64, D), BF16),
        ]
        + scatter_scratch() * 2
        + [
            pltpu.VMEM((320, D), BF16),
            pltpu.VMEM((D, 256), BF16),
            pltpu.VMEM((64, 128), BF16),
            pltpu.VMEM((15, 64, 128), BF16),
            pltpu.VMEM((64, 128), BF16),
            pltpu.VMEM((8, D), F32),
            pltpu.VMEM((7, 8, 256), F32),
            pltpu.VMEM((8, 256), F32),
            pltpu.VMEM((16, 8, 256), F32),
        ]
        + two_sums_scratch(EARLY_ROWS)
        + sems(15 + 2 * SCATTER_EDGES + PLANE_EDGES + 4 * SUM_EDGES + 2)
        + [many((40,)), many, many((16,)), many, many((2,)), many((2,))]
        + [many((7,)), many, many((16,)), many, many((15,)), many, many((5,))],
        compiler_params=pltpu.CompilerParams(
            collective_id=3, has_side_effects=True, vmem_limit_bytes=61 * 2**20
        ),
        name="ending",
    )(
        dkv, dq, kv_table, wq, tokens, gain, grad_middle, gain_two, z_piece, x_piece, middle,
        gwo, xs, branch,
    )


def widen_kernel(
    z_ref, x_ref, wq_ref, wo_ref, out_ref, tokens_ref, gains_ref,
    gu_ref, dn_ref, gq_ref, go_ref, output_ref, grad_ref, one_ref, two_ref,
):
    i = pl.program_id(0)
    output_ref[...] = out_ref[...]
    grad_ref[...] = tokens_ref[...]
    one_ref[...] = gains_ref[0:1, :]
    two_ref[...] = gains_ref[1:2, :]

    @pl.when(i < 3)
    def _():
        gu_ref[...] = z_ref[...].astype(F32)

    @pl.when(i == 3)
    def _():
        gu_ref[...] = x_ref[...].astype(F32)

    @pl.when(i > 3)
    def _():
        dn_ref[...] = x_ref[...].astype(F32)

    gq_ref[...] = wq_ref[...].astype(F32)
    go_ref[...] = wo_ref[...].astype(F32).T


def widen(z_all, x_all, wq, wo, output, grad_tokens, gains):
    rows = PART // 3
    return pl.pallas_call(
        widen_kernel,
        out_shape=(
            shape((2 * FF_DEV, D), F32),
            shape((FF_DEV, D), F32),
            shape((320, D), F32),
            shape((256, D), F32),
            shape((TOK, D)),
            shape((TOK, D), F32),
            shape((1, 256), F32),
            shape((1, 256), F32),
        ),
        grid=(6,),
        in_specs=[
            pl.BlockSpec((rows, D), lambda i: (jnp.minimum(i, 2), 0)),
            pl.BlockSpec((rows, D), lambda i: (jnp.maximum(i - 3, 0), 0)),
            pl.BlockSpec((64, D), lambda i: (jnp.minimum(i, 4), 0)),
            pl.BlockSpec((512, 256), lambda i: (jnp.minimum(i, 3), 0)),
            pl.BlockSpec((32, D), lambda i: (jnp.minimum(i, 3), 0)),
            pl.BlockSpec((32, D), lambda i: (jnp.minimum(i, 3), 0)),
            pl.BlockSpec((8, 256), lambda i: (0, 0)),
        ],
        out_specs=(
            pl.BlockSpec((rows, D), lambda i: (jnp.minimum(i, 3), 0)),
            pl.BlockSpec((rows, D), lambda i: (jnp.maximum(i - 4, 0), 0)),
            pl.BlockSpec((64, D), lambda i: (jnp.minimum(i, 4), 0)),
            pl.BlockSpec((256, 512), lambda i: (0, jnp.minimum(i, 3))),
            pl.BlockSpec((32, D), lambda i: (jnp.minimum(i, 3), 0)),
            pl.BlockSpec((32, D), lambda i: (jnp.minimum(i, 3), 0)),
            pl.BlockSpec((1, 256), lambda i: (0, 0)),
            pl.BlockSpec((1, 256), lambda i: (0, 0)),
        ),
        compiler_params=pltpu.CompilerParams(vmem_limit_bytes=61 * 2**20),
        name="widen",
    )(z_all, x_all, wq, wo, output, grad_tokens, gains)


def route(dz):
    pairs = []
    for i in range(128):
        z, xl, c, y, xh = i // 32, i // 16 % 2, i // 8 % 2, i // 2 % 4, i % 2
        if c != xh:
            pairs.append((i, (((((z + dz) % 4) * 2 + xl) * 2 + c) * 4 + y) * 2 + xh))
    return pairs


def body(hidden, positions, gain_attn, w_qkv, w_out, gain_mlp, w_gate_up, w_down, cotangent):
    gain_one = gain_attn.astype(F32).reshape(1, D)
    gain_two = gain_mlp.astype(F32).reshape(1, D)
    wgu = w_gate_up.reshape(2 * FF_DEV, D)
    wdn = w_down.T
    query, kv_table, trigs, runs, xs, wq, kvs, places, cots, wo, wswap = begin(
        hidden[0],
        gain_one,
        jnp.broadcast_to(positions, (8, TOK)),
        rotary_rows(positions[0]),
        w_qkv,
        wgu,
        wdn,
        cotangent[0],
        w_out,
    )
    wo = wo.reshape(D, Q_DEV)
    query_runs = runs[0, :16]
    key_runs = places[:, 0, :16].reshape(128)
    wnear_up = lax.ppermute(wswap, AXES, route(1))
    wnear_down = lax.ppermute(wswap, AXES, route(3))
    att, ot, lse = attend(key_runs, query_runs, query, kvs)
    middle, grad_middle, gain_grad, grad_att, grad_wo, z_piece, x_piece, branch = feed_forward(
        att, wo, hidden[0], cotangent[0], gain_two, cots, wgu, wdn, wswap, wnear_up, wnear_down
    )
    dq, dkv = attend_back(key_runs, query_runs, query, kvs, grad_att, ot, lse, trigs)
    output, grad_tokens, gains, grad_w_qkv, grad_w_out, z_all, x_all = ending(
        dkv,
        dq,
        kv_table,
        wq,
        hidden[0],
        gain_one,
        grad_middle,
        gain_grad,
        z_piece,
        x_piece,
        middle,
        grad_wo,
        xs,
        branch,
    )
    grad_gu, grad_dn, grad_w_qkv, grad_w_out, output, grad_tokens, gain_a, gain_b = widen(
        z_all, x_all, grad_w_qkv, grad_w_out, output, grad_tokens, gains
    )
    return (
        output[None],
        grad_tokens[None],
        gain_a.reshape(256),
        grad_w_qkv,
        grad_w_out,
        gain_b.reshape(256),
        grad_gu.reshape(2, FF_DEV, D),
        grad_dn.T,
    )


def solution(mesh):
    fine = Mesh(mesh.devices.reshape(4, 2, 2, 4, 2), AXES)
    ctx, fsdp = ("z", "xl", "c"), ("y", "xh")
    weight = P(fsdp, None)
    return jax.shard_map(
        body,
        mesh=fine,
        in_specs=(
            P(fsdp, ctx, None),
            P(fsdp, ctx),
            P(),
            weight,
            weight,
            P(),
            P(None, fsdp, None),
            P(None, fsdp),
            P(fsdp, ctx, None),
        ),
        out_specs=(
            P(fsdp, ctx, None),
            P(fsdp, ctx, None),
            P(fsdp),
            weight,
            weight,
            P(fsdp),
            P(None, fsdp, None),
            P(None, fsdp),
        ),
        check_vma=False,
    )
```
